32 devices in a mesh: scen: 8 (over z, core), row: 4 (over y, x).
Axes of the slice: x: 2, y: 2, z: 4, core: 2. Of those that a mesh axis runs over, the one named last changes fastest.
Arguments:
- coupling: bfloat16 [8, 1536, 4096], P('scen', None, 'row'), may hold values from -40 to 40
- solves: bfloat16 [8, 1536, 512], P('scen', 'row'), may hold values from -1.25 to 1.25
- border_diagonal: float32 [1024, 4], P('scen', 'row'), may hold values from 32 to 64
- panel_rows: int32 [512], replicated, may hold values from 0 to 4095, as said below
Outputs:
- first_factor: float32 [1024, 4, 256], P('scen', 'row')
- second_factor: float32 [1024, 4, 256], P('scen', 'row')
The draws below stay inside these ranges and needn't reach their ends.
Inputs may be any that keep to these rules, and one draw needn't show every extreme that they name: `panel_rows`: 512 distinct border rows; the first 256 are the first panel's pivot rows and columns, the rest the second's.
All inputs are finite; a program needn't handle non-finite values. Where the reference program divides by a largest or mean magnitude, that divisor is 1e-20 or more.
Results may differ from the reference program's by a relative error of at most 0.0003.
Values may be sent and summed in bfloat16 or wider, within the bound.
No kernel may reach another device: no remote copies, remote signals or barrier semaphores. Data moves between devices by JAX's collectives and lax.ppermute only.
A program may use at most 64 MiB of HBM per device.

```python
import math
import jax
import jax.numpy as jnp
from jax import lax

NLOC = 1536
HALF = 256
NEWTON = 8
ROW_DEV = 1024
PANEL = 512
SCENARIOS = 8
BORDER = 4096
N_ROW = 4


def pick_panel(key):
    key_pick = jax.random.fold_in(key, 11)
    key_order = jax.random.fold_in(key, 12)
    inner = jax.random.permutation(key_pick, BORDER - 2)[:PANEL - 2].astype(jnp.int32) + 1
    ends = jnp.array([0, BORDER - 1], dtype=jnp.int32)
    whole = jnp.concatenate([inner, ends])
    return whole[jax.random.permutation(key_order, PANEL)]


def draw_panel_rows(key, part):
    return pick_panel(key)


def draw_coupling(key, part):
    chosen = pick_panel(key)
    glob = jnp.arange(BORDER, dtype=jnp.int32)
    is_pivot = jnp.any(glob[:, None] == chosen[None, :], axis=1)
    key_scale = jax.random.fold_in(key, 21)
    key_value = jax.random.fold_in(key, 22)
    logs = jax.random.uniform(key_scale, (BORDER,), jnp.float32, jnp.log(64.0), jnp.log(256.0))
    column_scale = jnp.where(is_pivot, jnp.float32(1.0), jnp.exp(logs))
    values = jnp.clip(jax.random.normal(key_value, (SCENARIOS, NLOC, BORDER), jnp.float32), -6.0, 6.0)
    scaled = values * float(NLOC) ** (-0.5) * column_scale[None, None, :]
    scaled = jnp.clip(scaled, -40.0, 40.0)
    return scaled.astype(jnp.bfloat16)


def level_of(stream_key, shape, split, smallest, largest):
    def one(dim, blocks):
        steps = jax.random.uniform(jax.random.fold_in(jax.random.fold_in(stream_key, 6), dim), (blocks,), jnp.float32, smallest / len(split), largest / len(split))
        return jnp.repeat(jnp.exp(steps), shape[dim] // blocks).reshape((-1,) + (1,) * (len(shape) - dim - 1))

    factor_of = one(*split[0])
    for cut in split[1:]:
        factor_of = factor_of * one(*cut)
    return factor_of


def scatter_about(rng, dims, scale, bound, cuts=(), held_as=jnp.bfloat16):
    values = jax.random.normal(rng, dims, jnp.float32) * scale
    if len(cuts) > 0:
        values = level_of(rng, dims, cuts, -0.22, 0.18) * values
    return jnp.clip(values, min=-bound, max=bound).astype(held_as)


def setup_inputs(seed: int = 0) -> dict:
    keys = jax.random.split(jax.random.key(seed), 5)
    return {
        "coupling": draw_coupling(jax.random.fold_in(keys[4], 71), 0),
        "solves": scatter_about(keys[1], (SCENARIOS, NLOC, PANEL), (0.25 / SCENARIOS ** 0.5), 1.25, ((0, 8), (1, 4))),
        "border_diagonal": jnp.clip(jnp.exp(math.log(64.0) - 0.6931472 * jax.random.uniform(keys[2], (ROW_DEV, N_ROW), jnp.float32) ** level_of(keys[2], (ROW_DEV, N_ROW), ((0, 8), (1, 4)), -0.2, 0.2)), 32.0, 64.0),
        "panel_rows": draw_panel_rows(jax.random.fold_in(keys[4], 71), 0),
    }


def newton(pivot):
    norm_one = jnp.max(jnp.sum(jnp.abs(pivot), axis=0))
    norm_inf = jnp.max(jnp.sum(jnp.abs(pivot), axis=1))
    approx = pivot.T / (norm_one * norm_inf)
    for step in range(NEWTON):
        left = jnp.dot(approx, pivot, precision=lax.Precision.HIGHEST)
        approx = 2.0 * approx - jnp.dot(left, approx, precision=lax.Precision.HIGHEST)
    return approx


def reference(coupling, solves, border_diagonal, panel_rows):
    def add_one(total, pair):
        block, result = pair
        return total + jnp.dot(block.T, result, preferred_element_type=jnp.float32), None

    schur, unused = lax.scan(add_one, jnp.zeros((BORDER, PANEL), jnp.float32), (coupling, solves))
    glob = jnp.arange(BORDER, dtype=jnp.int32)
    diag_flat = border_diagonal.T.reshape(BORDER)
    schur = schur + jnp.where(glob[:, None] == panel_rows[None, :], diag_flat[:, None], jnp.float32(0.0))
    pivots = schur[panel_rows]
    inverse_first = newton(pivots[:HALF, :HALF])
    first_factor = jnp.dot(schur[:, :HALF], inverse_first, precision=lax.Precision.HIGHEST)
    updated = schur[:, HALF:] - jnp.dot(first_factor, pivots[:HALF, HALF:], precision=lax.Precision.HIGHEST)
    inverse_second = newton(updated[panel_rows[HALF:]])
    second_factor = jnp.dot(updated, inverse_second, precision=lax.Precision.HIGHEST)
    first_out = first_factor.reshape(N_ROW, ROW_DEV, HALF).transpose(1, 0, 2)
    second_out = second_factor.reshape(N_ROW, ROW_DEV, HALF).transpose(1, 0, 2)
    return first_out, second_out
```

```python
import functools

import jax
import jax.numpy as jnp
from jax import lax
from jax.experimental import pallas as pl
from jax.experimental.pallas import tpu as pltpu
from jax.sharding import PartitionSpec as P

HALF = 256
NEWTON = 8
BOTH = ("scen", "row")
F32 = jnp.float32
BF16 = jnp.bfloat16


def halves(a):
    high = a.astype(BF16)
    low = (a - high.astype(F32)).astype(BF16)
    return high, low


def left_of(a):
    high, low = halves(a)
    return jnp.concatenate([high, high, low], axis=1)


def right_of(b):
    high, low = halves(b)
    return jnp.concatenate([high, low, high], axis=0)


def dot(a, b):
    return jnp.dot(a, b, preferred_element_type=F32)


def product(a, b):
    return dot(left_of(a), right_of(b))


def newton(pivot):
    size = jnp.abs(pivot)
    norm_one = jnp.max(jnp.sum(size, axis=0, keepdims=True))
    norm_inf = jnp.max(jnp.sum(size, axis=1, keepdims=True))
    approx = pivot.T / (norm_one * norm_inf)
    pivot_right = right_of(pivot)
    for step in range(NEWTON):
        left = dot(left_of(approx), pivot_right)
        approx = 2.0 * approx - product(left, approx)
    return approx


def first_kernel(pivot_ref, inverse_ref):
    inverse_ref[...] = newton(pivot_ref[...])


def second_kernel(inverse_first_ref, upper_ref, lower_ref, corner_ref, inverse_ref):
    lower_factor = product(lower_ref[...], inverse_first_ref[...])
    inverse_ref[...] = newton(corner_ref[...] - product(lower_factor, upper_ref[...]))


def factor_kernel(first_ref, second_ref, inverse_first_ref, inverse_second_ref, upper_ref, first_out, second_out):
    first_factor = product(first_ref[...], inverse_first_ref[...])
    updated = second_ref[...] - product(first_factor, upper_ref[...])
    first_out[...] = first_factor[:, None, :]
    second_out[...] = product(updated, inverse_second_ref[...])[:, None, :]


def in_vmem(kernel, out_shape, flops, *args):
    spec = pl.BlockSpec(memory_space=pltpu.VMEM)
    return pl.pallas_call(
        kernel,
        out_shape=out_shape,
        in_specs=[spec] * len(args),
        out_specs=jax.tree.map(lambda _: spec, out_shape),
        compiler_params=pltpu.CompilerParams(vmem_limit_bytes=24 * 1024 * 1024),
        cost_estimate=pl.CostEstimate(flops=flops, bytes_accessed=1 << 20, transcendentals=0),
    )(*args)


def swap(x, axis, bit):
    count = lax.axis_size(axis)
    return lax.ppermute(x, axis, [(i, i ^ bit) for i in range(count)])


def gather_rows(block, flip):
    count = lax.axis_size("row")
    bits = [1 << i for i in range(count.bit_length() - 1)]
    held = {0: block}
    for bit in reversed(bits) if flip else bits:
        keys = sorted(held)
        sent = held[keys[0]] if len(keys) == 1 else jnp.concatenate([held[k] for k in keys], axis=0)
        got = jnp.split(swap(sent, "row", bit), len(keys), axis=0)
        held.update({k ^ bit: piece for k, piece in zip(keys, got)})
    return jnp.concatenate([held[k] for k in range(count)], axis=0)


def exchange_sum(x, axis, step=1):
    count = x.shape[0]
    place = lax.axis_index(axis) // step
    total = lax.dynamic_index_in_dim(x, place, 0, keepdims=False)
    for k in range(1, count):
        total = total + swap(lax.dynamic_index_in_dim(x, place ^ k, 0, keepdims=False), axis, k * step)
    return total


def exchange_gather(piece, axis, count, step=1):
    place = lax.axis_index(axis) // step
    out = jnp.zeros((count,) + piece.shape, piece.dtype)
    out = lax.dynamic_update_index_in_dim(out, piece, place, 0)
    for k in range(1, count):
        out = lax.dynamic_update_index_in_dim(out, swap(piece, axis, k * step), place ^ k, 0)
    return out


def sum_at_once(x):
    devices = lax.axis_size("scen") * lax.axis_size("row")
    rows = x.shape[0]
    if rows % (8 * devices):
        return lax.psum(x, BOTH)
    pieces = x.reshape(devices, rows // devices, -1)
    own = jnp.sum(lax.all_to_all(pieces, BOTH, 0, 0, tiled=True), axis=0)
    everyone = jnp.broadcast_to(own[None], (devices,) + own.shape)
    return lax.all_to_all(everyone, BOTH, 0, 0, tiled=True).reshape(x.shape)


def sum_in_stages(x):
    scen, row = lax.axis_size("scen"), lax.axis_size("row")
    rows = x.shape[0]
    if rows % (8 * scen * row):
        return lax.psum(x, BOTH)
    core = lax.axis_index("scen") % 2
    pair = x.reshape(2, rows // 2, -1)
    part = lax.dynamic_index_in_dim(pair, core, 0, keepdims=False)
    part = part + swap(lax.dynamic_index_in_dim(pair, 1 - core, 0, keepdims=False), "scen", 1)
    part = exchange_sum(part.reshape(row, part.shape[0] // row, -1), "row")
    layers = scen // 2
    part = exchange_sum(part.reshape(layers, part.shape[0] // layers, -1), "scen", 2)
    part = exchange_gather(part, "scen", layers, 2).reshape(-1, x.shape[1])
    part = exchange_gather(part, "row", row).reshape(-1, x.shape[1])
    other = swap(part, "scen", 1)
    return jnp.where(core == 0, jnp.concatenate([part, other]), jnp.concatenate([other, part]))


def scatter_sum(x):
    scen = lax.axis_size("scen")
    layers = scen // 2
    place = lax.axis_index("scen")
    layer, core = place // 2, place % 2
    pieces = x.reshape(layers, 2, x.shape[0] // scen, -1)
    mine = lax.dynamic_index_in_dim(pieces, core, 1, keepdims=False)
    theirs = lax.dynamic_index_in_dim(pieces, 1 - core, 1, keepdims=False)
    mine = mine + swap(theirs, "scen", 1)
    total = lax.dynamic_index_in_dim(mine, layer, 0, keepdims=False)
    for way in (1, -1):
        carried = None
        for step in range(1, layers):
            index = jnp.clip(layer + way * (layers - step), 0, layers - 1)
            sent = lax.dynamic_index_in_dim(mine, index, 0, keepdims=False)
            if carried is not None:
                sent = sent + carried
            senders = range(step) if way == 1 else range(layers - step, layers)
            pairs = [(2 * i + c, 2 * (i + way) + c) for i in senders for c in range(2)]
            carried = lax.ppermute(sent, "scen", pairs)
        total = total + carried
    return total


def shards(coupling, solves, border_diagonal, panel_rows):
    half = HALF
    coupling, solves = coupling[0], solves[0]
    local, row_count = coupling.shape
    block = solves.shape[0]
    panel = solves.shape[1]
    scen, rows = lax.axis_size("scen"), lax.axis_size("row")
    row = lax.axis_index("row")
    share = row_count // scen
    base = row * row_count + lax.axis_index("scen") * share
    quarter = half // 2

    gathered = [gather_rows(solves[:, i * quarter:(i + 1) * quarter], i % 2 == 1) for i in range(panel // quarter)]
    solves_first = jnp.concatenate(gathered[:2], axis=1)
    solves_second = jnp.concatenate(gathered[2:], axis=1)

    coupling_t = jnp.concatenate(
        [lax.dynamic_slice_in_dim(coupling, (row ^ k) * block, block, 0) for k in range(rows)], axis=0
    ).T
    columns = row * row_count + jnp.arange(row_count, dtype=jnp.int32)
    chosen = (panel_rows[:, None] == columns[None, :]).astype(BF16)
    picked = dot(chosen, coupling_t).astype(BF16)

    glob = base + jnp.arange(share, dtype=jnp.int32)
    at_diagonal = panel_rows[:, None] == glob[None, :]
    diagonal = jnp.sum(jnp.where(at_diagonal, border_diagonal[:, 0][None, :], F32(0.0)), axis=1)
    on_diagonal = jnp.where(jnp.eye(panel, dtype=bool), diagonal[:, None], F32(0.0))

    pivots_left = dot(picked, solves_first) + on_diagonal[:, :half]
    pivot_first = sum_at_once(pivots_left[:half])
    lower = sum_in_stages(pivots_left[half:])
    right = sum_in_stages(dot(picked, solves_second) + on_diagonal[:, half:])
    upper, corner = right[:half], right[half:]

    diag_part = jnp.where(at_diagonal.T, border_diagonal[:, 0][:, None], F32(0.0))
    first = scatter_sum(dot(coupling_t, solves_first)) + diag_part[:, :half]
    second = scatter_sum(dot(coupling_t, solves_second)) + diag_part[:, half:]

    square = jax.ShapeDtypeStruct((half, half), F32)
    inverse_first = in_vmem(first_kernel, square, 2 * 16 * 3 * half**3, pivot_first)
    inverse_second = in_vmem(second_kernel, square, 2 * 18 * 3 * half**3, inverse_first, upper, lower, corner)
    out = jax.ShapeDtypeStruct((share, 1, half), F32)
    return in_vmem(
        factor_kernel, (out, out), 2 * 9 * share * half**2, first, second, inverse_first, inverse_second, upper
    )


def solution(mesh):
    placed = (P("scen", None, "row"), P("scen", "row", None), P("scen", "row"), P())
    return jax.shard_map(
        shards,
        mesh=mesh,
        in_specs=placed,
        out_specs=(P("scen", "row", None), P("scen", "row", None)),
        check_vma=False,
    )
```

```python
import functools

import jax
import jax.numpy as jnp
from jax import lax
from jax.experimental import pallas as pl
from jax.experimental.pallas import tpu as pltpu
from jax.sharding import PartitionSpec as P

HALF = 256
NEWTON = 8
BOTH = ("scen", "row")
F32 = jnp.float32
BF16 = jnp.bfloat16


def halves(a):
    high = a.astype(BF16)
    low = (a - high.astype(F32)).astype(BF16)
    return high, low


def left_of(a):
    high, low = halves(a)
    return jnp.concatenate([high, high, low], axis=1)


def right_of(b):
    high, low = halves(b)
    return jnp.concatenate([high, low, high], axis=0)


def dot(a, b):
    return jnp.dot(a, b, preferred_element_type=F32)


def product(a, b):
    return dot(left_of(a), right_of(b))


def newton(pivot):
    size = jnp.abs(pivot)
    norm_one = jnp.max(jnp.sum(size, axis=0, keepdims=True))
    norm_inf = jnp.max(jnp.sum(size, axis=1, keepdims=True))
    approx = pivot.T / (norm_one * norm_inf)
    pivot_right = right_of(pivot)
    for step in range(NEWTON):
        left = dot(left_of(approx), pivot_right)
        approx = 2.0 * approx - product(left, approx)
    return approx


def first_kernel(pivot_ref, inverse_ref):
    inverse_ref[...] = newton(pivot_ref[...])


def second_kernel(inverse_first_ref, upper_ref, lower_ref, corner_ref, inverse_ref):
    lower_factor = product(lower_ref[...], inverse_first_ref[...])
    inverse_ref[...] = newton(corner_ref[...] - product(lower_factor, upper_ref[...]))


def factor_kernel(first_ref, second_ref, inverse_first_ref, inverse_second_ref, upper_ref, first_out, second_out):
    first_factor = product(first_ref[...], inverse_first_ref[...])
    updated = second_ref[...] - product(first_factor, upper_ref[...])
    first_out[...] = first_factor[:, None, :]
    second_out[...] = product(updated, inverse_second_ref[...])[:, None, :]


def in_vmem(kernel, out_shape, flops, *args):
    spec = pl.BlockSpec(memory_space=pltpu.VMEM)
    return pl.pallas_call(
        kernel,
        out_shape=out_shape,
        in_specs=[spec] * len(args),
        out_specs=jax.tree.map(lambda _: spec, out_shape),
        compiler_params=pltpu.CompilerParams(vmem_limit_bytes=24 * 1024 * 1024),
        cost_estimate=pl.CostEstimate(flops=flops, bytes_accessed=1 << 20, transcendentals=0),
    )(*args)


def swap(x, axis, bit):
    count = lax.axis_size(axis)
    return lax.ppermute(x, axis, [(i, i ^ bit) for i in range(count)])


def everyone(x, count):
    return jnp.broadcast_to(x[None], (count,) + x.shape)


def by_core(rows):
    scen = lax.axis_size("scen")
    return [[s * rows + r for s in range(c, scen, 2) for r in range(rows)] for c in range(2)]


def trade(x, axis, groups=None):
    return lax.all_to_all(x, axis, 0, 0, axis_index_groups=groups, tiled=True)


def sum_at_once(x):
    devices = lax.axis_size("scen") * lax.axis_size("row")
    rows = x.shape[0]
    if rows % (8 * devices):
        return lax.psum(x, BOTH)
    own = jnp.sum(trade(x.reshape(devices, rows // devices, -1), BOTH), axis=0)
    return trade(everyone(own, devices), BOTH).reshape(x.shape)


def sum_by_core(x):
    scen, row = lax.axis_size("scen"), lax.axis_size("row")
    rows, devices = x.shape[0], scen * row // 2
    if rows % (16 * devices):
        return lax.psum(x, BOTH)
    core = lax.axis_index("scen") % 2
    pair = x.reshape(2, rows // 2, -1)
    part = lax.dynamic_index_in_dim(pair, core, 0, keepdims=False)
    part = part + swap(lax.dynamic_index_in_dim(pair, 1 - core, 0, keepdims=False), "scen", 1)
    groups = by_core(row)
    own = jnp.sum(trade(part.reshape(devices, rows // 2 // devices, -1), BOTH, groups), axis=0)
    part = trade(everyone(own, devices), BOTH, groups).reshape(part.shape)
    other = swap(part, "scen", 1)
    return jnp.where(core == 0, jnp.concatenate([part, other]), jnp.concatenate([other, part]))


def scatter_sum(x):
    scen = lax.axis_size("scen")
    core = lax.axis_index("scen") % 2
    pieces = x.reshape(scen // 2, 2, x.shape[0] // scen, -1)
    mine = lax.dynamic_index_in_dim(pieces, core, 1, keepdims=False)
    theirs = lax.dynamic_index_in_dim(pieces, 1 - core, 1, keepdims=False)
    mine = mine + swap(theirs, "scen", 1)
    groups = [list(range(c, scen, 2)) for c in range(2)]
    return jnp.sum(trade(mine, "scen", groups), axis=0)


def shards(coupling, solves, border_diagonal, panel_rows):
    half = HALF
    coupling, solves = coupling[0], solves[0]
    local, row_count = coupling.shape
    panel = solves.shape[1]
    scen, rows = lax.axis_size("scen"), lax.axis_size("row")
    row = lax.axis_index("row")
    share = row_count // scen
    base = row * row_count + lax.axis_index("scen") * share

    solves_first = trade(everyone(solves[:, :half], rows), "row").reshape(local, half)
    solves_second = trade(everyone(solves[:, half:], rows), "row").reshape(local, panel - half)

    coupling_t = coupling.T
    columns = row * row_count + jnp.arange(row_count, dtype=jnp.int32)
    chosen = (panel_rows[:, None] == columns[None, :]).astype(BF16)
    picked = dot(chosen, coupling_t).astype(BF16)

    glob = base + jnp.arange(share, dtype=jnp.int32)
    at_diagonal = panel_rows[:, None] == glob[None, :]
    diagonal = jnp.sum(jnp.where(at_diagonal, border_diagonal[:, 0][None, :], F32(0.0)), axis=1)
    on_diagonal = jnp.where(jnp.eye(panel, dtype=bool), diagonal[:, None], F32(0.0))

    pivots_left = dot(picked, solves_first) + on_diagonal[:, :half]
    pivots_right = dot(picked, solves_second) + on_diagonal[:, half:]
    pivot_first = sum_at_once(pivots_left[:half])
    rest = sum_by_core(jnp.concatenate([pivots_left[half:], pivots_right]))
    lower, upper, corner = rest[:half], rest[half:2 * half], rest[2 * half:]

    diag_part = jnp.where(at_diagonal.T, border_diagonal[:, 0][:, None], F32(0.0))
    solves_all = jnp.concatenate([solves_first, solves_second], axis=1)
    own_rows = scatter_sum(dot(coupling_t, solves_all)) + diag_part
    first, second = own_rows[:, :half], own_rows[:, half:]

    square = jax.ShapeDtypeStruct((half, half), F32)
    inverse_first = in_vmem(first_kernel, square, 2 * 16 * 3 * half**3, pivot_first)
    inverse_second = in_vmem(second_kernel, square, 2 * 18 * 3 * half**3, inverse_first, upper, lower, corner)
    out = jax.ShapeDtypeStruct((share, 1, half), F32)
    return in_vmem(
        factor_kernel, (out, out), 2 * 9 * share * half**2, first, second, inverse_first, inverse_second, upper
    )


def solution(mesh):
    placed = (P("scen", None, "row"), P("scen", "row", None), P("scen", "row"), P())
    return jax.shard_map(
        shards,
        mesh=mesh,
        in_specs=placed,
        out_specs=(P("scen", "row", None), P("scen", "row", None)),
        check_vma=False,
    )
```

```python
import functools

import jax
import jax.numpy as jnp
from jax import lax
from jax.experimental import pallas as pl
from jax.experimental.pallas import tpu as pltpu
from jax.sharding import PartitionSpec as P

HALF = 256
NEWTON = 8
F32 = jnp.float32
BF16 = jnp.bfloat16


def halves(a):
    high = a.astype(BF16)
    low = (a - high.astype(F32)).astype(BF16)
    return high, low


def left_of(a):
    high, low = halves(a)
    return jnp.concatenate([high, high, low], axis=1)


def right_of(b):
    high, low = halves(b)
    return jnp.concatenate([high, low, high], axis=0)


def dot(a, b):
    return jnp.dot(a, b, preferred_element_type=F32)


def product(a, b):
    return dot(left_of(a), right_of(b))


def newton(pivot):
    size = jnp.abs(pivot)
    norm_one = jnp.max(jnp.sum(size, axis=0, keepdims=True))
    norm_inf = jnp.max(jnp.sum(size, axis=1, keepdims=True))
    approx = pivot.T / (norm_one * norm_inf)
    pivot_right = right_of(pivot)
    for step in range(NEWTON):
        left = dot(left_of(approx), pivot_right)
        approx = 2.0 * approx - product(left, approx)
    return approx


def place_blocks(place_ref, own_ref, other_ref, rows_ref, blocks):
    size = rows_ref.shape[0] // blocks
    for k in range(blocks):
        source = own_ref if k < blocks // 2 else other_ref
        start = k % (blocks // 2) * size
        target = pl.multiple_of((place_ref[0] ^ k) * size, size)
        rows_ref[pl.ds(target, size), :] = source[start:start + size, :]


def first_kernel(blocks, place_ref, own_ref, other_ref, inverse_ref, lower_ref, rows_ref):
    place_blocks(place_ref, own_ref, other_ref, rows_ref, blocks)
    half = inverse_ref.shape[0]
    lower_ref[...] = rows_ref[half:, :]
    inverse_ref[...] = newton(rows_ref[:half, :])


def second_kernel(
    blocks, place_ref, own_ref, other_ref, inverse_first_ref, lower_ref, inverse_ref, upper_ref, rows_ref
):
    place_blocks(place_ref, own_ref, other_ref, rows_ref, blocks)
    half = inverse_ref.shape[0]
    upper = rows_ref[:half, :]
    upper_ref[...] = upper
    lower_factor = product(lower_ref[...], inverse_first_ref[...])
    inverse_ref[...] = newton(rows_ref[half:, :] - product(lower_factor, upper))


def factor_kernel(first_ref, second_ref, inverse_first_ref, inverse_second_ref, upper_ref, first_out, second_out):
    first_factor = product(first_ref[...], inverse_first_ref[...])
    updated = second_ref[...] - product(first_factor, upper_ref[...])
    first_out[...] = first_factor[:, None, :]
    second_out[...] = product(updated, inverse_second_ref[...])[:, None, :]


def pivot_kernel(picked_ref, diagonal_ref, *refs):
    *pieces, solves_ref, keep_ref, send_ref = refs
    start = 0
    for piece in pieces:
        solves_ref[start:start + piece.shape[0], :] = piece[...]
        start += piece.shape[0]
    total = dot(picked_ref[...], solves_ref[...]) + diagonal_ref[...]
    half = keep_ref.shape[0]
    keep_ref[...] = total[:half]
    send_ref[...] = total[half:]


def schur_kernel(order, place_ref, coupling_ref, first_ref, second_ref, keep_ref, send_ref):
    layer, core = place_ref[0], place_ref[1]
    size = keep_ref.shape[0] // len(order)
    half = first_ref.shape[1]
    for out_ref, whose in ((keep_ref, core), (send_ref, 1 - core)):
        for position, k in enumerate(order):
            start = pl.multiple_of((2 * (layer ^ k) + whose) * size, size)
            block = coupling_ref[pl.ds(start, size), :]
            rows = slice(position * size, (position + 1) * size)
            out_ref[rows, :half] = dot(block, first_ref[...])
            out_ref[rows, half:] = dot(block, second_ref[...])


def in_vmem(kernel, out_shape, flops, *args, scratch=(), scalars=0):
    vmem = pl.BlockSpec(memory_space=pltpu.VMEM)
    smem = pl.BlockSpec(memory_space=pltpu.SMEM)
    return pl.pallas_call(
        kernel,
        out_shape=out_shape,
        in_specs=[smem] * scalars + [vmem] * (len(args) - scalars),
        out_specs=jax.tree.map(lambda _: vmem, out_shape),
        scratch_shapes=scratch,
        compiler_params=pltpu.CompilerParams(vmem_limit_bytes=28 * 1024 * 1024),
        cost_estimate=pl.CostEstimate(flops=flops, bytes_accessed=1 << 20, transcendentals=0),
    )(*args)


def swap(x, axis, bit):
    count = lax.axis_size(axis)
    return lax.ppermute(x, axis, [(i, i ^ bit) for i in range(count)])


def after(x, *others):
    return lax.optimization_barrier((x,) + others)[0]


def bits_of(count):
    return [1 << i for i in range(count.bit_length() - 1)]


def gather_pieces(block, rows):
    if rows != 4:
        return [lax.all_gather(block, "row", axis=0, tiled=True)], block
    along_x, along_y = swap(block, "row", 1), swap(block, "row", 2)
    half = block.shape[0] // 2
    far = [swap(along_y[:half], "row", 1), swap(along_x[half:], "row", 2)]
    return [block, along_x, along_y] + far, along_y


def sum_pivots(keep, send, rows, layers):
    part = keep + swap(send, "scen", 1)
    for bit in bits_of(rows):
        half = part.shape[0] // 2
        part = part[:half] + swap(part[half:], "row", bit)
    for bit in bits_of(layers):
        part = part + swap(part, "scen", 2 * bit)
    summed = part
    for bit in reversed(bits_of(rows)):
        part = jnp.concatenate([part, swap(part, "row", bit)], axis=0)
    return part, swap(part, "scen", 1), summed


def shards(coupling, solves, border_diagonal, panel_rows):
    half = HALF
    coupling, solves = coupling[0], solves[0]
    local, row_count = coupling.shape
    block, panel = solves.shape
    scen, rows = lax.axis_size("scen"), lax.axis_size("row")
    layers = scen // 2
    row, place = lax.axis_index("row"), lax.axis_index("scen")
    layer, core = place // 2, place % 2
    share = row_count // scen
    base = row * row_count + place * share

    own_first, own_second = solves[:, :half], solves[:, half:]
    pieces_first, arrived = gather_pieces(own_first, rows)
    pieces_second, _ = gather_pieces(after(own_second, arrived), rows)

    if rows == 4:
        coupling = jnp.concatenate(
            [lax.dynamic_slice_in_dim(coupling, (row ^ k) * block, block, 0) for k in range(rows)], axis=0
        )
    coupling_t = coupling.T

    blocks = 2 * rows
    size = panel // blocks
    turned = sum(((row >> i) & 1) << (len(bits_of(rows)) - 1 - i) for i in range(len(bits_of(rows))))
    me = core * rows + turned
    index = jnp.concatenate([(me ^ k) * size + jnp.arange(size, dtype=jnp.int32) for k in range(blocks)])
    wanted = jnp.concatenate(
        [lax.dynamic_slice_in_dim(panel_rows, (me ^ k) * size, size, 0) for k in range(blocks)]
    )
    columns = row * row_count + jnp.arange(row_count, dtype=jnp.int32)
    picked = dot((wanted[:, None] == columns[None, :]).astype(BF16), coupling_t).astype(BF16)

    glob = base + jnp.arange(share, dtype=jnp.int32)
    diagonal = jnp.sum(jnp.where(wanted[:, None] == glob[None, :], border_diagonal[:, 0][None, :], F32(0.0)), axis=1)
    on_diagonal = jnp.where(
        index[:, None] == jnp.arange(panel, dtype=jnp.int32)[None, :], diagonal[:, None], F32(0.0)
    )
    diag_part = jnp.where(glob[:, None] == panel_rows[None, :], border_diagonal[:, 0][:, None], F32(0.0))

    piece = jax.ShapeDtypeStruct((panel // 2, half), F32)
    gathered = jax.ShapeDtypeStruct((local, half), BF16)
    chains = []
    for pieces, diag in ((pieces_first, on_diagonal[:, :half]), (pieces_second, on_diagonal[:, half:])):
        whole, keep, send = in_vmem(
            pivot_kernel, (gathered, piece, piece), 2 * panel * half * local, picked, diag, *pieces
        )
        chains.append((whole, *sum_pivots(keep, send, rows, layers)))
    (solves_first, first_own, first_other, first_summed), (solves_second, second_own, second_other, _) = chains

    where = jnp.stack([layer, core]).astype(jnp.int32)
    order = [int(f"{p:0{len(bits_of(layers))}b}"[::-1], 2) for p in range(layers)]
    rowsum = jax.ShapeDtypeStruct((layers * share, panel), F32)
    keep, send = in_vmem(
        functools.partial(schur_kernel, order), (rowsum, rowsum), 2 * row_count * panel * local,
        where, coupling_t, solves_first, solves_second, scalars=1,
    )
    part = keep + swap(send, "scen", 1)
    part = after(part, first_summed)
    for bit in bits_of(layers):
        middle = part.shape[0] // 2
        part = part[:middle] + swap(part[middle:], "scen", 2 * bit)
    own_rows = part + diag_part
    first, second = own_rows[:, :half], own_rows[:, half:]

    square = jax.ShapeDtypeStruct((half, half), F32)
    scratch = [pltpu.VMEM((panel, half), F32)]
    at = me.astype(jnp.int32)[None]
    inverse_first, lower = in_vmem(
        functools.partial(first_kernel, blocks), (square, square), 2 * 16 * 3 * half**3,
        at, first_own, first_other, scratch=scratch, scalars=1,
    )
    inverse_second, upper = in_vmem(
        functools.partial(second_kernel, blocks), (square, square), 2 * 18 * 3 * half**3,
        at, second_own, second_other, inverse_first, lower, scratch=scratch, scalars=1,
    )
    out = jax.ShapeDtypeStruct((share, 1, half), F32)
    return in_vmem(
        factor_kernel, (out, out), 2 * 9 * share * half**2, first, second, inverse_first, inverse_second, upper
    )


def solution(mesh):
    placed = (P("scen", None, "row"), P("scen", "row", None), P("scen", "row"), P())
    return jax.shard_map(
        shards,
        mesh=mesh,
        in_specs=placed,
        out_specs=(P("scen", "row", None), P("scen", "row", None)),
        check_vma=False,
    )
```

```python
import functools

import jax
import jax.numpy as jnp
from jax import lax
from jax.experimental import pallas as pl
from jax.experimental.pallas import tpu as pltpu
from jax.sharding import PartitionSpec as P

HALF = 256
NEWTON = 8
F32 = jnp.float32
BF16 = jnp.bfloat16


def halves(a):
    high = a.astype(BF16)
    low = (a - high.astype(F32)).astype(BF16)
    return high, low


def left_of(a):
    high, low = halves(a)
    return jnp.concatenate([high, high, low], axis=1)


def right_of(b):
    high, low = halves(b)
    return jnp.concatenate([high, low, high], axis=0)


def dot(a, b):
    return jnp.dot(a, b, preferred_element_type=F32)


def product(a, b):
    return dot(left_of(a), right_of(b))


def newton(pivot):
    size = jnp.abs(pivot)
    norm_one = jnp.max(jnp.sum(size, axis=0, keepdims=True))
    norm_inf = jnp.max(jnp.sum(size, axis=1, keepdims=True))
    approx = pivot.T / (norm_one * norm_inf)
    pivot_right = right_of(pivot)
    for step in range(NEWTON):
        left = dot(left_of(approx), pivot_right)
        approx = 2.0 * approx - product(left, approx)
    return approx


def place_blocks(place_ref, own_ref, other_ref, rows_ref, blocks):
    size = rows_ref.shape[0] // blocks
    for k in range(blocks):
        source = own_ref if k < blocks // 2 else other_ref
        start = k % (blocks // 2) * size
        target = pl.multiple_of((place_ref[0] ^ k) * size, size)
        rows_ref[pl.ds(target, size), :] = source[start:start + size, :]


def first_kernel(blocks, place_ref, own_ref, other_ref, inverse_ref, lower_ref, rows_ref):
    place_blocks(place_ref, own_ref, other_ref, rows_ref, blocks)
    half = inverse_ref.shape[0]
    lower_ref[...] = rows_ref[half:, :]
    inverse_ref[...] = newton(rows_ref[:half, :])


def second_kernel(
    blocks, place_ref, own_ref, other_ref, inverse_first_ref, lower_ref, inverse_ref, upper_ref, rows_ref
):
    place_blocks(place_ref, own_ref, other_ref, rows_ref, blocks)
    half = inverse_ref.shape[0]
    upper = rows_ref[:half, :]
    upper_ref[...] = upper
    lower_factor = product(lower_ref[...], inverse_first_ref[...])
    inverse_ref[...] = newton(rows_ref[half:, :] - product(lower_factor, upper))


def factor_kernel(rows_ref, inverse_first_ref, inverse_second_ref, upper_ref, first_out, second_out):
    half = upper_ref.shape[0]
    first_factor = product(rows_ref[:half, :].T, inverse_first_ref[...])
    updated = rows_ref[half:, :].T - product(first_factor, upper_ref[...])
    first_out[...] = first_factor[:, None, :]
    second_out[...] = product(updated, inverse_second_ref[...])[:, None, :]


def contract(a, b, dims):
    return lax.dot_general(a, b, (dims, ((), ())), preferred_element_type=F32)


def pick_kernel(blocks, place_ref, wanted_ref, own_diagonal_ref, coupling_ref, picked_ref, left_ref, right_ref):
    first_column, first_row, me = place_ref[0], place_ref[1], place_ref[2]
    panel = picked_ref.shape[0]
    columns, share = coupling_ref.shape[1], own_diagonal_ref.shape[1]
    wanted = jnp.broadcast_to(wanted_ref[...], (8, panel)).astype(F32).T[:, :1].astype(jnp.int32)
    here = wanted - first_column == lax.broadcasted_iota(jnp.int32, (panel, columns), 1)
    chosen = jnp.where(here, F32(1.0), F32(0.0)).astype(BF16)
    picked_ref[...] = contract(chosen, coupling_ref[...], ((1,), (1,))).astype(BF16)
    owned = wanted - first_row == lax.broadcasted_iota(jnp.int32, (panel, share), 1)
    entry = jnp.sum(jnp.where(owned, own_diagonal_ref[...], F32(0.0)), axis=1, keepdims=True)
    size = panel // blocks
    half = left_ref.shape[1]
    for k in range(blocks):
        rows = slice(k * size, (k + 1) * size)
        index = lax.broadcasted_iota(jnp.int32, (size, half), 0) + (me ^ k) * size
        column = lax.broadcasted_iota(jnp.int32, (size, half), 1)
        left_ref[rows, :] = jnp.where(index == column, entry[rows], F32(0.0))
        right_ref[rows, :] = jnp.where(index == column + half, entry[rows], F32(0.0))


def pivot_kernel(place_ref, picked_ref, diagonal_ref, *refs):
    *pieces, solves_ref, keep_ref, send_ref = refs
    if len(pieces) == 1:
        solves_ref[...] = pieces[0][...]
    else:
        block, far = pieces[0].shape[0], pieces[3].shape[0]
        for k, offset, piece in zip((0, 1, 2, 3, 3), (0, 0, 0, 0, far), pieces):
            start = pl.multiple_of((place_ref[0] ^ k) * block + offset, far)
            solves_ref[pl.ds(start, piece.shape[0]), :] = piece[...]
    total = dot(picked_ref[...], solves_ref[...]) + diagonal_ref[...]
    half = keep_ref.shape[0]
    keep_ref[...] = total[:half]
    send_ref[...] = total[half:]


def schur_kernel(order, place_ref, coupling_ref, first_ref, second_ref, keep_ref, send_ref, turned_ref):
    layer, core = place_ref[0], place_ref[1]
    half = first_ref.shape[1]
    panel = 2 * half
    turned_ref[:half, :] = first_ref[...].T
    turned_ref[half:, :] = second_ref[...].T
    share = keep_ref.shape[1]
    for position, k in enumerate(order):
        start = pl.multiple_of((layer ^ k) * 2 * share, 2 * share)
        both = dot(turned_ref[...], coupling_ref[:, pl.ds(start, 2 * share)])
        rows = slice(position * panel, (position + 1) * panel)
        one, two = both[:, :share], both[:, share:]
        keep_ref[rows, :] = jnp.where(core == 0, one, two)
        send_ref[rows, :] = jnp.where(core == 0, two, one)


def in_vmem(kernel, out_shape, flops, *args, scratch=(), scalars=0):
    vmem = pl.BlockSpec(memory_space=pltpu.VMEM)
    smem = pl.BlockSpec(memory_space=pltpu.SMEM)
    return pl.pallas_call(
        kernel,
        out_shape=out_shape,
        in_specs=[smem] * scalars + [vmem] * (len(args) - scalars),
        out_specs=jax.tree.map(lambda _: vmem, out_shape),
        scratch_shapes=scratch,
        compiler_params=pltpu.CompilerParams(vmem_limit_bytes=28 * 1024 * 1024),
        cost_estimate=pl.CostEstimate(flops=flops, bytes_accessed=1 << 20, transcendentals=0),
    )(*args)


def swap(x, axis, bit):
    count = lax.axis_size(axis)
    return lax.ppermute(x, axis, [(i, i ^ bit) for i in range(count)])


def after(x, *others):
    return lax.optimization_barrier((x,) + others)[0]


def bits_of(count):
    return [1 << i for i in range(count.bit_length() - 1)]


def gather_pieces(block, rows):
    if rows != 4:
        return [lax.all_gather(block, "row", axis=0, tiled=True)], block
    along_x, along_y = swap(block, "row", 1), swap(block, "row", 2)
    half = block.shape[0] // 2
    far = [swap(along_y[:half], "row", 1), swap(along_x[half:], "row", 2)]
    return [block, along_x, along_y] + far, along_y


def sum_pivots(keep, send, rows, layers):
    part = keep + swap(send, "scen", 1)
    for bit in bits_of(rows):
        half = part.shape[0] // 2
        part = part[:half] + swap(part[half:], "row", bit)
    for bit in bits_of(layers):
        part = part + swap(part, "scen", 2 * bit)
    summed = part
    for bit in reversed(bits_of(rows)):
        part = jnp.concatenate([part, swap(part, "row", bit)], axis=0)
    return part, swap(part, "scen", 1), summed


def shards(coupling, solves, border_diagonal, panel_rows):
    half = HALF
    coupling, solves = coupling[0], solves[0]
    local, row_count = coupling.shape
    block, panel = solves.shape
    scen, rows = lax.axis_size("scen"), lax.axis_size("row")
    layers = scen // 2
    row, place = lax.axis_index("row"), lax.axis_index("scen")
    layer, core = place // 2, place % 2
    share = row_count // scen
    base = row * row_count + place * share

    own_first, own_second = solves[:, :half], solves[:, half:]
    pieces_first, arrived = gather_pieces(own_first, rows)
    pieces_second, _ = gather_pieces(after(own_second, arrived), rows)

    blocks = 2 * rows
    size = panel // blocks
    turned = sum(((row >> i) & 1) << (len(bits_of(rows)) - 1 - i) for i in range(len(bits_of(rows))))
    me = core * rows + turned
    wanted = jnp.concatenate(
        [lax.dynamic_slice_in_dim(panel_rows, (me ^ k) * size, size, 0) for k in range(blocks)]
    )
    places = jnp.stack([row * row_count, base, me]).astype(jnp.int32)
    corner_shape = jax.ShapeDtypeStruct((panel, half), F32)
    picked, *diagonals = in_vmem(
        functools.partial(pick_kernel, blocks),
        (jax.ShapeDtypeStruct((panel, local), BF16), corner_shape, corner_shape),
        2 * panel * row_count * local,
        places, wanted[None, :], border_diagonal.T, coupling, scalars=1,
    )
    glob = base + jnp.arange(share, dtype=jnp.int32)
    diag_part = jnp.where(panel_rows[:, None] == glob[None, :], border_diagonal[:, 0][None, :], F32(0.0))

    piece = jax.ShapeDtypeStruct((panel // 2, half), F32)
    gathered = jax.ShapeDtypeStruct((local, half), BF16)
    chains = []
    for pieces, diag in ((pieces_first, diagonals[0]), (pieces_second, diagonals[1])):
        whole, keep, send = in_vmem(
            pivot_kernel, (gathered, piece, piece), 2 * panel * half * local,
            row.astype(jnp.int32)[None], picked, diag, *pieces, scalars=1,
        )
        chains.append((whole, *sum_pivots(keep, send, rows, layers)))
    (solves_first, first_own, first_other, first_summed), (solves_second, second_own, second_other, _) = chains

    if share % 128:
        solves_all = jnp.concatenate([solves_first, solves_second], axis=1)
        terms = contract(solves_all, coupling, ((0,), (0,)))
        part = lax.psum_scatter(terms, "scen", scatter_dimension=1, tiled=True)
    else:
        where = jnp.stack([layer, core]).astype(jnp.int32)
        order = [int(f"{p:0{len(bits_of(layers))}b}"[::-1], 2) for p in range(layers)]
        rowsum = jax.ShapeDtypeStruct((layers * panel, share), F32)
        keep, send = in_vmem(
            functools.partial(schur_kernel, order), (rowsum, rowsum), 2 * row_count * panel * local,
            where, coupling, solves_first, solves_second, scalars=1, scratch=[pltpu.VMEM((panel, local), BF16)],
        )
        part = keep + swap(send, "scen", 1)
        part = after(part, first_summed)
        for bit in bits_of(layers):
            middle = part.shape[0] // 2
            part = part[:middle] + swap(part[middle:], "scen", 2 * bit)
    own_rows = part + diag_part

    square = jax.ShapeDtypeStruct((half, half), F32)
    scratch = [pltpu.VMEM((panel, half), F32)]
    at = me.astype(jnp.int32)[None]
    inverse_first, lower = in_vmem(
        functools.partial(first_kernel, blocks), (square, square), 2 * 16 * 3 * half**3,
        at, first_own, first_other, scratch=scratch, scalars=1,
    )
    inverse_second, upper = in_vmem(
        functools.partial(second_kernel, blocks), (square, square), 2 * 18 * 3 * half**3,
        at, second_own, second_other, inverse_first, lower, scratch=scratch, scalars=1,
    )
    out = jax.ShapeDtypeStruct((share, 1, half), F32)
    return in_vmem(
        factor_kernel, (out, out), 2 * 9 * share * half**2, own_rows, inverse_first, inverse_second, upper
    )


def solution(mesh):
    placed = (P("scen", None, "row"), P("scen", "row", None), P("scen", "row"), P())
    return jax.shard_map(
        shards,
        mesh=mesh,
        in_specs=placed,
        out_specs=(P("scen", "row", None), P("scen", "row", None)),
        check_vma=False,
    )
```

```python
import functools

import jax
import jax.numpy as jnp
from jax import lax
from jax.experimental import pallas as pl
from jax.experimental.pallas import tpu as pltpu
from jax.sharding import PartitionSpec as P

HALF = 256
NEWTON = 8
STEPS = 4
LARGE = 61 << 20
NEWTON_BYTES = 16 << 20
F32 = jnp.float32
BF16 = jnp.bfloat16


def halves(a):
    high = a.astype(BF16)
    low = (a - high.astype(F32)).astype(BF16)
    return high, low


def left_of(a):
    high, low = halves(a)
    return jnp.concatenate([high, high, low], axis=1)


def right_of(b):
    high, low = halves(b)
    return jnp.concatenate([high, low, high], axis=0)


def dot(a, b):
    return jnp.dot(a, b, preferred_element_type=F32)


def product(a, b):
    return dot(left_of(a), right_of(b))


def newton(pivot):
    size = jnp.abs(pivot)
    norm_one = jnp.max(jnp.sum(size, axis=0, keepdims=True))
    norm_inf = jnp.max(jnp.sum(size, axis=1, keepdims=True))
    approx = pivot.T / (norm_one * norm_inf)
    pivot_right = right_of(pivot)
    for step in range(NEWTON):
        left = dot(left_of(approx), pivot_right)
        approx = 2.0 * approx - product(left, approx)
    return approx


def place_blocks(place_ref, own_ref, other_ref, rows_ref, blocks):
    size = rows_ref.shape[0] // blocks
    for k in range(blocks):
        source = own_ref if k < blocks // 2 else other_ref
        start = k % (blocks // 2) * size
        target = pl.multiple_of((place_ref[0] ^ k) * size, size)
        rows_ref[pl.ds(target, size), :] = source[start:start + size, :]


def first_kernel(blocks, place_ref, own_ref, other_ref, inverse_ref, lower_ref, rows_ref):
    place_blocks(place_ref, own_ref, other_ref, rows_ref, blocks)
    half = inverse_ref.shape[0]
    lower_ref[...] = rows_ref[half:, :]
    inverse_ref[...] = newton(rows_ref[:half, :])


def second_kernel(
    blocks, place_ref, own_ref, other_ref, inverse_first_ref, lower_ref, inverse_ref, upper_ref, rows_ref
):
    place_blocks(place_ref, own_ref, other_ref, rows_ref, blocks)
    half = inverse_ref.shape[0]
    upper = rows_ref[:half, :]
    upper_ref[...] = upper
    lower_factor = product(lower_ref[...], inverse_first_ref[...])
    inverse_ref[...] = newton(rows_ref[half:, :] - product(lower_factor, upper))


def factor_kernel(rows_ref, inverse_first_ref, inverse_second_ref, upper_ref, first_out, second_out):
    half = upper_ref.shape[0]
    first_factor = product(rows_ref[:half, :].T, inverse_first_ref[...])
    updated = rows_ref[half:, :].T - product(first_factor, upper_ref[...])
    first_out[...] = first_factor[:, None, :]
    second_out[...] = product(updated, inverse_second_ref[...])[:, None, :]


def contract(a, b, dims):
    return lax.dot_general(a, b, (dims, ((), ())), preferred_element_type=F32)


def pick_kernel(
    blocks, place_ref, wanted_ref, own_diagonal_ref, coupling_ref, picked_ref, left_ref, right_ref,
    column_ref, chosen_ref,
):
    @pl.when(pl.program_id(0) == 0)
    def _():
        first_column, first_row, me = place_ref[0], place_ref[1], place_ref[2]
        panel, columns = chosen_ref.shape
        share = own_diagonal_ref.shape[1]
        lanes = column_ref.shape[1]
        column_ref[...] = jnp.broadcast_to(wanted_ref[...], (lanes, panel)).astype(F32).T.astype(jnp.int32)
        size = panel // blocks
        half = left_ref.shape[1]
        for k in range(blocks):
            rows = slice(k * size, (k + 1) * size)
            start = pl.multiple_of((me ^ k) * size, size)
            wanted = column_ref[pl.ds(start, size), :][:, :1]
            here = wanted - first_column == lax.broadcasted_iota(jnp.int32, (size, columns), 1)
            chosen_ref[rows, :] = jnp.where(here, F32(1.0), F32(0.0)).astype(BF16)
            owned = wanted - first_row == lax.broadcasted_iota(jnp.int32, (size, share), 1)
            entry = jnp.sum(jnp.where(owned, own_diagonal_ref[...], F32(0.0)), axis=1, keepdims=True)
            index = lax.broadcasted_iota(jnp.int32, (size, half), 0) + start
            column = lax.broadcasted_iota(jnp.int32, (size, half), 1)
            left_ref[rows, :] = jnp.where(index == column, entry, F32(0.0))
            right_ref[rows, :] = jnp.where(index == column + half, entry, F32(0.0))

    picked_ref[...] = contract(chosen_ref[...], coupling_ref[...], ((1,), (1,))).astype(BF16)


def pivot_terms(total, keep_ref, send_ref):
    half = keep_ref.shape[0]
    keep_ref[...] = total[:half]
    send_ref[...] = total[half:]


def left_kernel(place_ref, picked_ref, diagonal_ref, *refs):
    *pieces, solves_ref, keep_ref, send_ref = refs
    if len(pieces) == 1:
        solves_ref[...] = pieces[0][...]
    else:
        size = pieces[0].shape[0] // 2
        solves_ref[pl.ds(pl.multiple_of(place_ref[0] * 2 * size, size), 2 * size), :] = pieces[0][...]
        for i, piece in enumerate(pieces[1:]):
            start = pl.multiple_of((place_ref[0] ^ (1 + i // 2)) * 2 * size + i % 2 * size, size)
            solves_ref[pl.ds(start, size), :] = piece[...]
    half = diagonal_ref.shape[1]
    pivot_terms(dot(picked_ref[...], solves_ref[:, :half]) + diagonal_ref[...], keep_ref, send_ref)


def right_kernel(picked_ref, diagonal_ref, solves_ref, keep_ref, send_ref):
    half = diagonal_ref.shape[1]
    pivot_terms(dot(picked_ref[...], solves_ref[:, half:]) + diagonal_ref[...], keep_ref, send_ref)


def schur_kernel(place_ref, coupling_ref, solves_ref, keep_ref, send_ref, turned_ref):
    core = place_ref[1]
    share = keep_ref.shape[1]

    @pl.when(pl.program_id(0) == 0)
    def _():
        turned_ref[...] = solves_ref[...].T

    both = dot(turned_ref[...], coupling_ref[...])
    one, two = both[:, :share], both[:, share:]
    keep_ref[...] = jnp.where(core == 0, one, two)
    send_ref[...] = jnp.where(core == 0, two, one)


def in_vmem(kernel, out_shape, flops, *args, scratch=(), scalars=0, grid=(), in_blocks=None, out_blocks=None, limit=28 << 20, moved=1 << 10):
    vmem = pl.BlockSpec(memory_space=pltpu.VMEM)
    smem = pl.BlockSpec(memory_space=pltpu.SMEM)
    return pl.pallas_call(
        kernel,
        out_shape=out_shape,
        grid=grid,
        in_specs=[smem] * scalars + list(in_blocks or [vmem] * (len(args) - scalars)),
        out_specs=out_blocks or jax.tree.map(lambda _: vmem, out_shape),
        scratch_shapes=scratch,
        compiler_params=pltpu.CompilerParams(vmem_limit_bytes=limit),
        cost_estimate=pl.CostEstimate(flops=flops, bytes_accessed=moved, transcendentals=0),
    )(*args)


def swap(x, axis, bit):
    count = lax.axis_size(axis)
    return lax.ppermute(x, axis, [(i, i ^ bit) for i in range(count)])


def after(x, *others):
    return lax.optimization_barrier((x,) + others)[0]


def bits_of(count):
    return [1 << i for i in range(count.bit_length() - 1)]


def gather_pieces(block, rows, first):
    if rows != 4:
        return [lax.all_gather(block, "row", axis=0, tiled=True)]
    half = block.shape[0] // 2
    upper, lower = block[:half], block[half:]
    lower_x, upper_y = swap(lower, "row", 1), swap(upper, "row", 2)
    upper_x, lower_y = swap(upper, "row", 1), swap(lower, "row", 2)
    upper_far, lower_far = swap(after(upper_y, *first), "row", 1), swap(after(lower_x, *first), "row", 2)
    return [block, upper_x, lower_x, upper_y, lower_y, upper_far, lower_far]


def halved(keep, got):
    half = keep.shape[0] // 2
    goes = keep[half:] + got[half:]
    return keep[:half] + got[:half], goes


def sum_pivots(keep, send, rows, layers):
    got = swap(send, "scen", 1)
    size = keep.shape[0] // rows
    block = lambda x, k: x[k * size:(k + 1) * size]
    arrived = [swap(block(keep, k) + block(got, k), "row", k) for k in range(1, rows)]
    part = sum(arrived, block(keep, 0) + block(got, 0))
    for bit in bits_of(layers):
        part = part + swap(part, "scen", 2 * bit)
    whole = jnp.concatenate([part] + [swap(part, "row", k) for k in range(1, rows)], axis=0)
    return whole, swap(whole, "scen", 1), part


def shards(coupling, solves, border_diagonal, panel_rows):
    half = HALF
    coupling, solves = coupling[0], solves[0]
    local, row_count = coupling.shape
    block, panel = solves.shape
    scen, rows = lax.axis_size("scen"), lax.axis_size("row")
    layers = scen // 2
    row, place = lax.axis_index("row"), lax.axis_index("scen")
    layer, core = place // 2, place % 2
    share = row_count // scen
    base = row * row_count + place * share

    blocks = 2 * rows
    size = panel // blocks
    me = core * rows + row
    corner_shape = jax.ShapeDtypeStruct((panel, half), F32)
    places = jnp.stack([row * row_count, base, me]).astype(jnp.int32)
    corner_shape = jax.ShapeDtypeStruct((panel, half), F32)
    whole = lambda *shape: pl.BlockSpec(shape, lambda i: (0, 0))
    picked, *diagonals = in_vmem(
        functools.partial(pick_kernel, blocks),
        (jax.ShapeDtypeStruct((panel, local), BF16), corner_shape, corner_shape),
        0,
        places, panel_rows[None, :], border_diagonal.T, coupling, scalars=1,
        grid=(STEPS,),
        in_blocks=[whole(1, panel), whole(1, share), pl.BlockSpec((local // STEPS, row_count), lambda i: (i, 0))],
        out_blocks=(pl.BlockSpec((panel, local // STEPS), lambda i: (0, i)), whole(panel, half), whole(panel, half)),
        scratch=[pltpu.VMEM((panel, 128), jnp.int32), pltpu.VMEM((panel, row_count), BF16)], limit=LARGE,
    )
    pieces = gather_pieces(solves, rows, (picked,))

    glob = base + jnp.arange(share, dtype=jnp.int32)
    diag_part = jnp.where(panel_rows[:, None] == glob[None, :], border_diagonal[:, 0][None, :], F32(0.0))

    piece = jax.ShapeDtypeStruct((panel // 2, half), F32)
    gathered = jax.ShapeDtypeStruct((local, panel), BF16)
    cost = 0
    solves_all, keep, send = in_vmem(
        left_kernel, (gathered, piece, piece), cost,
        row.astype(jnp.int32)[None], picked, diagonals[0], *pieces, scalars=1,
    )
    first_own, first_other, first_summed = sum_pivots(keep, send, rows, layers)
    keep, send = in_vmem(right_kernel, (piece, piece), cost, picked, diagonals[1], solves_all)
    second_own, second_other, _ = sum_pivots(keep, send, rows, layers)

    if share % 128:
        terms = contract(solves_all, coupling, ((0,), (0,)))
        part = lax.psum_scatter(terms, "scen", scatter_dimension=1, tiled=True)
    else:
        where = jnp.stack([layer, core]).astype(jnp.int32)
        rowsum = jax.ShapeDtypeStruct((layers * panel, share), F32)

        def relative(i):
            last = layers.bit_length() - 2
            return sum(((i >> b) & 1) << (last - b) for b in range(last + 1)) ^ (lax.axis_index("scen") // 2)

        keep, send = in_vmem(
            schur_kernel, (rowsum, rowsum), 0,
            where, coupling, solves_all, scalars=1,
            grid=(layers,),
            in_blocks=[pl.BlockSpec((local, 2 * share), lambda i: (0, relative(i))), whole(local, panel)],
            out_blocks=(pl.BlockSpec((panel, share), lambda i: (i, 0)),) * 2,
            scratch=[pltpu.VMEM((panel, local), BF16)],
        )
        keep, goes = halved(keep, swap(send, "scen", 1))
        goes = after(goes, first_summed)
        for bit in bits_of(layers)[:-1]:
            keep, goes = halved(keep, swap(goes, "scen", 2 * bit))
        part = keep + swap(goes, "scen", layers)
    own_rows = part + diag_part

    square = jax.ShapeDtypeStruct((half, half), F32)
    scratch = [pltpu.VMEM((panel, half), F32)]
    at = me.astype(jnp.int32)[None]
    inverse_first, lower = in_vmem(
        functools.partial(first_kernel, blocks), (square, square), 2 * 16 * 3 * half**3,
        at, first_own, first_other, scratch=scratch, scalars=1, moved=NEWTON_BYTES,
    )
    inverse_second, upper = in_vmem(
        functools.partial(second_kernel, blocks), (square, square), 2 * 18 * 3 * half**3,
        at, second_own, second_other, inverse_first, lower, scratch=scratch, scalars=1, moved=NEWTON_BYTES,
    )
    out = jax.ShapeDtypeStruct((share, 1, half), F32)
    return in_vmem(
        factor_kernel, (out, out), 2 * 9 * share * half**2, own_rows, inverse_first, inverse_second, upper
    )


def solution(mesh):
    placed = (P("scen", None, "row"), P("scen", "row", None), P("scen", "row"), P())
    return jax.shard_map(
        shards,
        mesh=mesh,
        in_specs=placed,
        out_specs=(P("scen", "row", None), P("scen", "row", None)),
        check_vma=False,
    )
```

```python
import functools

import jax
import jax.numpy as jnp
from jax import lax
from jax.experimental import pallas as pl
from jax.experimental.pallas import tpu as pltpu
from jax.sharding import PartitionSpec as P

HALF = 256
NEWTON = 8
TAIL = 16
LEVELS = 32000.0
F32 = jnp.float32
BF16 = jnp.bfloat16
I16 = jnp.int16


def halves(a):
    high = a.astype(BF16)
    low = (a - high.astype(F32)).astype(BF16)
    return high, low


def left_of(a):
    high, low = halves(a)
    return jnp.concatenate([high, high, low], axis=1)


def right_of(b):
    high, low = halves(b)
    return jnp.concatenate([high, low, high], axis=0)


def dot(a, b):
    return jnp.dot(a, b, preferred_element_type=F32)


def product(a, b):
    return dot(left_of(a), right_of(b))


def newton(pivot):
    size = jnp.abs(pivot)
    norm_one = jnp.max(jnp.sum(size, axis=0, keepdims=True))
    norm_inf = jnp.max(jnp.sum(size, axis=1, keepdims=True))
    approx = pivot.T / (norm_one * norm_inf)
    pivot_right = right_of(pivot)
    for step in range(NEWTON):
        left = dot(left_of(approx), pivot_right)
        approx = 2.0 * approx - product(left, approx)
    return approx


def aligned(index, size):
    return pl.multiple_of(index * size, size)


def encode(values, out_ref, base, diagonal=None):
    rows, lanes = values.shape
    top = jnp.maximum(jnp.max(jnp.abs(values), axis=0, keepdims=True), F32(1e-30))
    power = jnp.ceil(jnp.log2(top))
    unit = jnp.exp2(power)
    mantissa = jnp.ceil(top / unit * F32(16384.0))
    scale = mantissa * unit * F32(1.0 / (16384.0 * LEVELS))
    codes = jnp.round(values * (F32(1.0) / scale)).astype(jnp.int32)
    out_ref[base:base + rows, :] = codes.astype(I16)
    row = lax.broadcasted_iota(jnp.int32, (TAIL, lanes), 0)
    tail = jnp.where(row == 0, power, jnp.where(row == 1, mantissa, F32(0.0)))
    if diagonal is not None:
        coarse = jnp.floor(diagonal * F32(64.0))
        fine = (diagonal * F32(64.0) - coarse) * F32(4096.0)
        tail = jnp.where(row == 2, coarse, jnp.where(row == 3, fine, tail))
    out_ref[base + rows:base + rows + TAIL, :] = tail.astype(jnp.int32).astype(I16)


def decode(ref, base, rows):
    tail = ref[base + rows:base + rows + TAIL, :].astype(jnp.int32).astype(F32)
    scale = tail[1:2] * jnp.exp2(tail[0:1]) * F32(1.0 / (16384.0 * LEVELS))
    diagonal = tail[2:3] * F32(1.0 / 64.0) + tail[3:4] * F32(1.0 / (64.0 * 4096.0))
    return ref[base:base + rows, :].astype(jnp.int32).astype(F32) * scale, diagonal


def turn_kernel(solves_ref, upper_ref, lower_ref):
    turned = solves_ref[...].T
    half = upper_ref.shape[0]
    upper_ref[...] = turned[:half]
    lower_ref[...] = turned[half:]


def pick_kernel(place_ref, panel_ref, own_diagonal_ref, coupling_ref, chosen_ref, entry_ref):
    first_column, first_row = place_ref[0], place_ref[1]
    panel = panel_ref.shape[1]
    columns, share = coupling_ref.shape[1], own_diagonal_ref.shape[1]
    here = panel_ref[...] - first_column == lax.broadcasted_iota(jnp.int32, (columns, panel), 0)
    chosen = jnp.where(here, F32(1.0), F32(0.0)).astype(BF16)
    chosen_ref[...] = dot(coupling_ref[...], chosen).astype(BF16)
    owned = panel_ref[...] - first_row == lax.broadcasted_iota(jnp.int32, (share, panel), 0)
    own = jnp.broadcast_to(own_diagonal_ref[...], (8, share)).T[:, :1]
    entry = jnp.sum(jnp.where(owned, own, F32(0.0)), axis=0, keepdims=True)
    entry_ref[...] = jnp.broadcast_to(entry, entry_ref.shape)


def terms_kernel(rows, place_ref, chosen_ref, entry_ref, *refs):
    *pieces, turned_ref, keep_ref, send_ref, all_ref = refs
    row, core = place_ref[0], place_ref[1]
    if len(pieces) == 1:
        turned_ref[...] = pieces[0][...]
    else:
        half, width = pieces[0].shape
        for i, piece in enumerate(pieces):
            turned_ref[i % 2 * half:(i % 2 + 1) * half, pl.ds(aligned(row ^ (i // 2), width), width)] = piece[...]
    all_ref[...] = dot(turned_ref[...], chosen_ref[...])
    size = keep_ref.shape[0] // rows
    for out_ref, whose in ((keep_ref, core), (send_ref, 1 - core)):
        for k in range(rows):
            out_ref[k * size:(k + 1) * size, :] = all_ref[pl.ds(aligned(whose * rows + (row ^ k), size), size), :]
    send_ref[rows * size:, :] = entry_ref[...]


def pair_kernel(rows, keep_ref, got_ref, entry_ref, *out_refs):
    size = keep_ref.shape[0] // rows
    entry = entry_ref[:1, :] + got_ref[rows * size:rows * size + 1, :]
    for k, out_ref in enumerate(out_refs):
        part = slice(k * size, (k + 1) * size)
        encode(keep_ref[part, :] + got_ref[part, :], out_ref, 0, entry)


def sum_kernel(*refs):
    *in_refs, out_ref = refs
    size = out_ref.shape[0] - TAIL
    parts = [decode(ref, 0, size) for ref in in_refs]
    encode(sum(p[0] for p in parts), out_ref, 0, sum(p[1] for p in parts))


def join_kernel(*refs):
    *in_refs, out_ref = refs
    size = in_refs[0].shape[0]
    for k, ref in enumerate(in_refs):
        out_ref[k * size:(k + 1) * size, :] = ref[...]


def first_kernel(rows, place_ref, own_ref, other_ref, inverse_ref, pivots_ref):
    row, core = place_ref[0], place_ref[1]
    panel = pivots_ref.shape[0]
    size = panel // (2 * rows)
    index = lax.broadcasted_iota(jnp.int32, (size, panel), 1)
    for ref, whose in ((own_ref, core), (other_ref, 1 - core)):
        for k in range(rows):
            start = aligned(whose * rows + (row ^ k), size)
            values, diagonal = decode(ref, k * (size + TAIL), size)
            at = lax.broadcasted_iota(jnp.int32, (size, panel), 0) + start == index
            pivots_ref[pl.ds(start, size), :] = values + jnp.where(at, diagonal, F32(0.0))
    half = inverse_ref.shape[0]
    inverse_ref[...] = newton(pivots_ref[:half, :half])


def second_kernel(pivots_ref, inverse_first_ref, inverse_ref):
    half = inverse_ref.shape[0]
    lower_factor = product(inverse_first_ref[...], pivots_ref[:half, half:])
    inverse_ref[...] = newton(pivots_ref[half:, half:] - product(pivots_ref[half:, :half], lower_factor))


def schur_kernel(place_ref, coupling_ref, turned_ref, keep_ref, send_ref):
    core, layer = place_ref[1], place_ref[2]
    panel, share = turned_ref.shape[0], keep_ref.shape[1]
    layers = keep_ref.shape[0] // panel
    for position, k in enumerate(reversed_order(layers)):
        start = aligned(layer ^ k, 2 * share)
        both = dot(turned_ref[...], coupling_ref[:, pl.ds(start, 2 * share)])
        rows = slice(position * panel, (position + 1) * panel)
        one, two = both[:, :share], both[:, share:]
        keep_ref[rows, :] = jnp.where(core == 0, one, two)
        send_ref[rows, :] = jnp.where(core == 0, two, one)


def bulk_pair_kernel(panel, keep_ref, got_ref, own_ref, coded_ref):
    half = own_ref.shape[0]
    own_ref[...] = keep_ref[:half, :] + got_ref[:half, :]
    for i in range(half // panel):
        part = slice(half + i * panel, half + (i + 1) * panel)
        encode(keep_ref[part, :] + got_ref[part, :], coded_ref, i * (panel + TAIL))


def bulk_sum_kernel(panel, keep_ref, got_ref, own_ref, coded_ref):
    half = own_ref.shape[0]
    for i in range(keep_ref.shape[0] // panel):
        value = keep_ref[i * panel:(i + 1) * panel, :] + decode(got_ref, i * (panel + TAIL), panel)[0]
        if i * panel < half:
            own_ref[i * panel:(i + 1) * panel, :] = value
        else:
            encode(value, coded_ref, (i - half // panel) * (panel + TAIL))


def factor_kernel(
    place_ref, panel_ref, own_diagonal_ref, inverse_first_ref, inverse_second_ref, pivots_ref, rows_ref, *refs
):
    *got, first_out, second_out = refs
    panel, share = rows_ref.shape
    half = panel // 2
    turned = jnp.broadcast_to(panel_ref[...].astype(F32), (share, panel)).T.astype(jnp.int32)
    here = turned - place_ref[1] == lax.broadcasted_iota(jnp.int32, (panel, share), 1)
    rows = rows_ref[...] + jnp.where(here, own_diagonal_ref[...], F32(0.0))
    for ref in got:
        rows = rows + decode(ref, 0, panel)[0]
    first_factor = product(inverse_first_ref[...], rows[:half])
    updated = rows[half:] - product(pivots_ref[half:, :half], first_factor)
    first_out[...] = first_factor.T[:, None, :]
    second_out[...] = product(inverse_second_ref[...], updated).T[:, None, :]


def call(kernel, out_shape, *args, scratch=(), scalars=0, micros=0.0):
    vmem = pl.BlockSpec(memory_space=pltpu.VMEM)
    smem = pl.BlockSpec(memory_space=pltpu.SMEM)
    return pl.pallas_call(
        kernel,
        out_shape=out_shape,
        in_specs=[smem] * scalars + [vmem] * (len(args) - scalars),
        out_specs=jax.tree.map(lambda _: vmem, out_shape),
        scratch_shapes=scratch,
        compiler_params=pltpu.CompilerParams(vmem_limit_bytes=28 << 20),
        cost_estimate=pl.CostEstimate(flops=0, bytes_accessed=int(micros * 3.69e6) + 1024, transcendentals=0),
    )(*args)


def swap(x, axis, bit):
    count = lax.axis_size(axis)
    return lax.ppermute(x, axis, [(i, i ^ bit) for i in range(count)])


def after(x, *others):
    return lax.optimization_barrier((x,) + others)[0]


def bits_of(count):
    return [1 << i for i in range(count.bit_length() - 1)]


def reversed_order(count):
    width = count.bit_length() - 1
    return [int(f"{p:0{width}b}"[::-1], 2) for p in range(count)]


def gather_pieces(solves, rows, ready):
    block, panel = solves.shape
    if rows != 4:
        return [lax.all_gather(solves.T, "row", axis=1, tiled=True)]
    half = jax.ShapeDtypeStruct((panel // 2, block), BF16)
    upper, lower = call(turn_kernel, (half, half), solves)
    lower_x, upper_y = swap(lower, "row", 1), swap(upper, "row", 2)
    upper_x, lower_y = swap(upper, "row", 1), swap(lower, "row", 2)
    upper_far, lower_far = swap(after(upper_y, *ready), "row", 1), swap(after(lower_x, *ready), "row", 2)
    return [upper, lower, upper_x, lower_x, upper_y, lower_y, upper_far, lower_far]


def shards(coupling, solves, border_diagonal, panel_rows):
    half = HALF
    coupling, solves = coupling[0], solves[0]
    local, row_count = coupling.shape
    panel = solves.shape[1]
    scen, rows = lax.axis_size("scen"), lax.axis_size("row")
    layers = scen // 2
    row, place = lax.axis_index("row"), lax.axis_index("scen")
    share = row_count // scen
    size = panel // (2 * rows)
    shape = jax.ShapeDtypeStruct
    panel_row, diagonal_row = panel_rows[None, :], border_diagonal.T
    starts = jnp.stack([row * row_count, row * row_count + place * share]).astype(jnp.int32)
    at = jnp.stack([row, place % 2, place // 2]).astype(jnp.int32)

    chosen, entry = call(
        pick_kernel, (shape((local, panel), BF16), shape((8, panel), F32)),
        starts, panel_row, diagonal_row, coupling, scalars=1, micros=3.0,
    )
    pieces = gather_pieces(solves, rows, (entry,))
    turned, keep, send = call(
        functools.partial(terms_kernel, rows),
        (shape((panel, local), BF16), shape((panel // 2, panel), F32), shape((panel // 2 + 8, panel), F32)),
        at, chosen, entry, *pieces, scalars=1, scratch=[pltpu.VMEM((panel, panel), F32)],
    )
    coded = shape((size + TAIL, panel), I16)
    codes = call(
        functools.partial(pair_kernel, rows), (coded,) * rows, keep, swap(send, "scen", 1), entry
    )
    arrived = [swap(codes[k], "row", k) for k in range(1, rows)]

    if share % 128:
        terms = dot(turned, coupling)
        own, got = lax.psum_scatter(terms, "scen", scatter_dimension=1, tiled=True), []
        part = call(sum_kernel, coded, codes[0], *arrived)
        for bit in bits_of(layers):
            part = call(sum_kernel, coded, part, swap(part, "scen", 2 * bit))
    else:
        bulk = shape((layers * panel, share), F32)
        keep, send = call(schur_kernel, (bulk, bulk), at, coupling, after(turned, codes[0]), scalars=1)
        got = swap(send, "scen", 1)
        part = call(sum_kernel, coded, after(codes[0], keep), *arrived)
        steps = bits_of(layers)
        count = layers // 2
        own, bulk_codes = call(
            functools.partial(bulk_pair_kernel, panel),
            (shape((count * panel, share), F32), shape((count * (panel + TAIL), share), I16)),
            after(keep, part), got,
        )
        for bit in steps:
            other = swap(part, "scen", 2 * bit)
            part = call(sum_kernel, coded, after(part, bulk_codes), other)
        for bit in steps[:-1]:
            count //= 2
            own, bulk_codes = call(
                functools.partial(bulk_sum_kernel, panel),
                (shape((count * panel, share), F32), shape((count * (panel + TAIL), share), I16)),
                own, swap(after(bulk_codes, part), "scen", 2 * bit),
            )
        got = [swap(bulk_codes, "scen", layers)]

    joined = call(
        join_kernel, shape((rows * (size + TAIL), panel), I16), part, *[swap(part, "row", k) for k in range(1, rows)]
    )
    square = shape((half, half), F32)
    inverse_first, pivots = call(
        functools.partial(first_kernel, rows), (square, shape((panel, panel), F32)),
        at, joined, swap(joined, "scen", 1), scalars=1, micros=4.5,
    )
    inverse_second = call(second_kernel, square, pivots, inverse_first, micros=4.5)
    out = shape((share, 1, half), F32)
    return call(
        factor_kernel, (out, out),
        starts, panel_row, diagonal_row, inverse_first, inverse_second, pivots, own, *got, scalars=1,
    )


def solution(mesh):
    placed = (P("scen", None, "row"), P("scen", "row", None), P("scen", "row"), P())
    return jax.shard_map(
        shards,
        mesh=mesh,
        in_specs=placed,
        out_specs=(P("scen", "row", None), P("scen", "row", None)),
        check_vma=False,
    )
```

```python
import functools

import jax
import jax.numpy as jnp
from jax import lax
from jax.experimental import pallas as pl
from jax.experimental.pallas import tpu as pltpu
from jax.sharding import PartitionSpec as P

HALF = 256
NEWTON = 8
TAIL = 16
CHUNKS = 4
LEVELS = 32000.0
F32 = jnp.float32
BF16 = jnp.bfloat16
I16 = jnp.int16


def halves(a):
    high = a.astype(BF16)
    low = (a - high.astype(F32)).astype(BF16)
    return high, low


def left_of(a):
    high, low = halves(a)
    return jnp.concatenate([high, high, low], axis=1)


def right_of(b):
    high, low = halves(b)
    return jnp.concatenate([high, low, high], axis=0)


def dot(a, b):
    return jnp.dot(a, b, preferred_element_type=F32)


def product(a, b):
    return dot(left_of(a), right_of(b))


def newton(pivot):
    size = jnp.abs(pivot)
    norm_one = jnp.max(jnp.sum(size, axis=0, keepdims=True))
    norm_inf = jnp.max(jnp.sum(size, axis=1, keepdims=True))
    approx = pivot.T / (norm_one * norm_inf)
    count = pivot.shape[0]
    one = lax.broadcasted_iota(jnp.int32, pivot.shape, 0) == lax.broadcasted_iota(jnp.int32, pivot.shape, 1)
    pivot_right = right_of(pivot)
    rest = jnp.where(one, F32(1.0), F32(0.0)) - dot(left_of(approx), pivot_right)
    for step in range(NEWTON - 1):
        if step < NEWTON - 2:
            both = product(rest, jnp.concatenate([rest, approx], axis=1))
            rest, approx = both[:, :count], approx + both[:, count:]
        else:
            approx = approx + product(rest, approx)
    left = dot(left_of(approx), pivot_right)
    return 2.0 * approx - product(left, approx)


def aligned(index, size):
    return pl.multiple_of(index * size, size)


def encode(values, out_ref, base, diagonal=None):
    rows, lanes = values.shape
    top = jnp.maximum(jnp.max(jnp.abs(values), axis=0, keepdims=True), F32(1e-30))
    power = jnp.ceil(jnp.log2(top))
    unit = jnp.exp2(power)
    mantissa = jnp.ceil(top / unit * F32(16384.0))
    scale = mantissa * unit * F32(1.0 / (16384.0 * LEVELS))
    codes = jnp.round(values * (F32(1.0) / scale)).astype(jnp.int32)
    out_ref[base:base + rows, :] = codes.astype(I16)
    row = lax.broadcasted_iota(jnp.int32, (TAIL, lanes), 0)
    tail = jnp.where(row == 0, power, jnp.where(row == 1, mantissa, F32(0.0)))
    if diagonal is not None:
        coarse = jnp.floor(diagonal * F32(64.0))
        fine = (diagonal * F32(64.0) - coarse) * F32(4096.0)
        tail = jnp.where(row == 2, coarse, jnp.where(row == 3, fine, tail))
    out_ref[base + rows:base + rows + TAIL, :] = tail.astype(jnp.int32).astype(I16)


def decode(ref, base, rows):
    tail = ref[base + rows:base + rows + TAIL, :].astype(jnp.int32).astype(F32)
    scale = tail[1:2] * jnp.exp2(tail[0:1]) * F32(1.0 / (16384.0 * LEVELS))
    diagonal = tail[2:3] * F32(1.0 / 64.0) + tail[3:4] * F32(1.0 / (64.0 * 4096.0))
    return ref[base:base + rows, :].astype(jnp.int32).astype(F32) * scale, diagonal


def turn_kernel(solves_ref, upper_ref, lower_ref, solves_copy, done):
    copy = pltpu.make_async_copy(solves_ref, solves_copy, done)
    copy.start()
    copy.wait()
    turned = solves_copy[...].T
    half = upper_ref.shape[0]
    upper_ref[...] = turned[:half]
    lower_ref[...] = turned[half:]


def pick_kernel(
    place_ref, panel_ref, own_diagonal_ref, coupling_ref, chosen_ref, entry_ref,
    panel_copy, diagonal_copy, coupling_copy, one_ref, small_done, done,
):
    chunks, rows, columns = coupling_copy.shape
    small = [
        pltpu.make_async_copy(panel_ref, panel_copy, small_done.at[0]),
        pltpu.make_async_copy(own_diagonal_ref, diagonal_copy, small_done.at[1]),
    ]
    large = [
        pltpu.make_async_copy(coupling_ref.at[pl.ds(i * rows, rows), :], coupling_copy.at[i], done.at[i])
        for i in range(chunks)
    ]
    for copy in small + large:
        copy.start()
    for copy in small:
        copy.wait()
    first_column, first_row = place_ref[0], place_ref[1]
    panel, share = panel_copy.shape[1], diagonal_copy.shape[1]
    here = panel_copy[...] - first_column == lax.broadcasted_iota(jnp.int32, (columns, panel), 0)
    one_ref[...] = jnp.where(here, F32(1.0), F32(0.0)).astype(BF16)
    owned = panel_copy[...] - first_row == lax.broadcasted_iota(jnp.int32, (share, panel), 0)
    own = jnp.broadcast_to(diagonal_copy[...], (8, share)).T[:, :1]
    entry = jnp.sum(jnp.where(owned, own, F32(0.0)), axis=0, keepdims=True)
    entry_ref[...] = jnp.broadcast_to(entry, entry_ref.shape)
    for i, copy in enumerate(large):
        copy.wait()
        chosen_ref[i * rows:(i + 1) * rows, :] = dot(coupling_copy[i], one_ref[...]).astype(BF16)


def terms_kernel(rows, place_ref, chosen_ref, entry_ref, *refs):
    *pieces, turned_ref, keep_ref, send_ref, all_ref = refs
    row, core = place_ref[0], place_ref[1]
    if len(pieces) == 1:
        turned_ref[...] = pieces[0][...]
    else:
        half, width = pieces[0].shape
        for i, piece in enumerate(pieces):
            turned_ref[i % 2 * half:(i % 2 + 1) * half, pl.ds(aligned(row ^ (i // 2), width), width)] = piece[...]
    all_ref[...] = dot(turned_ref[...], chosen_ref[...])
    size = keep_ref.shape[0] // rows
    for out_ref, whose in ((keep_ref, core), (send_ref, 1 - core)):
        for k in range(rows):
            out_ref[k * size:(k + 1) * size, :] = all_ref[pl.ds(aligned(whose * rows + (row ^ k), size), size), :]
    send_ref[rows * size:, :] = entry_ref[...]


def pair_kernel(rows, keep_ref, got_ref, entry_ref, *out_refs):
    size = keep_ref.shape[0] // rows
    entry = entry_ref[:1, :] + got_ref[rows * size:rows * size + 1, :]
    for k, out_ref in enumerate(out_refs):
        part = slice(k * size, (k + 1) * size)
        encode(keep_ref[part, :] + got_ref[part, :], out_ref, 0, entry)


def sum_kernel(*refs):
    *in_refs, out_ref = refs
    size = out_ref.shape[0] - TAIL
    parts = [decode(ref, 0, size) for ref in in_refs]
    encode(sum(p[0] for p in parts), out_ref, 0, sum(p[1] for p in parts))


def join_kernel(*refs):
    *in_refs, out_ref = refs
    size = in_refs[0].shape[0]
    for k, ref in enumerate(in_refs):
        out_ref[k * size:(k + 1) * size, :] = ref[...]


def first_kernel(rows, place_ref, own_ref, other_ref, inverse_ref, pivots_ref):
    row, core = place_ref[0], place_ref[1]
    panel = pivots_ref.shape[0]
    size = panel // (2 * rows)
    index = lax.broadcasted_iota(jnp.int32, (size, panel), 1)
    for ref, whose in ((own_ref, core), (other_ref, 1 - core)):
        for k in range(rows):
            start = aligned(whose * rows + (row ^ k), size)
            values, diagonal = decode(ref, k * (size + TAIL), size)
            at = lax.broadcasted_iota(jnp.int32, (size, panel), 0) + start == index
            pivots_ref[pl.ds(start, size), :] = values + jnp.where(at, diagonal, F32(0.0))
    half = inverse_ref.shape[0]
    inverse_ref[...] = newton(pivots_ref[:half, :half])


def second_kernel(pivots_ref, inverse_first_ref, inverse_ref):
    half = inverse_ref.shape[0]
    lower_factor = product(inverse_first_ref[...], pivots_ref[:half, half:])
    inverse_ref[...] = newton(pivots_ref[half:, half:] - product(pivots_ref[half:, :half], lower_factor))


def schur_kernel(place_ref, coupling_ref, turned_ref, keep_ref, send_ref):
    core, layer = place_ref[1], place_ref[2]
    panel, share = turned_ref.shape[0], keep_ref.shape[1]
    layers = keep_ref.shape[0] // panel
    for position, k in enumerate(reversed_order(layers)):
        start = aligned(layer ^ k, 2 * share)
        both = dot(turned_ref[...], coupling_ref[:, pl.ds(start, 2 * share)])
        rows = slice(position * panel, (position + 1) * panel)
        one, two = both[:, :share], both[:, share:]
        keep_ref[rows, :] = jnp.where(core == 0, one, two)
        send_ref[rows, :] = jnp.where(core == 0, two, one)


def bulk_pair_kernel(panel, keep_ref, got_ref, own_ref, coded_ref):
    half = own_ref.shape[0]
    own_ref[...] = keep_ref[:half, :] + got_ref[:half, :]
    for i in range(half // panel):
        part = slice(half + i * panel, half + (i + 1) * panel)
        encode(keep_ref[part, :] + got_ref[part, :], coded_ref, i * (panel + TAIL))


def bulk_sum_kernel(panel, keep_ref, got_ref, own_ref, coded_ref):
    half = own_ref.shape[0]
    for i in range(keep_ref.shape[0] // panel):
        value = keep_ref[i * panel:(i + 1) * panel, :] + decode(got_ref, i * (panel + TAIL), panel)[0]
        if i * panel < half:
            own_ref[i * panel:(i + 1) * panel, :] = value
        else:
            encode(value, coded_ref, (i - half // panel) * (panel + TAIL))


def factor_kernel(
    place_ref, panel_ref, own_diagonal_ref, inverse_first_ref, inverse_second_ref, pivots_ref, rows_ref, *refs
):
    *got, first_out, second_out = refs
    panel, share = rows_ref.shape
    half = panel // 2
    turned = jnp.broadcast_to(panel_ref[...].astype(F32), (share, panel)).T.astype(jnp.int32)
    here = turned - place_ref[1] == lax.broadcasted_iota(jnp.int32, (panel, share), 1)
    rows = rows_ref[...] + jnp.where(here, own_diagonal_ref[...], F32(0.0))
    for ref in got:
        rows = rows + decode(ref, 0, panel)[0]
    first_factor = product(inverse_first_ref[...], rows[:half])
    updated = rows[half:] - product(pivots_ref[half:, :half], first_factor)
    first_out[...] = first_factor.T[:, None, :]
    second_out[...] = product(inverse_second_ref[...], updated).T[:, None, :]


def call(kernel, out_shape, *args, scratch=(), scalars=0, remain=0, micros=0.0):
    hbm = pl.BlockSpec(memory_space=pltpu.HBM)
    vmem = pl.BlockSpec(memory_space=pltpu.VMEM)
    smem = pl.BlockSpec(memory_space=pltpu.SMEM)
    stay = len(args) - remain
    args = args[:stay] + tuple(pltpu.with_memory_space_constraint(x, pltpu.HBM) for x in args[stay:])
    return pl.pallas_call(
        kernel,
        out_shape=out_shape,
        in_specs=[smem] * scalars + [vmem] * (len(args) - scalars - remain) + [hbm] * remain,
        out_specs=jax.tree.map(lambda _: vmem, out_shape),
        scratch_shapes=scratch,
        compiler_params=pltpu.CompilerParams(vmem_limit_bytes=28 << 20),
        cost_estimate=pl.CostEstimate(flops=0, bytes_accessed=int(micros * 3.69e6) + 1024, transcendentals=0),
    )(*args)


def swap(x, axis, bit):
    count = lax.axis_size(axis)
    return lax.ppermute(x, axis, [(i, i ^ bit) for i in range(count)])


def after(x, *others):
    return lax.optimization_barrier((x,) + others)[0]


def bits_of(count):
    return [1 << i for i in range(count.bit_length() - 1)]


def reversed_order(count):
    width = count.bit_length() - 1
    return [int(f"{p:0{width}b}"[::-1], 2) for p in range(count)]


def gather_pieces(solves, rows, ready):
    block, panel = solves.shape
    if rows != 4:
        return [lax.all_gather(solves.T, "row", axis=1, tiled=True)]
    half = jax.ShapeDtypeStruct((panel // 2, block), BF16)
    upper, lower = call(
        turn_kernel, (half, half), solves, remain=1,
        scratch=[pltpu.VMEM((block, panel), BF16), pltpu.SemaphoreType.DMA],
    )
    lower_x, upper_y = swap(lower, "row", 1), swap(upper, "row", 2)
    upper_x, lower_y = swap(upper, "row", 1), swap(lower, "row", 2)
    upper_far, lower_far = swap(after(upper_y, *ready), "row", 1), swap(after(lower_x, *ready), "row", 2)
    return [upper, lower, upper_x, lower_x, upper_y, lower_y, upper_far, lower_far]


def shards(coupling, solves, border_diagonal, panel_rows):
    half = HALF
    coupling, solves = coupling[0], solves[0]
    local, row_count = coupling.shape
    panel = solves.shape[1]
    scen, rows = lax.axis_size("scen"), lax.axis_size("row")
    layers = scen // 2
    row, place = lax.axis_index("row"), lax.axis_index("scen")
    share = row_count // scen
    size = panel // (2 * rows)
    shape = jax.ShapeDtypeStruct
    panel_row, diagonal_row = panel_rows[None, :], border_diagonal.T
    starts = jnp.stack([row * row_count, row * row_count + place * share]).astype(jnp.int32)
    at = jnp.stack([row, place % 2, place // 2]).astype(jnp.int32)

    chosen, entry = call(
        pick_kernel, (pltpu.VMEM((local, panel), BF16), pltpu.VMEM((8, panel), F32)),
        starts, panel_row, diagonal_row, coupling, scalars=1, remain=3, micros=3.0,
        scratch=[
            pltpu.VMEM((1, panel), jnp.int32),
            pltpu.VMEM((1, share), F32),
            pltpu.VMEM((CHUNKS, local // CHUNKS, row_count), BF16),
            pltpu.VMEM((row_count, panel), BF16),
            pltpu.SemaphoreType.DMA((2,)),
            pltpu.SemaphoreType.DMA((CHUNKS,)),
        ],
    )
    pieces = gather_pieces(solves, rows, (entry,))
    turned, keep, send = call(
        functools.partial(terms_kernel, rows),
        (shape((panel, local), BF16), shape((panel // 2, panel), F32), shape((panel // 2 + 8, panel), F32)),
        at, chosen, entry, *pieces, scalars=1, scratch=[pltpu.VMEM((panel, panel), F32)],
    )
    coded = shape((size + TAIL, panel), I16)
    codes = call(
        functools.partial(pair_kernel, rows), (coded,) * rows, keep, swap(send, "scen", 1), entry
    )
    arrived = [swap(codes[k], "row", k) for k in range(1, rows)]

    if share % 128:
        terms = dot(turned, coupling)
        own, got = lax.psum_scatter(terms, "scen", scatter_dimension=1, tiled=True), []
        part = call(sum_kernel, coded, codes[0], *arrived)
        for bit in bits_of(layers):
            part = call(sum_kernel, coded, part, swap(part, "scen", 2 * bit))
    else:
        bulk = shape((layers * panel, share), F32)
        keep, send = call(schur_kernel, (bulk, bulk), at, coupling, after(turned, arrived[0]), scalars=1)
        got = swap(send, "scen", 1)
        part = call(sum_kernel, coded, after(codes[0], keep), *arrived)
        steps = bits_of(layers)
        count = layers // 2
        own, bulk_codes = call(
            functools.partial(bulk_pair_kernel, panel),
            (shape((count * panel, share), F32), shape((count * (panel + TAIL), share), I16)),
            after(keep, part), got,
        )
        for bit in steps:
            before, other = part, swap(part, "scen", 2 * bit)
            part = call(sum_kernel, coded, after(part, bulk_codes), other)
        for bit in steps[:-1]:
            count //= 2
            own, bulk_codes = call(
                functools.partial(bulk_sum_kernel, panel),
                (shape((count * panel, share), F32), shape((count * (panel + TAIL), share), I16)),
                own, swap(after(bulk_codes, before), "scen", 2 * bit),
            )
        got = [swap(bulk_codes, "scen", layers)]

    joined = call(
        join_kernel, shape((rows * (size + TAIL), panel), I16), part, *[swap(part, "row", k) for k in range(1, rows)]
    )
    square = shape((half, half), F32)
    inverse_first, pivots = call(
        functools.partial(first_kernel, rows), (square, shape((panel, panel), F32)),
        at, joined, swap(joined, "scen", 1), scalars=1, micros=4.5,
    )
    inverse_second = call(second_kernel, square, pivots, inverse_first, micros=4.5)
    out = shape((share, 1, half), F32)
    return call(
        factor_kernel, (out, out),
        starts, panel_row, diagonal_row, inverse_first, inverse_second, pivots, own, *got, scalars=1,
    )


def solution(mesh):
    placed = (P("scen", None, "row"), P("scen", "row", None), P("scen", "row"), P())
    return jax.shard_map(
        shards,
        mesh=mesh,
        in_specs=placed,
        out_specs=(P("scen", "row", None), P("scen", "row", None)),
        check_vma=False,
    )
```

```python
import functools

import jax
import jax.numpy as jnp
from jax import lax
from jax.experimental import pallas as pl
from jax.experimental.pallas import tpu as pltpu
from jax.sharding import PartitionSpec as P

HALF = 256
NEWTON = 8
TAIL = 16
CHUNKS = 4
LEVELS = 32000.0
F32 = jnp.float32
BF16 = jnp.bfloat16
I16 = jnp.int16


def halves(a):
    high = a.astype(BF16)
    low = (a - high.astype(F32)).astype(BF16)
    return high, low


def left_of(a):
    high, low = halves(a)
    return jnp.concatenate([high, high, low], axis=1)


def right_of(b):
    high, low = halves(b)
    return jnp.concatenate([high, low, high], axis=0)


def dot(a, b):
    return jnp.dot(a, b, preferred_element_type=F32)


def product(a, b):
    return dot(left_of(a), right_of(b))


def newton(pivot):
    size = jnp.abs(pivot)
    norm_one = jnp.max(jnp.sum(size, axis=0, keepdims=True))
    norm_inf = jnp.max(jnp.sum(size, axis=1, keepdims=True))
    approx = pivot.T / (norm_one * norm_inf)
    count = pivot.shape[0]
    one = lax.broadcasted_iota(jnp.int32, pivot.shape, 0) == lax.broadcasted_iota(jnp.int32, pivot.shape, 1)
    pivot_right = right_of(pivot)
    rest = jnp.where(one, F32(1.0), F32(0.0)) - dot(left_of(approx), pivot_right)
    for step in range(NEWTON - 1):
        if step < NEWTON - 2:
            both = product(rest, jnp.concatenate([rest, approx], axis=1))
            rest, approx = both[:, :count], approx + both[:, count:]
        else:
            approx = approx + product(rest, approx)
    left = dot(left_of(approx), pivot_right)
    return 2.0 * approx - product(left, approx)


def aligned(index, size):
    return pl.multiple_of(index * size, size)


def encode(values, out_ref, base, diagonal=None):
    rows, lanes = values.shape
    top = jnp.maximum(jnp.max(jnp.abs(values), axis=0, keepdims=True), F32(1e-30))
    power = jnp.ceil(jnp.log2(top))
    unit = jnp.exp2(power)
    mantissa = jnp.ceil(top / unit * F32(16384.0))
    scale = mantissa * unit * F32(1.0 / (16384.0 * LEVELS))
    codes = jnp.round(values * (F32(1.0) / scale)).astype(jnp.int32)
    out_ref[base:base + rows, :] = codes.astype(I16)
    row = lax.broadcasted_iota(jnp.int32, (TAIL, lanes), 0)
    tail = jnp.where(row == 0, power, jnp.where(row == 1, mantissa, F32(0.0)))
    if diagonal is not None:
        coarse = jnp.floor(diagonal * F32(64.0))
        fine = (diagonal * F32(64.0) - coarse) * F32(4096.0)
        tail = jnp.where(row == 2, coarse, jnp.where(row == 3, fine, tail))
    out_ref[base + rows:base + rows + TAIL, :] = tail.astype(jnp.int32).astype(I16)


def decode(ref, base, rows):
    tail = ref[base + rows:base + rows + TAIL, :].astype(jnp.int32).astype(F32)
    scale = tail[1:2] * jnp.exp2(tail[0:1]) * F32(1.0 / (16384.0 * LEVELS))
    diagonal = tail[2:3] * F32(1.0 / 64.0) + tail[3:4] * F32(1.0 / (64.0 * 4096.0))
    return ref[base:base + rows, :].astype(jnp.int32).astype(F32) * scale, diagonal


def turn_kernel(solves_ref, upper_ref, lower_ref, solves_copy, done):
    copy = pltpu.make_async_copy(solves_ref, solves_copy, done)
    copy.start()
    copy.wait()
    turned = solves_copy[...].T
    half = upper_ref.shape[0]
    upper_ref[...] = turned[:half]
    lower_ref[...] = turned[half:]


def fetch(source_ref, target_ref, done, first):
    rows = target_ref.shape[1]
    copies = [
        pltpu.make_async_copy(source_ref.at[pl.ds((first + i) * rows, rows), :], target_ref.at[i], done.at[i])
        for i in range(target_ref.shape[0])
    ]
    for copy in copies:
        copy.start()
    return copies


def choose(copies, coupling_copy, one_ref, chosen_ref):
    rows = coupling_copy.shape[1]
    for i, copy in enumerate(copies):
        copy.wait()
        chosen_ref[i * rows:(i + 1) * rows, :] = dot(coupling_copy[i], one_ref[...]).astype(BF16)


def pick_kernel(
    place_ref, panel_ref, own_diagonal_ref, coupling_ref,
    chosen_ref, entry_ref, one_ref, panel_out, diagonal_out, coupling_copy, small_done, done,
):
    small = [
        pltpu.make_async_copy(panel_ref, panel_out, small_done.at[0]),
        pltpu.make_async_copy(own_diagonal_ref, diagonal_out, small_done.at[1]),
    ]
    for copy in small:
        copy.start()
    copies = fetch(coupling_ref, coupling_copy, done, 0)
    for copy in small:
        copy.wait()
    first_column, first_row = place_ref[0], place_ref[1]
    columns, panel = one_ref.shape
    share = diagonal_out.shape[1]
    here = panel_out[...] - first_column == lax.broadcasted_iota(jnp.int32, (columns, panel), 0)
    one_ref[...] = jnp.where(here, F32(1.0), F32(0.0)).astype(BF16)
    owned = panel_out[...] - first_row == lax.broadcasted_iota(jnp.int32, (share, panel), 0)
    own = jnp.broadcast_to(diagonal_out[...], (8, share)).T[:, :1]
    entry = jnp.sum(jnp.where(owned, own, F32(0.0)), axis=0, keepdims=True)
    entry_ref[...] = jnp.broadcast_to(entry, entry_ref.shape)
    choose(copies, coupling_copy, one_ref, chosen_ref)


def rest_kernel(one_ref, coupling_ref, chosen_ref, coupling_copy, done):
    copies = fetch(coupling_ref, coupling_copy, done, coupling_copy.shape[0])
    choose(copies, coupling_copy, one_ref, chosen_ref)


def pivot_terms(place_ref, turned_ref, chosen_ref, more_ref, out_ref, all_ref, rows, whose):
    half = all_ref.shape[0]
    size = half // rows
    middle = chosen_ref.shape[0]
    block = turned_ref[pl.ds(aligned(whose, half), half), :]
    all_ref[...] = dot(block[:, :middle], chosen_ref[...]) + dot(block[:, middle:], more_ref[...])
    for k in range(rows):
        out_ref[k * size:(k + 1) * size, :] = all_ref[pl.ds(aligned(place_ref[0] ^ k, size), size), :]


def send_kernel(rows, place_ref, chosen_ref, more_ref, entry_ref, *refs):
    *pieces, turned_ref, send_ref, all_ref = refs
    if len(pieces) == 1:
        turned_ref[...] = pieces[0][...]
    else:
        half, width = pieces[0].shape
        for i, piece in enumerate(pieces):
            start = aligned(place_ref[0] ^ (i // 2), width)
            turned_ref[i % 2 * half:(i % 2 + 1) * half, pl.ds(start, width)] = piece[...]
    pivot_terms(place_ref, turned_ref, chosen_ref, more_ref, send_ref, all_ref, rows, 1 - place_ref[1])
    send_ref[all_ref.shape[0]:, :] = entry_ref[...]


def keep_kernel(rows, place_ref, chosen_ref, more_ref, turned_ref, keep_ref, all_ref):
    pivot_terms(place_ref, turned_ref, chosen_ref, more_ref, keep_ref, all_ref, rows, place_ref[1])


def pair_kernel(rows, keep_ref, got_ref, entry_ref, *out_refs):
    size = keep_ref.shape[0] // rows
    entry = entry_ref[:1, :] + got_ref[rows * size:rows * size + 1, :]
    for k, out_ref in enumerate(out_refs):
        part = slice(k * size, (k + 1) * size)
        encode(keep_ref[part, :] + got_ref[part, :], out_ref, 0, entry)


def sum_kernel(*refs):
    *in_refs, out_ref = refs
    size = out_ref.shape[0] - TAIL
    parts = [decode(ref, 0, size) for ref in in_refs]
    encode(sum(p[0] for p in parts), out_ref, 0, sum(p[1] for p in parts))


def join_kernel(*refs):
    *in_refs, out_ref = refs
    size = in_refs[0].shape[0]
    for k, ref in enumerate(in_refs):
        out_ref[k * size:(k + 1) * size, :] = ref[...]


def first_kernel(rows, place_ref, own_ref, other_ref, inverse_ref, pivots_ref):
    row, core = place_ref[0], place_ref[1]
    panel = pivots_ref.shape[0]
    size = panel // (2 * rows)
    index = lax.broadcasted_iota(jnp.int32, (size, panel), 1)
    for ref, whose in ((own_ref, core), (other_ref, 1 - core)):
        for k in range(rows):
            start = aligned(whose * rows + (row ^ k), size)
            values, diagonal = decode(ref, k * (size + TAIL), size)
            at = lax.broadcasted_iota(jnp.int32, (size, panel), 0) + start == index
            pivots_ref[pl.ds(start, size), :] = values + jnp.where(at, diagonal, F32(0.0))
    half = inverse_ref.shape[0]
    inverse_ref[...] = newton(pivots_ref[:half, :half])


def second_kernel(pivots_ref, inverse_first_ref, inverse_ref):
    half = inverse_ref.shape[0]
    lower_factor = product(inverse_first_ref[...], pivots_ref[:half, half:])
    inverse_ref[...] = newton(pivots_ref[half:, half:] - product(pivots_ref[half:, :half], lower_factor))


def schur_kernel(place_ref, panel_ref, own_diagonal_ref, coupling_ref, turned_ref, keep_ref, send_ref):
    core, layer = place_ref[1], place_ref[2]
    panel, share = turned_ref.shape[0], keep_ref.shape[1]
    layers = keep_ref.shape[0] // panel
    for position, k in enumerate(reversed_order(layers)):
        start = aligned(layer ^ k, 2 * share)
        both = dot(turned_ref[...], coupling_ref[:, pl.ds(start, 2 * share)])
        rows = slice(position * panel, (position + 1) * panel)
        one, two = both[:, :share], both[:, share:]
        kept = jnp.where(core == 0, one, two)
        if position == 0:
            wanted = jnp.broadcast_to(panel_ref[...].astype(F32), (share, panel)).T.astype(jnp.int32)
            here = wanted - place_ref[3] == lax.broadcasted_iota(jnp.int32, (panel, share), 1)
            kept = kept + jnp.where(here, own_diagonal_ref[...], F32(0.0))
        keep_ref[rows, :] = kept
        send_ref[rows, :] = jnp.where(core == 0, two, one)


def bulk_pair_kernel(panel, keep_ref, got_ref, own_ref, coded_ref):
    half = own_ref.shape[0]
    own_ref[...] = keep_ref[:half, :] + got_ref[:half, :]
    for i in range(half // panel):
        part = slice(half + i * panel, half + (i + 1) * panel)
        encode(keep_ref[part, :] + got_ref[part, :], coded_ref, i * (panel + TAIL))


def bulk_sum_kernel(panel, keep_ref, got_ref, own_ref, coded_ref):
    half = own_ref.shape[0]
    for i in range(keep_ref.shape[0] // panel):
        value = keep_ref[i * panel:(i + 1) * panel, :] + decode(got_ref, i * (panel + TAIL), panel)[0]
        if i * panel < half:
            own_ref[i * panel:(i + 1) * panel, :] = value
        else:
            encode(value, coded_ref, (i - half // panel) * (panel + TAIL))


def factor_kernel(inverse_first_ref, inverse_second_ref, pivots_ref, rows_ref, *refs):
    *got, first_out, second_out = refs
    panel = rows_ref.shape[0]
    half = panel // 2
    rows = rows_ref[...]
    for ref in got:
        rows = rows + decode(ref, 0, panel)[0]
    first_factor = product(inverse_first_ref[...], rows[:half])
    updated = rows[half:] - product(pivots_ref[half:, :half], first_factor)
    first_out[...] = first_factor.T[:, None, :]
    second_out[...] = product(inverse_second_ref[...], updated).T[:, None, :]


def call(kernel, out_shape, *args, scratch=(), scalars=0, remain=0, micros=0.0):
    hbm = pl.BlockSpec(memory_space=pltpu.HBM)
    vmem = pl.BlockSpec(memory_space=pltpu.VMEM)
    smem = pl.BlockSpec(memory_space=pltpu.SMEM)
    stay = len(args) - remain
    args = args[:stay] + tuple(pltpu.with_memory_space_constraint(x, pltpu.HBM) for x in args[stay:])
    return pl.pallas_call(
        kernel,
        name=getattr(kernel, "func", kernel).__name__,
        out_shape=out_shape,
        in_specs=[smem] * scalars + [vmem] * (len(args) - scalars - remain) + [hbm] * remain,
        out_specs=jax.tree.map(lambda _: vmem, out_shape),
        scratch_shapes=scratch,
        compiler_params=pltpu.CompilerParams(vmem_limit_bytes=28 << 20),
        cost_estimate=pl.CostEstimate(flops=0, bytes_accessed=int(micros * 3.69e6) + 1024, transcendentals=0),
    )(*args)


def swap(x, axis, bit):
    count = lax.axis_size(axis)
    return lax.ppermute(x, axis, [(i, i ^ bit) for i in range(count)])


def after(x, *others):
    return lax.optimization_barrier((x,) + others)[0]


def bits_of(count):
    return [1 << i for i in range(count.bit_length() - 1)]


def reversed_order(count):
    width = count.bit_length() - 1
    return [int(f"{p:0{width}b}"[::-1], 2) for p in range(count)]


def gather_pieces(solves, rows, ready):
    block, panel = solves.shape
    if rows != 4:
        return [lax.all_gather(solves.T, "row", axis=1, tiled=True)]
    half = jax.ShapeDtypeStruct((panel // 2, block), BF16)
    upper, lower = call(
        turn_kernel, (half, half), solves, remain=1,
        scratch=[pltpu.VMEM((block, panel), BF16), pltpu.SemaphoreType.DMA],
    )
    lower_x, upper_y = swap(lower, "row", 1), swap(upper, "row", 2)
    upper_x, lower_y = swap(upper, "row", 1), swap(lower, "row", 2)
    upper_far, lower_far = swap(after(upper_y, *ready), "row", 1), swap(after(lower_x, *ready), "row", 2)
    return [upper, lower, upper_x, lower_x, upper_y, lower_y, upper_far, lower_far]


def shards(coupling, solves, border_diagonal, panel_rows):
    half = HALF
    coupling, solves = coupling[0], solves[0]
    local, row_count = coupling.shape
    panel = solves.shape[1]
    scen, rows = lax.axis_size("scen"), lax.axis_size("row")
    layers = scen // 2
    row, place = lax.axis_index("row"), lax.axis_index("scen")
    share = row_count // scen
    size = panel // (2 * rows)
    shape = jax.ShapeDtypeStruct
    panel_row, diagonal_row = panel_rows[None, :], border_diagonal.T
    first_row = row * row_count + place * share
    starts = jnp.stack([row * row_count, first_row]).astype(jnp.int32)
    at = jnp.stack([row, place % 2, place // 2, first_row]).astype(jnp.int32)

    picked = shape((local // 2, panel), BF16)
    chunk_room = [
        pltpu.VMEM((CHUNKS // 2, local // CHUNKS, row_count), BF16), pltpu.SemaphoreType.DMA((CHUNKS // 2,))
    ]
    chosen, entry, one, panel_row, diagonal_row = call(
        pick_kernel,
        (
            picked, shape((8, panel), F32), shape((row_count, panel), BF16),
            shape((1, panel), jnp.int32), shape((1, share), F32),
        ),
        starts, panel_row, diagonal_row, coupling, scalars=1, remain=3,
        scratch=[chunk_room[0], pltpu.SemaphoreType.DMA((2,)), chunk_room[1]],
    )
    pieces = gather_pieces(solves, rows, (entry,))
    more = call(rest_kernel, picked, one, coupling, remain=1, scratch=chunk_room)
    room = [pltpu.VMEM((panel // 2, panel), F32)]
    turned, send = call(
        functools.partial(send_kernel, rows),
        (shape((panel, local), BF16), shape((panel // 2 + 8, panel), F32)),
        at, chosen, more, entry, *pieces, scalars=1, scratch=room,
    )
    keep = call(
        functools.partial(keep_kernel, rows), shape((panel // 2, panel), F32),
        at, chosen, more, turned, scalars=1, scratch=room,
    )
    coded = shape((size + TAIL, panel), I16)
    codes = call(
        functools.partial(pair_kernel, rows), (coded,) * rows, keep, swap(send, "scen", 1), entry
    )
    arrived = [swap(codes[k], "row", k) for k in range(rows - 1, 0, -1)]
    part = codes[0]
    steps = bits_of(layers)
    split = share % 128 == 0
    if split:
        count = layers // 2
        bulk = shape((layers * panel, share), F32)
        halved = lambda count: (shape((count * panel, share), F32), shape((count * (panel + TAIL), share), I16))
        own, send_rows = call(
            schur_kernel, (bulk, bulk), at, panel_row, diagonal_row, coupling, after(turned, part), scalars=1
        )
        part = call(sum_kernel, coded, after(part, own), *arrived)
        got = swap(after(send_rows, part), "scen", 1)
    else:
        own, got = lax.psum_scatter(dot(turned, coupling), "scen", scatter_dimension=1, tiled=True), []
        mine = first_row + jnp.arange(share, dtype=jnp.int32)
        own = own + jnp.where(panel_rows[:, None] == mine[None, :], border_diagonal[:, 0][None, :], F32(0.0))
        part = call(sum_kernel, coded, part, *arrived)
    for bit in steps:
        other = swap(part, "scen", 2 * bit)
        if split and bit == steps[-1]:
            own, bulk_codes = call(functools.partial(bulk_pair_kernel, panel), halved(count), after(own, part), got)
            part = after(part, bulk_codes)
        part = call(sum_kernel, coded, part, other)
    shared = [swap(part, "row", k) for k in range(1, rows)]
    if split:
        for bit in steps[:-1]:
            count //= 2
            got = swap(bulk_codes, "scen", 2 * bit)
            own, bulk_codes = call(functools.partial(bulk_sum_kernel, panel), halved(count), own, got)
        got = [swap(bulk_codes, "scen", layers)]
    joined = call(join_kernel, shape((rows * (size + TAIL), panel), I16), part, *shared)
    square = shape((half, half), F32)
    inverse_first, pivots = call(
        functools.partial(first_kernel, rows), (square, shape((panel, panel), F32)),
        at, joined, swap(joined, "scen", 1), scalars=1, micros=4.5,
    )
    inverse_second = call(second_kernel, square, pivots, inverse_first, micros=4.5)
    out = shape((share, 1, half), F32)
    return call(
        factor_kernel, (out, out),
        inverse_first, inverse_second, pivots, own, *got,
    )


def solution(mesh):
    placed = (P("scen", None, "row"), P("scen", "row", None), P("scen", "row"), P())
    return jax.shard_map(
        shards,
        mesh=mesh,
        in_specs=placed,
        out_specs=(P("scen", "row", None), P("scen", "row", None)),
        check_vma=False,
    )
```

```python
import functools

import jax
import jax.numpy as jnp
from jax import lax
from jax.experimental import pallas as pl
from jax.experimental.pallas import tpu as pltpu
from jax.sharding import PartitionSpec as P

HALF = 256
NEWTON = 8
TAIL = 16
SHORT = 8
CHUNKS = 4
LEVELS = 32000.0
F32 = jnp.float32
BF16 = jnp.bfloat16
I16 = jnp.int16


def halves(a):
    high = a.astype(BF16)
    low = (a - high.astype(F32)).astype(BF16)
    return high, low


def left_of(a):
    high, low = halves(a)
    return jnp.concatenate([high, high, low], axis=1)


def right_of(b):
    high, low = halves(b)
    return jnp.concatenate([high, low, high], axis=0)


def dot(a, b):
    return jnp.dot(a, b, preferred_element_type=F32)


def product(a, b):
    return dot(left_of(a), right_of(b))


def newton(pivot):
    size = jnp.abs(pivot)
    norm_one = jnp.max(jnp.sum(size, axis=0, keepdims=True))
    norm_inf = jnp.max(jnp.sum(size, axis=1, keepdims=True))
    approx = pivot.T / (norm_one * norm_inf)
    count = pivot.shape[0]
    one = lax.broadcasted_iota(jnp.int32, pivot.shape, 0) == lax.broadcasted_iota(jnp.int32, pivot.shape, 1)
    pivot_right = right_of(pivot)
    rest = jnp.where(one, F32(1.0), F32(0.0)) - dot(left_of(approx), pivot_right)
    for step in range(NEWTON - 1):
        if step < NEWTON - 2:
            both = product(rest, jnp.concatenate([rest, approx], axis=1))
            rest, approx = both[:, :count], approx + both[:, count:]
        else:
            approx = approx + product(rest, approx)
    left = dot(left_of(approx), pivot_right)
    return 2.0 * approx - product(left, approx)


def aligned(index, size):
    return pl.multiple_of(index * size, size)


def encode(values, out_ref, base, tail_rows, diagonal=None):
    rows, lanes = values.shape
    top = jnp.maximum(jnp.max(jnp.abs(values), axis=0, keepdims=True), F32(1e-30))
    power = jnp.ceil(jnp.log2(top))
    unit = jnp.exp2(power)
    mantissa = jnp.ceil(top / unit * F32(16384.0))
    scale = mantissa * unit * F32(1.0 / (16384.0 * LEVELS))
    codes = jnp.round(values * (F32(1.0) / scale)).astype(jnp.int32)
    out_ref[base:base + rows, :] = codes.astype(I16)
    row = lax.broadcasted_iota(jnp.int32, (tail_rows, lanes), 0)
    tail = jnp.where(row == 0, power, jnp.where(row == 1, mantissa, F32(0.0)))
    if diagonal is not None:
        coarse = jnp.floor(diagonal * F32(64.0))
        fine = (diagonal * F32(64.0) - coarse) * F32(4096.0)
        tail = jnp.where(row == 2, coarse, jnp.where(row == 3, fine, tail))
    out_ref[base + rows:base + rows + tail_rows, :] = tail.astype(jnp.int32).astype(I16)


def decode(ref, base, rows, tail_rows):
    tail = ref[base + rows:base + rows + tail_rows, :].astype(jnp.int32).astype(F32)
    scale = tail[1:2] * jnp.exp2(tail[0:1]) * F32(1.0 / (16384.0 * LEVELS))
    diagonal = tail[2:3] * F32(1.0 / 64.0) + tail[3:4] * F32(1.0 / (64.0 * 4096.0))
    return ref[base:base + rows, :].astype(jnp.int32).astype(F32) * scale, diagonal


def turn_kernel(solves_ref, upper_ref, lower_ref, solves_copy, done):
    copy = pltpu.make_async_copy(solves_ref, solves_copy, done)
    copy.start()
    copy.wait()
    turned = solves_copy[...].T
    half = upper_ref.shape[0]
    upper_ref[...] = turned[:half]
    lower_ref[...] = turned[half:]


def fetch(source_ref, target_ref, done, first):
    rows = target_ref.shape[1]
    copies = [
        pltpu.make_async_copy(source_ref.at[pl.ds((first + i) * rows, rows), :], target_ref.at[i], done.at[i])
        for i in range(target_ref.shape[0])
    ]
    for copy in copies:
        copy.start()
    return copies


def choose(copies, coupling_copy, one_ref, chosen_ref, first):
    rows = coupling_copy.shape[1]
    for i, copy in enumerate(copies):
        copy.wait()
        chosen_ref[(first + i) * rows:(first + i + 1) * rows, :] = dot(coupling_copy[i], one_ref[...]).astype(BF16)


def pick_kernel(
    place_ref, panel_ref, own_diagonal_ref, coupling_ref,
    chosen_ref, entry_ref, one_ref, panel_out, diagonal_out, coupling_copy, small_done, done,
):
    small = [
        pltpu.make_async_copy(panel_ref, panel_out, small_done.at[0]),
        pltpu.make_async_copy(own_diagonal_ref, diagonal_out, small_done.at[1]),
    ]
    for copy in small:
        copy.start()
    copies = fetch(coupling_ref, coupling_copy, done, 0)
    for copy in small:
        copy.wait()
    first_column, first_row = place_ref[0], place_ref[1]
    columns, panel = one_ref.shape
    share = diagonal_out.shape[1]
    here = panel_out[...] - first_column == lax.broadcasted_iota(jnp.int32, (columns, panel), 0)
    one_ref[...] = jnp.where(here, F32(1.0), F32(0.0)).astype(BF16)
    owned = panel_out[...] - first_row == lax.broadcasted_iota(jnp.int32, (share, panel), 0)
    own = jnp.broadcast_to(diagonal_out[...], (8, share)).T[:, :1]
    entry = jnp.sum(jnp.where(owned, own, F32(0.0)), axis=0, keepdims=True)
    entry_ref[...] = jnp.broadcast_to(entry, entry_ref.shape)
    choose(copies, coupling_copy, one_ref, chosen_ref, 0)


def rest_kernel(chosen_in, one_ref, coupling_ref, chosen_ref, coupling_copy, done):
    first = coupling_copy.shape[0]
    copies = fetch(coupling_ref, coupling_copy, done, first)
    choose(copies, coupling_copy, one_ref, chosen_ref, first)


def early_kernel(place_ref, chosen_ref, *refs):
    *pieces, turned_ref, terms_ref = refs
    if len(pieces) == 1:
        turned_ref[...] = pieces[0][...]
    else:
        half, width = pieces[0].shape
        for i, piece in enumerate(pieces):
            start = aligned(place_ref[0] ^ (i // 2), width)
            turned_ref[i % 2 * half:(i % 2 + 1) * half, pl.ds(start, width)] = piece[...]
        start = aligned(place_ref[0] ^ (len(pieces) // 2), width)
        turned_ref[:, pl.ds(start, width)] = jnp.zeros((2 * half, width), BF16)
    terms_ref[...] = dot(turned_ref[...], chosen_ref[...])


def half_terms(rows, place_ref, chosen_ref, terms_ref, far, whose, out_ref, all_ref):
    half = all_ref.shape[0]
    size = half // rows
    total = terms_ref[pl.ds(aligned(whose, half), half), :]
    if far:
        width = far[0].shape[1]
        block = jnp.where(whose == 0, far[0][...], far[1][...])
        total = total + dot(block, chosen_ref[pl.ds(aligned(place_ref[0] ^ (rows - 1), width), width), :])
    all_ref[...] = total
    for k in range(rows):
        out_ref[k * size:(k + 1) * size, :] = all_ref[pl.ds(aligned(place_ref[0] ^ k, size), size), :]


def send_kernel(rows, place_ref, chosen_ref, entry_ref, terms_ref, *refs):
    *far, send_ref, all_ref = refs
    half_terms(rows, place_ref, chosen_ref, terms_ref, far, 1 - place_ref[1], send_ref, all_ref)
    send_ref[all_ref.shape[0]:, :] = entry_ref[...]


def keep_kernel(rows, place_ref, turned_in, chosen_ref, terms_ref, *refs):
    *far, turned_ref, keep_ref, all_ref = refs
    half_terms(rows, place_ref, chosen_ref, terms_ref, far, place_ref[1], keep_ref, all_ref)
    for i, piece in enumerate(far):
        half, width = piece.shape
        start = aligned(place_ref[0] ^ (rows - 1), width)
        turned_ref[i * half:(i + 1) * half, pl.ds(start, width)] = piece[...]


def pair_kernel(rows, keep_ref, got_ref, entry_ref, *out_refs):
    size = keep_ref.shape[0] // rows
    entry = entry_ref[:1, :] + got_ref[rows * size:rows * size + 1, :]
    for k, out_ref in enumerate(out_refs):
        part = slice(k * size, (k + 1) * size)
        encode(keep_ref[part, :] + got_ref[part, :], out_ref, 0, SHORT, entry)


def sum_kernel(*refs):
    *in_refs, out_ref = refs
    size = out_ref.shape[0] - SHORT
    parts = [decode(ref, 0, size, SHORT) for ref in in_refs]
    encode(sum(p[0] for p in parts), out_ref, 0, SHORT, sum(p[1] for p in parts))


def join_kernel(*refs):
    *in_refs, out_ref = refs
    size = in_refs[0].shape[0] - SHORT
    for k, ref in enumerate(in_refs):
        start = k * (size + TAIL)
        out_ref[start:start + size, :] = ref[:size, :]
        tail = ref[size:, :].astype(jnp.int32)
        out_ref[start + size:start + size + TAIL, :] = jnp.concatenate([tail, jnp.zeros_like(tail)], axis=0).astype(I16)


def place_pieces(row, whose, ref, pivots_ref, rows, base):
    panel = pivots_ref.shape[1]
    size = panel // (2 * rows)
    index = lax.broadcasted_iota(jnp.int32, (size, panel), 1)
    for k in range(rows):
        start = aligned(whose * rows + (row ^ k), size)
        values, diagonal = decode(ref, k * (size + TAIL), size, TAIL)
        at = lax.broadcasted_iota(jnp.int32, (size, panel), 0) + start == index
        pivots_ref[pl.ds(start - base, size), :] = values + jnp.where(at, diagonal, F32(0.0))


def own_kernel(rows, place_ref, own_ref, half_ref):
    place_pieces(place_ref[0], place_ref[1], own_ref, half_ref, rows, place_ref[1] * half_ref.shape[0])


def first_kernel(rows, place_ref, half_ref, other_ref, inverse_ref, pivots_ref):
    row, core = place_ref[0], place_ref[1]
    half = inverse_ref.shape[0]
    pivots_ref[pl.ds(aligned(core, half), half), :] = half_ref[...]
    place_pieces(row, 1 - core, other_ref, pivots_ref, rows, 0)
    inverse_ref[...] = newton(pivots_ref[:half, :half])


def second_kernel(pivots_ref, inverse_first_ref, inverse_ref):
    half = inverse_ref.shape[0]
    lower_factor = product(inverse_first_ref[...], pivots_ref[:half, half:])
    inverse_ref[...] = newton(pivots_ref[half:, half:] - product(pivots_ref[half:, :half], lower_factor))


def schur_kernel(place_ref, panel_ref, own_diagonal_ref, coupling_ref, turned_ref, keep_ref, send_ref):
    core, layer = place_ref[1], place_ref[2]
    panel, share = turned_ref.shape[0], keep_ref.shape[1]
    layers = keep_ref.shape[0] // panel
    for position, k in enumerate(reversed_order(layers)):
        start = aligned(layer ^ k, 2 * share)
        both = dot(turned_ref[...], coupling_ref[:, pl.ds(start, 2 * share)])
        rows = slice(position * panel, (position + 1) * panel)
        one, two = both[:, :share], both[:, share:]
        kept = jnp.where(core == 0, one, two)
        if position == 0:
            wanted = jnp.broadcast_to(panel_ref[...].astype(F32), (share, panel)).T.astype(jnp.int32)
            here = wanted - place_ref[3] == lax.broadcasted_iota(jnp.int32, (panel, share), 1)
            kept = kept + jnp.where(here, own_diagonal_ref[...], F32(0.0))
        keep_ref[rows, :] = kept
        send_ref[rows, :] = jnp.where(core == 0, two, one)


def bulk_pair_kernel(panel, keep_ref, got_ref, own_ref, coded_ref):
    half = own_ref.shape[0]
    own_ref[...] = keep_ref[:half, :] + got_ref[:half, :]
    for i in range(half // panel):
        part = slice(half + i * panel, half + (i + 1) * panel)
        encode(keep_ref[part, :] + got_ref[part, :], coded_ref, i * (panel + TAIL), TAIL)


def bulk_sum_kernel(panel, keep_ref, got_ref, own_ref, coded_ref):
    half = own_ref.shape[0]
    for i in range(keep_ref.shape[0] // panel):
        value = keep_ref[i * panel:(i + 1) * panel, :] + decode(got_ref, i * (panel + TAIL), panel, TAIL)[0]
        if i * panel < half:
            own_ref[i * panel:(i + 1) * panel, :] = value
        else:
            encode(value, coded_ref, (i - half // panel) * (panel + TAIL), TAIL)


def factor_kernel(inverse_first_ref, inverse_second_ref, pivots_ref, rows_ref, *refs):
    *got, first_out, second_out = refs
    panel = rows_ref.shape[0]
    half = panel // 2
    rows = rows_ref[...]
    for ref in got:
        rows = rows + decode(ref, 0, panel, TAIL)[0]
    first_factor = product(inverse_first_ref[...], rows[:half])
    updated = rows[half:] - product(pivots_ref[half:, :half], first_factor)
    first_out[...] = first_factor.T[:, None, :]
    second_out[...] = product(inverse_second_ref[...], updated).T[:, None, :]


def call(kernel, out_shape, *args, scratch=(), scalars=0, remain=0, micros=0.0, aliases=None):
    hbm = pl.BlockSpec(memory_space=pltpu.HBM)
    vmem = pl.BlockSpec(memory_space=pltpu.VMEM)
    smem = pl.BlockSpec(memory_space=pltpu.SMEM)
    stay = len(args) - remain
    args = args[:stay] + tuple(pltpu.with_memory_space_constraint(x, pltpu.HBM) for x in args[stay:])
    return pl.pallas_call(
        kernel,
        name=getattr(kernel, "func", kernel).__name__,
        out_shape=out_shape,
        in_specs=[smem] * scalars + [vmem] * (len(args) - scalars - remain) + [hbm] * remain,
        out_specs=jax.tree.map(lambda _: vmem, out_shape),
        scratch_shapes=scratch,
        input_output_aliases=aliases or {},
        compiler_params=pltpu.CompilerParams(vmem_limit_bytes=28 << 20),
        cost_estimate=pl.CostEstimate(flops=0, bytes_accessed=int(micros * 3.69e6) + 1024, transcendentals=0),
    )(*args)


def swap(x, axis, bit):
    count = lax.axis_size(axis)
    return lax.ppermute(x, axis, [(i, i ^ bit) for i in range(count)])


def after(x, *others):
    return lax.optimization_barrier((x,) + others)[0]


def bits_of(count):
    return [1 << i for i in range(count.bit_length() - 1)]


def reversed_order(count):
    width = count.bit_length() - 1
    return [int(f"{p:0{width}b}"[::-1], 2) for p in range(count)]


def gather_pieces(solves, rows, ready):
    block, panel = solves.shape
    if rows != 4:
        return [lax.all_gather(solves.T, "row", axis=1, tiled=True)]
    half = jax.ShapeDtypeStruct((panel // 2, block), BF16)
    upper, lower = call(
        turn_kernel, (half, half), solves, remain=1,
        scratch=[pltpu.VMEM((block, panel), BF16), pltpu.SemaphoreType.DMA],
    )
    lower_x, upper_y = swap(lower, "row", 1), swap(upper, "row", 2)
    upper_x, lower_y = swap(upper, "row", 1), swap(lower, "row", 2)
    upper_far, lower_far = swap(after(upper_y, *ready), "row", 1), swap(after(lower_x, *ready), "row", 2)
    return [upper, lower, upper_x, lower_x, upper_y, lower_y, upper_far, lower_far]


def shards(coupling, solves, border_diagonal, panel_rows):
    half = HALF
    coupling, solves = coupling[0], solves[0]
    local, row_count = coupling.shape
    panel = solves.shape[1]
    scen, rows = lax.axis_size("scen"), lax.axis_size("row")
    layers = scen // 2
    row, place = lax.axis_index("row"), lax.axis_index("scen")
    share = row_count // scen
    size = panel // (2 * rows)
    shape = jax.ShapeDtypeStruct
    panel_row, diagonal_row = panel_rows[None, :], border_diagonal.T
    first_row = row * row_count + place * share
    starts = jnp.stack([row * row_count, first_row]).astype(jnp.int32)
    at = jnp.stack([row, place % 2, place // 2, first_row]).astype(jnp.int32)

    picked = shape((local, panel), BF16)
    chunk_room = [
        pltpu.VMEM((CHUNKS // 2, local // CHUNKS, row_count), BF16), pltpu.SemaphoreType.DMA((CHUNKS // 2,))
    ]
    chosen, entry, one, panel_row, diagonal_row = call(
        pick_kernel,
        (
            picked, shape((8, panel), F32), shape((row_count, panel), BF16),
            shape((1, panel), jnp.int32), shape((1, share), F32),
        ),
        starts, panel_row, diagonal_row, coupling, scalars=1, remain=3,
        scratch=[chunk_room[0], pltpu.SemaphoreType.DMA((2,)), chunk_room[1]],
    )
    pieces = gather_pieces(solves, rows, (entry,))
    near, far = pieces[:6], pieces[6:]
    chosen = call(rest_kernel, picked, chosen, one, coupling, remain=1, scratch=chunk_room, aliases={0: 0})
    room = [pltpu.VMEM((panel // 2, panel), F32)]
    turned, terms = call(
        early_kernel, (shape((panel, local), BF16), shape((panel, panel), F32)), at, chosen, *near, scalars=1
    )
    send = call(
        functools.partial(send_kernel, rows), shape((panel // 2 + 8, panel), F32),
        at, chosen, entry, terms, *far, scalars=1, scratch=room,
    )
    turned, keep = call(
        functools.partial(keep_kernel, rows), (shape((panel, local), BF16), shape((panel // 2, panel), F32)),
        at, turned, chosen, terms, *far, scalars=1, scratch=room, aliases={1: 0},
    )
    coded = shape((size + SHORT, panel), I16)
    codes = call(
        functools.partial(pair_kernel, rows), (coded,) * rows, keep, swap(send, "scen", 1), entry
    )
    arrived = [swap(codes[k], "row", k) for k in range(rows - 1, 0, -1)]
    part = codes[0]
    steps = bits_of(layers)
    split = share % 128 == 0
    if split:
        count = layers // 2
        bulk = shape((layers * panel, share), F32)
        halved = lambda count: (shape((count * panel, share), F32), shape((count * (panel + TAIL), share), I16))
        own, send_rows = call(
            schur_kernel, (bulk, bulk), at, panel_row, diagonal_row, coupling, after(turned, part), scalars=1
        )
        part = call(sum_kernel, coded, after(part, own), *arrived)
        got = swap(after(send_rows, part), "scen", 1)
    else:
        own, got = lax.psum_scatter(dot(turned, coupling), "scen", scatter_dimension=1, tiled=True), []
        mine = first_row + jnp.arange(share, dtype=jnp.int32)
        own = own + jnp.where(panel_rows[:, None] == mine[None, :], border_diagonal[:, 0][None, :], F32(0.0))
        part = call(sum_kernel, coded, part, *arrived)
    for bit in steps:
        other = swap(part, "scen", 2 * bit)
        if split and bit == steps[-1]:
            own, bulk_codes = call(functools.partial(bulk_pair_kernel, panel), halved(count), after(own, part), got)
            part = after(part, bulk_codes)
        part = call(sum_kernel, coded, part, other)
    shared = [swap(part, "row", k) for k in range(1, rows)]
    if split:
        for bit in steps[:-1]:
            count //= 2
            got = swap(after(bulk_codes, part), "scen", 2 * bit)
            own, bulk_codes = call(functools.partial(bulk_sum_kernel, panel), halved(count), own, got)
        got = [swap(bulk_codes, "scen", layers)]
    joined = call(join_kernel, shape((rows * (size + TAIL), panel), I16), part, *shared)
    if split:
        joined = after(joined, bulk_codes)
    other = swap(joined, "scen", 1)
    own_half = call(
        functools.partial(own_kernel, rows), shape((panel // 2, panel), F32), at, joined, scalars=1
    )
    square = shape((half, half), F32)
    inverse_first, pivots = call(
        functools.partial(first_kernel, rows), (square, shape((panel, panel), F32)),
        at, own_half, other, scalars=1, micros=4.5,
    )
    inverse_second = call(second_kernel, square, pivots, inverse_first, micros=4.5)
    out = shape((share, 1, half), F32)
    return call(
        factor_kernel, (out, out),
        inverse_first, inverse_second, pivots, own, *got,
    )


def solution(mesh):
    placed = (P("scen", None, "row"), P("scen", "row", None), P("scen", "row"), P())
    return jax.shard_map(
        shards,
        mesh=mesh,
        in_specs=placed,
        out_specs=(P("scen", "row", None), P("scen", "row", None)),
        check_vma=False,
    )
```

```python
import functools

import jax
import jax.numpy as jnp
from jax import lax
from jax.experimental import pallas as pl
from jax.experimental.pallas import tpu as pltpu
from jax.sharding import PartitionSpec as P

HALF = 256
NEWTON = 8
TAIL = 16
SHORT = 8
CHUNKS = 4
LEVELS = 32000.0
F32 = jnp.float32
BF16 = jnp.bfloat16
I16 = jnp.int16


def halves(a):
    high = a.astype(BF16)
    low = (a - high.astype(F32)).astype(BF16)
    return high, low


def left_of(a):
    high, low = halves(a)
    return jnp.concatenate([high, high, low], axis=1)


def right_of(b):
    high, low = halves(b)
    return jnp.concatenate([high, low, high], axis=0)


def dot(a, b):
    return jnp.dot(a, b, preferred_element_type=F32)


def product(a, b):
    return dot(left_of(a), right_of(b))


def nearly(pivot):
    size = jnp.abs(pivot)
    norm_one = jnp.max(jnp.sum(size, axis=0, keepdims=True))
    norm_inf = jnp.max(jnp.sum(size, axis=1, keepdims=True))
    approx = pivot.T / (norm_one * norm_inf)
    count = pivot.shape[0]
    one = lax.broadcasted_iota(jnp.int32, pivot.shape, 0) == lax.broadcasted_iota(jnp.int32, pivot.shape, 1)
    rest = jnp.where(one, F32(1.0), F32(0.0)) - product(approx, pivot)
    for step in range(NEWTON - 2):
        both = product(rest, jnp.concatenate([rest, approx], axis=1))
        rest, approx = both[:, :count], approx + both[:, count:]
    return approx + product(rest, approx)


def newton_below(pivot, below):
    approx = nearly(pivot)
    count = pivot.shape[0]
    both = product(jnp.concatenate([pivot, below], axis=0), approx)
    stacked = jnp.concatenate([approx, both[count:]], axis=0)
    return 2.0 * stacked - product(stacked, both[:count])


def newton_beside(pivot, beside):
    approx = nearly(pivot)
    count = pivot.shape[0]
    both = product(approx, jnp.concatenate([pivot, beside], axis=1))
    stacked = jnp.concatenate([approx, both[:, count:]], axis=1)
    return 2.0 * stacked - product(both[:, :count], stacked)


def aligned(index, size):
    return pl.multiple_of(index * size, size)


def encode(values, out_ref, base, tail_rows, diagonal=None):
    rows, lanes = values.shape
    top = jnp.maximum(jnp.max(jnp.abs(values), axis=0, keepdims=True), F32(1e-30))
    power = jnp.ceil(jnp.log2(top))
    unit = jnp.exp2(power)
    mantissa = jnp.ceil(top / unit * F32(16384.0))
    scale = mantissa * unit * F32(1.0 / (16384.0 * LEVELS))
    codes = jnp.round(values * (F32(1.0) / scale)).astype(jnp.int32)
    out_ref[base:base + rows, :] = codes.astype(I16)
    row = lax.broadcasted_iota(jnp.int32, (tail_rows, lanes), 0)
    tail = jnp.where(row == 0, power, jnp.where(row == 1, mantissa, F32(0.0)))
    if diagonal is not None:
        coarse = jnp.floor(diagonal * F32(64.0))
        fine = (diagonal * F32(64.0) - coarse) * F32(4096.0)
        tail = jnp.where(row == 2, coarse, jnp.where(row == 3, fine, tail))
    out_ref[base + rows:base + rows + tail_rows, :] = tail.astype(jnp.int32).astype(I16)


def decode(ref, base, rows, tail_rows):
    tail = ref[base + rows:base + rows + tail_rows, :].astype(jnp.int32).astype(F32)
    scale = tail[1:2] * jnp.exp2(tail[0:1]) * F32(1.0 / (16384.0 * LEVELS))
    diagonal = tail[2:3] * F32(1.0 / 64.0) + tail[3:4] * F32(1.0 / (64.0 * 4096.0))
    return ref[base:base + rows, :].astype(jnp.int32).astype(F32) * scale, diagonal


def turn_kernel(solves_ref, upper_ref, lower_ref, solves_copy, done):
    copy = pltpu.make_async_copy(solves_ref, solves_copy, done)
    copy.start()
    copy.wait()
    turned = solves_copy[...].T
    half = upper_ref.shape[0]
    upper_ref[...] = turned[:half]
    lower_ref[...] = turned[half:]


def fetch(source_ref, target_ref, done, first):
    rows = target_ref.shape[1]
    copies = [
        pltpu.make_async_copy(source_ref.at[pl.ds((first + i) * rows, rows), :], target_ref.at[i], done.at[i])
        for i in range(target_ref.shape[0])
    ]
    for copy in copies:
        copy.start()
    return copies


def choose(copies, coupling_copy, one_ref, chosen_ref, first):
    rows = coupling_copy.shape[1]
    for i, copy in enumerate(copies):
        copy.wait()
        chosen_ref[(first + i) * rows:(first + i + 1) * rows, :] = dot(coupling_copy[i], one_ref[...]).astype(BF16)


def pick_kernel(
    place_ref, panel_ref, own_diagonal_ref, coupling_ref,
    chosen_ref, entry_ref, one_ref, panel_out, diagonal_out, coupling_copy, small_done, done,
):
    small = [
        pltpu.make_async_copy(panel_ref, panel_out, small_done.at[0]),
        pltpu.make_async_copy(own_diagonal_ref, diagonal_out, small_done.at[1]),
    ]
    for copy in small:
        copy.start()
    copies = fetch(coupling_ref, coupling_copy, done, 0)
    for copy in small:
        copy.wait()
    first_column, first_row = place_ref[0], place_ref[1]
    columns, panel = one_ref.shape
    share = diagonal_out.shape[1]
    here = panel_out[...] - first_column == lax.broadcasted_iota(jnp.int32, (columns, panel), 0)
    one_ref[...] = jnp.where(here, F32(1.0), F32(0.0)).astype(BF16)
    owned = panel_out[...] - first_row == lax.broadcasted_iota(jnp.int32, (share, panel), 0)
    own = jnp.broadcast_to(diagonal_out[...], (8, share)).T[:, :1]
    entry = jnp.sum(jnp.where(owned, own, F32(0.0)), axis=0, keepdims=True)
    entry_ref[...] = jnp.broadcast_to(entry, entry_ref.shape)
    choose(copies, coupling_copy, one_ref, chosen_ref, 0)


def rest_kernel(chosen_in, one_ref, coupling_ref, chosen_ref, coupling_copy, done):
    first = coupling_copy.shape[0]
    copies = fetch(coupling_ref, coupling_copy, done, first)
    choose(copies, coupling_copy, one_ref, chosen_ref, first)


def early_kernel(place_ref, chosen_ref, *refs):
    *pieces, turned_ref, terms_ref = refs
    if len(pieces) == 1:
        turned_ref[...] = pieces[0][...]
    else:
        half, width = pieces[0].shape
        for i, piece in enumerate(pieces):
            start = aligned(place_ref[0] ^ (i // 2), width)
            turned_ref[i % 2 * half:(i % 2 + 1) * half, pl.ds(start, width)] = piece[...]
        start = aligned(place_ref[0] ^ (len(pieces) // 2), width)
        turned_ref[:, pl.ds(start, width)] = jnp.zeros((2 * half, width), BF16)
    terms_ref[...] = dot(turned_ref[...], chosen_ref[...])


def half_terms(rows, place_ref, chosen_ref, terms_ref, far, whose, out_ref, all_ref):
    half = all_ref.shape[0]
    size = half // rows
    total = terms_ref[pl.ds(aligned(whose, half), half), :]
    if far:
        width = far[0].shape[1]
        block = jnp.where(whose == 0, far[0][...], far[1][...])
        total = total + dot(block, chosen_ref[pl.ds(aligned(place_ref[0] ^ (rows - 1), width), width), :])
    all_ref[...] = total
    for k in range(rows):
        out_ref[k * size:(k + 1) * size, :] = all_ref[pl.ds(aligned(place_ref[0] ^ k, size), size), :]


def send_kernel(rows, place_ref, chosen_ref, entry_ref, terms_ref, *refs):
    *far, send_ref, all_ref = refs
    half_terms(rows, place_ref, chosen_ref, terms_ref, far, 1 - place_ref[1], send_ref, all_ref)
    send_ref[all_ref.shape[0]:, :] = entry_ref[...]


def keep_kernel(rows, place_ref, turned_in, chosen_ref, terms_ref, *refs):
    *far, turned_ref, keep_ref, all_ref = refs
    half_terms(rows, place_ref, chosen_ref, terms_ref, far, place_ref[1], keep_ref, all_ref)
    for i, piece in enumerate(far):
        half, width = piece.shape
        start = aligned(place_ref[0] ^ (rows - 1), width)
        turned_ref[i * half:(i + 1) * half, pl.ds(start, width)] = piece[...]


def pair_kernel(rows, keep_ref, got_ref, entry_ref, *out_refs):
    size = keep_ref.shape[0] // rows
    entry = entry_ref[:1, :] + got_ref[rows * size:rows * size + 1, :]
    for k, out_ref in enumerate(out_refs):
        part = slice(k * size, (k + 1) * size)
        encode(keep_ref[part, :] + got_ref[part, :], out_ref, 0, SHORT, entry)


def sum_kernel(*refs):
    *in_refs, out_ref = refs
    size = out_ref.shape[0] - SHORT
    parts = [decode(ref, 0, size, SHORT) for ref in in_refs]
    encode(sum(p[0] for p in parts), out_ref, 0, SHORT, sum(p[1] for p in parts))


def join_kernel(*refs):
    *in_refs, out_ref = refs
    size = in_refs[0].shape[0] - SHORT
    for k, ref in enumerate(in_refs):
        start = k * (size + TAIL)
        out_ref[start:start + size, :] = ref[:size, :]
        tail = ref[size:, :].astype(jnp.int32)
        out_ref[start + size:start + size + TAIL, :] = jnp.concatenate([tail, jnp.zeros_like(tail)], axis=0).astype(I16)


def place_pieces(row, whose, ref, pivots_ref, rows, base):
    panel = pivots_ref.shape[1]
    size = panel // (2 * rows)
    index = lax.broadcasted_iota(jnp.int32, (size, panel), 1)
    for k in range(rows):
        start = aligned(whose * rows + (row ^ k), size)
        values, diagonal = decode(ref, k * (size + TAIL), size, TAIL)
        at = lax.broadcasted_iota(jnp.int32, (size, panel), 0) + start == index
        pivots_ref[pl.ds(start - base, size), :] = values + jnp.where(at, diagonal, F32(0.0))


def own_kernel(rows, place_ref, own_ref, half_ref):
    place_pieces(place_ref[0], place_ref[1], own_ref, half_ref, rows, place_ref[1] * half_ref.shape[0])


def first_kernel(rows, place_ref, half_ref, other_ref, inverse_ref, pivots_ref):
    row, core = place_ref[0], place_ref[1]
    half = half_ref.shape[0]
    pivots_ref[pl.ds(aligned(core, half), half), :] = half_ref[...]
    place_pieces(row, 1 - core, other_ref, pivots_ref, rows, 0)
    inverse_ref[...] = newton_below(pivots_ref[:half, :half], pivots_ref[half:, :half])


def second_kernel(pivots_ref, inverse_first_ref, inverse_ref):
    half = inverse_ref.shape[0]
    below = inverse_first_ref[half:, :]
    pivot = pivots_ref[half:, half:] - product(below, pivots_ref[:half, half:])
    inverse_ref[...] = newton_beside(pivot, -below)


def schur_kernel(place_ref, panel_ref, own_diagonal_ref, coupling_ref, turned_ref, keep_ref, send_ref):
    core, layer = place_ref[1], place_ref[2]
    panel, share = turned_ref.shape[0], keep_ref.shape[1]
    layers = keep_ref.shape[0] // panel
    for position, k in enumerate(reversed_order(layers)):
        start = aligned(layer ^ k, 2 * share)
        both = dot(turned_ref[...], coupling_ref[:, pl.ds(start, 2 * share)])
        rows = slice(position * panel, (position + 1) * panel)
        one, two = both[:, :share], both[:, share:]
        kept = jnp.where(core == 0, one, two)
        if position == 0:
            wanted = jnp.broadcast_to(panel_ref[...].astype(F32), (share, panel)).T.astype(jnp.int32)
            here = wanted - place_ref[3] == lax.broadcasted_iota(jnp.int32, (panel, share), 1)
            kept = kept + jnp.where(here, own_diagonal_ref[...], F32(0.0))
        keep_ref[rows, :] = kept
        send_ref[rows, :] = jnp.where(core == 0, two, one)


def bulk_pair_kernel(panel, keep_ref, got_ref, own_ref, coded_ref):
    half = own_ref.shape[0]
    own_ref[...] = keep_ref[:half, :] + got_ref[:half, :]
    for i in range(half // panel):
        part = slice(half + i * panel, half + (i + 1) * panel)
        encode(keep_ref[part, :] + got_ref[part, :], coded_ref, i * (panel + TAIL), TAIL)


def bulk_sum_kernel(panel, keep_ref, got_ref, own_ref, coded_ref):
    half = own_ref.shape[0]
    for i in range(keep_ref.shape[0] // panel):
        value = keep_ref[i * panel:(i + 1) * panel, :] + decode(got_ref, i * (panel + TAIL), panel, TAIL)[0]
        if i * panel < half:
            own_ref[i * panel:(i + 1) * panel, :] = value
        else:
            encode(value, coded_ref, (i - half // panel) * (panel + TAIL), TAIL)


def factor_kernel(inverse_first_ref, inverse_second_ref, rows_ref, *refs):
    *got, first_out, second_out = refs
    panel = rows_ref.shape[0]
    half = panel // 2
    rows = rows_ref[...]
    for ref in got:
        rows = rows + decode(ref, 0, panel, TAIL)[0]
    first, second = rows[:half], rows[half:]
    first_out[...] = product(inverse_first_ref[:half, :], first).T[:, None, :]
    second_out[...] = product(inverse_second_ref[...], jnp.concatenate([second, first], axis=0)).T[:, None, :]


def call(kernel, out_shape, *args, scratch=(), scalars=0, remain=0, micros=0.0, aliases=None):
    hbm = pl.BlockSpec(memory_space=pltpu.HBM)
    vmem = pl.BlockSpec(memory_space=pltpu.VMEM)
    smem = pl.BlockSpec(memory_space=pltpu.SMEM)
    stay = len(args) - remain
    args = args[:stay] + tuple(pltpu.with_memory_space_constraint(x, pltpu.HBM) for x in args[stay:])
    return pl.pallas_call(
        kernel,
        name=getattr(kernel, "func", kernel).__name__,
        out_shape=out_shape,
        in_specs=[smem] * scalars + [vmem] * (len(args) - scalars - remain) + [hbm] * remain,
        out_specs=jax.tree.map(lambda _: vmem, out_shape),
        scratch_shapes=scratch,
        input_output_aliases=aliases or {},
        compiler_params=pltpu.CompilerParams(vmem_limit_bytes=28 << 20),
        cost_estimate=pl.CostEstimate(flops=0, bytes_accessed=int(micros * 3.69e6) + 1024, transcendentals=0),
    )(*args)


def swap(x, axis, bit):
    count = lax.axis_size(axis)
    return lax.ppermute(x, axis, [(i, i ^ bit) for i in range(count)])


def after(x, *others):
    return lax.optimization_barrier((x,) + others)[0]


def bits_of(count):
    return [1 << i for i in range(count.bit_length() - 1)]


def reversed_order(count):
    width = count.bit_length() - 1
    return [int(f"{p:0{width}b}"[::-1], 2) for p in range(count)]


def gather_pieces(solves, rows, ready):
    block, panel = solves.shape
    if rows != 4:
        return [lax.all_gather(solves.T, "row", axis=1, tiled=True)]
    half = pltpu.VMEM((panel // 2, block), BF16)
    upper, lower = call(
        turn_kernel, (half, half), solves, remain=1,
        scratch=[pltpu.VMEM((block, panel), BF16), pltpu.SemaphoreType.DMA],
    )
    lower_x, upper_y = swap(lower, "row", 1), swap(upper, "row", 2)
    upper_x, lower_y = swap(upper, "row", 1), swap(lower, "row", 2)
    upper_far, lower_far = swap(after(upper_y, *ready), "row", 1), swap(after(lower_x, *ready), "row", 2)
    return [upper, lower, upper_x, lower_x, upper_y, lower_y, upper_far, lower_far]


def shards(coupling, solves, border_diagonal, panel_rows):
    half = HALF
    coupling, solves = coupling[0], solves[0]
    local, row_count = coupling.shape
    panel = solves.shape[1]
    scen, rows = lax.axis_size("scen"), lax.axis_size("row")
    layers = scen // 2
    row, place = lax.axis_index("row"), lax.axis_index("scen")
    share = row_count // scen
    size = panel // (2 * rows)
    shape = pltpu.VMEM
    panel_row, diagonal_row = panel_rows[None, :], border_diagonal.T
    first_row = row * row_count + place * share
    starts = jnp.stack([row * row_count, first_row]).astype(jnp.int32)
    at = jnp.stack([row, place % 2, place // 2, first_row]).astype(jnp.int32)

    picked = shape((local, panel), BF16)
    chunk_room = [
        pltpu.VMEM((CHUNKS // 2, local // CHUNKS, row_count), BF16), pltpu.SemaphoreType.DMA((CHUNKS // 2,))
    ]
    chosen, entry, one, panel_row, diagonal_row = call(
        pick_kernel,
        (
            picked, shape((8, panel), F32), shape((row_count, panel), BF16),
            shape((1, panel), jnp.int32), shape((1, share), F32),
        ),
        starts, panel_row, diagonal_row, coupling, scalars=1, remain=3,
        scratch=[chunk_room[0], pltpu.SemaphoreType.DMA((2,)), chunk_room[1]],
    )
    pieces = gather_pieces(solves, rows, (entry,))
    near, far = pieces[:6], pieces[6:]
    chosen = call(rest_kernel, picked, chosen, one, coupling, remain=1, scratch=chunk_room, aliases={0: 0})
    room = [pltpu.VMEM((panel // 2, panel), F32)]
    turned, terms = call(
        early_kernel, (shape((panel, local), BF16), shape((panel, panel), F32)), at, chosen, *near, scalars=1
    )
    send = call(
        functools.partial(send_kernel, rows), shape((panel // 2 + 8, panel), F32),
        at, chosen, entry, terms, *far, scalars=1, scratch=room,
    )
    turned, keep = call(
        functools.partial(keep_kernel, rows), (shape((panel, local), BF16), shape((panel // 2, panel), F32)),
        at, turned, chosen, terms, *far, scalars=1, scratch=room, aliases={1: 0},
    )
    coded = shape((size + SHORT, panel), I16)
    codes = call(
        functools.partial(pair_kernel, rows), (coded,) * rows, keep, swap(send, "scen", 1), entry
    )
    arrived = [swap(codes[k], "row", k) for k in range(rows - 1, 0, -1)]
    part = codes[0]
    steps = bits_of(layers)
    split = share % 128 == 0
    if split:
        count = layers // 2
        bulk = shape((layers * panel, share), F32)
        halved = lambda count: (shape((count * panel, share), F32), shape((count * (panel + TAIL), share), I16))
        own, send_rows = call(
            schur_kernel, (bulk, bulk), at, panel_row, diagonal_row, coupling, after(turned, part), scalars=1
        )
        part = call(sum_kernel, coded, after(part, own), *arrived)
        got = swap(after(send_rows, part), "scen", 1)
    else:
        own, got = lax.psum_scatter(dot(turned, coupling), "scen", scatter_dimension=1, tiled=True), []
        mine = first_row + jnp.arange(share, dtype=jnp.int32)
        own = own + jnp.where(panel_rows[:, None] == mine[None, :], border_diagonal[:, 0][None, :], F32(0.0))
        part = call(sum_kernel, coded, part, *arrived)
    for bit in steps:
        other = swap(part, "scen", 2 * bit)
        if split and bit == steps[-1]:
            own, bulk_codes = call(functools.partial(bulk_pair_kernel, panel), halved(count), after(own, part), got)
            part = after(part, bulk_codes)
        part = call(sum_kernel, coded, part, other)
    shared = [swap(part, "row", k) for k in range(1, rows)]
    if split:
        for bit in steps[:-1]:
            count //= 2
            got = swap(after(bulk_codes, part), "scen", 2 * bit)
            own, bulk_codes = call(functools.partial(bulk_sum_kernel, panel), halved(count), own, got)
        got = [swap(bulk_codes, "scen", layers)]
    joined = call(join_kernel, shape((rows * (size + TAIL), panel), I16), part, *shared)
    if split:
        joined = after(joined, bulk_codes)
    other = swap(joined, "scen", 1)
    own_half = call(
        functools.partial(own_kernel, rows), shape((panel // 2, panel), F32), at, joined, scalars=1
    )
    inverse_first, pivots = call(
        functools.partial(first_kernel, rows), (shape((panel, half), F32), shape((panel, panel), F32)),
        at, own_half, other, scalars=1, micros=4.5,
    )
    inverse_second = call(second_kernel, shape((half, panel), F32), pivots, inverse_first, micros=4.5)
    out = jax.ShapeDtypeStruct((share, 1, half), F32)
    return call(
        factor_kernel, (out, out),
        inverse_first, inverse_second, own, *got,
    )


def solution(mesh):
    placed = (P("scen", None, "row"), P("scen", "row", None), P("scen", "row"), P())
    return jax.shard_map(
        shards,
        mesh=mesh,
        in_specs=placed,
        out_specs=(P("scen", "row", None), P("scen", "row", None)),
        check_vma=False,
    )
```

```python
import functools

import jax
import jax.numpy as jnp
from jax import lax
from jax.experimental import pallas as pl
from jax.experimental.pallas import tpu as pltpu
from jax.sharding import PartitionSpec as P

HALF = 256
NEWTON = 8
TAIL = 16
SHORT = 8
CHUNKS = 4
LEVELS = 32000.0
F32 = jnp.float32
BF16 = jnp.bfloat16
I16 = jnp.int16


def halves(a):
    high = a.astype(BF16)
    low = (a - high.astype(F32)).astype(BF16)
    return high, low


def left_of(a):
    high, low = halves(a)
    return jnp.concatenate([high, high, low], axis=1)


def right_of(b):
    high, low = halves(b)
    return jnp.concatenate([high, low, high], axis=0)


def dot(a, b):
    return jnp.dot(a, b, preferred_element_type=F32)


def product(a, b):
    return dot(left_of(a), right_of(b))


def nearly(pivot):
    size = jnp.abs(pivot)
    norm_one = jnp.max(jnp.sum(size, axis=0, keepdims=True))
    norm_inf = jnp.max(jnp.sum(size, axis=1, keepdims=True))
    approx = pivot.T / (norm_one * norm_inf)
    count = pivot.shape[0]
    one = lax.broadcasted_iota(jnp.int32, pivot.shape, 0) == lax.broadcasted_iota(jnp.int32, pivot.shape, 1)
    rest = jnp.where(one, F32(1.0), F32(0.0)) - product(approx, pivot)
    for step in range(NEWTON - 2):
        both = product(rest, jnp.concatenate([rest, approx], axis=1))
        rest, approx = both[:, :count], approx + both[:, count:]
    return approx + product(rest, approx)


def newton_below(pivot, below):
    approx = nearly(pivot)
    count = pivot.shape[0]
    both = product(jnp.concatenate([pivot, below], axis=0), approx)
    stacked = jnp.concatenate([approx, both[count:]], axis=0)
    return 2.0 * stacked - product(stacked, both[:count])


def newton_beside(pivot, beside):
    approx = nearly(pivot)
    count = pivot.shape[0]
    both = product(approx, jnp.concatenate([pivot, beside], axis=1))
    stacked = jnp.concatenate([approx, both[:, count:]], axis=1)
    return 2.0 * stacked - product(both[:, :count], stacked)


def aligned(index, size):
    return pl.multiple_of(index * size, size)


def encode(values, out_ref, base, tail_rows, diagonal=None):
    rows, lanes = values.shape
    top = jnp.maximum(jnp.max(jnp.abs(values), axis=0, keepdims=True), F32(1e-30))
    power = jnp.ceil(jnp.log2(top))
    unit = jnp.exp2(power)
    mantissa = jnp.ceil(top / unit * F32(16384.0))
    scale = mantissa * unit * F32(1.0 / (16384.0 * LEVELS))
    codes = jnp.round(values * (F32(1.0) / scale)).astype(jnp.int32)
    out_ref[base:base + rows, :] = codes.astype(I16)
    row = lax.broadcasted_iota(jnp.int32, (tail_rows, lanes), 0)
    tail = jnp.where(row == 0, power, jnp.where(row == 1, mantissa, F32(0.0)))
    if diagonal is not None:
        coarse = jnp.floor(diagonal * F32(64.0))
        fine = (diagonal * F32(64.0) - coarse) * F32(4096.0)
        tail = jnp.where(row == 2, coarse, jnp.where(row == 3, fine, tail))
    out_ref[base + rows:base + rows + tail_rows, :] = tail.astype(jnp.int32).astype(I16)


def decode(ref, base, rows, tail_rows):
    tail = ref[base + rows:base + rows + tail_rows, :].astype(jnp.int32).astype(F32)
    scale = tail[1:2] * jnp.exp2(tail[0:1]) * F32(1.0 / (16384.0 * LEVELS))
    diagonal = tail[2:3] * F32(1.0 / 64.0) + tail[3:4] * F32(1.0 / (64.0 * 4096.0))
    return ref[base:base + rows, :].astype(jnp.int32).astype(F32) * scale, diagonal


def turn_kernel(solves_ref, upper_ref, lower_ref, solves_copy, done):
    copy = pltpu.make_async_copy(solves_ref, solves_copy, done)
    copy.start()
    copy.wait()
    turned = solves_copy[...].T
    half = upper_ref.shape[0]
    upper_ref[...] = turned[:half]
    lower_ref[...] = turned[half:]


def fetch(source_ref, target_ref, done, first):
    rows = target_ref.shape[1]
    copies = [
        pltpu.make_async_copy(source_ref.at[pl.ds((first + i) * rows, rows), :], target_ref.at[i], done.at[i])
        for i in range(target_ref.shape[0])
    ]
    for copy in copies:
        copy.start()
    return copies


def choose(copies, coupling_copy, one_ref, chosen_ref, first):
    rows = coupling_copy.shape[1]
    for i, copy in enumerate(copies):
        copy.wait()
        chosen_ref[(first + i) * rows:(first + i + 1) * rows, :] = dot(coupling_copy[i], one_ref[...]).astype(BF16)


def pick_kernel(
    place_ref, panel_ref, own_diagonal_ref, coupling_ref,
    chosen_ref, entry_ref, one_ref, panel_out, diagonal_out, coupling_copy, small_done, done,
):
    small = [
        pltpu.make_async_copy(panel_ref, panel_out, small_done.at[0]),
        pltpu.make_async_copy(own_diagonal_ref, diagonal_out, small_done.at[1]),
    ]
    for copy in small:
        copy.start()
    copies = fetch(coupling_ref, coupling_copy, done, 0)
    for copy in small:
        copy.wait()
    first_column, first_row = place_ref[0], place_ref[1]
    columns, panel = one_ref.shape
    share = diagonal_out.shape[1]
    here = panel_out[...] - first_column == lax.broadcasted_iota(jnp.int32, (columns, panel), 0)
    one_ref[...] = jnp.where(here, F32(1.0), F32(0.0)).astype(BF16)
    owned = panel_out[...] - first_row == lax.broadcasted_iota(jnp.int32, (share, panel), 0)
    own = jnp.broadcast_to(diagonal_out[...], (8, share)).T[:, :1]
    entry = jnp.sum(jnp.where(owned, own, F32(0.0)), axis=0, keepdims=True)
    entry_ref[...] = jnp.broadcast_to(entry, entry_ref.shape)
    choose(copies, coupling_copy, one_ref, chosen_ref, 0)


def rest_kernel(chosen_in, one_ref, coupling_ref, chosen_ref, coupling_copy, done):
    first = coupling_copy.shape[0]
    copies = fetch(coupling_ref, coupling_copy, done, first)
    choose(copies, coupling_copy, one_ref, chosen_ref, first)


def early_kernel(place_ref, chosen_ref, *refs):
    *pieces, turned_ref, terms_ref = refs
    if len(pieces) == 1:
        turned_ref[...] = pieces[0][...]
    else:
        half, width = pieces[0].shape
        for i, piece in enumerate(pieces):
            start = aligned(place_ref[0] ^ (i // 2), width)
            turned_ref[i % 2 * half:(i % 2 + 1) * half, pl.ds(start, width)] = piece[...]
        start = aligned(place_ref[0] ^ (len(pieces) // 2), width)
        turned_ref[:, pl.ds(start, width)] = jnp.zeros((2 * half, width), BF16)
    terms_ref[...] = dot(turned_ref[...], chosen_ref[...])


def half_terms(rows, place_ref, chosen_ref, terms_ref, far, whose, out_ref, all_ref):
    half = all_ref.shape[0]
    size = half // rows
    total = terms_ref[pl.ds(aligned(whose, half), half), :]
    if far:
        width = far[0].shape[1]
        block = jnp.where(whose == 0, far[0][...], far[1][...])
        total = total + dot(block, chosen_ref[pl.ds(aligned(place_ref[0] ^ (rows - 1), width), width), :])
    all_ref[...] = total
    for k in range(rows):
        out_ref[k * size:(k + 1) * size, :] = all_ref[pl.ds(aligned(place_ref[0] ^ k, size), size), :]


def send_kernel(rows, place_ref, chosen_ref, entry_ref, terms_ref, *refs):
    *far, send_ref, all_ref = refs
    half_terms(rows, place_ref, chosen_ref, terms_ref, far, 1 - place_ref[1], send_ref, all_ref)
    send_ref[all_ref.shape[0]:, :] = entry_ref[...]


def keep_kernel(rows, place_ref, turned_in, chosen_ref, terms_ref, *refs):
    *far, turned_ref, keep_ref, all_ref = refs
    half_terms(rows, place_ref, chosen_ref, terms_ref, far, place_ref[1], keep_ref, all_ref)
    for i, piece in enumerate(far):
        half, width = piece.shape
        start = aligned(place_ref[0] ^ (rows - 1), width)
        turned_ref[i * half:(i + 1) * half, pl.ds(start, width)] = piece[...]


def pair_kernel(rows, keep_ref, got_ref, entry_ref, *out_refs):
    size = keep_ref.shape[0] // rows
    entry = entry_ref[:1, :] + got_ref[rows * size:rows * size + 1, :]
    for k, out_ref in enumerate(out_refs):
        part = slice(k * size, (k + 1) * size)
        encode(keep_ref[part, :] + got_ref[part, :], out_ref, 0, SHORT, entry)


def sum_kernel(*refs):
    *in_refs, out_ref = refs
    size = out_ref.shape[0] - SHORT
    parts = [decode(ref, 0, size, SHORT) for ref in in_refs]
    encode(sum(p[0] for p in parts), out_ref, 0, SHORT, sum(p[1] for p in parts))


def join_kernel(*refs):
    *in_refs, out_ref = refs
    size = in_refs[0].shape[0] - SHORT
    for k, ref in enumerate(in_refs):
        start = k * (size + TAIL)
        out_ref[start:start + size, :] = ref[:size, :]
        tail = ref[size:, :].astype(jnp.int32)
        out_ref[start + size:start + size + TAIL, :] = jnp.concatenate([tail, jnp.zeros_like(tail)], axis=0).astype(I16)


def place_pieces(row, whose, ref, pivots_ref, rows, base):
    panel = pivots_ref.shape[1]
    size = panel // (2 * rows)
    index = lax.broadcasted_iota(jnp.int32, (size, panel), 1)
    for k in range(rows):
        start = aligned(whose * rows + (row ^ k), size)
        values, diagonal = decode(ref, k * (size + TAIL), size, TAIL)
        at = lax.broadcasted_iota(jnp.int32, (size, panel), 0) + start == index
        pivots_ref[pl.ds(start - base, size), :] = values + jnp.where(at, diagonal, F32(0.0))


def own_kernel(rows, place_ref, own_ref, half_ref):
    place_pieces(place_ref[0], place_ref[1], own_ref, half_ref, rows, place_ref[1] * half_ref.shape[0])


def first_kernel(rows, place_ref, half_ref, other_ref, inverse_ref, pivots_ref):
    row, core = place_ref[0], place_ref[1]
    half = half_ref.shape[0]
    pivots_ref[pl.ds(aligned(core, half), half), :] = half_ref[...]
    place_pieces(row, 1 - core, other_ref, pivots_ref, rows, 0)
    inverse_ref[...] = newton_below(pivots_ref[:half, :half], pivots_ref[half:, :half])


def second_kernel(pivots_ref, inverse_first_ref, inverse_ref):
    half = inverse_ref.shape[0]
    below = inverse_first_ref[half:, :]
    pivot = pivots_ref[half:, half:] - product(below, pivots_ref[:half, half:])
    inverse_ref[...] = newton_beside(pivot, -below)


def schur_kernel(place_ref, panel_ref, own_diagonal_ref, coupling_ref, turned_ref, keep_ref, send_ref):
    core, layer = place_ref[1], place_ref[2]
    panel, share = turned_ref.shape[0], keep_ref.shape[1]
    layers = keep_ref.shape[0] // panel
    for position, k in enumerate(reversed_order(layers)):
        start = aligned(layer ^ k, 2 * share)
        both = dot(turned_ref[...], coupling_ref[:, pl.ds(start, 2 * share)])
        rows = slice(position * panel, (position + 1) * panel)
        one, two = both[:, :share], both[:, share:]
        kept = jnp.where(core == 0, one, two)
        if position == 0:
            wanted = jnp.broadcast_to(panel_ref[...].astype(F32), (share, panel)).T.astype(jnp.int32)
            here = wanted - place_ref[3] == lax.broadcasted_iota(jnp.int32, (panel, share), 1)
            kept = kept + jnp.where(here, own_diagonal_ref[...], F32(0.0))
        keep_ref[rows, :] = kept
        send_ref[rows, :] = jnp.where(core == 0, two, one)


def bulk_pair_kernel(panel, keep_ref, got_ref, own_ref, coded_ref):
    half = own_ref.shape[0]
    own_ref[...] = keep_ref[:half, :] + got_ref[:half, :]
    for i in range(half // panel):
        part = slice(half + i * panel, half + (i + 1) * panel)
        encode(keep_ref[part, :] + got_ref[part, :], coded_ref, i * (panel + TAIL), TAIL)


def bulk_sum_kernel(panel, keep_ref, got_ref, own_ref, coded_ref):
    half = own_ref.shape[0]
    for i in range(keep_ref.shape[0] // panel):
        value = keep_ref[i * panel:(i + 1) * panel, :] + decode(got_ref, i * (panel + TAIL), panel, TAIL)[0]
        if i * panel < half:
            own_ref[i * panel:(i + 1) * panel, :] = value
        else:
            encode(value, coded_ref, (i - half // panel) * (panel + TAIL), TAIL)


def factor_kernel(inverse_first_ref, inverse_second_ref, rows_ref, *refs):
    *got, first_out, second_out = refs
    panel = rows_ref.shape[0]
    half = panel // 2
    rows = rows_ref[...]
    for ref in got:
        rows = rows + decode(ref, 0, panel, TAIL)[0]
    first, second = rows[:half], rows[half:]
    first_out[...] = product(inverse_first_ref[:half, :], first).T[:, None, :]
    second_out[...] = product(inverse_second_ref[...], jnp.concatenate([second, first], axis=0)).T[:, None, :]


def call(kernel, out_shape, *args, scratch=(), scalars=0, remain=0, micros=0.0, aliases=None):
    hbm = pl.BlockSpec(memory_space=pltpu.HBM)
    vmem = pl.BlockSpec(memory_space=pltpu.VMEM)
    smem = pl.BlockSpec(memory_space=pltpu.SMEM)
    stay = len(args) - remain
    args = args[:stay] + tuple(pltpu.with_memory_space_constraint(x, pltpu.HBM) for x in args[stay:])
    return pl.pallas_call(
        kernel,
        name=getattr(kernel, "func", kernel).__name__,
        out_shape=out_shape,
        in_specs=[smem] * scalars + [vmem] * (len(args) - scalars - remain) + [hbm] * remain,
        out_specs=jax.tree.map(lambda _: vmem, out_shape),
        scratch_shapes=scratch,
        input_output_aliases=aliases or {},
        compiler_params=pltpu.CompilerParams(vmem_limit_bytes=12 << 20),
        cost_estimate=pl.CostEstimate(flops=0, bytes_accessed=int(micros * 3.69e6) + 1024, transcendentals=0),
    )(*args)


def swap(x, axis, bit):
    count = lax.axis_size(axis)
    return lax.ppermute(x, axis, [(i, i ^ bit) for i in range(count)])


def after(x, *others):
    return lax.optimization_barrier((x,) + others)[0]


def bits_of(count):
    return [1 << i for i in range(count.bit_length() - 1)]


def reversed_order(count):
    width = count.bit_length() - 1
    return [int(f"{p:0{width}b}"[::-1], 2) for p in range(count)]


def gather_pieces(solves, rows, ready):
    block, panel = solves.shape
    if rows != 4:
        return [lax.all_gather(solves.T, "row", axis=1, tiled=True)]
    half = pltpu.VMEM((panel // 2, block), BF16)
    upper, lower = call(
        turn_kernel, (half, half), solves, remain=1,
        scratch=[pltpu.VMEM((block, panel), BF16), pltpu.SemaphoreType.DMA],
    )
    lower_x, upper_y = swap(lower, "row", 1), swap(upper, "row", 2)
    upper_x, lower_y = swap(upper, "row", 1), swap(lower, "row", 2)
    upper_far, lower_far = swap(after(upper_y, *ready), "row", 1), swap(after(lower_x, *ready), "row", 2)
    return [upper, lower, upper_x, lower_x, upper_y, lower_y, upper_far, lower_far]


def shards(coupling, solves, border_diagonal, panel_rows):
    half = HALF
    coupling, solves = coupling[0], solves[0]
    local, row_count = coupling.shape
    panel = solves.shape[1]
    scen, rows = lax.axis_size("scen"), lax.axis_size("row")
    layers = scen // 2
    row, place = lax.axis_index("row"), lax.axis_index("scen")
    share = row_count // scen
    size = panel // (2 * rows)
    shape = pltpu.VMEM
    panel_row, diagonal_row = panel_rows[None, :], border_diagonal.T
    first_row = row * row_count + place * share
    starts = jnp.stack([row * row_count, first_row]).astype(jnp.int32)
    at = jnp.stack([row, place % 2, place // 2, first_row]).astype(jnp.int32)

    picked = shape((local, panel), BF16)
    chunk_room = [
        pltpu.VMEM((CHUNKS // 2, local // CHUNKS, row_count), BF16), pltpu.SemaphoreType.DMA((CHUNKS // 2,))
    ]
    chosen, entry, one, panel_row, diagonal_row = call(
        pick_kernel,
        (
            picked, shape((8, panel), F32), shape((row_count, panel), BF16),
            shape((1, panel), jnp.int32), shape((1, share), F32),
        ),
        starts, panel_row, diagonal_row, coupling, scalars=1, remain=3,
        scratch=[chunk_room[0], pltpu.SemaphoreType.DMA((2,)), chunk_room[1]],
    )
    pieces = gather_pieces(solves, rows, (entry,))
    near, far = pieces[:6], pieces[6:]
    chosen = call(rest_kernel, picked, chosen, one, coupling, remain=1, scratch=chunk_room, aliases={0: 0})
    room = [pltpu.VMEM((panel // 2, panel), F32)]
    turned, terms = call(
        early_kernel, (shape((panel, local), BF16), shape((panel, panel), F32)), at, chosen, *near, scalars=1
    )
    send = call(
        functools.partial(send_kernel, rows), shape((panel // 2 + 8, panel), F32),
        at, chosen, entry, terms, *far, scalars=1, scratch=room,
    )
    turned, keep = call(
        functools.partial(keep_kernel, rows), (shape((panel, local), BF16), shape((panel // 2, panel), F32)),
        at, turned, chosen, terms, *far, scalars=1, scratch=room, aliases={1: 0},
    )
    coded = shape((size + SHORT, panel), I16)
    codes = call(
        functools.partial(pair_kernel, rows), (coded,) * rows, keep, swap(send, "scen", 1), entry
    )
    arrived = [swap(codes[k], "row", k) for k in range(rows - 1, 0, -1)]
    part = codes[0]
    steps = bits_of(layers)
    split = share % 128 == 0
    if split:
        count = layers // 2
        bulk = shape((layers * panel, share), F32)
        halved = lambda count: (shape((count * panel, share), F32), shape((count * (panel + TAIL), share), I16))
        own, send_rows = call(
            schur_kernel, (bulk, bulk), at, panel_row, diagonal_row, coupling, after(turned, part), scalars=1
        )
        part = call(sum_kernel, coded, after(part, own), *arrived)
        got = swap(after(send_rows, part), "scen", 1)
    else:
        own, got = lax.psum_scatter(dot(turned, coupling), "scen", scatter_dimension=1, tiled=True), []
        mine = first_row + jnp.arange(share, dtype=jnp.int32)
        own = own + jnp.where(panel_rows[:, None] == mine[None, :], border_diagonal[:, 0][None, :], F32(0.0))
        part = call(sum_kernel, coded, part, *arrived)
    for bit in steps:
        other = swap(part, "scen", 2 * bit)
        if split and bit == steps[-1]:
            own, bulk_codes = call(functools.partial(bulk_pair_kernel, panel), halved(count), after(own, part), got)
            part = after(part, bulk_codes)
        part = call(sum_kernel, coded, part, other)
    shared = [swap(part, "row", k) for k in range(1, rows)]
    if split:
        for bit in steps[:-1]:
            count //= 2
            got = swap(after(bulk_codes, part), "scen", 2 * bit)
            own, bulk_codes = call(functools.partial(bulk_sum_kernel, panel), halved(count), own, got)
        got = [swap(bulk_codes, "scen", layers)]
    joined = call(join_kernel, shape((rows * (size + TAIL), panel), I16), part, *shared)
    if split:
        joined = after(joined, bulk_codes)
    other = swap(joined, "scen", 1)
    own_half = call(
        functools.partial(own_kernel, rows), shape((panel // 2, panel), F32), at, joined, scalars=1
    )
    inverse_first, pivots = call(
        functools.partial(first_kernel, rows), (shape((panel, half), F32), shape((panel, panel), F32)),
        at, own_half, other, scalars=1, micros=4.5,
    )
    inverse_second = call(second_kernel, shape((half, panel), F32), pivots, inverse_first, micros=4.5)
    out = jax.ShapeDtypeStruct((share, 1, half), F32)
    return call(
        factor_kernel, (out, out),
        inverse_first, inverse_second, own, *got,
    )


def solution(mesh):
    placed = (P("scen", None, "row"), P("scen", "row", None), P("scen", "row"), P())
    return jax.shard_map(
        shards,
        mesh=mesh,
        in_specs=placed,
        out_specs=(P("scen", "row", None), P("scen", "row", None)),
        check_vma=False,
    )
```

```python
import functools

import jax
import jax.numpy as jnp
from jax import lax
from jax.experimental import pallas as pl
from jax.experimental.pallas import tpu as pltpu
from jax.sharding import PartitionSpec as P

HALF = 256
NEWTON = 8
TAIL = 16
SHORT = 8
CHUNKS = 4
LEVELS = 32000.0
F32 = jnp.float32
BF16 = jnp.bfloat16
I16 = jnp.int16


def halves(a):
    high = a.astype(BF16)
    low = (a - high.astype(F32)).astype(BF16)
    return high, low


def left_of(a):
    high, low = halves(a)
    return jnp.concatenate([high, high, low], axis=1)


def right_of(b):
    high, low = halves(b)
    return jnp.concatenate([high, low, high], axis=0)


def dot(a, b):
    return jnp.dot(a, b, preferred_element_type=F32)


def product(a, b):
    return dot(left_of(a), right_of(b))


def nearly(pivot):
    size = jnp.abs(pivot)
    norm_one = jnp.max(jnp.sum(size, axis=0, keepdims=True))
    norm_inf = jnp.max(jnp.sum(size, axis=1, keepdims=True))
    approx = pivot.T / (norm_one * norm_inf)
    count = pivot.shape[0]
    one = lax.broadcasted_iota(jnp.int32, pivot.shape, 0) == lax.broadcasted_iota(jnp.int32, pivot.shape, 1)
    rest = jnp.where(one, F32(1.0), F32(0.0)) - product(approx, pivot)
    for step in range(NEWTON - 2):
        both = product(rest, jnp.concatenate([rest, approx], axis=1))
        rest, approx = both[:, :count], approx + both[:, count:]
    return approx + product(rest, approx)


def newton_below(pivot, below):
    approx = nearly(pivot)
    count = pivot.shape[0]
    both = product(jnp.concatenate([pivot, below], axis=0), approx)
    stacked = jnp.concatenate([approx, both[count:]], axis=0)
    return 2.0 * stacked - product(stacked, both[:count])


def newton_beside(pivot, beside):
    approx = nearly(pivot)
    count = pivot.shape[0]
    both = product(approx, jnp.concatenate([pivot, beside], axis=1))
    stacked = jnp.concatenate([approx, both[:, count:]], axis=1)
    return 2.0 * stacked - product(both[:, :count], stacked)


def whereabouts():
    place = lax.axis_index("scen")
    return lax.axis_index("row"), lax.rem(place, 2), lax.div(place, 2)


def aligned(index, size):
    return pl.multiple_of(index * size, size)


def encode(values, out_ref, base, tail_rows, diagonal=None):
    rows, lanes = values.shape
    top = jnp.maximum(jnp.max(jnp.abs(values), axis=0, keepdims=True), F32(1e-30))
    power = jnp.ceil(jnp.log2(top))
    unit = jnp.exp2(power)
    mantissa = jnp.ceil(top / unit * F32(16384.0))
    scale = mantissa * unit * F32(1.0 / (16384.0 * LEVELS))
    codes = jnp.round(values * (F32(1.0) / scale)).astype(jnp.int32)
    out_ref[base:base + rows, :] = codes.astype(I16)
    row = lax.broadcasted_iota(jnp.int32, (tail_rows, lanes), 0)
    tail = jnp.where(row == 0, power, jnp.where(row == 1, mantissa, F32(0.0)))
    if diagonal is not None:
        coarse = jnp.floor(diagonal * F32(64.0))
        fine = (diagonal * F32(64.0) - coarse) * F32(4096.0)
        tail = jnp.where(row == 2, coarse, jnp.where(row == 3, fine, tail))
    out_ref[base + rows:base + rows + tail_rows, :] = tail.astype(jnp.int32).astype(I16)


def decode(ref, base, rows, tail_rows):
    tail = ref[base + rows:base + rows + tail_rows, :].astype(jnp.int32).astype(F32)
    scale = tail[1:2] * jnp.exp2(tail[0:1]) * F32(1.0 / (16384.0 * LEVELS))
    diagonal = tail[2:3] * F32(1.0 / 64.0) + tail[3:4] * F32(1.0 / (64.0 * 4096.0))
    return ref[base:base + rows, :].astype(jnp.int32).astype(F32) * scale, diagonal


def turn_kernel(solves_ref, upper_ref, lower_ref, solves_copy, done):
    copy = pltpu.make_async_copy(solves_ref, solves_copy, done)
    copy.start()
    copy.wait()
    turned = solves_copy[...].T
    half = upper_ref.shape[0]
    upper_ref[...] = turned[:half]
    lower_ref[...] = turned[half:]


def fetch(source_ref, target_ref, done, first):
    rows = target_ref.shape[1]
    copies = [
        pltpu.make_async_copy(source_ref.at[pl.ds((first + i) * rows, rows), :], target_ref.at[i], done.at[i])
        for i in range(target_ref.shape[0])
    ]
    for copy in copies:
        copy.start()
    return copies


def choose(copies, coupling_copy, one_ref, chosen_ref, first):
    rows = coupling_copy.shape[1]
    for i, copy in enumerate(copies):
        copy.wait()
        chosen_ref[(first + i) * rows:(first + i + 1) * rows, :] = dot(coupling_copy[i], one_ref[...]).astype(BF16)


def pick_kernel(
    panel_ref, own_diagonal_ref, coupling_ref,
    chosen_ref, entry_ref, one_ref, panel_out, diagonal_out, coupling_copy, small_done, done,
):
    small = [
        pltpu.make_async_copy(panel_ref, panel_out, small_done.at[0]),
        pltpu.make_async_copy(own_diagonal_ref, diagonal_out, small_done.at[1]),
    ]
    for copy in small:
        copy.start()
    copies = fetch(coupling_ref, coupling_copy, done, 0)
    for copy in small:
        copy.wait()
    columns, panel = one_ref.shape
    share = diagonal_out.shape[1]
    first_column = lax.axis_index("row") * columns
    first_row = first_column + lax.axis_index("scen") * share
    here = panel_out[...] - first_column == lax.broadcasted_iota(jnp.int32, (columns, panel), 0)
    one_ref[...] = jnp.where(here, F32(1.0), F32(0.0)).astype(BF16)
    owned = panel_out[...] - first_row == lax.broadcasted_iota(jnp.int32, (share, panel), 0)
    own = jnp.broadcast_to(diagonal_out[...], (8, share)).T[:, :1]
    entry = jnp.sum(jnp.where(owned, own, F32(0.0)), axis=0, keepdims=True)
    entry_ref[...] = jnp.broadcast_to(entry, entry_ref.shape)
    choose(copies, coupling_copy, one_ref, chosen_ref, 0)


def rest_kernel(chosen_in, one_ref, coupling_ref, chosen_ref, coupling_copy, done):
    first = coupling_copy.shape[0]
    copies = fetch(coupling_ref, coupling_copy, done, first)
    choose(copies, coupling_copy, one_ref, chosen_ref, first)


def early_kernel(chosen_ref, *refs):
    *pieces, turned_ref, terms_ref = refs
    row, _, _ = whereabouts()
    if len(pieces) == 1:
        turned_ref[...] = pieces[0][...]
    else:
        half, width = pieces[0].shape
        for i, piece in enumerate(pieces):
            start = aligned(row ^ (i // 2), width)
            turned_ref[i % 2 * half:(i % 2 + 1) * half, pl.ds(start, width)] = piece[...]
        start = aligned(row ^ (len(pieces) // 2), width)
        turned_ref[:, pl.ds(start, width)] = jnp.zeros((2 * half, width), BF16)
    terms_ref[...] = dot(turned_ref[...], chosen_ref[...])


def half_terms(rows, row, chosen_ref, terms_ref, far, whose, out_ref, all_ref):
    half = all_ref.shape[0]
    size = half // rows
    total = terms_ref[pl.ds(aligned(whose, half), half), :]
    if far:
        width = far[0].shape[1]
        block = jnp.where(whose == 0, far[0][...], far[1][...])
        total = total + dot(block, chosen_ref[pl.ds(aligned(row ^ (rows - 1), width), width), :])
    all_ref[...] = total
    for k in range(rows):
        out_ref[k * size:(k + 1) * size, :] = all_ref[pl.ds(aligned(row ^ k, size), size), :]


def send_kernel(rows, chosen_ref, entry_ref, terms_ref, *refs):
    *far, send_ref, all_ref = refs
    row, core, _ = whereabouts()
    half_terms(rows, row, chosen_ref, terms_ref, far, 1 - core, send_ref, all_ref)
    send_ref[all_ref.shape[0]:, :] = entry_ref[...]


def keep_kernel(rows, turned_in, chosen_ref, terms_ref, *refs):
    *far, turned_ref, keep_ref, all_ref = refs
    row, core, _ = whereabouts()
    half_terms(rows, row, chosen_ref, terms_ref, far, core, keep_ref, all_ref)
    for i, piece in enumerate(far):
        half, width = piece.shape
        start = aligned(row ^ (rows - 1), width)
        turned_ref[i * half:(i + 1) * half, pl.ds(start, width)] = piece[...]


def pair_kernel(rows, keep_ref, got_ref, entry_ref, *out_refs):
    size = keep_ref.shape[0] // rows
    entry = entry_ref[:1, :] + got_ref[rows * size:rows * size + 1, :]
    for k, out_ref in enumerate(out_refs):
        part = slice(k * size, (k + 1) * size)
        encode(keep_ref[part, :] + got_ref[part, :], out_ref, 0, SHORT, entry)


def sum_kernel(*refs):
    *in_refs, out_ref = refs
    size = out_ref.shape[0] - SHORT
    parts = [decode(ref, 0, size, SHORT) for ref in in_refs]
    encode(sum(p[0] for p in parts), out_ref, 0, SHORT, sum(p[1] for p in parts))


def join_kernel(*refs):
    *in_refs, out_ref = refs
    size = in_refs[0].shape[0] - SHORT
    for k, ref in enumerate(in_refs):
        start = k * (size + TAIL)
        out_ref[start:start + size, :] = ref[:size, :]
        tail = ref[size:, :].astype(jnp.int32)
        out_ref[start + size:start + size + TAIL, :] = jnp.concatenate([tail, jnp.zeros_like(tail)], axis=0).astype(I16)


def place_pieces(row, whose, ref, pivots_ref, rows, base):
    panel = pivots_ref.shape[1]
    size = panel // (2 * rows)
    index = lax.broadcasted_iota(jnp.int32, (size, panel), 1)
    for k in range(rows):
        start = aligned(whose * rows + (row ^ k), size)
        values, diagonal = decode(ref, k * (size + TAIL), size, TAIL)
        at = lax.broadcasted_iota(jnp.int32, (size, panel), 0) + start == index
        pivots_ref[pl.ds(start - base, size), :] = values + jnp.where(at, diagonal, F32(0.0))


def own_kernel(rows, own_ref, half_ref):
    row, core, _ = whereabouts()
    place_pieces(row, core, own_ref, half_ref, rows, core * half_ref.shape[0])


def first_kernel(rows, half_ref, other_ref, inverse_ref, pivots_ref):
    row, core, _ = whereabouts()
    half = half_ref.shape[0]
    pivots_ref[pl.ds(aligned(core, half), half), :] = half_ref[...]
    place_pieces(row, 1 - core, other_ref, pivots_ref, rows, 0)
    inverse_ref[...] = newton_below(pivots_ref[:half, :half], pivots_ref[half:, :half])


def second_kernel(pivots_ref, inverse_first_ref, inverse_ref):
    half = inverse_ref.shape[0]
    below = inverse_first_ref[half:, :]
    pivot = pivots_ref[half:, half:] - product(below, pivots_ref[:half, half:])
    inverse_ref[...] = newton_beside(pivot, -below)


def schur_kernel(panel_ref, own_diagonal_ref, coupling_ref, turned_ref, keep_ref, send_ref):
    row, core, layer = whereabouts()
    panel, share = turned_ref.shape[0], keep_ref.shape[1]
    first_row = row * coupling_ref.shape[1] + (2 * layer + core) * share
    layers = keep_ref.shape[0] // panel
    for position, k in enumerate(reversed_order(layers)):
        start = aligned(layer ^ k, 2 * share)
        both = dot(turned_ref[...], coupling_ref[:, pl.ds(start, 2 * share)])
        rows = slice(position * panel, (position + 1) * panel)
        one, two = both[:, :share], both[:, share:]
        kept = jnp.where(core == 0, one, two)
        if position == 0:
            wanted = jnp.broadcast_to(panel_ref[...].astype(F32), (share, panel)).T.astype(jnp.int32)
            here = wanted - first_row == lax.broadcasted_iota(jnp.int32, (panel, share), 1)
            kept = kept + jnp.where(here, own_diagonal_ref[...], F32(0.0))
        keep_ref[rows, :] = kept
        send_ref[rows, :] = jnp.where(core == 0, two, one)


def bulk_pair_kernel(panel, keep_ref, got_ref, own_ref, coded_ref):
    half = own_ref.shape[0]
    own_ref[...] = keep_ref[:half, :] + got_ref[:half, :]
    for i in range(half // panel):
        part = slice(half + i * panel, half + (i + 1) * panel)
        encode(keep_ref[part, :] + got_ref[part, :], coded_ref, i * (panel + TAIL), TAIL)


def bulk_sum_kernel(panel, keep_ref, got_ref, own_ref, coded_ref):
    half = own_ref.shape[0]
    for i in range(keep_ref.shape[0] // panel):
        value = keep_ref[i * panel:(i + 1) * panel, :] + decode(got_ref, i * (panel + TAIL), panel, TAIL)[0]
        if i * panel < half:
            own_ref[i * panel:(i + 1) * panel, :] = value
        else:
            encode(value, coded_ref, (i - half // panel) * (panel + TAIL), TAIL)


def factor_kernel(inverse_first_ref, inverse_second_ref, rows_ref, *refs):
    *got, first_out, second_out = refs
    panel = rows_ref.shape[0]
    half = panel // 2
    rows = rows_ref[...]
    for ref in got:
        rows = rows + decode(ref, 0, panel, TAIL)[0]
    first, second = rows[:half], rows[half:]
    first_out[...] = product(inverse_first_ref[:half, :], first).T[:, None, :]
    second_out[...] = product(inverse_second_ref[...], jnp.concatenate([second, first], axis=0)).T[:, None, :]


def call(kernel, out_shape, *args, scratch=(), remain=0, micros=0.0, aliases=None):
    hbm = pl.BlockSpec(memory_space=pltpu.HBM)
    vmem = pl.BlockSpec(memory_space=pltpu.VMEM)
    stay = len(args) - remain
    args = args[:stay] + tuple(pltpu.with_memory_space_constraint(x, pltpu.HBM) for x in args[stay:])
    return pl.pallas_call(
        kernel,
        name=getattr(kernel, "func", kernel).__name__,
        out_shape=out_shape,
        in_specs=[vmem] * (len(args) - remain) + [hbm] * remain,
        out_specs=jax.tree.map(lambda _: vmem, out_shape),
        scratch_shapes=scratch,
        input_output_aliases=aliases or {},
        compiler_params=pltpu.CompilerParams(vmem_limit_bytes=12 << 20),
        cost_estimate=pl.CostEstimate(flops=0, bytes_accessed=int(micros * 3.69e6) + 1024, transcendentals=0),
    )(*args)


def swap(x, axis, bit):
    count = lax.axis_size(axis)
    return lax.ppermute(x, axis, [(i, i ^ bit) for i in range(count)])


def after(x, *others):
    return lax.optimization_barrier((x,) + others)[0]


def bits_of(count):
    return [1 << i for i in range(count.bit_length() - 1)]


def reversed_order(count):
    width = count.bit_length() - 1
    return [int(f"{p:0{width}b}"[::-1], 2) for p in range(count)]


def gather_pieces(solves, rows, ready):
    block, panel = solves.shape
    if rows != 4:
        return [lax.all_gather(solves.T, "row", axis=1, tiled=True)]
    half = pltpu.VMEM((panel // 2, block), BF16)
    upper, lower = call(
        turn_kernel, (half, half), solves, remain=1,
        scratch=[pltpu.VMEM((block, panel), BF16), pltpu.SemaphoreType.DMA],
    )
    lower_x, upper_y = swap(lower, "row", 1), swap(upper, "row", 2)
    upper_x, lower_y = swap(upper, "row", 1), swap(lower, "row", 2)
    upper_far, lower_far = swap(after(upper_y, *ready), "row", 1), swap(after(lower_x, *ready), "row", 2)
    return [upper, lower, upper_x, lower_x, upper_y, lower_y, upper_far, lower_far]


def shards(coupling, solves, border_diagonal, panel_rows):
    half = HALF
    coupling, solves = coupling[0], solves[0]
    local, row_count = coupling.shape
    panel = solves.shape[1]
    scen, rows = lax.axis_size("scen"), lax.axis_size("row")
    layers = scen // 2
    row, place = lax.axis_index("row"), lax.axis_index("scen")
    share = row_count // scen
    size = panel // (2 * rows)
    shape = pltpu.VMEM
    panel_row, diagonal_row = panel_rows[None, :], border_diagonal.T
    first_row = row * row_count + place * share
    picked = shape((local, panel), BF16)
    chunk_room = [
        pltpu.VMEM((CHUNKS // 2, local // CHUNKS, row_count), BF16), pltpu.SemaphoreType.DMA((CHUNKS // 2,))
    ]
    chosen, entry, one, panel_row, diagonal_row = call(
        pick_kernel,
        (
            picked, shape((8, panel), F32), shape((row_count, panel), BF16),
            shape((1, panel), jnp.int32), shape((1, share), F32),
        ),
        panel_row, diagonal_row, coupling, remain=3,
        scratch=[chunk_room[0], pltpu.SemaphoreType.DMA((2,)), chunk_room[1]],
    )
    pieces = gather_pieces(solves, rows, (entry,))
    near, far = pieces[:6], pieces[6:]
    chosen = call(rest_kernel, picked, chosen, one, coupling, remain=1, scratch=chunk_room, aliases={0: 0})
    room = [pltpu.VMEM((panel // 2, panel), F32)]
    turned, terms = call(
        early_kernel, (shape((panel, local), BF16), shape((panel, panel), F32)), chosen, *near
    )
    send = call(
        functools.partial(send_kernel, rows), shape((panel // 2 + 8, panel), F32),
        chosen, entry, terms, *far, scratch=room,
    )
    turned, keep = call(
        functools.partial(keep_kernel, rows), (shape((panel, local), BF16), shape((panel // 2, panel), F32)),
        turned, chosen, terms, *far, scratch=room, aliases={0: 0},
    )
    coded = shape((size + SHORT, panel), I16)
    codes = call(
        functools.partial(pair_kernel, rows), (coded,) * rows, keep, swap(send, "scen", 1), entry
    )
    arrived = [swap(codes[k], "row", k) for k in range(rows - 1, 0, -1)]
    part = codes[0]
    steps = bits_of(layers)
    split = share % 128 == 0
    if split:
        count = layers // 2
        bulk = shape((layers * panel, share), F32)
        halved = lambda count: (shape((count * panel, share), F32), shape((count * (panel + TAIL), share), I16))
        own, send_rows = call(
            schur_kernel, (bulk, bulk), panel_row, diagonal_row, coupling, after(turned, part)
        )
        part = call(sum_kernel, coded, after(part, own), *arrived)
        got = swap(after(send_rows, part), "scen", 1)
    else:
        own, got = lax.psum_scatter(dot(turned, coupling), "scen", scatter_dimension=1, tiled=True), []
        mine = first_row + jnp.arange(share, dtype=jnp.int32)
        own = own + jnp.where(panel_rows[:, None] == mine[None, :], border_diagonal[:, 0][None, :], F32(0.0))
        part = call(sum_kernel, coded, part, *arrived)
    for bit in steps:
        other = swap(part, "scen", 2 * bit)
        if split and bit == steps[-1]:
            own, bulk_codes = call(functools.partial(bulk_pair_kernel, panel), halved(count), after(own, part), got)
            part = after(part, bulk_codes)
        part = call(sum_kernel, coded, part, other)
    shared = [swap(part, "row", k) for k in range(1, rows)]
    if split:
        for bit in steps[:-1]:
            count //= 2
            got = swap(after(bulk_codes, part), "scen", 2 * bit)
            own, bulk_codes = call(functools.partial(bulk_sum_kernel, panel), halved(count), own, got)
        got = [swap(bulk_codes, "scen", layers)]
    joined = call(join_kernel, shape((rows * (size + TAIL), panel), I16), part, *shared)
    if split:
        joined = after(joined, bulk_codes)
    other = swap(joined, "scen", 1)
    own_half = call(
        functools.partial(own_kernel, rows), shape((panel // 2, panel), F32), joined
    )
    inverse_first, pivots = call(
        functools.partial(first_kernel, rows), (shape((panel, half), F32), shape((panel, panel), F32)),
        own_half, other, micros=4.5,
    )
    inverse_second = call(second_kernel, shape((half, panel), F32), pivots, inverse_first, micros=4.5)
    out = jax.ShapeDtypeStruct((share, 1, half), F32)
    return call(
        factor_kernel, (out, out),
        inverse_first, inverse_second, own, *got,
    )


def solution(mesh):
    placed = (P("scen", None, "row"), P("scen", "row", None), P("scen", "row"), P())
    return jax.shard_map(
        shards,
        mesh=mesh,
        in_specs=placed,
        out_specs=(P("scen", "row", None), P("scen", "row", None)),
        check_vma=False,
    )
```

```python
import functools

import jax
import jax.numpy as jnp
from jax import lax
from jax.experimental import pallas as pl
from jax.experimental.pallas import tpu as pltpu
from jax.sharding import PartitionSpec as P

HALF = 256
NEWTON = 8
TAIL = 16
SHORT = 8
CHUNKS = 4
LEVELS = 32000.0
F32 = jnp.float32
BF16 = jnp.bfloat16
I16 = jnp.int16


def halves(a):
    high = a.astype(BF16)
    low = (a - high.astype(F32)).astype(BF16)
    return high, low


def left_of(a):
    high, low = halves(a)
    return jnp.concatenate([high, high, low], axis=1)


def right_of(b):
    high, low = halves(b)
    return jnp.concatenate([high, low, high], axis=0)


def dot(a, b):
    return jnp.dot(a, b, preferred_element_type=F32)


def product(a, b):
    return dot(left_of(a), right_of(b))


def nearly(pivot):
    size = jnp.abs(pivot)
    turned = pivot.T
    square = product(pivot, turned)
    norm_one = jnp.max(jnp.sum(size, axis=0, keepdims=True))
    norm_inf = jnp.max(jnp.sum(size, axis=1, keepdims=True))
    scale = F32(1.0) / (norm_one * norm_inf)
    count = pivot.shape[0]
    one = lax.broadcasted_iota(jnp.int32, pivot.shape, 0) == lax.broadcasted_iota(jnp.int32, pivot.shape, 1)
    rest = jnp.where(one, F32(1.0), F32(0.0)) - square * scale
    approx = turned * scale
    for step in range(NEWTON - 2):
        both = product(jnp.concatenate([rest, approx], axis=0), rest)
        rest, approx = both[:count], approx + both[count:]
    return approx + product(approx, rest)


def newton_below(pivot, below):
    approx = nearly(pivot)
    count = pivot.shape[0]
    both = product(jnp.concatenate([pivot, below], axis=0), approx)
    stacked = jnp.concatenate([approx, both[count:]], axis=0)
    return 2.0 * stacked - product(stacked, both[:count])


def newton_beside(pivot, beside):
    approx = nearly(pivot)
    count = pivot.shape[0]
    both = product(approx, jnp.concatenate([pivot, beside], axis=1))
    stacked = jnp.concatenate([approx, both[:, count:]], axis=1)
    return 2.0 * stacked - product(both[:, :count], stacked)


def whereabouts():
    place = lax.axis_index("scen")
    return lax.axis_index("row"), lax.rem(place, 2), lax.div(place, 2)


def aligned(index, size):
    return pl.multiple_of(index * size, size)


def encode(values, out_ref, base, tail_rows, diagonal=None):
    rows, lanes = values.shape
    top = jnp.maximum(jnp.max(jnp.abs(values), axis=0, keepdims=True), F32(1e-30))
    power = jnp.ceil(jnp.log2(top))
    unit = jnp.exp2(power)
    mantissa = jnp.ceil(top / unit * F32(16384.0))
    scale = mantissa * unit * F32(1.0 / (16384.0 * LEVELS))
    codes = jnp.round(values * (F32(1.0) / scale)).astype(jnp.int32)
    out_ref[base:base + rows, :] = codes.astype(I16)
    row = lax.broadcasted_iota(jnp.int32, (tail_rows, lanes), 0)
    tail = jnp.where(row == 0, power, jnp.where(row == 1, mantissa, F32(0.0)))
    if diagonal is not None:
        coarse = jnp.floor(diagonal * F32(64.0))
        fine = (diagonal * F32(64.0) - coarse) * F32(4096.0)
        tail = jnp.where(row == 2, coarse, jnp.where(row == 3, fine, tail))
    out_ref[base + rows:base + rows + tail_rows, :] = tail.astype(jnp.int32).astype(I16)


def decode(ref, base, rows, tail_rows):
    tail = ref[base + rows:base + rows + tail_rows, :].astype(jnp.int32).astype(F32)
    scale = tail[1:2] * jnp.exp2(tail[0:1]) * F32(1.0 / (16384.0 * LEVELS))
    diagonal = tail[2:3] * F32(1.0 / 64.0) + tail[3:4] * F32(1.0 / (64.0 * 4096.0))
    return ref[base:base + rows, :].astype(jnp.int32).astype(F32) * scale, diagonal


def turn_kernel(solves_ref, upper_ref, lower_ref, solves_copy, done):
    copy = pltpu.make_async_copy(solves_ref, solves_copy, done)
    copy.start()
    copy.wait()
    turned = solves_copy[...].T
    half = upper_ref.shape[0]
    upper_ref[...] = turned[:half]
    lower_ref[...] = turned[half:]


def fetch(source_ref, target_ref, done, first):
    rows = target_ref.shape[1]
    copies = [
        pltpu.make_async_copy(source_ref.at[pl.ds((first + i) * rows, rows), :], target_ref.at[i], done.at[i])
        for i in range(target_ref.shape[0])
    ]
    for copy in copies:
        copy.start()
    return copies


def choose(copies, coupling_copy, one_ref, chosen_ref, first):
    rows = coupling_copy.shape[1]
    for i, copy in enumerate(copies):
        copy.wait()
        chosen_ref[(first + i) * rows:(first + i + 1) * rows, :] = dot(coupling_copy[i], one_ref[...]).astype(BF16)


def pick_kernel(
    panel_ref, own_diagonal_ref, coupling_ref,
    chosen_ref, entry_ref, one_ref, panel_out, diagonal_out, coupling_copy, small_done, done,
):
    small = [
        pltpu.make_async_copy(panel_ref, panel_out, small_done.at[0]),
        pltpu.make_async_copy(own_diagonal_ref, diagonal_out, small_done.at[1]),
    ]
    for copy in small:
        copy.start()
    copies = fetch(coupling_ref, coupling_copy, done, 0)
    for copy in small:
        copy.wait()
    columns, panel = one_ref.shape
    share = diagonal_out.shape[1]
    first_column = lax.axis_index("row") * columns
    first_row = first_column + lax.axis_index("scen") * share
    here = panel_out[...] - first_column == lax.broadcasted_iota(jnp.int32, (columns, panel), 0)
    one_ref[...] = jnp.where(here, F32(1.0), F32(0.0)).astype(BF16)
    owned = panel_out[...] - first_row == lax.broadcasted_iota(jnp.int32, (share, panel), 0)
    own = jnp.broadcast_to(diagonal_out[...], (8, share)).T[:, :1]
    entry = jnp.sum(jnp.where(owned, own, F32(0.0)), axis=0, keepdims=True)
    entry_ref[...] = jnp.broadcast_to(entry, entry_ref.shape)
    choose(copies, coupling_copy, one_ref, chosen_ref, 0)


def rest_kernel(chosen_in, one_ref, coupling_ref, chosen_ref, coupling_copy, done):
    first = coupling_copy.shape[0]
    copies = fetch(coupling_ref, coupling_copy, done, first)
    choose(copies, coupling_copy, one_ref, chosen_ref, first)


def early_kernel(chosen_ref, *refs):
    *pieces, turned_ref, terms_ref = refs
    row, _, _ = whereabouts()
    if len(pieces) == 1:
        turned_ref[...] = pieces[0][...]
    else:
        half, width = pieces[0].shape
        for i, piece in enumerate(pieces):
            start = aligned(row ^ (i // 2), width)
            turned_ref[i % 2 * half:(i % 2 + 1) * half, pl.ds(start, width)] = piece[...]
        start = aligned(row ^ (len(pieces) // 2), width)
        turned_ref[:, pl.ds(start, width)] = jnp.zeros((2 * half, width), BF16)
    terms_ref[...] = dot(turned_ref[...], chosen_ref[...])


def half_terms(rows, row, chosen_ref, terms_ref, far, whose, out_ref, all_ref):
    half = all_ref.shape[0]
    size = half // rows
    total = terms_ref[pl.ds(aligned(whose, half), half), :]
    if far:
        width = far[0].shape[1]
        block = jnp.where(whose == 0, far[0][...], far[1][...])
        total = total + dot(block, chosen_ref[pl.ds(aligned(row ^ (rows - 1), width), width), :])
    all_ref[...] = total
    for k in range(rows):
        out_ref[k * size:(k + 1) * size, :] = all_ref[pl.ds(aligned(row ^ k, size), size), :]


def send_kernel(rows, chosen_ref, entry_ref, terms_ref, *refs):
    *far, send_ref, all_ref = refs
    row, core, _ = whereabouts()
    half_terms(rows, row, chosen_ref, terms_ref, far, 1 - core, send_ref, all_ref)
    send_ref[all_ref.shape[0]:, :] = entry_ref[...]


def keep_kernel(rows, turned_in, chosen_ref, terms_ref, *refs):
    *far, turned_ref, keep_ref, all_ref = refs
    row, core, _ = whereabouts()
    half_terms(rows, row, chosen_ref, terms_ref, far, core, keep_ref, all_ref)
    for i, piece in enumerate(far):
        half, width = piece.shape
        start = aligned(row ^ (rows - 1), width)
        turned_ref[i * half:(i + 1) * half, pl.ds(start, width)] = piece[...]


def pair_kernel(rows, keep_ref, got_ref, entry_ref, *out_refs):
    size = keep_ref.shape[0] // rows
    entry = entry_ref[:1, :] + got_ref[rows * size:rows * size + 1, :]
    for k, out_ref in enumerate(out_refs):
        part = slice(k * size, (k + 1) * size)
        encode(keep_ref[part, :] + got_ref[part, :], out_ref, 0, SHORT, entry)


def sum_kernel(*refs):
    *in_refs, out_ref = refs
    size = out_ref.shape[0] - SHORT
    parts = [decode(ref, 0, size, SHORT) for ref in in_refs]
    encode(sum(p[0] for p in parts), out_ref, 0, SHORT, sum(p[1] for p in parts))


def join_kernel(*refs):
    *in_refs, out_ref = refs
    size = in_refs[0].shape[0] - SHORT
    for k, ref in enumerate(in_refs):
        start = k * (size + TAIL)
        out_ref[start:start + size, :] = ref[:size, :]
        tail = ref[size:, :].astype(jnp.int32)
        out_ref[start + size:start + size + TAIL, :] = jnp.concatenate([tail, jnp.zeros_like(tail)], axis=0).astype(I16)


def place_pieces(row, whose, ref, pivots_ref, rows, base):
    panel = pivots_ref.shape[1]
    size = panel // (2 * rows)
    index = lax.broadcasted_iota(jnp.int32, (size, panel), 1)
    for k in range(rows):
        start = aligned(whose * rows + (row ^ k), size)
        values, diagonal = decode(ref, k * (size + TAIL), size, TAIL)
        at = lax.broadcasted_iota(jnp.int32, (size, panel), 0) + start == index
        pivots_ref[pl.ds(start - base, size), :] = values + jnp.where(at, diagonal, F32(0.0))


def own_kernel(rows, own_ref, half_ref):
    row, core, _ = whereabouts()
    place_pieces(row, core, own_ref, half_ref, rows, core * half_ref.shape[0])


def first_kernel(rows, half_ref, other_ref, inverse_ref, pivots_ref):
    row, core, _ = whereabouts()
    half = half_ref.shape[0]
    pivots_ref[pl.ds(aligned(core, half), half), :] = half_ref[...]
    place_pieces(row, 1 - core, other_ref, pivots_ref, rows, 0)
    inverse_ref[...] = newton_below(pivots_ref[:half, :half], pivots_ref[half:, :half])


def second_kernel(pivots_ref, inverse_first_ref, inverse_ref):
    half = inverse_ref.shape[0]
    below = inverse_first_ref[half:, :]
    pivot = pivots_ref[half:, half:] - product(below, pivots_ref[:half, half:])
    inverse_ref[...] = newton_beside(pivot, -below)


def schur_kernel(panel_ref, own_diagonal_ref, coupling_ref, turned_ref, keep_ref, send_ref):
    row, core, layer = whereabouts()
    panel, share = turned_ref.shape[0], keep_ref.shape[1]
    first_row = row * coupling_ref.shape[1] + (2 * layer + core) * share
    layers = keep_ref.shape[0] // panel
    for position, k in enumerate(reversed_order(layers)):
        start = aligned(layer ^ k, 2 * share)
        both = dot(turned_ref[...], coupling_ref[:, pl.ds(start, 2 * share)])
        rows = slice(position * panel, (position + 1) * panel)
        one, two = both[:, :share], both[:, share:]
        kept = jnp.where(core == 0, one, two)
        if position == 0:
            wanted = jnp.broadcast_to(panel_ref[...].astype(F32), (share, panel)).T.astype(jnp.int32)
            here = wanted - first_row == lax.broadcasted_iota(jnp.int32, (panel, share), 1)
            kept = kept + jnp.where(here, own_diagonal_ref[...], F32(0.0))
        keep_ref[rows, :] = kept
        send_ref[rows, :] = jnp.where(core == 0, two, one)


def bulk_pair_kernel(panel, keep_ref, got_ref, own_ref, coded_ref):
    half = own_ref.shape[0]
    own_ref[...] = keep_ref[:half, :] + got_ref[:half, :]
    for i in range(half // panel):
        part = slice(half + i * panel, half + (i + 1) * panel)
        encode(keep_ref[part, :] + got_ref[part, :], coded_ref, i * (panel + TAIL), TAIL)


def bulk_sum_kernel(panel, keep_ref, got_ref, own_ref, coded_ref):
    half = own_ref.shape[0]
    for i in range(keep_ref.shape[0] // panel):
        value = keep_ref[i * panel:(i + 1) * panel, :] + decode(got_ref, i * (panel + TAIL), panel, TAIL)[0]
        if i * panel < half:
            own_ref[i * panel:(i + 1) * panel, :] = value
        else:
            encode(value, coded_ref, (i - half // panel) * (panel + TAIL), TAIL)


def factor_kernel(inverse_first_ref, inverse_second_ref, rows_ref, *refs):
    *got, first_out, second_out = refs
    panel = rows_ref.shape[0]
    half = panel // 2
    rows = rows_ref[...]
    for ref in got:
        rows = rows + decode(ref, 0, panel, TAIL)[0]
    first, second = rows[:half], rows[half:]
    first_out[...] = product(inverse_first_ref[:half, :], first).T[:, None, :]
    second_out[...] = product(inverse_second_ref[...], jnp.concatenate([second, first], axis=0)).T[:, None, :]


def call(kernel, out_shape, *args, scratch=(), remain=0, micros=0.0, aliases=None):
    hbm = pl.BlockSpec(memory_space=pltpu.HBM)
    vmem = pl.BlockSpec(memory_space=pltpu.VMEM)
    stay = len(args) - remain
    args = args[:stay] + tuple(pltpu.with_memory_space_constraint(x, pltpu.HBM) for x in args[stay:])
    return pl.pallas_call(
        kernel,
        name=getattr(kernel, "func", kernel).__name__,
        out_shape=out_shape,
        in_specs=[vmem] * (len(args) - remain) + [hbm] * remain,
        out_specs=jax.tree.map(lambda _: vmem, out_shape),
        scratch_shapes=scratch,
        input_output_aliases=aliases or {},
        compiler_params=pltpu.CompilerParams(vmem_limit_bytes=12 << 20),
        cost_estimate=pl.CostEstimate(flops=0, bytes_accessed=int(micros * 3.69e6) + 1024, transcendentals=0),
    )(*args)


def swap(x, axis, bit):
    count = lax.axis_size(axis)
    return lax.ppermute(x, axis, [(i, i ^ bit) for i in range(count)])


def after(x, *others):
    return lax.optimization_barrier((x,) + others)[0]


def bits_of(count):
    return [1 << i for i in range(count.bit_length() - 1)]


def reversed_order(count):
    width = count.bit_length() - 1
    return [int(f"{p:0{width}b}"[::-1], 2) for p in range(count)]


def gather_pieces(solves, rows, ready):
    block, panel = solves.shape
    if rows != 4:
        return [lax.all_gather(solves.T, "row", axis=1, tiled=True)]
    half = pltpu.VMEM((panel // 2, block), BF16)
    upper, lower = call(
        turn_kernel, (half, half), solves, remain=1,
        scratch=[pltpu.VMEM((block, panel), BF16), pltpu.SemaphoreType.DMA],
    )
    lower_x, upper_y = swap(lower, "row", 1), swap(upper, "row", 2)
    upper_x, lower_y = swap(upper, "row", 1), swap(lower, "row", 2)
    upper_far, lower_far = swap(after(upper_y, *ready), "row", 1), swap(after(lower_x, *ready), "row", 2)
    return [upper, lower, upper_x, lower_x, upper_y, lower_y, upper_far, lower_far]


def shards(coupling, solves, border_diagonal, panel_rows):
    half = HALF
    coupling, solves = coupling[0], solves[0]
    local, row_count = coupling.shape
    panel = solves.shape[1]
    scen, rows = lax.axis_size("scen"), lax.axis_size("row")
    layers = scen // 2
    row, place = lax.axis_index("row"), lax.axis_index("scen")
    share = row_count // scen
    size = panel // (2 * rows)
    shape = pltpu.VMEM
    panel_row, diagonal_row = panel_rows[None, :], border_diagonal.T
    first_row = row * row_count + place * share
    picked = shape((local, panel), BF16)
    chunk_room = [
        pltpu.VMEM((CHUNKS // 2, local // CHUNKS, row_count), BF16), pltpu.SemaphoreType.DMA((CHUNKS // 2,))
    ]
    chosen, entry, one, panel_row, diagonal_row = call(
        pick_kernel,
        (
            picked, shape((8, panel), F32), shape((row_count, panel), BF16),
            shape((1, panel), jnp.int32), shape((1, share), F32),
        ),
        panel_row, diagonal_row, coupling, remain=3,
        scratch=[chunk_room[0], pltpu.SemaphoreType.DMA((2,)), chunk_room[1]],
    )
    pieces = gather_pieces(solves, rows, (entry,))
    near, far = pieces[:6], pieces[6:]
    chosen = call(rest_kernel, picked, chosen, one, coupling, remain=1, scratch=chunk_room, aliases={0: 0})
    room = [pltpu.VMEM((panel // 2, panel), F32)]
    turned, terms = call(
        early_kernel, (shape((panel, local), BF16), shape((panel, panel), F32)), chosen, *near
    )
    send = call(
        functools.partial(send_kernel, rows), shape((panel // 2 + 8, panel), F32),
        chosen, entry, terms, *far, scratch=room,
    )
    turned, keep = call(
        functools.partial(keep_kernel, rows), (shape((panel, local), BF16), shape((panel // 2, panel), F32)),
        turned, chosen, terms, *far, scratch=room, aliases={0: 0},
    )
    coded = shape((size + SHORT, panel), I16)
    codes = call(
        functools.partial(pair_kernel, rows), (coded,) * rows, keep, swap(send, "scen", 1), entry
    )
    arrived = [swap(codes[k], "row", k) for k in range(rows - 1, 0, -1)]
    part = codes[0]
    steps = bits_of(layers)
    split = share % 128 == 0
    if split:
        count = layers // 2
        bulk = shape((layers * panel, share), F32)
        halved = lambda count: (shape((count * panel, share), F32), shape((count * (panel + TAIL), share), I16))
        own, send_rows = call(
            schur_kernel, (bulk, bulk), panel_row, diagonal_row, coupling, after(turned, part)
        )
        part = call(sum_kernel, coded, after(part, own), *arrived)
        got = swap(after(send_rows, part), "scen", 1)
    else:
        own, got = lax.psum_scatter(dot(turned, coupling), "scen", scatter_dimension=1, tiled=True), []
        mine = first_row + jnp.arange(share, dtype=jnp.int32)
        own = own + jnp.where(panel_rows[:, None] == mine[None, :], border_diagonal[:, 0][None, :], F32(0.0))
        part = call(sum_kernel, coded, part, *arrived)
    for bit in steps:
        other = swap(part, "scen", 2 * bit)
        if split and bit == steps[-1]:
            own, bulk_codes = call(functools.partial(bulk_pair_kernel, panel), halved(count), after(own, part), got)
            part = after(part, bulk_codes)
        part = call(sum_kernel, coded, part, other)
    shared = [swap(part, "row", k) for k in range(1, rows)]
    if split:
        for bit in steps[:-1]:
            count //= 2
            got = swap(after(bulk_codes, part), "scen", 2 * bit)
            own, bulk_codes = call(functools.partial(bulk_sum_kernel, panel), halved(count), own, got)
        got = [swap(bulk_codes, "scen", layers)]
    joined = call(join_kernel, shape((rows * (size + TAIL), panel), I16), part, *shared)
    if split:
        joined = after(joined, bulk_codes)
    other = swap(joined, "scen", 1)
    own_half = call(
        functools.partial(own_kernel, rows), shape((panel // 2, panel), F32), joined
    )
    inverse_first, pivots = call(
        functools.partial(first_kernel, rows), (shape((panel, half), F32), shape((panel, panel), F32)),
        own_half, other, micros=4.5,
    )
    inverse_second = call(second_kernel, shape((half, panel), F32), pivots, inverse_first, micros=4.5)
    out = jax.ShapeDtypeStruct((share, 1, half), F32)
    return call(
        factor_kernel, (out, out),
        inverse_first, inverse_second, own, *got,
    )


def solution(mesh):
    placed = (P("scen", None, "row"), P("scen", "row", None), P("scen", "row"), P())
    return jax.shard_map(
        shards,
        mesh=mesh,
        in_specs=placed,
        out_specs=(P("scen", "row", None), P("scen", "row", None)),
        check_vma=False,
    )
```

```python
import functools

import jax
import jax.numpy as jnp
from jax import lax
from jax.experimental import pallas as pl
from jax.experimental.pallas import tpu as pltpu
from jax.sharding import PartitionSpec as P

HALF = 256
NEWTON = 8
TAIL = 16
SHORT = 8
CHUNKS = 4
LEVELS = 32000.0
F32 = jnp.float32
BF16 = jnp.bfloat16
I16 = jnp.int16


def halves(a):
    high = a.astype(BF16)
    low = (a - high.astype(F32)).astype(BF16)
    return high, low


def left_of(a):
    high, low = halves(a)
    return jnp.concatenate([high, high, low], axis=1)


def right_of(b):
    high, low = halves(b)
    return jnp.concatenate([high, low, high], axis=0)


def dot(a, b):
    return jnp.dot(a, b, preferred_element_type=F32)


def product(a, b):
    return dot(left_of(a), right_of(b))


def nearly(pivot):
    size = jnp.abs(pivot)
    turned = pivot.T
    square = product(turned, pivot)
    norm_one = jnp.max(jnp.sum(size, axis=0, keepdims=True))
    norm_inf = jnp.max(jnp.sum(size, axis=1, keepdims=True))
    scale = F32(1.0) / (norm_one * norm_inf)
    count = pivot.shape[0]
    one = lax.broadcasted_iota(jnp.int32, pivot.shape, 0) == lax.broadcasted_iota(jnp.int32, pivot.shape, 1)
    rest = jnp.where(one, F32(1.0), F32(0.0)) - square * scale
    approx = turned * scale
    for step in range(NEWTON - 2):
        both = product(rest, jnp.concatenate([rest, approx], axis=1))
        rest, approx = both[:, :count], approx + both[:, count:]
    return approx + product(rest, approx)


def newton_beside(pivot, beside):
    approx = nearly(pivot)
    count = pivot.shape[0]
    both = product(approx, jnp.concatenate([pivot, beside], axis=1))
    stacked = jnp.concatenate([approx, both[:, count:]], axis=1)
    return 2.0 * stacked - product(both[:, :count], stacked)


def whereabouts():
    place = lax.axis_index("scen")
    return lax.axis_index("row"), lax.rem(place, 2), lax.div(place, 2)


def aligned(index, size):
    return pl.multiple_of(index * size, size)


def encode(values, out_ref, base, tail_rows, diagonal=None):
    rows, lanes = values.shape
    top = jnp.maximum(jnp.max(jnp.abs(values), axis=0, keepdims=True), F32(1e-30))
    power = jnp.ceil(jnp.log2(top))
    unit = jnp.exp2(power)
    mantissa = jnp.ceil(top / unit * F32(16384.0))
    scale = mantissa * unit * F32(1.0 / (16384.0 * LEVELS))
    codes = jnp.round(values * (F32(1.0) / scale)).astype(jnp.int32)
    out_ref[base:base + rows, :] = codes.astype(I16)
    row = lax.broadcasted_iota(jnp.int32, (tail_rows, lanes), 0)
    tail = jnp.where(row == 0, power, jnp.where(row == 1, mantissa, F32(0.0)))
    if diagonal is not None:
        coarse = jnp.floor(diagonal * F32(64.0))
        fine = (diagonal * F32(64.0) - coarse) * F32(4096.0)
        tail = jnp.where(row == 2, coarse, jnp.where(row == 3, fine, tail))
    out_ref[base + rows:base + rows + tail_rows, :] = tail.astype(jnp.int32).astype(I16)


def decode(ref, base, rows, tail_rows):
    tail = ref[base + rows:base + rows + tail_rows, :].astype(jnp.int32).astype(F32)
    scale = tail[1:2] * jnp.exp2(tail[0:1]) * F32(1.0 / (16384.0 * LEVELS))
    diagonal = tail[2:3] * F32(1.0 / 64.0) + tail[3:4] * F32(1.0 / (64.0 * 4096.0))
    return ref[base:base + rows, :].astype(jnp.int32).astype(F32) * scale, diagonal


def turn_kernel(solves_ref, upper_ref, lower_ref, solves_copy, done):
    copy = pltpu.make_async_copy(solves_ref, solves_copy, done)
    copy.start()
    copy.wait()
    turned = solves_copy[...].T
    half = upper_ref.shape[0]
    upper_ref[...] = turned[:half]
    lower_ref[...] = turned[half:]


def fetch(source_ref, target_ref, done, first):
    rows = target_ref.shape[1]
    copies = [
        pltpu.make_async_copy(source_ref.at[pl.ds((first + i) * rows, rows), :], target_ref.at[i], done.at[i])
        for i in range(target_ref.shape[0])
    ]
    for copy in copies:
        copy.start()
    return copies


def choose(copies, coupling_copy, one_ref, chosen_ref, first):
    rows = coupling_copy.shape[1]
    for i, copy in enumerate(copies):
        copy.wait()
        chosen_ref[(first + i) * rows:(first + i + 1) * rows, :] = dot(coupling_copy[i], one_ref[...]).astype(BF16)


def pick_kernel(
    panel_ref, own_diagonal_ref, coupling_ref,
    chosen_ref, entry_ref, one_ref, panel_out, diagonal_out, coupling_copy, small_done, done,
):
    small = [
        pltpu.make_async_copy(panel_ref, panel_out, small_done.at[0]),
        pltpu.make_async_copy(own_diagonal_ref, diagonal_out, small_done.at[1]),
    ]
    for copy in small:
        copy.start()
    copies = fetch(coupling_ref, coupling_copy, done, 0)
    for copy in small:
        copy.wait()
    columns, panel = one_ref.shape
    share = diagonal_out.shape[1]
    first_column = lax.axis_index("row") * columns
    first_row = first_column + lax.axis_index("scen") * share
    here = panel_out[...] - first_column == lax.broadcasted_iota(jnp.int32, (columns, panel), 0)
    one_ref[...] = jnp.where(here, F32(1.0), F32(0.0)).astype(BF16)
    owned = panel_out[...] - first_row == lax.broadcasted_iota(jnp.int32, (share, panel), 0)
    own = jnp.broadcast_to(diagonal_out[...], (8, share)).T[:, :1]
    entry = jnp.sum(jnp.where(owned, own, F32(0.0)), axis=0, keepdims=True)
    entry_ref[...] = jnp.broadcast_to(entry, entry_ref.shape)
    choose(copies, coupling_copy, one_ref, chosen_ref, 0)


def rest_kernel(chosen_in, one_ref, coupling_ref, chosen_ref, coupling_copy, done):
    first = coupling_copy.shape[0]
    copies = fetch(coupling_ref, coupling_copy, done, first)
    choose(copies, coupling_copy, one_ref, chosen_ref, first)


def early_kernel(chosen_ref, *refs):
    *pieces, turned_ref, terms_ref = refs
    row, _, _ = whereabouts()
    if len(pieces) == 1:
        turned_ref[...] = pieces[0][...]
    else:
        half, width = pieces[0].shape
        for i, piece in enumerate(pieces):
            start = aligned(row ^ (i // 2), width)
            turned_ref[i % 2 * half:(i % 2 + 1) * half, pl.ds(start, width)] = piece[...]
        start = aligned(row ^ (len(pieces) // 2), width)
        turned_ref[:, pl.ds(start, width)] = jnp.zeros((2 * half, width), BF16)
    terms_ref[...] = dot(turned_ref[...], chosen_ref[...])


def half_terms(rows, row, chosen_ref, terms_ref, far, whose, out_ref, all_ref):
    half = all_ref.shape[0]
    size = half // rows
    total = terms_ref[pl.ds(aligned(whose, half), half), :]
    if far:
        width = far[0].shape[1]
        block = jnp.where(whose == 0, far[0][...], far[1][...])
        total = total + dot(block, chosen_ref[pl.ds(aligned(row ^ (rows - 1), width), width), :])
    all_ref[...] = total
    for k in range(rows):
        out_ref[k * size:(k + 1) * size, :] = all_ref[pl.ds(aligned(row ^ k, size), size), :]


def send_kernel(rows, chosen_ref, entry_ref, terms_ref, *refs):
    *far, send_ref, all_ref = refs
    row, core, _ = whereabouts()
    half_terms(rows, row, chosen_ref, terms_ref, far, 1 - core, send_ref, all_ref)
    send_ref[all_ref.shape[0]:, :] = entry_ref[...]


def keep_kernel(rows, turned_in, chosen_ref, terms_ref, *refs):
    *far, turned_ref, keep_ref, all_ref = refs
    row, core, _ = whereabouts()
    half_terms(rows, row, chosen_ref, terms_ref, far, core, keep_ref, all_ref)
    for i, piece in enumerate(far):
        half, width = piece.shape
        start = aligned(row ^ (rows - 1), width)
        turned_ref[i * half:(i + 1) * half, pl.ds(start, width)] = piece[...]


def pair_kernel(rows, keep_ref, got_ref, entry_ref, *out_refs):
    size = keep_ref.shape[0] // rows
    entry = entry_ref[:1, :] + got_ref[rows * size:rows * size + 1, :]
    for k, out_ref in enumerate(out_refs):
        part = slice(k * size, (k + 1) * size)
        encode(keep_ref[part, :] + got_ref[part, :], out_ref, 0, SHORT, entry)


def sum_kernel(*refs):
    *in_refs, out_ref = refs
    size = out_ref.shape[0] - SHORT
    parts = [decode(ref, 0, size, SHORT) for ref in in_refs]
    encode(sum(p[0] for p in parts), out_ref, 0, SHORT, sum(p[1] for p in parts))


def join_kernel(*refs):
    *in_refs, out_ref = refs
    size = in_refs[0].shape[0] - SHORT
    for k, ref in enumerate(in_refs):
        start = k * (size + TAIL)
        out_ref[start:start + size, :] = ref[:size, :]
        tail = ref[size:, :].astype(jnp.int32)
        out_ref[start + size:start + size + TAIL, :] = jnp.concatenate([tail, jnp.zeros_like(tail)], axis=0).astype(I16)


def place_pieces(row, whose, ref, pivots_ref, rows, base):
    panel = pivots_ref.shape[1]
    size = panel // (2 * rows)
    index = lax.broadcasted_iota(jnp.int32, (size, panel), 1)
    for k in range(rows):
        start = aligned(whose * rows + (row ^ k), size)
        values, diagonal = decode(ref, k * (size + TAIL), size, TAIL)
        at = lax.broadcasted_iota(jnp.int32, (size, panel), 0) + start == index
        pivots_ref[pl.ds(start - base, size), :] = values + jnp.where(at, diagonal, F32(0.0))


def own_kernel(rows, own_ref, half_ref):
    row, core, _ = whereabouts()
    place_pieces(row, core, own_ref, half_ref, rows, core * half_ref.shape[0])


def first_kernel(rows, half_ref, other_ref, inverse_ref, pivots_ref):
    row, core, _ = whereabouts()
    half = half_ref.shape[0]
    pivots_ref[pl.ds(aligned(core, half), half), :] = half_ref[...]
    place_pieces(row, 1 - core, other_ref, pivots_ref, rows, 0)
    inverse_ref[...] = newton_beside(pivots_ref[:half, :half], pivots_ref[:half, half:])


def second_kernel(pivots_ref, inverse_first_ref, inverse_ref):
    half = inverse_ref.shape[0]
    corner = pivots_ref[half:, :half]
    pivot = pivots_ref[half:, half:] - product(corner, inverse_first_ref[:, half:])
    inverse_ref[...] = newton_beside(pivot, -product(corner, inverse_first_ref[:, :half]))


def schur_kernel(panel_ref, own_diagonal_ref, coupling_ref, turned_ref, keep_ref, send_ref):
    row, core, layer = whereabouts()
    panel, share = turned_ref.shape[0], keep_ref.shape[1]
    first_row = row * coupling_ref.shape[1] + (2 * layer + core) * share
    layers = keep_ref.shape[0] // panel
    for position, k in enumerate(reversed_order(layers)):
        start = aligned(layer ^ k, 2 * share)
        both = dot(turned_ref[...], coupling_ref[:, pl.ds(start, 2 * share)])
        rows = slice(position * panel, (position + 1) * panel)
        one, two = both[:, :share], both[:, share:]
        kept = jnp.where(core == 0, one, two)
        if position == 0:
            wanted = jnp.broadcast_to(panel_ref[...].astype(F32), (share, panel)).T.astype(jnp.int32)
            here = wanted - first_row == lax.broadcasted_iota(jnp.int32, (panel, share), 1)
            kept = kept + jnp.where(here, own_diagonal_ref[...], F32(0.0))
        keep_ref[rows, :] = kept
        send_ref[rows, :] = jnp.where(core == 0, two, one)


def bulk_pair_kernel(panel, keep_ref, got_ref, own_ref, coded_ref):
    half = own_ref.shape[0]
    own_ref[...] = keep_ref[:half, :] + got_ref[:half, :]
    for i in range(half // panel):
        part = slice(half + i * panel, half + (i + 1) * panel)
        encode(keep_ref[part, :] + got_ref[part, :], coded_ref, i * (panel + TAIL), TAIL)


def bulk_sum_kernel(panel, keep_ref, got_ref, own_ref, coded_ref):
    half = own_ref.shape[0]
    for i in range(keep_ref.shape[0] // panel):
        value = keep_ref[i * panel:(i + 1) * panel, :] + decode(got_ref, i * (panel + TAIL), panel, TAIL)[0]
        if i * panel < half:
            own_ref[i * panel:(i + 1) * panel, :] = value
        else:
            encode(value, coded_ref, (i - half // panel) * (panel + TAIL), TAIL)


def factor_kernel(inverse_first_ref, inverse_second_ref, rows_ref, *refs):
    *got, first_out, second_out = refs
    panel = rows_ref.shape[0]
    half = panel // 2
    rows = rows_ref[...]
    for ref in got:
        rows = rows + decode(ref, 0, panel, TAIL)[0]
    first, second = rows[:half], rows[half:]
    first_out[...] = product(inverse_first_ref[:, :half], first).T[:, None, :]
    second_out[...] = product(inverse_second_ref[...], jnp.concatenate([second, first], axis=0)).T[:, None, :]


def call(kernel, out_shape, *args, scratch=(), remain=0, micros=0.0, aliases=None):
    hbm = pl.BlockSpec(memory_space=pltpu.HBM)
    vmem = pl.BlockSpec(memory_space=pltpu.VMEM)
    stay = len(args) - remain
    args = args[:stay] + tuple(pltpu.with_memory_space_constraint(x, pltpu.HBM) for x in args[stay:])
    return pl.pallas_call(
        kernel,
        name=getattr(kernel, "func", kernel).__name__,
        out_shape=out_shape,
        in_specs=[vmem] * (len(args) - remain) + [hbm] * remain,
        out_specs=jax.tree.map(lambda _: vmem, out_shape),
        scratch_shapes=scratch,
        input_output_aliases=aliases or {},
        compiler_params=pltpu.CompilerParams(vmem_limit_bytes=12 << 20),
        cost_estimate=pl.CostEstimate(flops=0, bytes_accessed=int(micros * 3.69e6) + 1024, transcendentals=0),
    )(*args)


def swap(x, axis, bit):
    count = lax.axis_size(axis)
    return lax.ppermute(x, axis, [(i, i ^ bit) for i in range(count)])


def after(x, *others):
    return lax.optimization_barrier((x,) + others)[0]


def bits_of(count):
    return [1 << i for i in range(count.bit_length() - 1)]


def reversed_order(count):
    width = count.bit_length() - 1
    return [int(f"{p:0{width}b}"[::-1], 2) for p in range(count)]


def gather_pieces(solves, rows, ready):
    block, panel = solves.shape
    if rows != 4:
        return [lax.all_gather(solves.T, "row", axis=1, tiled=True)]
    half = pltpu.VMEM((panel // 2, block), BF16)
    upper, lower = call(
        turn_kernel, (half, half), solves, remain=1,
        scratch=[pltpu.VMEM((block, panel), BF16), pltpu.SemaphoreType.DMA],
    )
    lower_x, upper_y = swap(lower, "row", 1), swap(upper, "row", 2)
    upper_x, lower_y = swap(upper, "row", 1), swap(lower, "row", 2)
    upper_far, lower_far = swap(after(upper_y, *ready), "row", 1), swap(after(lower_x, *ready), "row", 2)
    return [upper, lower, upper_x, lower_x, upper_y, lower_y, upper_far, lower_far]


def shards(coupling, solves, border_diagonal, panel_rows):
    half = HALF
    coupling, solves = coupling[0], solves[0]
    local, row_count = coupling.shape
    panel = solves.shape[1]
    scen, rows = lax.axis_size("scen"), lax.axis_size("row")
    layers = scen // 2
    row, place = lax.axis_index("row"), lax.axis_index("scen")
    share = row_count // scen
    size = panel // (2 * rows)
    shape = pltpu.VMEM
    panel_row, diagonal_row = panel_rows[None, :], border_diagonal.T
    first_row = row * row_count + place * share
    picked = shape((local, panel), BF16)
    chunk_room = [
        pltpu.VMEM((CHUNKS // 2, local // CHUNKS, row_count), BF16), pltpu.SemaphoreType.DMA((CHUNKS // 2,))
    ]
    chosen, entry, one, panel_row, diagonal_row = call(
        pick_kernel,
        (
            picked, shape((8, panel), F32), shape((row_count, panel), BF16),
            shape((1, panel), jnp.int32), shape((1, share), F32),
        ),
        panel_row, diagonal_row, coupling, remain=3,
        scratch=[chunk_room[0], pltpu.SemaphoreType.DMA((2,)), chunk_room[1]],
    )
    pieces = gather_pieces(solves, rows, (entry,))
    near, far = pieces[:6], pieces[6:]
    chosen = call(rest_kernel, picked, chosen, one, coupling, remain=1, scratch=chunk_room, aliases={0: 0})
    room = [pltpu.VMEM((panel // 2, panel), F32)]
    turned, terms = call(
        early_kernel, (shape((panel, local), BF16), shape((panel, panel), F32)), chosen, *near
    )
    send = call(
        functools.partial(send_kernel, rows), shape((panel // 2 + 8, panel), F32),
        chosen, entry, terms, *far, scratch=room,
    )
    turned, keep = call(
        functools.partial(keep_kernel, rows), (shape((panel, local), BF16), shape((panel // 2, panel), F32)),
        turned, chosen, terms, *far, scratch=room, aliases={0: 0},
    )
    coded = shape((size + SHORT, panel), I16)
    codes = call(
        functools.partial(pair_kernel, rows), (coded,) * rows, keep, swap(send, "scen", 1), entry
    )
    arrived = [swap(codes[k], "row", k) for k in range(rows - 1, 0, -1)]
    part = codes[0]
    steps = bits_of(layers)
    split = share % 128 == 0
    if split:
        count = layers // 2
        bulk = shape((layers * panel, share), F32)
        halved = lambda count: (shape((count * panel, share), F32), shape((count * (panel + TAIL), share), I16))
        own, send_rows = call(
            schur_kernel, (bulk, bulk), panel_row, diagonal_row, coupling, after(turned, part)
        )
        part = call(sum_kernel, coded, after(part, own), *arrived)
        got = swap(after(send_rows, part), "scen", 1)
    else:
        own, got = lax.psum_scatter(dot(turned, coupling), "scen", scatter_dimension=1, tiled=True), []
        mine = first_row + jnp.arange(share, dtype=jnp.int32)
        own = own + jnp.where(panel_rows[:, None] == mine[None, :], border_diagonal[:, 0][None, :], F32(0.0))
        part = call(sum_kernel, coded, part, *arrived)
    for bit in steps:
        other = swap(part, "scen", 2 * bit)
        if split and bit == steps[-1]:
            own, bulk_codes = call(functools.partial(bulk_pair_kernel, panel), halved(count), after(own, part), got)
            part = after(part, bulk_codes)
        part = call(sum_kernel, coded, part, other)
    shared = [swap(part, "row", k) for k in range(1, rows)]
    if split:
        for bit in steps[:-1]:
            count //= 2
            got = swap(after(bulk_codes, part), "scen", 2 * bit)
            own, bulk_codes = call(functools.partial(bulk_sum_kernel, panel), halved(count), own, got)
        got = [swap(bulk_codes, "scen", layers)]
    joined = call(join_kernel, shape((rows * (size + TAIL), panel), I16), part, *shared)
    if split:
        joined = after(joined, bulk_codes)
    other = swap(joined, "scen", 1)
    own_half = call(
        functools.partial(own_kernel, rows), shape((panel // 2, panel), F32), joined
    )
    inverse_first, pivots = call(
        functools.partial(first_kernel, rows), (shape((half, panel), F32), shape((panel, panel), F32)),
        own_half, other, micros=4.5,
    )
    inverse_second = call(second_kernel, shape((half, panel), F32), pivots, inverse_first, micros=4.5)
    out = jax.ShapeDtypeStruct((share, 1, half), F32)
    return call(
        factor_kernel, (out, out),
        inverse_first, inverse_second, own, *got,
    )


def solution(mesh):
    placed = (P("scen", None, "row"), P("scen", "row", None), P("scen", "row"), P())
    return jax.shard_map(
        shards,
        mesh=mesh,
        in_specs=placed,
        out_specs=(P("scen", "row", None), P("scen", "row", None)),
        check_vma=False,
    )
```

```python
import functools

import jax
import jax.numpy as jnp
from jax import lax
from jax.experimental import pallas as pl
from jax.experimental.pallas import tpu as pltpu
from jax.sharding import PartitionSpec as P

HALF = 256
NEWTON = 8
TAIL = 16
SHORT = 8
CHUNKS = 4
LEVELS = 32000.0
F32 = jnp.float32
BF16 = jnp.bfloat16
I16 = jnp.int16


def halves(a):
    high = a.astype(BF16)
    low = (a - high.astype(F32)).astype(BF16)
    return high, low


def left_of(a):
    high, low = halves(a)
    return jnp.concatenate([high, high, low], axis=1)


def right_of(b):
    high, low = halves(b)
    return jnp.concatenate([high, low, high], axis=0)


def dot(a, b):
    return jnp.dot(a, b, preferred_element_type=F32)


def product(a, b):
    return dot(left_of(a), right_of(b))


def nearly(pivot):
    size = jnp.abs(pivot)
    turned = pivot.T
    square = product(turned, pivot)
    norm_one = jnp.max(jnp.sum(size, axis=0, keepdims=True))
    norm_inf = jnp.max(jnp.sum(size, axis=1, keepdims=True))
    scale = F32(1.0) / (norm_one * norm_inf)
    count = pivot.shape[0]
    one = lax.broadcasted_iota(jnp.int32, pivot.shape, 0) == lax.broadcasted_iota(jnp.int32, pivot.shape, 1)
    rest = jnp.where(one, F32(1.0), F32(0.0)) - square * scale
    approx = turned * scale
    for step in range(NEWTON - 2):
        both = product(rest, jnp.concatenate([rest, approx], axis=1))
        rest, approx = both[:, :count], approx + both[:, count:]
    return approx + product(rest, approx)


def newton_beside(pivot, beside):
    approx = nearly(pivot)
    count = pivot.shape[0]
    both = product(approx, jnp.concatenate([pivot, beside], axis=1))
    stacked = jnp.concatenate([approx, both[:, count:]], axis=1)
    return 2.0 * stacked - product(both[:, :count], stacked)


def whereabouts():
    place = lax.axis_index("scen")
    return lax.axis_index("row"), lax.rem(place, 2), lax.div(place, 2)


def aligned(index, size):
    return pl.multiple_of(index * size, size)


def encode(values, out_ref, base, tail_rows, diagonal=None):
    rows, lanes = values.shape
    top = jnp.maximum(jnp.max(jnp.abs(values), axis=0, keepdims=True), F32(1e-30))
    power = jnp.ceil(jnp.log2(top))
    unit = jnp.exp2(power)
    mantissa = jnp.ceil(top / unit * F32(16384.0))
    scale = mantissa * unit * F32(1.0 / (16384.0 * LEVELS))
    codes = jnp.round(values * (F32(1.0) / scale)).astype(jnp.int32)
    out_ref[base:base + rows, :] = codes.astype(I16)
    row = lax.broadcasted_iota(jnp.int32, (tail_rows, lanes), 0)
    tail = jnp.where(row == 0, power, jnp.where(row == 1, mantissa, F32(0.0)))
    if diagonal is not None:
        coarse = jnp.floor(diagonal * F32(64.0))
        fine = (diagonal * F32(64.0) - coarse) * F32(4096.0)
        tail = jnp.where(row == 2, coarse, jnp.where(row == 3, fine, tail))
    out_ref[base + rows:base + rows + tail_rows, :] = tail.astype(jnp.int32).astype(I16)


def decode(ref, base, rows, tail_rows):
    tail = ref[base + rows:base + rows + tail_rows, :].astype(jnp.int32).astype(F32)
    scale = tail[1:2] * jnp.exp2(tail[0:1]) * F32(1.0 / (16384.0 * LEVELS))
    diagonal = tail[2:3] * F32(1.0 / 64.0) + tail[3:4] * F32(1.0 / (64.0 * 4096.0))
    return ref[base:base + rows, :].astype(jnp.int32).astype(F32) * scale, diagonal


def turn_kernel(solves_ref, upper_ref, lower_ref, solves_copy, done):
    copy = pltpu.make_async_copy(solves_ref, solves_copy, done)
    copy.start()
    copy.wait()
    turned = solves_copy[...].T
    half = upper_ref.shape[0]
    upper_ref[...] = turned[:half]
    lower_ref[...] = turned[half:]


def fetch(source_ref, target_ref, done, first):
    rows = target_ref.shape[1]
    copies = [
        pltpu.make_async_copy(source_ref.at[pl.ds((first + i) * rows, rows), :], target_ref.at[i], done.at[i])
        for i in range(target_ref.shape[0])
    ]
    for copy in copies:
        copy.start()
    return copies


def choose(copies, coupling_copy, one_ref, chosen_ref, first):
    rows = coupling_copy.shape[1]
    for i, copy in enumerate(copies):
        copy.wait()
        chosen_ref[(first + i) * rows:(first + i + 1) * rows, :] = dot(coupling_copy[i], one_ref[...]).astype(BF16)


def pick_kernel(
    panel_ref, own_diagonal_ref, coupling_ref,
    chosen_ref, entry_ref, one_ref, panel_out, diagonal_out, coupling_copy, small_done, done,
):
    small = [
        pltpu.make_async_copy(panel_ref, panel_out, small_done.at[0]),
        pltpu.make_async_copy(own_diagonal_ref, diagonal_out, small_done.at[1]),
    ]
    for copy in small:
        copy.start()
    copies = fetch(coupling_ref, coupling_copy, done, 0)
    for copy in small:
        copy.wait()
    columns, panel = one_ref.shape
    share = diagonal_out.shape[1]
    first_column = lax.axis_index("row") * columns
    first_row = first_column + lax.axis_index("scen") * share
    here = panel_out[...] - first_column == lax.broadcasted_iota(jnp.int32, (columns, panel), 0)
    one_ref[...] = jnp.where(here, F32(1.0), F32(0.0)).astype(BF16)
    owned = panel_out[...] - first_row == lax.broadcasted_iota(jnp.int32, (share, panel), 0)
    own = jnp.broadcast_to(diagonal_out[...], (8, share)).T[:, :1]
    entry = jnp.sum(jnp.where(owned, own, F32(0.0)), axis=0, keepdims=True)
    entry_ref[...] = jnp.broadcast_to(entry, entry_ref.shape)
    choose(copies, coupling_copy, one_ref, chosen_ref, 0)


def rest_kernel(chosen_in, one_ref, coupling_ref, chosen_ref, coupling_copy, done):
    first = coupling_copy.shape[0]
    copies = fetch(coupling_ref, coupling_copy, done, first)
    choose(copies, coupling_copy, one_ref, chosen_ref, first)


def early_kernel(chosen_ref, *refs):
    *pieces, turned_ref, terms_ref = refs
    row, _, _ = whereabouts()
    if len(pieces) == 1:
        turned_ref[...] = pieces[0][...]
    else:
        half, width = pieces[0].shape
        for i, piece in enumerate(pieces):
            start = aligned(row ^ (i // 2), width)
            turned_ref[i % 2 * half:(i % 2 + 1) * half, pl.ds(start, width)] = piece[...]
        start = aligned(row ^ (len(pieces) // 2), width)
        turned_ref[:, pl.ds(start, width)] = jnp.zeros((2 * half, width), BF16)
    terms_ref[...] = dot(turned_ref[...], chosen_ref[...])


def half_terms(rows, row, chosen_ref, terms_ref, far, whose, out_ref, all_ref):
    half = all_ref.shape[0]
    size = half // rows
    total = terms_ref[pl.ds(aligned(whose, half), half), :]
    if far:
        width = far[0].shape[1]
        block = jnp.where(whose == 0, far[0][...], far[1][...])
        total = total + dot(block, chosen_ref[pl.ds(aligned(row ^ (rows - 1), width), width), :])
    all_ref[...] = total
    for k in range(rows):
        out_ref[k * size:(k + 1) * size, :] = all_ref[pl.ds(aligned(row ^ k, size), size), :]


def send_kernel(rows, chosen_ref, entry_ref, terms_ref, *refs):
    *far, send_ref, all_ref = refs
    row, core, _ = whereabouts()
    half_terms(rows, row, chosen_ref, terms_ref, far, 1 - core, send_ref, all_ref)
    send_ref[all_ref.shape[0]:, :] = entry_ref[...]


def keep_kernel(rows, turned_in, chosen_ref, terms_ref, *refs):
    *far, turned_ref, keep_ref, all_ref = refs
    row, core, _ = whereabouts()
    half_terms(rows, row, chosen_ref, terms_ref, far, core, keep_ref, all_ref)
    for i, piece in enumerate(far):
        half, width = piece.shape
        start = aligned(row ^ (rows - 1), width)
        turned_ref[i * half:(i + 1) * half, pl.ds(start, width)] = piece[...]


def pair_kernel(rows, keep_ref, got_ref, entry_ref, *out_refs):
    size = keep_ref.shape[0] // rows
    entry = entry_ref[:1, :] + got_ref[rows * size:rows * size + 1, :]
    for k, out_ref in enumerate(out_refs):
        part = slice(k * size, (k + 1) * size)
        encode(keep_ref[part, :] + got_ref[part, :], out_ref, 0, SHORT, entry)


def sum_kernel(*refs):
    *in_refs, out_ref = refs
    size = out_ref.shape[0] - SHORT
    parts = [decode(ref, 0, size, SHORT) for ref in in_refs]
    encode(sum(p[0] for p in parts), out_ref, 0, SHORT, sum(p[1] for p in parts))


def join_kernel(*refs):
    *in_refs, out_ref = refs
    size = in_refs[0].shape[0] - SHORT
    for k, ref in enumerate(in_refs):
        start = k * (size + TAIL)
        out_ref[start:start + size, :] = ref[:size, :]
        tail = ref[size:, :].astype(jnp.int32)
        out_ref[start + size:start + size + TAIL, :] = jnp.concatenate([tail, jnp.zeros_like(tail)], axis=0).astype(I16)


def place_pieces(row, whose, ref, pivots_ref, rows, base):
    panel = pivots_ref.shape[1]
    size = panel // (2 * rows)
    index = lax.broadcasted_iota(jnp.int32, (size, panel), 1)
    for k in range(rows):
        start = aligned(whose * rows + (row ^ k), size)
        values, diagonal = decode(ref, k * (size + TAIL), size, TAIL)
        at = lax.broadcasted_iota(jnp.int32, (size, panel), 0) + start == index
        pivots_ref[pl.ds(start - base, size), :] = values + jnp.where(at, diagonal, F32(0.0))


def own_kernel(rows, own_ref, half_ref):
    row, core, _ = whereabouts()
    place_pieces(row, core, own_ref, half_ref, rows, core * half_ref.shape[0])


def newton_kernel(rows, half_ref, other_ref, inverse_ref, second_ref, pivots_ref):
    row, core, _ = whereabouts()
    half = half_ref.shape[0]
    pivots_ref[pl.ds(aligned(core, half), half), :] = half_ref[...]
    place_pieces(row, 1 - core, other_ref, pivots_ref, rows, 0)
    both = newton_beside(pivots_ref[:half, :half], pivots_ref[:half, half:])
    inverse_first = both[:, :half]
    inverse_ref[...] = inverse_first
    corner = pivots_ref[half:, :half]
    pivot = pivots_ref[half:, half:] - product(corner, both[:, half:])
    second_ref[...] = newton_beside(pivot, -product(corner, inverse_first))


def schur_kernel(panel_ref, own_diagonal_ref, coupling_ref, turned_ref, keep_ref, send_ref):
    row, core, layer = whereabouts()
    panel, share = turned_ref.shape[0], keep_ref.shape[1]
    first_row = row * coupling_ref.shape[1] + (2 * layer + core) * share
    layers = keep_ref.shape[0] // panel
    for position, k in enumerate(reversed_order(layers)):
        start = aligned(layer ^ k, 2 * share)
        both = dot(turned_ref[...], coupling_ref[:, pl.ds(start, 2 * share)])
        rows = slice(position * panel, (position + 1) * panel)
        one, two = both[:, :share], both[:, share:]
        kept = jnp.where(core == 0, one, two)
        if position == 0:
            wanted = jnp.broadcast_to(panel_ref[...].astype(F32), (share, panel)).T.astype(jnp.int32)
            here = wanted - first_row == lax.broadcasted_iota(jnp.int32, (panel, share), 1)
            kept = kept + jnp.where(here, own_diagonal_ref[...], F32(0.0))
        keep_ref[rows, :] = kept
        send_ref[rows, :] = jnp.where(core == 0, two, one)


def bulk_pair_kernel(panel, keep_ref, got_ref, own_ref, coded_ref):
    half = own_ref.shape[0]
    own_ref[...] = keep_ref[:half, :] + got_ref[:half, :]
    for i in range(half // panel):
        part = slice(half + i * panel, half + (i + 1) * panel)
        encode(keep_ref[part, :] + got_ref[part, :], coded_ref, i * (panel + TAIL), TAIL)


def bulk_sum_kernel(panel, keep_ref, got_ref, own_ref, coded_ref):
    half = own_ref.shape[0]
    for i in range(keep_ref.shape[0] // panel):
        value = keep_ref[i * panel:(i + 1) * panel, :] + decode(got_ref, i * (panel + TAIL), panel, TAIL)[0]
        if i * panel < half:
            own_ref[i * panel:(i + 1) * panel, :] = value
        else:
            encode(value, coded_ref, (i - half // panel) * (panel + TAIL), TAIL)


def factor_kernel(inverse_first_ref, inverse_second_ref, rows_ref, *refs):
    *got, first_out, second_out = refs
    panel = rows_ref.shape[0]
    half = panel // 2
    rows = rows_ref[...]
    for ref in got:
        rows = rows + decode(ref, 0, panel, TAIL)[0]
    first, second = rows[:half], rows[half:]
    first_out[...] = product(inverse_first_ref[...], first).T[:, None, :]
    second_out[...] = product(inverse_second_ref[...], jnp.concatenate([second, first], axis=0)).T[:, None, :]


def call(kernel, out_shape, *args, scratch=(), remain=0, micros=0.0, aliases=None):
    hbm = pl.BlockSpec(memory_space=pltpu.HBM)
    vmem = pl.BlockSpec(memory_space=pltpu.VMEM)
    stay = len(args) - remain
    args = args[:stay] + tuple(pltpu.with_memory_space_constraint(x, pltpu.HBM) for x in args[stay:])
    return pl.pallas_call(
        kernel,
        name=getattr(kernel, "func", kernel).__name__,
        out_shape=out_shape,
        in_specs=[vmem] * (len(args) - remain) + [hbm] * remain,
        out_specs=jax.tree.map(lambda _: vmem, out_shape),
        scratch_shapes=scratch,
        input_output_aliases=aliases or {},
        compiler_params=pltpu.CompilerParams(vmem_limit_bytes=12 << 20),
        cost_estimate=pl.CostEstimate(flops=0, bytes_accessed=int(micros * 3.69e6) + 1024, transcendentals=0),
    )(*args)


def swap(x, axis, bit):
    count = lax.axis_size(axis)
    return lax.ppermute(x, axis, [(i, i ^ bit) for i in range(count)])


def after(x, *others):
    return lax.optimization_barrier((x,) + others)[0]


def bits_of(count):
    return [1 << i for i in range(count.bit_length() - 1)]


def reversed_order(count):
    width = count.bit_length() - 1
    return [int(f"{p:0{width}b}"[::-1], 2) for p in range(count)]


def gather_pieces(solves, rows, ready):
    block, panel = solves.shape
    if rows != 4:
        return [lax.all_gather(solves.T, "row", axis=1, tiled=True)]
    half = pltpu.VMEM((panel // 2, block), BF16)
    upper, lower = call(
        turn_kernel, (half, half), solves, remain=1,
        scratch=[pltpu.VMEM((block, panel), BF16), pltpu.SemaphoreType.DMA],
    )
    lower_x, upper_y = swap(lower, "row", 1), swap(upper, "row", 2)
    upper_x, lower_y = swap(upper, "row", 1), swap(lower, "row", 2)
    upper_far, lower_far = swap(after(upper_y, *ready), "row", 1), swap(after(lower_x, *ready), "row", 2)
    return [upper, lower, upper_x, lower_x, upper_y, lower_y, upper_far, lower_far]


def shards(coupling, solves, border_diagonal, panel_rows):
    half = HALF
    coupling, solves = coupling[0], solves[0]
    local, row_count = coupling.shape
    panel = solves.shape[1]
    scen, rows = lax.axis_size("scen"), lax.axis_size("row")
    layers = scen // 2
    row, place = lax.axis_index("row"), lax.axis_index("scen")
    share = row_count // scen
    size = panel // (2 * rows)
    shape = pltpu.VMEM
    panel_row, diagonal_row = panel_rows[None, :], border_diagonal.T
    first_row = row * row_count + place * share
    picked = shape((local, panel), BF16)
    chunk_room = [
        pltpu.VMEM((CHUNKS // 2, local // CHUNKS, row_count), BF16), pltpu.SemaphoreType.DMA((CHUNKS // 2,))
    ]
    chosen, entry, one, panel_row, diagonal_row = call(
        pick_kernel,
        (
            picked, shape((8, panel), F32), shape((row_count, panel), BF16),
            shape((1, panel), jnp.int32), shape((1, share), F32),
        ),
        panel_row, diagonal_row, coupling, remain=3,
        scratch=[chunk_room[0], pltpu.SemaphoreType.DMA((2,)), chunk_room[1]],
    )
    pieces = gather_pieces(solves, rows, (entry,))
    near, far = pieces[:6], pieces[6:]
    chosen = call(rest_kernel, picked, chosen, one, coupling, remain=1, scratch=chunk_room, aliases={0: 0})
    room = [pltpu.VMEM((panel // 2, panel), F32)]
    turned, terms = call(
        early_kernel, (shape((panel, local), BF16), shape((panel, panel), F32)), chosen, *near
    )
    send = call(
        functools.partial(send_kernel, rows), shape((panel // 2 + 8, panel), F32),
        chosen, entry, terms, *far, scratch=room,
    )
    turned, keep = call(
        functools.partial(keep_kernel, rows), (shape((panel, local), BF16), shape((panel // 2, panel), F32)),
        turned, chosen, terms, *far, scratch=room, aliases={0: 0},
    )
    coded = shape((size + SHORT, panel), I16)
    codes = call(
        functools.partial(pair_kernel, rows), (coded,) * rows, keep, swap(send, "scen", 1), entry
    )
    arrived = [swap(codes[k], "row", k) for k in range(rows - 1, 0, -1)]
    part = codes[0]
    steps = bits_of(layers)
    split = share % 128 == 0
    if split:
        count = layers // 2
        bulk = shape((layers * panel, share), F32)
        halved = lambda count: (shape((count * panel, share), F32), shape((count * (panel + TAIL), share), I16))
        own, send_rows = call(
            schur_kernel, (bulk, bulk), panel_row, diagonal_row, coupling, after(turned, part)
        )
        part = call(sum_kernel, coded, after(part, own), *arrived)
        got = swap(after(send_rows, part), "scen", 1)
    else:
        own, got = lax.psum_scatter(dot(turned, coupling), "scen", scatter_dimension=1, tiled=True), []
        mine = first_row + jnp.arange(share, dtype=jnp.int32)
        own = own + jnp.where(panel_rows[:, None] == mine[None, :], border_diagonal[:, 0][None, :], F32(0.0))
        part = call(sum_kernel, coded, part, *arrived)
    if split:
        others = [swap(part, "scen", 2 * k) for k in range(1, layers)]
        own, bulk_codes = call(functools.partial(bulk_pair_kernel, panel), halved(count), after(own, part), got)
        part = call(sum_kernel, coded, after(part, bulk_codes), *others)
    else:
        for bit in steps:
            part = call(sum_kernel, coded, part, swap(part, "scen", 2 * bit))
    shared = [swap(part, "row", k) for k in range(1, rows)]
    if split:
        for bit in steps[:-1]:
            count //= 2
            got = swap(after(bulk_codes, part), "scen", 2 * bit)
            own, bulk_codes = call(functools.partial(bulk_sum_kernel, panel), halved(count), own, got)
        got = [swap(bulk_codes, "scen", layers)]
    joined = call(join_kernel, shape((rows * (size + TAIL), panel), I16), part, *shared)
    if split:
        joined = after(joined, bulk_codes)
    other = swap(joined, "scen", 1)
    own_half = call(
        functools.partial(own_kernel, rows), shape((panel // 2, panel), F32), joined
    )
    inverse_first, inverse_second = call(
        functools.partial(newton_kernel, rows), (shape((half, half), F32), shape((half, panel), F32)),
        own_half, other, micros=9.0, scratch=[pltpu.VMEM((panel, panel), F32)],
    )
    out = jax.ShapeDtypeStruct((share, 1, half), F32)
    return call(
        factor_kernel, (out, out),
        inverse_first, inverse_second, own, *got,
    )


def solution(mesh):
    placed = (P("scen", None, "row"), P("scen", "row", None), P("scen", "row"), P())
    return jax.shard_map(
        shards,
        mesh=mesh,
        in_specs=placed,
        out_specs=(P("scen", "row", None), P("scen", "row", None)),
        check_vma=False,
    )
```

```python
import functools

import jax
import jax.numpy as jnp
from jax import lax
from jax.experimental import pallas as pl
from jax.experimental.pallas import tpu as pltpu
from jax.sharding import PartitionSpec as P

HALF = 256
NEWTON = 8
TAIL = 16
SHORT = 8
CHUNKS = 4
LEVELS = 32000.0
F32 = jnp.float32
BF16 = jnp.bfloat16
I16 = jnp.int16


def halves(a):
    high = a.astype(BF16)
    low = (a - high.astype(F32)).astype(BF16)
    return high, low


def left_of(a):
    high, low = halves(a)
    return jnp.concatenate([high, high, low], axis=1)


def right_of(b):
    high, low = halves(b)
    return jnp.concatenate([high, low, high], axis=0)


def dot(a, b):
    return jnp.dot(a, b, preferred_element_type=F32)


def product(a, b):
    return dot(left_of(a), right_of(b))


def nearly(pivot):
    size = jnp.abs(pivot)
    turned = pivot.T
    square = product(turned, pivot)
    norm_one = jnp.max(jnp.sum(size, axis=0, keepdims=True))
    norm_inf = jnp.max(jnp.sum(size, axis=1, keepdims=True))
    scale = F32(1.0) / (norm_one * norm_inf)
    count = pivot.shape[0]
    one = lax.broadcasted_iota(jnp.int32, pivot.shape, 0) == lax.broadcasted_iota(jnp.int32, pivot.shape, 1)
    rest = jnp.where(one, F32(1.0), F32(0.0)) - square * scale
    approx = turned * scale
    for step in range(NEWTON - 2):
        both = product(rest, jnp.concatenate([rest, approx], axis=1))
        rest, approx = both[:, :count], approx + both[:, count:]
    return approx + product(rest, approx)


def newton_beside(pivot, beside):
    approx = nearly(pivot)
    count = pivot.shape[0]
    both = product(approx, jnp.concatenate([pivot, beside], axis=1))
    stacked = jnp.concatenate([approx, both[:, count:]], axis=1)
    return 2.0 * stacked - product(both[:, :count], stacked)


def whereabouts():
    place = lax.axis_index("scen")
    return lax.axis_index("row"), lax.rem(place, 2), lax.div(place, 2)


def aligned(index, size):
    return pl.multiple_of(index * size, size)


def encode(values, out_ref, base, tail_rows, diagonal=None):
    rows, lanes = values.shape
    top = jnp.maximum(jnp.max(jnp.abs(values), axis=0, keepdims=True), F32(1e-30))
    power = jnp.ceil(jnp.log2(top))
    unit = jnp.exp2(power)
    mantissa = jnp.ceil(top / unit * F32(16384.0))
    scale = mantissa * unit * F32(1.0 / (16384.0 * LEVELS))
    codes = jnp.round(values * (F32(1.0) / scale)).astype(jnp.int32)
    out_ref[base:base + rows, :] = codes.astype(I16)
    row = lax.broadcasted_iota(jnp.int32, (tail_rows, lanes), 0)
    tail = jnp.where(row == 0, power, jnp.where(row == 1, mantissa, F32(0.0)))
    if diagonal is not None:
        coarse = jnp.floor(diagonal * F32(64.0))
        fine = (diagonal * F32(64.0) - coarse) * F32(4096.0)
        tail = jnp.where(row == 2, coarse, jnp.where(row == 3, fine, tail))
    out_ref[base + rows:base + rows + tail_rows, :] = tail.astype(jnp.int32).astype(I16)


def decode(ref, base, rows, tail_rows):
    tail = ref[base + rows:base + rows + tail_rows, :].astype(jnp.int32).astype(F32)
    scale = tail[1:2] * jnp.exp2(tail[0:1]) * F32(1.0 / (16384.0 * LEVELS))
    diagonal = tail[2:3] * F32(1.0 / 64.0) + tail[3:4] * F32(1.0 / (64.0 * 4096.0))
    return ref[base:base + rows, :].astype(jnp.int32).astype(F32) * scale, diagonal


def turn_kernel(solves_ref, upper_ref, lower_ref, solves_copy, done):
    half = upper_ref.shape[0]
    copies = [
        pltpu.make_async_copy(solves_ref.at[:, pl.ds(i * half, half)], solves_copy.at[i], done.at[i]) for i in (0, 1)
    ]
    for copy in copies:
        copy.start()
    for i, out_ref in enumerate((upper_ref, lower_ref)):
        copies[i].wait()
        out_ref[...] = solves_copy[i].T


def fetch(source_ref, target_ref, done, first):
    rows = target_ref.shape[1]
    copies = [
        pltpu.make_async_copy(source_ref.at[pl.ds((first + i) * rows, rows), :], target_ref.at[i], done.at[i])
        for i in range(target_ref.shape[0])
    ]
    for copy in copies:
        copy.start()
    return copies


def choose(copies, coupling_copy, one_ref, chosen_ref, first):
    rows = coupling_copy.shape[1]
    for i, copy in enumerate(copies):
        copy.wait()
        chosen_ref[(first + i) * rows:(first + i + 1) * rows, :] = dot(coupling_copy[i], one_ref[...]).astype(BF16)


def pick_kernel(
    panel_ref, own_diagonal_ref, coupling_ref,
    chosen_ref, entry_ref, one_ref, panel_out, diagonal_out, coupling_copy, small_done, done,
):
    small = [
        pltpu.make_async_copy(panel_ref, panel_out, small_done.at[0]),
        pltpu.make_async_copy(own_diagonal_ref, diagonal_out, small_done.at[1]),
    ]
    for copy in small:
        copy.start()
    copies = fetch(coupling_ref, coupling_copy, done, 0)
    for copy in small:
        copy.wait()
    columns, panel = one_ref.shape
    share = diagonal_out.shape[1]
    first_column = lax.axis_index("row") * columns
    first_row = first_column + lax.axis_index("scen") * share
    here = panel_out[...] - first_column == lax.broadcasted_iota(jnp.int32, (columns, panel), 0)
    one_ref[...] = jnp.where(here, F32(1.0), F32(0.0)).astype(BF16)
    owned = panel_out[...] - first_row == lax.broadcasted_iota(jnp.int32, (share, panel), 0)
    own = jnp.broadcast_to(diagonal_out[...], (8, share)).T[:, :1]
    entry = jnp.sum(jnp.where(owned, own, F32(0.0)), axis=0, keepdims=True)
    entry_ref[...] = jnp.broadcast_to(entry, entry_ref.shape)
    choose(copies, coupling_copy, one_ref, chosen_ref, 0)


def rest_kernel(chosen_in, one_ref, coupling_ref, chosen_ref, coupling_copy, done):
    first = coupling_copy.shape[0]
    copies = fetch(coupling_ref, coupling_copy, done, first)
    choose(copies, coupling_copy, one_ref, chosen_ref, first)


def early_kernel(chosen_ref, *refs):
    *pieces, turned_ref, terms_ref = refs
    row, _, _ = whereabouts()
    if len(pieces) == 1:
        turned_ref[...] = pieces[0][...]
    else:
        half, width = pieces[0].shape
        for i, piece in enumerate(pieces):
            start = aligned(row ^ (i // 2), width)
            turned_ref[i % 2 * half:(i % 2 + 1) * half, pl.ds(start, width)] = piece[...]
        start = aligned(row ^ (len(pieces) // 2), width)
        turned_ref[:, pl.ds(start, width)] = jnp.zeros((2 * half, width), BF16)
    terms_ref[...] = dot(turned_ref[...], chosen_ref[...])


def half_terms(rows, row, chosen_ref, terms_ref, far, whose, out_ref, all_ref):
    half = all_ref.shape[0]
    size = half // rows
    total = terms_ref[pl.ds(aligned(whose, half), half), :]
    if far:
        width = far[0].shape[1]
        block = jnp.where(whose == 0, far[0][...], far[1][...])
        total = total + dot(block, chosen_ref[pl.ds(aligned(row ^ (rows - 1), width), width), :])
    all_ref[...] = total
    for k in range(rows):
        out_ref[k * size:(k + 1) * size, :] = all_ref[pl.ds(aligned(row ^ k, size), size), :]


def send_kernel(rows, chosen_ref, entry_ref, terms_ref, *refs):
    *far, send_ref, all_ref = refs
    row, core, _ = whereabouts()
    half_terms(rows, row, chosen_ref, terms_ref, far, 1 - core, send_ref, all_ref)
    send_ref[all_ref.shape[0]:, :] = entry_ref[...]


def keep_kernel(rows, turned_in, chosen_ref, terms_ref, *refs):
    *far, turned_ref, keep_ref, all_ref = refs
    row, core, _ = whereabouts()
    half_terms(rows, row, chosen_ref, terms_ref, far, core, keep_ref, all_ref)
    for i, piece in enumerate(far):
        half, width = piece.shape
        start = aligned(row ^ (rows - 1), width)
        turned_ref[i * half:(i + 1) * half, pl.ds(start, width)] = piece[...]


def pair_kernel(rows, keep_ref, got_ref, entry_ref, *out_refs):
    size = keep_ref.shape[0] // rows
    entry = entry_ref[:1, :] + got_ref[rows * size:rows * size + 1, :]
    for k, out_ref in enumerate(out_refs):
        part = slice(k * size, (k + 1) * size)
        encode(keep_ref[part, :] + got_ref[part, :], out_ref, 0, SHORT, entry)


def sum_kernel(*refs):
    *in_refs, out_ref = refs
    size = out_ref.shape[0] - SHORT
    parts = [decode(ref, 0, size, SHORT) for ref in in_refs]
    encode(sum(p[0] for p in parts), out_ref, 0, SHORT, sum(p[1] for p in parts))


def join_kernel(*refs):
    *in_refs, out_ref = refs
    size = in_refs[0].shape[0] - SHORT
    for k, ref in enumerate(in_refs):
        start = k * (size + TAIL)
        out_ref[start:start + size, :] = ref[:size, :]
        tail = ref[size:, :].astype(jnp.int32)
        out_ref[start + size:start + size + TAIL, :] = jnp.concatenate([tail, jnp.zeros_like(tail)], axis=0).astype(I16)


def place_pieces(row, whose, ref, pivots_ref, rows, base):
    panel = pivots_ref.shape[1]
    size = panel // (2 * rows)
    index = lax.broadcasted_iota(jnp.int32, (size, panel), 1)
    for k in range(rows):
        start = aligned(whose * rows + (row ^ k), size)
        values, diagonal = decode(ref, k * (size + TAIL), size, TAIL)
        at = lax.broadcasted_iota(jnp.int32, (size, panel), 0) + start == index
        pivots_ref[pl.ds(start - base, size), :] = values + jnp.where(at, diagonal, F32(0.0))


def own_kernel(rows, own_ref, half_ref):
    row, core, _ = whereabouts()
    place_pieces(row, core, own_ref, half_ref, rows, core * half_ref.shape[0])


def newton_kernel(rows, half_ref, other_ref, inverse_ref, second_ref, pivots_ref):
    row, core, _ = whereabouts()
    half = half_ref.shape[0]
    pivots_ref[pl.ds(aligned(core, half), half), :] = half_ref[...]
    place_pieces(row, 1 - core, other_ref, pivots_ref, rows, 0)
    both = newton_beside(pivots_ref[:half, :half], pivots_ref[:half, half:])
    inverse_first = both[:, :half]
    inverse_ref[...] = inverse_first
    corner = pivots_ref[half:, :half]
    pivot = pivots_ref[half:, half:] - product(corner, both[:, half:])
    second_ref[...] = newton_beside(pivot, -product(corner, inverse_first))


def schur_kernel(panel_ref, own_diagonal_ref, coupling_ref, turned_ref, keep_ref, send_ref):
    row, core, layer = whereabouts()
    panel, share = turned_ref.shape[0], keep_ref.shape[1]
    first_row = row * coupling_ref.shape[1] + (2 * layer + core) * share
    layers = keep_ref.shape[0] // panel
    for position, k in enumerate(reversed_order(layers)):
        start = aligned(layer ^ k, 2 * share)
        both = dot(turned_ref[...], coupling_ref[:, pl.ds(start, 2 * share)])
        rows = slice(position * panel, (position + 1) * panel)
        one, two = both[:, :share], both[:, share:]
        kept = jnp.where(core == 0, one, two)
        if position == 0:
            wanted = jnp.broadcast_to(panel_ref[...].astype(F32), (share, panel)).T.astype(jnp.int32)
            here = wanted - first_row == lax.broadcasted_iota(jnp.int32, (panel, share), 1)
            kept = kept + jnp.where(here, own_diagonal_ref[...], F32(0.0))
        keep_ref[rows, :] = kept
        send_ref[rows, :] = jnp.where(core == 0, two, one)


def bulk_pair_kernel(panel, keep_ref, got_ref, own_ref, coded_ref):
    half = own_ref.shape[0]
    own_ref[...] = keep_ref[:half, :] + got_ref[:half, :]
    for i in range(half // panel):
        part = slice(half + i * panel, half + (i + 1) * panel)
        encode(keep_ref[part, :] + got_ref[part, :], coded_ref, i * (panel + TAIL), TAIL)


def bulk_sum_kernel(panel, keep_ref, got_ref, own_ref, coded_ref):
    half = own_ref.shape[0]
    for i in range(keep_ref.shape[0] // panel):
        value = keep_ref[i * panel:(i + 1) * panel, :] + decode(got_ref, i * (panel + TAIL), panel, TAIL)[0]
        if i * panel < half:
            own_ref[i * panel:(i + 1) * panel, :] = value
        else:
            encode(value, coded_ref, (i - half // panel) * (panel + TAIL), TAIL)


def factor_kernel(inverse_first_ref, inverse_second_ref, rows_ref, *refs):
    *got, first_out, second_out = refs
    panel = rows_ref.shape[0]
    half = panel // 2
    rows = rows_ref[...]
    for ref in got:
        rows = rows + decode(ref, 0, panel, TAIL)[0]
    first, second = rows[:half], rows[half:]
    first_out[...] = product(inverse_first_ref[...], first).T[:, None, :]
    second_out[...] = product(inverse_second_ref[...], jnp.concatenate([second, first], axis=0)).T[:, None, :]


def call(kernel, out_shape, *args, scratch=(), remain=0, micros=0.0, aliases=None):
    hbm = pl.BlockSpec(memory_space=pltpu.HBM)
    vmem = pl.BlockSpec(memory_space=pltpu.VMEM)
    stay = len(args) - remain
    args = args[:stay] + tuple(pltpu.with_memory_space_constraint(x, pltpu.HBM) for x in args[stay:])
    return pl.pallas_call(
        kernel,
        name=getattr(kernel, "func", kernel).__name__,
        out_shape=out_shape,
        in_specs=[vmem] * (len(args) - remain) + [hbm] * remain,
        out_specs=jax.tree.map(lambda _: vmem, out_shape),
        scratch_shapes=scratch,
        input_output_aliases=aliases or {},
        compiler_params=pltpu.CompilerParams(vmem_limit_bytes=12 << 20),
        cost_estimate=pl.CostEstimate(flops=0, bytes_accessed=int(micros * 3.69e6) + 1024, transcendentals=0),
    )(*args)


def swap(x, axis, bit):
    count = lax.axis_size(axis)
    return lax.ppermute(x, axis, [(i, i ^ bit) for i in range(count)])


def after(x, *others):
    return lax.optimization_barrier((x,) + others)[0]


def bits_of(count):
    return [1 << i for i in range(count.bit_length() - 1)]


def reversed_order(count):
    width = count.bit_length() - 1
    return [int(f"{p:0{width}b}"[::-1], 2) for p in range(count)]


def gather_pieces(solves, rows, ready):
    block, panel = solves.shape
    if rows != 4:
        return [lax.all_gather(solves.T, "row", axis=1, tiled=True)]
    half = pltpu.VMEM((panel // 2, block), BF16)
    upper, lower = call(
        turn_kernel, (half, half), solves, remain=1,
        scratch=[pltpu.VMEM((2, block, panel // 2), BF16), pltpu.SemaphoreType.DMA((2,))],
    )
    lower_x, upper_y = swap(lower, "row", 1), swap(upper, "row", 2)
    upper_x, lower_y = swap(upper, "row", 1), swap(lower, "row", 2)
    upper_far, lower_far = swap(after(upper_y, *ready), "row", 1), swap(after(lower_x, *ready), "row", 2)
    return [upper, lower, upper_x, lower_x, upper_y, lower_y, upper_far, lower_far]


def shards(coupling, solves, border_diagonal, panel_rows):
    half = HALF
    coupling, solves = coupling[0], solves[0]
    local, row_count = coupling.shape
    panel = solves.shape[1]
    scen, rows = lax.axis_size("scen"), lax.axis_size("row")
    layers = scen // 2
    row, place = lax.axis_index("row"), lax.axis_index("scen")
    share = row_count // scen
    size = panel // (2 * rows)
    shape = pltpu.VMEM
    panel_row, diagonal_row = panel_rows[None, :], border_diagonal.T
    first_row = row * row_count + place * share
    picked = shape((local, panel), BF16)
    chunk_room = [
        pltpu.VMEM((CHUNKS // 2, local // CHUNKS, row_count), BF16), pltpu.SemaphoreType.DMA((CHUNKS // 2,))
    ]
    chosen, entry, one, panel_row, diagonal_row = call(
        pick_kernel,
        (
            picked, shape((8, panel), F32), shape((row_count, panel), BF16),
            shape((1, panel), jnp.int32), shape((1, share), F32),
        ),
        panel_row, diagonal_row, coupling, remain=3,
        scratch=[chunk_room[0], pltpu.SemaphoreType.DMA((2,)), chunk_room[1]],
    )
    pieces = gather_pieces(solves, rows, (entry,))
    near, far = pieces[:6], pieces[6:]
    chosen = call(rest_kernel, picked, chosen, one, coupling, remain=1, scratch=chunk_room, aliases={0: 0})
    room = [pltpu.VMEM((panel // 2, panel), F32)]
    turned, terms = call(
        early_kernel, (shape((panel, local), BF16), shape((panel, panel), F32)), chosen, *near
    )
    send = call(
        functools.partial(send_kernel, rows), shape((panel // 2 + 8, panel), F32),
        chosen, entry, terms, *far, scratch=room,
    )
    turned, keep = call(
        functools.partial(keep_kernel, rows), (shape((panel, local), BF16), shape((panel // 2, panel), F32)),
        turned, chosen, terms, *far, scratch=room, aliases={0: 0},
    )
    coded = shape((size + SHORT, panel), I16)
    codes = call(
        functools.partial(pair_kernel, rows), (coded,) * rows, keep, swap(send, "scen", 1), entry
    )
    arrived = [swap(codes[k], "row", k) for k in range(rows - 1, 0, -1)]
    part = codes[0]
    steps = bits_of(layers)
    split = share % 128 == 0
    if split:
        count = layers // 2
        bulk = shape((layers * panel, share), F32)
        halved = lambda count: (shape((count * panel, share), F32), shape((count * (panel + TAIL), share), I16))
        own, send_rows = call(
            schur_kernel, (bulk, bulk), panel_row, diagonal_row, coupling, after(turned, part)
        )
        part = call(sum_kernel, coded, after(part, own), *arrived)
        got = swap(after(send_rows, part), "scen", 1)
    else:
        own, got = lax.psum_scatter(dot(turned, coupling), "scen", scatter_dimension=1, tiled=True), []
        mine = first_row + jnp.arange(share, dtype=jnp.int32)
        own = own + jnp.where(panel_rows[:, None] == mine[None, :], border_diagonal[:, 0][None, :], F32(0.0))
        part = call(sum_kernel, coded, part, *arrived)
    if split:
        others = [swap(part, "scen", 2 * k) for k in range(1, layers)]
        own, bulk_codes = call(functools.partial(bulk_pair_kernel, panel), halved(count), after(own, part), got)
        part = call(sum_kernel, coded, after(part, bulk_codes), *others)
    else:
        for bit in steps:
            part = call(sum_kernel, coded, part, swap(part, "scen", 2 * bit))
    shared = [swap(part, "row", k) for k in range(1, rows)]
    if split:
        for bit in steps[:-1]:
            count //= 2
            got = swap(bulk_codes, "scen", 2 * bit)
            own, bulk_codes = call(functools.partial(bulk_sum_kernel, panel), halved(count), own, got)
        got = [swap(bulk_codes, "scen", layers)]
    joined = call(join_kernel, shape((rows * (size + TAIL), panel), I16), part, *shared)
    other = swap(joined, "scen", 1)
    own_half = call(
        functools.partial(own_kernel, rows), shape((panel // 2, panel), F32), joined
    )
    inverse_first, inverse_second = call(
        functools.partial(newton_kernel, rows), (shape((half, half), F32), shape((half, panel), F32)),
        own_half, other, micros=9.0, scratch=[pltpu.VMEM((panel, panel), F32)],
    )
    out = jax.ShapeDtypeStruct((share, 1, half), F32)
    return call(
        factor_kernel, (out, out),
        inverse_first, inverse_second, own, *got,
    )


def solution(mesh):
    placed = (P("scen", None, "row"), P("scen", "row", None), P("scen", "row"), P())
    return jax.shard_map(
        shards,
        mesh=mesh,
        in_specs=placed,
        out_specs=(P("scen", "row", None), P("scen", "row", None)),
        check_vma=False,
    )
```

```python
import functools

import jax
import jax.numpy as jnp
from jax import lax
from jax.experimental import pallas as pl
from jax.experimental.pallas import tpu as pltpu
from jax.sharding import PartitionSpec as P

HALF = 256
NEWTON = 8
TAIL = 16
SHORT = 8
CHUNKS = 4
LEVELS = 32000.0
UPPER = 288
F32 = jnp.float32
BF16 = jnp.bfloat16
I16 = jnp.int16


def halves(a):
    high = a.astype(BF16)
    low = (a - high.astype(F32)).astype(BF16)
    return high, low


def dot(a, b):
    return jnp.dot(a, b, preferred_element_type=F32)


def product(a, b):
    high, low = halves(a)
    other_high, other_low = halves(b)
    both = dot(jnp.concatenate([high, low], axis=0), other_high)
    count = a.shape[0]
    return both[:count] + (both[count:] + dot(high, other_low))


def nearly(pivot):
    size = jnp.abs(pivot)
    turned = pivot.T
    square = product(turned, pivot)
    norm_one = jnp.max(jnp.sum(size, axis=0, keepdims=True))
    norm_inf = jnp.max(jnp.sum(size, axis=1, keepdims=True))
    scale = F32(1.0) / (norm_one * norm_inf)
    count = pivot.shape[0]
    one = lax.broadcasted_iota(jnp.int32, pivot.shape, 0) == lax.broadcasted_iota(jnp.int32, pivot.shape, 1)
    rest = jnp.where(one, F32(1.0), F32(0.0)) - square * scale
    approx = turned * scale
    for step in range(NEWTON - 2):
        both = product(rest, jnp.concatenate([rest, approx], axis=1))
        rest, approx = both[:, :count], approx + both[:, count:]
    return approx + product(rest, approx)


def newton_beside(pivot, beside):
    approx = nearly(pivot)
    count = pivot.shape[0]
    both = product(approx, jnp.concatenate([pivot, beside], axis=1))
    stacked = jnp.concatenate([approx, both[:, count:]], axis=1)
    return 2.0 * stacked - product(both[:, :count], stacked)


def whereabouts():
    place = lax.axis_index("scen")
    return lax.axis_index("row"), lax.rem(place, 2), lax.div(place, 2)


def aligned(index, size):
    return pl.multiple_of(index * size, size)


def encode(values, out_ref, base, tail_rows, diagonal=None):
    rows, lanes = values.shape
    top = jnp.maximum(jnp.max(jnp.abs(values), axis=0, keepdims=True), F32(1e-30))
    power = jnp.ceil(jnp.log2(top))
    unit = jnp.exp2(power)
    mantissa = jnp.ceil(top / unit * F32(16384.0))
    scale = mantissa * unit * F32(1.0 / (16384.0 * LEVELS))
    codes = jnp.round(values * (F32(1.0) / scale)).astype(jnp.int32)
    out_ref[base:base + rows, :] = codes.astype(I16)
    row = lax.broadcasted_iota(jnp.int32, (tail_rows, lanes), 0)
    tail = jnp.where(row == 0, power, jnp.where(row == 1, mantissa, F32(0.0)))
    if diagonal is not None:
        coarse = jnp.floor(diagonal * F32(64.0))
        fine = (diagonal * F32(64.0) - coarse) * F32(4096.0)
        tail = jnp.where(row == 2, coarse, jnp.where(row == 3, fine, tail))
    out_ref[base + rows:base + rows + tail_rows, :] = tail.astype(jnp.int32).astype(I16)


def decode(ref, base, rows, tail_rows):
    tail = ref[base + rows:base + rows + tail_rows, :].astype(jnp.int32).astype(F32)
    scale = tail[1:2] * jnp.exp2(tail[0:1]) * F32(1.0 / (16384.0 * LEVELS))
    diagonal = tail[2:3] * F32(1.0 / 64.0) + tail[3:4] * F32(1.0 / (64.0 * 4096.0))
    return ref[base:base + rows, :].astype(jnp.int32).astype(F32) * scale, diagonal


def turn_kernel(solves_ref, upper_ref, lower_ref, solves_copy, done):
    copy = pltpu.make_async_copy(solves_ref, solves_copy, done)
    copy.start()
    copy.wait()
    turned = solves_copy[...].T
    upper_ref[...] = turned[:UPPER]
    lower_ref[...] = turned[UPPER:]


def fetch(source_ref, target_ref, done, first):
    rows = target_ref.shape[1]
    copies = [
        pltpu.make_async_copy(source_ref.at[pl.ds((first + i) * rows, rows), :], target_ref.at[i], done.at[i])
        for i in range(target_ref.shape[0])
    ]
    for copy in copies:
        copy.start()
    return copies


def choose(copies, coupling_copy, one_ref, chosen_ref, first):
    rows = coupling_copy.shape[1]
    for i, copy in enumerate(copies):
        copy.wait()
        chosen_ref[(first + i) * rows:(first + i + 1) * rows, :] = dot(coupling_copy[i], one_ref[...]).astype(BF16)


def pick_kernel(
    panel_ref, own_diagonal_ref, coupling_ref,
    chosen_ref, entry_ref, one_ref, panel_out, diagonal_out, coupling_copy, small_done, done,
):
    small = [
        pltpu.make_async_copy(panel_ref, panel_out, small_done.at[0]),
        pltpu.make_async_copy(own_diagonal_ref, diagonal_out, small_done.at[1]),
    ]
    for copy in small:
        copy.start()
    copies = fetch(coupling_ref, coupling_copy, done, 0)
    for copy in small:
        copy.wait()
    columns, panel = one_ref.shape
    share = diagonal_out.shape[1]
    first_column = lax.axis_index("row") * columns
    first_row = first_column + lax.axis_index("scen") * share
    here = panel_out[...] - first_column == lax.broadcasted_iota(jnp.int32, (columns, panel), 0)
    one_ref[...] = jnp.where(here, F32(1.0), F32(0.0)).astype(BF16)
    owned = panel_out[...] - first_row == lax.broadcasted_iota(jnp.int32, (share, panel), 0)
    own = jnp.broadcast_to(diagonal_out[...], (8, share)).T[:, :1]
    entry = jnp.sum(jnp.where(owned, own, F32(0.0)), axis=0, keepdims=True)
    entry_ref[...] = jnp.broadcast_to(entry, entry_ref.shape)
    choose(copies, coupling_copy, one_ref, chosen_ref, 0)


def rest_kernel(chosen_in, one_ref, coupling_ref, chosen_ref, coupling_copy, done):
    first = coupling_copy.shape[0]
    copies = fetch(coupling_ref, coupling_copy, done, first)
    choose(copies, coupling_copy, one_ref, chosen_ref, first)


def put_pieces(turned_ref, start, upper_ref, lower_ref):
    width = upper_ref.shape[1]
    turned_ref[:UPPER, pl.ds(start, width)] = upper_ref[...]
    turned_ref[UPPER:, pl.ds(start, width)] = lower_ref[...]


def early_kernel(chosen_ref, *refs):
    *pieces, turned_ref, terms_ref = refs
    row, _, _ = whereabouts()
    if len(pieces) == 1:
        turned_ref[...] = pieces[0][...]
    else:
        width = pieces[0].shape[1]
        for k in range(len(pieces) // 2):
            put_pieces(turned_ref, aligned(row ^ k, width), *pieces[2 * k:2 * k + 2])
        start = aligned(row ^ (len(pieces) // 2), width)
        turned_ref[:, pl.ds(start, width)] = jnp.zeros((turned_ref.shape[0], width), BF16)
    terms_ref[...] = dot(turned_ref[...], chosen_ref[...])


def half_terms(rows, chosen_ref, terms_ref, far, whose, out_ref, all_ref, far_ref):
    row, _, _ = whereabouts()
    half = all_ref.shape[0]
    size = half // rows
    total = terms_ref[pl.ds(aligned(whose, half), half), :]
    if far:
        put_pieces(far_ref, 0, *far)
        width = far_ref.shape[1]
        block = far_ref[pl.ds(aligned(whose, half), half), :]
        total = total + dot(block, chosen_ref[pl.ds(aligned(row ^ (rows - 1), width), width), :])
    all_ref[...] = total
    for k in range(rows):
        out_ref[k * size:(k + 1) * size, :] = all_ref[pl.ds(aligned(row ^ k, size), size), :]


def send_kernel(rows, chosen_ref, entry_ref, terms_ref, *refs):
    *far, send_ref, all_ref, far_ref = refs
    half_terms(rows, chosen_ref, terms_ref, far, 1 - whereabouts()[1], send_ref, all_ref, far_ref)
    send_ref[all_ref.shape[0]:, :] = entry_ref[...]


def keep_kernel(rows, turned_in, chosen_ref, terms_ref, *refs):
    *far, turned_ref, keep_ref, all_ref, far_ref = refs
    row, core, _ = whereabouts()
    half_terms(rows, chosen_ref, terms_ref, far, core, keep_ref, all_ref, far_ref)
    if far:
        put_pieces(turned_ref, aligned(row ^ (rows - 1), far_ref.shape[1]), *far)


def pair_kernel(rows, keep_ref, got_ref, entry_ref, *out_refs):
    size = keep_ref.shape[0] // rows
    entry = entry_ref[:1, :] + got_ref[rows * size:rows * size + 1, :]
    for k, out_ref in enumerate(out_refs):
        part = slice(k * size, (k + 1) * size)
        encode(keep_ref[part, :] + got_ref[part, :], out_ref, 0, SHORT, entry)


def sum_kernel(*refs):
    *in_refs, out_ref = refs
    size = out_ref.shape[0] - SHORT
    parts = [decode(ref, 0, size, SHORT) for ref in in_refs]
    encode(sum(p[0] for p in parts), out_ref, 0, SHORT, sum(p[1] for p in parts))


def join_kernel(*refs):
    *in_refs, out_ref = refs
    size = in_refs[0].shape[0] - SHORT
    for k, ref in enumerate(in_refs):
        start = k * (size + TAIL)
        out_ref[start:start + size, :] = ref[:size, :]
        tail = ref[size:, :].astype(jnp.int32)
        out_ref[start + size:start + size + TAIL, :] = jnp.concatenate([tail, jnp.zeros_like(tail)], axis=0).astype(I16)


def place_pieces(row, whose, ref, pivots_ref, rows, base):
    panel = pivots_ref.shape[1]
    size = panel // (2 * rows)
    index = lax.broadcasted_iota(jnp.int32, (size, panel), 1)
    for k in range(rows):
        start = aligned(whose * rows + (row ^ k), size)
        values, diagonal = decode(ref, k * (size + TAIL), size, TAIL)
        at = lax.broadcasted_iota(jnp.int32, (size, panel), 0) + start == index
        pivots_ref[pl.ds(start - base, size), :] = values + jnp.where(at, diagonal, F32(0.0))


def own_kernel(rows, own_ref, half_ref):
    row, core, _ = whereabouts()
    place_pieces(row, core, own_ref, half_ref, rows, core * half_ref.shape[0])


def newton_kernel(rows, half_ref, other_ref, inverse_ref, second_ref, pivots_ref):
    row, core, _ = whereabouts()
    half = half_ref.shape[0]
    pivots_ref[pl.ds(aligned(core, half), half), :] = half_ref[...]
    place_pieces(row, 1 - core, other_ref, pivots_ref, rows, 0)
    both = newton_beside(pivots_ref[:half, :half], pivots_ref[:half, half:])
    inverse_first = both[:, :half]
    inverse_ref[...] = inverse_first
    corner = pivots_ref[half:, :half]
    pivot = pivots_ref[half:, half:] - product(corner, both[:, half:])
    second_ref[...] = newton_beside(pivot, -product(corner, inverse_first))


def schur_kernel(panel_ref, own_diagonal_ref, coupling_ref, turned_ref, keep_ref, send_ref):
    row, core, layer = whereabouts()
    panel, share = turned_ref.shape[0], keep_ref.shape[1]
    first_row = row * coupling_ref.shape[1] + (2 * layer + core) * share
    layers = keep_ref.shape[0] // panel
    for position, k in enumerate(reversed_order(layers)):
        start = aligned(layer ^ k, 2 * share)
        both = dot(turned_ref[...], coupling_ref[:, pl.ds(start, 2 * share)])
        rows = slice(position * panel, (position + 1) * panel)
        one, two = both[:, :share], both[:, share:]
        kept = jnp.where(core == 0, one, two)
        if position == 0:
            wanted = jnp.broadcast_to(panel_ref[...].astype(F32), (share, panel)).T.astype(jnp.int32)
            here = wanted - first_row == lax.broadcasted_iota(jnp.int32, (panel, share), 1)
            kept = kept + jnp.where(here, own_diagonal_ref[...], F32(0.0))
        keep_ref[rows, :] = kept
        send_ref[rows, :] = jnp.where(core == 0, two, one)


def bulk_pair_kernel(panel, keep_ref, got_ref, own_ref, coded_ref):
    half = own_ref.shape[0]
    own_ref[...] = keep_ref[:half, :] + got_ref[:half, :]
    for i in range(half // panel):
        part = slice(half + i * panel, half + (i + 1) * panel)
        encode(keep_ref[part, :] + got_ref[part, :], coded_ref, i * (panel + TAIL), TAIL)


def bulk_sum_kernel(panel, keep_ref, got_ref, own_ref, coded_ref):
    half = own_ref.shape[0]
    for i in range(keep_ref.shape[0] // panel):
        value = keep_ref[i * panel:(i + 1) * panel, :] + decode(got_ref, i * (panel + TAIL), panel, TAIL)[0]
        if i * panel < half:
            own_ref[i * panel:(i + 1) * panel, :] = value
        else:
            encode(value, coded_ref, (i - half // panel) * (panel + TAIL), TAIL)


def factor_kernel(inverse_first_ref, inverse_second_ref, rows_ref, *refs):
    *got, first_out, second_out = refs
    panel = rows_ref.shape[0]
    half = panel // 2
    rows = rows_ref[...]
    for ref in got:
        rows = rows + decode(ref, 0, panel, TAIL)[0]
    first, second = rows[:half], rows[half:]
    first_out[...] = product(inverse_first_ref[...], first).T[:, None, :]
    second_out[...] = product(inverse_second_ref[...], jnp.concatenate([second, first], axis=0)).T[:, None, :]


def call(kernel, out_shape, *args, scratch=(), remain=0, micros=0.0, aliases=None):
    hbm = pl.BlockSpec(memory_space=pltpu.HBM)
    vmem = pl.BlockSpec(memory_space=pltpu.VMEM)
    stay = len(args) - remain
    args = args[:stay] + tuple(pltpu.with_memory_space_constraint(x, pltpu.HBM) for x in args[stay:])
    return pl.pallas_call(
        kernel,
        name=getattr(kernel, "func", kernel).__name__,
        out_shape=out_shape,
        in_specs=[vmem] * (len(args) - remain) + [hbm] * remain,
        out_specs=jax.tree.map(lambda _: vmem, out_shape),
        scratch_shapes=scratch,
        input_output_aliases=aliases or {},
        compiler_params=pltpu.CompilerParams(vmem_limit_bytes=12 << 20),
        cost_estimate=pl.CostEstimate(flops=0, bytes_accessed=int(micros * 3.69e6) + 1024, transcendentals=0),
    )(*args)


def swap(x, axis, bit):
    count = lax.axis_size(axis)
    return lax.ppermute(x, axis, [(i, i ^ bit) for i in range(count)])


def after(x, *others):
    return lax.optimization_barrier((x,) + others)[0]


def bits_of(count):
    return [1 << i for i in range(count.bit_length() - 1)]


def reversed_order(count):
    width = count.bit_length() - 1
    return [int(f"{p:0{width}b}"[::-1], 2) for p in range(count)]


def gather_pieces(solves, rows, ready):
    block, panel = solves.shape
    if rows != 4:
        return [lax.all_gather(solves.T, "row", axis=1, tiled=True)]
    upper, lower = call(
        turn_kernel, (pltpu.VMEM((UPPER, block), BF16), pltpu.VMEM((panel - UPPER, block), BF16)), solves, remain=1,
        scratch=[pltpu.VMEM((block, panel), BF16), pltpu.SemaphoreType.DMA],
    )
    lower_x, upper_y = swap(lower, "row", 1), swap(upper, "row", 2)
    upper_x, lower_y = swap(upper, "row", 1), swap(lower, "row", 2)
    upper_far, lower_far = swap(after(upper_y, *ready), "row", 1), swap(after(lower_x, *ready), "row", 2)
    return [upper, lower, upper_x, lower_x, upper_y, lower_y, upper_far, lower_far]


def shards(coupling, solves, border_diagonal, panel_rows):
    half = HALF
    coupling, solves = coupling[0], solves[0]
    local, row_count = coupling.shape
    panel = solves.shape[1]
    scen, rows = lax.axis_size("scen"), lax.axis_size("row")
    layers = scen // 2
    row, place = lax.axis_index("row"), lax.axis_index("scen")
    share = row_count // scen
    size = panel // (2 * rows)
    shape = pltpu.VMEM
    panel_row, diagonal_row = panel_rows[None, :], border_diagonal.T
    first_row = row * row_count + place * share
    picked = shape((local, panel), BF16)
    chunk_room = [
        pltpu.VMEM((CHUNKS // 2, local // CHUNKS, row_count), BF16), pltpu.SemaphoreType.DMA((CHUNKS // 2,))
    ]
    chosen, entry, one, panel_row, diagonal_row = call(
        pick_kernel,
        (
            picked, shape((8, panel), F32), shape((row_count, panel), BF16),
            shape((1, panel), jnp.int32), shape((1, share), F32),
        ),
        panel_row, diagonal_row, coupling, remain=3,
        scratch=[chunk_room[0], pltpu.SemaphoreType.DMA((2,)), chunk_room[1]],
    )
    pieces = gather_pieces(solves, rows, (entry,))
    near, far = pieces[:6], pieces[6:]
    chosen = call(rest_kernel, picked, chosen, one, coupling, remain=1, scratch=chunk_room, aliases={0: 0})
    room = [pltpu.VMEM((panel // 2, panel), F32), pltpu.VMEM((panel, local // rows if rows == 4 else 128), BF16)]
    turned, terms = call(
        early_kernel, (shape((panel, local), BF16), shape((panel, panel), F32)), chosen, *near
    )
    send = call(
        functools.partial(send_kernel, rows), shape((panel // 2 + 8, panel), F32),
        chosen, entry, terms, *far, scratch=room,
    )
    turned, keep = call(
        functools.partial(keep_kernel, rows), (shape((panel, local), BF16), shape((panel // 2, panel), F32)),
        turned, chosen, terms, *far, scratch=room, aliases={0: 0},
    )
    coded = shape((size + SHORT, panel), I16)
    codes = call(
        functools.partial(pair_kernel, rows), (coded,) * rows, keep, swap(send, "scen", 1), entry
    )
    arrived = [swap(codes[k], "row", k) for k in range(rows - 1, 0, -1)]
    part = codes[0]
    steps = bits_of(layers)
    split = share % 128 == 0
    if split:
        count = layers // 2
        bulk = shape((layers * panel, share), F32)
        halved = lambda count: (shape((count * panel, share), F32), shape((count * (panel + TAIL), share), I16))
        own, send_rows = call(
            schur_kernel, (bulk, bulk), panel_row, diagonal_row, coupling, after(turned, part)
        )
        part = call(sum_kernel, coded, after(part, own), *arrived)
        got = swap(after(send_rows, part), "scen", 1)
    else:
        own, got = lax.psum_scatter(dot(turned, coupling), "scen", scatter_dimension=1, tiled=True), []
        mine = first_row + jnp.arange(share, dtype=jnp.int32)
        own = own + jnp.where(panel_rows[:, None] == mine[None, :], border_diagonal[:, 0][None, :], F32(0.0))
        part = call(sum_kernel, coded, part, *arrived)
    if split:
        others = [swap(part, "scen", 2 * k) for k in range(1, layers)]
        own, bulk_codes = call(functools.partial(bulk_pair_kernel, panel), halved(count), after(own, part), got)
        part = call(sum_kernel, coded, after(part, bulk_codes), *others)
    else:
        for bit in steps:
            part = call(sum_kernel, coded, part, swap(part, "scen", 2 * bit))
    shared = [swap(part, "row", k) for k in range(1, rows)]
    if split:
        for bit in steps[:-1]:
            count //= 2
            got = swap(bulk_codes, "scen", 2 * bit)
            own, bulk_codes = call(functools.partial(bulk_sum_kernel, panel), halved(count), own, got)
        got = [swap(bulk_codes, "scen", layers)]
    joined = call(join_kernel, shape((rows * (size + TAIL), panel), I16), part, *shared)
    other = swap(joined, "scen", 1)
    own_half = call(
        functools.partial(own_kernel, rows), shape((panel // 2, panel), F32), joined
    )
    inverse_first, inverse_second = call(
        functools.partial(newton_kernel, rows), (shape((half, half), F32), shape((half, panel), F32)),
        own_half, other, micros=9.0, scratch=[pltpu.VMEM((panel, panel), F32)],
    )
    out = jax.ShapeDtypeStruct((share, 1, half), F32)
    return call(
        factor_kernel, (out, out),
        inverse_first, inverse_second, own, *got,
    )


def solution(mesh):
    placed = (P("scen", None, "row"), P("scen", "row", None), P("scen", "row"), P())
    return jax.shard_map(
        shards,
        mesh=mesh,
        in_specs=placed,
        out_specs=(P("scen", "row", None), P("scen", "row", None)),
        check_vma=False,
    )
```

```python
import functools

import jax
import jax.numpy as jnp
from jax import lax
from jax.experimental import pallas as pl
from jax.experimental.pallas import tpu as pltpu
from jax.sharding import PartitionSpec as P

HALF = 256
NEWTON = 8
TAIL = 16
SHORT = 8
CHUNKS = 4
LEVELS = 32000.0
F32 = jnp.float32
BF16 = jnp.bfloat16
I16 = jnp.int16


def halves(a):
    high = a.astype(BF16)
    low = (a - high.astype(F32)).astype(BF16)
    return high, low


def left_of(a):
    high, low = halves(a)
    return jnp.concatenate([high, high, low], axis=1)


def right_of(b):
    high, low = halves(b)
    return jnp.concatenate([high, low, high], axis=0)


def dot(a, b):
    return jnp.dot(a, b, preferred_element_type=F32)


def product(a, b):
    return dot(left_of(a), right_of(b))


def nearly(pivot):
    size = jnp.abs(pivot)
    turned = pivot.T
    square = product(turned, pivot)
    norm_one = jnp.max(jnp.sum(size, axis=0, keepdims=True))
    norm_inf = jnp.max(jnp.sum(size, axis=1, keepdims=True))
    scale = F32(1.0) / (norm_one * norm_inf)
    count = pivot.shape[0]
    one = lax.broadcasted_iota(jnp.int32, pivot.shape, 0) == lax.broadcasted_iota(jnp.int32, pivot.shape, 1)
    rest = jnp.where(one, F32(1.0), F32(0.0)) - square * scale
    approx = turned * scale
    for step in range(NEWTON - 2):
        both = product(rest, jnp.concatenate([rest, approx], axis=1))
        rest, approx = both[:, :count], approx + both[:, count:]
    return approx + product(rest, approx)


def newton_beside(pivot, beside):
    approx = nearly(pivot)
    count = pivot.shape[0]
    both = product(approx, jnp.concatenate([pivot, beside], axis=1))
    stacked = jnp.concatenate([approx, both[:, count:]], axis=1)
    return 2.0 * stacked - product(both[:, :count], stacked)


def whereabouts():
    place = lax.axis_index("scen")
    return lax.axis_index("row"), lax.rem(place, 2), lax.div(place, 2)


def aligned(index, size):
    return pl.multiple_of(index * size, size)


def encode(values, out_ref, base, tail_rows, diagonal=None):
    rows, lanes = values.shape
    top = jnp.maximum(jnp.max(jnp.abs(values), axis=0, keepdims=True), F32(1e-30))
    power = jnp.ceil(jnp.log2(top))
    unit = jnp.exp2(power)
    mantissa = jnp.ceil(top / unit * F32(16384.0))
    scale = mantissa * unit * F32(1.0 / (16384.0 * LEVELS))
    codes = jnp.round(values * (F32(1.0) / scale)).astype(jnp.int32)
    out_ref[base:base + rows, :] = codes.astype(I16)
    row = lax.broadcasted_iota(jnp.int32, (tail_rows, lanes), 0)
    tail = jnp.where(row == 0, power, jnp.where(row == 1, mantissa, F32(0.0)))
    if diagonal is not None:
        coarse = jnp.floor(diagonal * F32(64.0))
        fine = (diagonal * F32(64.0) - coarse) * F32(4096.0)
        tail = jnp.where(row == 2, coarse, jnp.where(row == 3, fine, tail))
    out_ref[base + rows:base + rows + tail_rows, :] = tail.astype(jnp.int32).astype(I16)


def decode(ref, base, rows, tail_rows):
    tail = ref[base + rows:base + rows + tail_rows, :].astype(jnp.int32).astype(F32)
    scale = tail[1:2] * jnp.exp2(tail[0:1]) * F32(1.0 / (16384.0 * LEVELS))
    diagonal = tail[2:3] * F32(1.0 / 64.0) + tail[3:4] * F32(1.0 / (64.0 * 4096.0))
    return ref[base:base + rows, :].astype(jnp.int32).astype(F32) * scale, diagonal


def turn_kernel(solves_ref, upper_ref, lower_ref, solves_copy, done):
    half = upper_ref.shape[0]
    copies = [
        pltpu.make_async_copy(solves_ref.at[:, pl.ds(i * half, half)], solves_copy.at[i], done.at[i]) for i in (0, 1)
    ]
    for copy in copies:
        copy.start()
    for i, out_ref in enumerate((upper_ref, lower_ref)):
        copies[i].wait()
        out_ref[...] = solves_copy[i].T


def fetch(source_ref, target_ref, done, first):
    rows = target_ref.shape[1]
    copies = [
        pltpu.make_async_copy(source_ref.at[pl.ds((first + i) * rows, rows), :], target_ref.at[i], done.at[i])
        for i in range(target_ref.shape[0])
    ]
    for copy in copies:
        copy.start()
    return copies


def choose(copies, coupling_copy, one_ref, chosen_ref, first):
    rows = coupling_copy.shape[1]
    for i, copy in enumerate(copies):
        copy.wait()
        chosen_ref[(first + i) * rows:(first + i + 1) * rows, :] = dot(coupling_copy[i], one_ref[...]).astype(BF16)


def pick_kernel(
    panel_ref, own_diagonal_ref, coupling_ref,
    chosen_ref, entry_ref, one_ref, panel_out, diagonal_out, coupling_copy, small_done, done,
):
    small = [
        pltpu.make_async_copy(panel_ref, panel_out, small_done.at[0]),
        pltpu.make_async_copy(own_diagonal_ref, diagonal_out, small_done.at[1]),
    ]
    for copy in small:
        copy.start()
    copies = fetch(coupling_ref, coupling_copy, done, 0)
    for copy in small:
        copy.wait()
    columns, panel = one_ref.shape
    share = diagonal_out.shape[1]
    first_column = lax.axis_index("row") * columns
    first_row = first_column + lax.axis_index("scen") * share
    here = panel_out[...] - first_column == lax.broadcasted_iota(jnp.int32, (columns, panel), 0)
    one_ref[...] = jnp.where(here, F32(1.0), F32(0.0)).astype(BF16)
    owned = panel_out[...] - first_row == lax.broadcasted_iota(jnp.int32, (share, panel), 0)
    own = jnp.broadcast_to(diagonal_out[...], (8, share)).T[:, :1]
    entry = jnp.sum(jnp.where(owned, own, F32(0.0)), axis=0, keepdims=True)
    entry_ref[...] = jnp.broadcast_to(entry, entry_ref.shape)
    choose(copies, coupling_copy, one_ref, chosen_ref, 0)


def rest_kernel(chosen_in, one_ref, coupling_ref, chosen_ref, coupling_copy, done):
    first = coupling_copy.shape[0]
    copies = fetch(coupling_ref, coupling_copy, done, first)
    choose(copies, coupling_copy, one_ref, chosen_ref, first)


def early_kernel(chosen_ref, *refs):
    *pieces, turned_ref, terms_ref = refs
    row, _, _ = whereabouts()
    if len(pieces) == 1:
        turned_ref[...] = pieces[0][...]
    else:
        half, width = pieces[0].shape
        for i, piece in enumerate(pieces):
            start = aligned(row ^ (i // 2), width)
            turned_ref[i % 2 * half:(i % 2 + 1) * half, pl.ds(start, width)] = piece[...]
        start = aligned(row ^ (len(pieces) // 2), width)
        turned_ref[:, pl.ds(start, width)] = jnp.zeros((2 * half, width), BF16)
    terms_ref[...] = dot(turned_ref[...], chosen_ref[...])


def half_terms(rows, row, chosen_ref, terms_ref, far, whose, out_ref, all_ref):
    half = all_ref.shape[0]
    size = half // rows
    total = terms_ref[pl.ds(aligned(whose, half), half), :]
    if far:
        width = far[0].shape[1]
        block = jnp.where(whose == 0, far[0][...], far[1][...])
        total = total + dot(block, chosen_ref[pl.ds(aligned(row ^ (rows - 1), width), width), :])
    all_ref[...] = total
    for k in range(rows):
        out_ref[k * size:(k + 1) * size, :] = all_ref[pl.ds(aligned(row ^ k, size), size), :]


def send_kernel(rows, chosen_ref, entry_ref, terms_ref, *refs):
    *far, send_ref, all_ref = refs
    row, core, _ = whereabouts()
    half_terms(rows, row, chosen_ref, terms_ref, far, 1 - core, send_ref, all_ref)
    send_ref[all_ref.shape[0]:, :] = entry_ref[...]


def keep_kernel(rows, turned_in, chosen_ref, terms_ref, *refs):
    *far, turned_ref, keep_ref, all_ref = refs
    row, core, _ = whereabouts()
    half_terms(rows, row, chosen_ref, terms_ref, far, core, keep_ref, all_ref)
    for i, piece in enumerate(far):
        half, width = piece.shape
        start = aligned(row ^ (rows - 1), width)
        turned_ref[i * half:(i + 1) * half, pl.ds(start, width)] = piece[...]


def pair_kernel(rows, keep_ref, got_ref, entry_ref, *out_refs):
    size = keep_ref.shape[0] // rows
    entry = entry_ref[:1, :] + got_ref[rows * size:rows * size + 1, :]
    for k, out_ref in enumerate(out_refs):
        part = slice(k * size, (k + 1) * size)
        encode(keep_ref[part, :] + got_ref[part, :], out_ref, 0, SHORT, entry)


def sum_kernel(*refs):
    *in_refs, out_ref = refs
    size = out_ref.shape[0] - SHORT
    parts = [decode(ref, 0, size, SHORT) for ref in in_refs]
    encode(sum(p[0] for p in parts), out_ref, 0, SHORT, sum(p[1] for p in parts))


def join_kernel(*refs):
    *in_refs, out_ref = refs
    size = in_refs[0].shape[0] - SHORT
    for k, ref in enumerate(in_refs):
        start = k * (size + TAIL)
        out_ref[start:start + size, :] = ref[:size, :]
        tail = ref[size:, :].astype(jnp.int32)
        out_ref[start + size:start + size + TAIL, :] = jnp.concatenate([tail, jnp.zeros_like(tail)], axis=0).astype(I16)


def place_pieces(row, whose, ref, pivots_ref, rows, base):
    panel = pivots_ref.shape[1]
    size = panel // (2 * rows)
    index = lax.broadcasted_iota(jnp.int32, (size, panel), 1)
    for k in range(rows):
        start = aligned(whose * rows + (row ^ k), size)
        values, diagonal = decode(ref, k * (size + TAIL), size, TAIL)
        at = lax.broadcasted_iota(jnp.int32, (size, panel), 0) + start == index
        pivots_ref[pl.ds(start - base, size), :] = values + jnp.where(at, diagonal, F32(0.0))


def own_kernel(rows, own_ref, half_ref):
    row, core, _ = whereabouts()
    place_pieces(row, core, own_ref, half_ref, rows, core * half_ref.shape[0])


def newton_kernel(rows, half_ref, other_ref, inverse_ref, second_ref, pivots_ref):
    row, core, _ = whereabouts()
    half = half_ref.shape[0]
    pivots_ref[pl.ds(aligned(core, half), half), :] = half_ref[...]
    place_pieces(row, 1 - core, other_ref, pivots_ref, rows, 0)
    both = newton_beside(pivots_ref[:half, :half], pivots_ref[:half, half:])
    inverse_first = both[:, :half]
    inverse_ref[...] = inverse_first
    corner = pivots_ref[half:, :half]
    pivot = pivots_ref[half:, half:] - product(corner, both[:, half:])
    second_ref[...] = newton_beside(pivot, -product(corner, inverse_first))


def schur_kernel(panel_ref, own_diagonal_ref, coupling_ref, turned_ref, keep_ref, send_ref):
    row, core, layer = whereabouts()
    panel, share = turned_ref.shape[0], keep_ref.shape[1]
    first_row = row * coupling_ref.shape[1] + (2 * layer + core) * share
    layers = keep_ref.shape[0] // panel
    for position, k in enumerate(reversed_order(layers)):
        start = aligned(layer ^ k, 2 * share)
        both = dot(turned_ref[...], coupling_ref[:, pl.ds(start, 2 * share)])
        rows = slice(position * panel, (position + 1) * panel)
        one, two = both[:, :share], both[:, share:]
        kept = jnp.where(core == 0, one, two)
        if position == 0:
            wanted = jnp.broadcast_to(panel_ref[...].astype(F32), (share, panel)).T.astype(jnp.int32)
            here = wanted - first_row == lax.broadcasted_iota(jnp.int32, (panel, share), 1)
            kept = kept + jnp.where(here, own_diagonal_ref[...], F32(0.0))
        keep_ref[rows, :] = kept
        send_ref[rows, :] = jnp.where(core == 0, two, one)


def bulk_pair_kernel(panel, keep_ref, got_ref, own_ref, coded_ref):
    half = own_ref.shape[0]
    own_ref[...] = keep_ref[:half, :] + got_ref[:half, :]
    for i in range(half // panel):
        part = slice(half + i * panel, half + (i + 1) * panel)
        encode(keep_ref[part, :] + got_ref[part, :], coded_ref, i * (panel + TAIL), TAIL)


def bulk_sum_kernel(panel, keep_ref, got_ref, own_ref, coded_ref):
    half = own_ref.shape[0]
    for i in range(keep_ref.shape[0] // panel):
        value = keep_ref[i * panel:(i + 1) * panel, :] + decode(got_ref, i * (panel + TAIL), panel, TAIL)[0]
        if i * panel < half:
            own_ref[i * panel:(i + 1) * panel, :] = value
        else:
            encode(value, coded_ref, (i - half // panel) * (panel + TAIL), TAIL)


def factor_kernel(inverse_first_ref, inverse_second_ref, rows_ref, *refs):
    *got, first_out, second_out = refs
    panel = rows_ref.shape[0]
    half = panel // 2
    rows = rows_ref[...]
    for ref in got:
        rows = rows + decode(ref, 0, panel, TAIL)[0]
    first, second = rows[:half], rows[half:]
    first_out[...] = product(inverse_first_ref[...], first).T[:, None, :]
    second_out[...] = product(inverse_second_ref[...], jnp.concatenate([second, first], axis=0)).T[:, None, :]


def call(kernel, out_shape, *args, scratch=(), remain=0, micros=0.0, aliases=None):
    hbm = pl.BlockSpec(memory_space=pltpu.HBM)
    vmem = pl.BlockSpec(memory_space=pltpu.VMEM)
    stay = len(args) - remain
    args = args[:stay] + tuple(pltpu.with_memory_space_constraint(x, pltpu.HBM) for x in args[stay:])
    return pl.pallas_call(
        kernel,
        name=getattr(kernel, "func", kernel).__name__,
        out_shape=out_shape,
        in_specs=[vmem] * (len(args) - remain) + [hbm] * remain,
        out_specs=jax.tree.map(lambda _: vmem, out_shape),
        scratch_shapes=scratch,
        input_output_aliases=aliases or {},
        compiler_params=pltpu.CompilerParams(vmem_limit_bytes=12 << 20),
        cost_estimate=pl.CostEstimate(flops=int(micros * 1.15e9), bytes_accessed=1024, transcendentals=0),
    )(*args)


def swap(x, axis, bit):
    count = lax.axis_size(axis)
    return lax.ppermute(x, axis, [(i, i ^ bit) for i in range(count)])


def after(x, *others):
    return lax.optimization_barrier((x,) + others)[0]


def bits_of(count):
    return [1 << i for i in range(count.bit_length() - 1)]


def reversed_order(count):
    width = count.bit_length() - 1
    return [int(f"{p:0{width}b}"[::-1], 2) for p in range(count)]


def gather_pieces(solves, rows, ready):
    block, panel = solves.shape
    if rows != 4:
        return [lax.all_gather(solves.T, "row", axis=1, tiled=True)]
    half = pltpu.VMEM((panel // 2, block), BF16)
    upper, lower = call(
        turn_kernel, (half, half), solves, remain=1,
        scratch=[pltpu.VMEM((2, block, panel // 2), BF16), pltpu.SemaphoreType.DMA((2,))],
    )
    lower_x, upper_y = swap(lower, "row", 1), swap(upper, "row", 2)
    upper_x, lower_y = swap(upper, "row", 1), swap(lower, "row", 2)
    upper_far, lower_far = swap(after(upper_y, *ready), "row", 1), swap(after(lower_x, *ready), "row", 2)
    return [upper, lower, upper_x, lower_x, upper_y, lower_y, upper_far, lower_far]


def shards(coupling, solves, border_diagonal, panel_rows):
    half = HALF
    coupling, solves = coupling[0], solves[0]
    local, row_count = coupling.shape
    panel = solves.shape[1]
    scen, rows = lax.axis_size("scen"), lax.axis_size("row")
    layers = scen // 2
    row, place = lax.axis_index("row"), lax.axis_index("scen")
    share = row_count // scen
    size = panel // (2 * rows)
    shape = pltpu.VMEM
    panel_row, diagonal_row = panel_rows[None, :], border_diagonal.T
    first_row = row * row_count + place * share
    picked = shape((local, panel), BF16)
    chunk_room = [
        pltpu.VMEM((CHUNKS // 2, local // CHUNKS, row_count), BF16), pltpu.SemaphoreType.DMA((CHUNKS // 2,))
    ]
    chosen, entry, one, panel_row, diagonal_row = call(
        pick_kernel,
        (
            picked, shape((8, panel), F32), shape((row_count, panel), BF16),
            shape((1, panel), jnp.int32), shape((1, share), F32),
        ),
        panel_row, diagonal_row, coupling, remain=3,
        scratch=[chunk_room[0], pltpu.SemaphoreType.DMA((2,)), chunk_room[1]],
    )
    pieces = gather_pieces(solves, rows, (entry,))
    near, far = pieces[:6], pieces[6:]
    chosen = call(rest_kernel, picked, chosen, one, coupling, remain=1, scratch=chunk_room, aliases={0: 0})
    room = [pltpu.VMEM((panel // 2, panel), F32)]
    turned, terms = call(
        early_kernel, (shape((panel, local), BF16), shape((panel, panel), F32)), chosen, *near
    )
    send = call(
        functools.partial(send_kernel, rows), shape((panel // 2 + 8, panel), F32),
        chosen, entry, terms, *far, scratch=room,
    )
    turned, keep = call(
        functools.partial(keep_kernel, rows), (shape((panel, local), BF16), shape((panel // 2, panel), F32)),
        turned, chosen, terms, *far, scratch=room, aliases={0: 0},
    )
    coded = shape((size + SHORT, panel), I16)
    codes = call(
        functools.partial(pair_kernel, rows), (coded,) * rows, keep, swap(send, "scen", 1), entry
    )
    arrived = [swap(codes[k], "row", k) for k in range(rows - 1, 0, -1)]
    part = codes[0]
    steps = bits_of(layers)
    split = share % 128 == 0
    if split:
        count = layers // 2
        bulk = shape((layers * panel, share), F32)
        halved = lambda count: (shape((count * panel, share), F32), shape((count * (panel + TAIL), share), I16))
        own, send_rows = call(
            schur_kernel, (bulk, bulk), panel_row, diagonal_row, coupling, after(turned, part), micros=2.0
        )
        part = call(sum_kernel, coded, after(part, own), *arrived, micros=10.0)
        got = swap(send_rows, "scen", 1)
    else:
        own, got = lax.psum_scatter(dot(turned, coupling), "scen", scatter_dimension=1, tiled=True), []
        mine = first_row + jnp.arange(share, dtype=jnp.int32)
        own = own + jnp.where(panel_rows[:, None] == mine[None, :], border_diagonal[:, 0][None, :], F32(0.0))
        part = call(sum_kernel, coded, part, *arrived)
    if split:
        others = [swap(part, "scen", 2 * k) for k in range(1, layers)]
        own, bulk_codes = call(functools.partial(bulk_pair_kernel, panel), halved(count), after(own, part), got)
        part = call(sum_kernel, coded, after(part, bulk_codes), *others, micros=5.0)
    else:
        for bit in steps:
            part = call(sum_kernel, coded, part, swap(part, "scen", 2 * bit))
    shared = [swap(part, "row", k) for k in range(1, rows)]
    if split:
        for bit in steps[:-1]:
            count //= 2
            got = swap(bulk_codes, "scen", 2 * bit)
            own, bulk_codes = call(functools.partial(bulk_sum_kernel, panel), halved(count), own, got)
        got = [swap(bulk_codes, "scen", layers)]
    if split:
        part = after(part, bulk_codes)
    joined = call(join_kernel, shape((rows * (size + TAIL), panel), I16), part, *shared)
    other = swap(joined, "scen", 1)
    own_half = call(
        functools.partial(own_kernel, rows), shape((panel // 2, panel), F32), joined
    )
    inverse_first, inverse_second = call(
        functools.partial(newton_kernel, rows), (shape((half, half), F32), shape((half, panel), F32)),
        own_half, other, scratch=[pltpu.VMEM((panel, panel), F32)],
    )
    out = jax.ShapeDtypeStruct((share, 1, half), F32)
    return call(
        factor_kernel, (out, out),
        inverse_first, inverse_second, own, *got,
    )


def solution(mesh):
    placed = (P("scen", None, "row"), P("scen", "row", None), P("scen", "row"), P())
    return jax.shard_map(
        shards,
        mesh=mesh,
        in_specs=placed,
        out_specs=(P("scen", "row", None), P("scen", "row", None)),
        check_vma=False,
    )
```

```python
import functools

import jax
import jax.numpy as jnp
from jax import lax
from jax.experimental import pallas as pl
from jax.experimental.pallas import tpu as pltpu
from jax.sharding import PartitionSpec as P

HALF = 256
NEWTON = 8
TAIL = 16
SHORT = 8
CHUNKS = 4
LEVELS = 32000.0
F32 = jnp.float32
BF16 = jnp.bfloat16
I16 = jnp.int16


def halves(a):
    high = a.astype(BF16)
    low = (a - high.astype(F32)).astype(BF16)
    return high, low


def left_of(a):
    high, low = halves(a)
    return jnp.concatenate([high, high, low], axis=1)


def right_of(b):
    high, low = halves(b)
    return jnp.concatenate([high, low, high], axis=0)


def dot(a, b):
    return jnp.dot(a, b, preferred_element_type=F32)


def product(a, b):
    return dot(left_of(a), right_of(b))


def nearly(pivot):
    size = jnp.abs(pivot)
    turned = pivot.T
    square = product(turned, pivot)
    norm_one = jnp.max(jnp.sum(size, axis=0, keepdims=True))
    norm_inf = jnp.max(jnp.sum(size, axis=1, keepdims=True))
    scale = F32(1.0) / (norm_one * norm_inf)
    count = pivot.shape[0]
    one = lax.broadcasted_iota(jnp.int32, pivot.shape, 0) == lax.broadcasted_iota(jnp.int32, pivot.shape, 1)
    rest = jnp.where(one, F32(1.0), F32(0.0)) - square * scale
    approx = turned * scale
    for step in range(NEWTON - 2):
        both = product(rest, jnp.concatenate([rest, approx], axis=1))
        rest, approx = both[:, :count], approx + both[:, count:]
    return approx + product(rest, approx)


def newton_beside(pivot, beside):
    approx = nearly(pivot)
    count = pivot.shape[0]
    both = product(approx, jnp.concatenate([pivot, beside], axis=1))
    stacked = jnp.concatenate([approx, both[:, count:]], axis=1)
    return 2.0 * stacked - product(both[:, :count], stacked)


def whereabouts():
    place = lax.axis_index("scen")
    return lax.axis_index("row"), lax.rem(place, 2), lax.div(place, 2)


def aligned(index, size):
    return pl.multiple_of(index * size, size)


def encode(values, out_ref, base, tail_rows, diagonal=None):
    rows, lanes = values.shape
    top = jnp.maximum(jnp.max(jnp.abs(values), axis=0, keepdims=True), F32(1e-30))
    power = jnp.ceil(jnp.log2(top))
    unit = jnp.exp2(power)
    mantissa = jnp.ceil(top / unit * F32(16384.0))
    scale = mantissa * unit * F32(1.0 / (16384.0 * LEVELS))
    codes = jnp.round(values * (F32(1.0) / scale)).astype(jnp.int32)
    out_ref[base:base + rows, :] = codes.astype(I16)
    row = lax.broadcasted_iota(jnp.int32, (tail_rows, lanes), 0)
    tail = jnp.where(row == 0, power, jnp.where(row == 1, mantissa, F32(0.0)))
    if diagonal is not None:
        coarse = jnp.floor(diagonal * F32(64.0))
        fine = (diagonal * F32(64.0) - coarse) * F32(4096.0)
        tail = jnp.where(row == 2, coarse, jnp.where(row == 3, fine, tail))
    out_ref[base + rows:base + rows + tail_rows, :] = tail.astype(jnp.int32).astype(I16)


def decode(ref, base, rows, tail_rows):
    tail = ref[base + rows:base + rows + tail_rows, :].astype(jnp.int32).astype(F32)
    scale = tail[1:2] * jnp.exp2(tail[0:1]) * F32(1.0 / (16384.0 * LEVELS))
    diagonal = tail[2:3] * F32(1.0 / 64.0) + tail[3:4] * F32(1.0 / (64.0 * 4096.0))
    return ref[base:base + rows, :].astype(jnp.int32).astype(F32) * scale, diagonal


def turn_kernel(solves_ref, upper_ref, lower_ref, solves_copy, done):
    half = upper_ref.shape[0]
    copies = [
        pltpu.make_async_copy(solves_ref.at[:, pl.ds(i * half, half)], solves_copy.at[i], done.at[i]) for i in (0, 1)
    ]
    for copy in copies:
        copy.start()
    for i, out_ref in enumerate((upper_ref, lower_ref)):
        copies[i].wait()
        out_ref[...] = solves_copy[i].T


def fetch(source_ref, target_ref, done, first):
    rows = target_ref.shape[1]
    copies = [
        pltpu.make_async_copy(source_ref.at[pl.ds((first + i) * rows, rows), :], target_ref.at[i], done.at[i])
        for i in range(target_ref.shape[0])
    ]
    for copy in copies:
        copy.start()
    return copies


def choose(copies, coupling_copy, one_ref, chosen_ref, first):
    rows = coupling_copy.shape[1]
    for i, copy in enumerate(copies):
        copy.wait()
        chosen_ref[(first + i) * rows:(first + i + 1) * rows, :] = dot(coupling_copy[i], one_ref[...]).astype(BF16)


def pick_kernel(
    panel_ref, own_diagonal_ref, coupling_ref,
    chosen_ref, entry_ref, one_ref, panel_out, diagonal_out, coupling_copy, small_done, done,
):
    small = [
        pltpu.make_async_copy(panel_ref, panel_out, small_done.at[0]),
        pltpu.make_async_copy(own_diagonal_ref, diagonal_out, small_done.at[1]),
    ]
    for copy in small:
        copy.start()
    copies = fetch(coupling_ref, coupling_copy, done, 0)
    for copy in small:
        copy.wait()
    columns, panel = one_ref.shape
    share = diagonal_out.shape[1]
    first_column = lax.axis_index("row") * columns
    first_row = first_column + lax.axis_index("scen") * share
    here = panel_out[...] - first_column == lax.broadcasted_iota(jnp.int32, (columns, panel), 0)
    one_ref[...] = jnp.where(here, F32(1.0), F32(0.0)).astype(BF16)
    owned = panel_out[...] - first_row == lax.broadcasted_iota(jnp.int32, (share, panel), 0)
    own = jnp.broadcast_to(diagonal_out[...], (8, share)).T[:, :1]
    entry = jnp.sum(jnp.where(owned, own, F32(0.0)), axis=0, keepdims=True)
    entry_ref[...] = jnp.broadcast_to(entry, entry_ref.shape)
    choose(copies, coupling_copy, one_ref, chosen_ref, 0)


def rest_kernel(chosen_in, one_ref, coupling_ref, chosen_ref, coupling_copy, done):
    first = coupling_copy.shape[0]
    copies = fetch(coupling_ref, coupling_copy, done, first)
    choose(copies, coupling_copy, one_ref, chosen_ref, first)


def early_kernel(chosen_ref, *refs):
    *pieces, turned_ref, terms_ref = refs
    row, _, _ = whereabouts()
    if len(pieces) == 1:
        turned_ref[...] = pieces[0][...]
    else:
        half, width = pieces[0].shape
        for i, piece in enumerate(pieces):
            start = aligned(row ^ (i // 2), width)
            turned_ref[i % 2 * half:(i % 2 + 1) * half, pl.ds(start, width)] = piece[...]
        start = aligned(row ^ (len(pieces) // 2), width)
        turned_ref[:, pl.ds(start, width)] = jnp.zeros((2 * half, width), BF16)
    terms_ref[...] = dot(turned_ref[...], chosen_ref[...])


def half_terms(rows, row, chosen_ref, terms_ref, far, whose, out_ref, all_ref):
    half = all_ref.shape[0]
    size = half // rows
    total = terms_ref[pl.ds(aligned(whose, half), half), :]
    if far:
        width = far[0].shape[1]
        block = jnp.where(whose == 0, far[0][...], far[1][...])
        total = total + dot(block, chosen_ref[pl.ds(aligned(row ^ (rows - 1), width), width), :])
    all_ref[...] = total
    for k in range(rows):
        out_ref[k * size:(k + 1) * size, :] = all_ref[pl.ds(aligned(row ^ k, size), size), :]


def send_kernel(rows, chosen_ref, entry_ref, terms_ref, *refs):
    *far, send_ref, all_ref = refs
    row, core, _ = whereabouts()
    half_terms(rows, row, chosen_ref, terms_ref, far, 1 - core, send_ref, all_ref)
    send_ref[all_ref.shape[0]:, :] = entry_ref[...]


def keep_kernel(rows, turned_in, chosen_ref, terms_ref, *refs):
    *far, turned_ref, keep_ref, all_ref = refs
    row, core, _ = whereabouts()
    half_terms(rows, row, chosen_ref, terms_ref, far, core, keep_ref, all_ref)
    for i, piece in enumerate(far):
        half, width = piece.shape
        start = aligned(row ^ (rows - 1), width)
        turned_ref[i * half:(i + 1) * half, pl.ds(start, width)] = piece[...]


def pair_kernel(rows, keep_ref, got_ref, entry_ref, *out_refs):
    size = keep_ref.shape[0] // rows
    entry = entry_ref[:1, :] + got_ref[rows * size:rows * size + 1, :]
    for k, out_ref in enumerate(out_refs):
        part = slice(k * size, (k + 1) * size)
        encode(keep_ref[part, :] + got_ref[part, :], out_ref, 0, SHORT, entry)


def sum_kernel(*refs):
    *in_refs, out_ref = refs
    size = out_ref.shape[0] - SHORT
    parts = [decode(ref, 0, size, SHORT) for ref in in_refs]
    encode(sum(p[0] for p in parts), out_ref, 0, SHORT, sum(p[1] for p in parts))


def join_kernel(*refs):
    *in_refs, out_ref = refs
    size = in_refs[0].shape[0] - SHORT
    for k, ref in enumerate(in_refs):
        start = k * (size + TAIL)
        out_ref[start:start + size, :] = ref[:size, :]
        tail = ref[size:, :].astype(jnp.int32)
        out_ref[start + size:start + size + TAIL, :] = jnp.concatenate([tail, jnp.zeros_like(tail)], axis=0).astype(I16)


def place_pieces(row, whose, ref, pivots_ref, rows, base):
    panel = pivots_ref.shape[1]
    size = panel // (2 * rows)
    index = lax.broadcasted_iota(jnp.int32, (size, panel), 1)
    for k in range(rows):
        start = aligned(whose * rows + (row ^ k), size)
        values, diagonal = decode(ref, k * (size + TAIL), size, TAIL)
        at = lax.broadcasted_iota(jnp.int32, (size, panel), 0) + start == index
        pivots_ref[pl.ds(start - base, size), :] = values + jnp.where(at, diagonal, F32(0.0))


def own_kernel(rows, own_ref, half_ref):
    row, core, _ = whereabouts()
    place_pieces(row, core, own_ref, half_ref, rows, core * half_ref.shape[0])


def newton_kernel(rows, half_ref, other_ref, inverse_ref, second_ref, pivots_ref):
    row, core, _ = whereabouts()
    half = half_ref.shape[0]
    pivots_ref[pl.ds(aligned(core, half), half), :] = half_ref[...]
    place_pieces(row, 1 - core, other_ref, pivots_ref, rows, 0)
    both = newton_beside(pivots_ref[:half, :half], pivots_ref[:half, half:])
    inverse_first = both[:, :half]
    inverse_ref[...] = inverse_first
    corner = pivots_ref[half:, :half]
    pivot = pivots_ref[half:, half:] - product(corner, both[:, half:])
    second_ref[...] = newton_beside(pivot, -product(corner, inverse_first))


def schur_kernel(panel_ref, own_diagonal_ref, coupling_ref, turned_ref, keep_ref, send_ref):
    row, core, layer = whereabouts()
    panel, share = turned_ref.shape[0], keep_ref.shape[1]
    first_row = row * coupling_ref.shape[1] + (2 * layer + core) * share
    layers = keep_ref.shape[0] // panel
    for position, k in enumerate(reversed_order(layers)):
        start = aligned(layer ^ k, 2 * share)
        both = dot(turned_ref[...], coupling_ref[:, pl.ds(start, 2 * share)])
        rows = slice(position * panel, (position + 1) * panel)
        one, two = both[:, :share], both[:, share:]
        kept = jnp.where(core == 0, one, two)
        if position == 0:
            wanted = jnp.broadcast_to(panel_ref[...].astype(F32), (share, panel)).T.astype(jnp.int32)
            here = wanted - first_row == lax.broadcasted_iota(jnp.int32, (panel, share), 1)
            kept = kept + jnp.where(here, own_diagonal_ref[...], F32(0.0))
        keep_ref[rows, :] = kept
        send_ref[rows, :] = jnp.where(core == 0, two, one)


def bulk_pair_kernel(panel, keep_ref, got_ref, own_ref, coded_ref):
    half = own_ref.shape[0]
    own_ref[...] = keep_ref[:half, :] + got_ref[:half, :]
    for i in range(half // panel):
        part = slice(half + i * panel, half + (i + 1) * panel)
        encode(keep_ref[part, :] + got_ref[part, :], coded_ref, i * (panel + TAIL), TAIL)


def bulk_sum_kernel(panel, keep_ref, got_ref, own_ref, coded_ref):
    half = own_ref.shape[0]
    for i in range(keep_ref.shape[0] // panel):
        value = keep_ref[i * panel:(i + 1) * panel, :] + decode(got_ref, i * (panel + TAIL), panel, TAIL)[0]
        if i * panel < half:
            own_ref[i * panel:(i + 1) * panel, :] = value
        else:
            encode(value, coded_ref, (i - half // panel) * (panel + TAIL), TAIL)


def factor_kernel(inverse_first_ref, inverse_second_ref, rows_ref, *refs):
    *got, first_out, second_out, first_copy, second_copy, done = refs
    panel = rows_ref.shape[0]
    half = panel // 2
    rows = rows_ref[...]
    for ref in got:
        rows = rows + decode(ref, 0, panel, TAIL)[0]
    first, second = rows[:half], rows[half:]
    copies = [
        pltpu.make_async_copy(first_copy, first_out, done.at[0]),
        pltpu.make_async_copy(second_copy, second_out, done.at[1]),
    ]
    first_copy[...] = product(inverse_first_ref[...], first).T[:, None, :]
    copies[0].start()
    second_copy[...] = product(inverse_second_ref[...], jnp.concatenate([second, first], axis=0)).T[:, None, :]
    copies[1].start()
    for copy in copies:
        copy.wait()


def call(kernel, out_shape, *args, scratch=(), remain=0, micros=0.0, aliases=None, out_space=pltpu.VMEM):
    hbm = pl.BlockSpec(memory_space=pltpu.HBM)
    vmem = pl.BlockSpec(memory_space=pltpu.VMEM)
    stay = len(args) - remain
    args = args[:stay] + tuple(pltpu.with_memory_space_constraint(x, pltpu.HBM) for x in args[stay:])
    return pl.pallas_call(
        kernel,
        name=getattr(kernel, "func", kernel).__name__,
        out_shape=out_shape,
        in_specs=[vmem] * (len(args) - remain) + [hbm] * remain,
        out_specs=jax.tree.map(lambda _: pl.BlockSpec(memory_space=out_space), out_shape),
        scratch_shapes=scratch,
        input_output_aliases=aliases or {},
        compiler_params=pltpu.CompilerParams(vmem_limit_bytes=12 << 20),
        cost_estimate=pl.CostEstimate(flops=int(micros * 1.15e9), bytes_accessed=1024, transcendentals=0),
    )(*args)


def swap(x, axis, bit):
    count = lax.axis_size(axis)
    return lax.ppermute(x, axis, [(i, i ^ bit) for i in range(count)])


def after(x, *others):
    return lax.optimization_barrier((x,) + others)[0]


def bits_of(count):
    return [1 << i for i in range(count.bit_length() - 1)]


def reversed_order(count):
    width = count.bit_length() - 1
    return [int(f"{p:0{width}b}"[::-1], 2) for p in range(count)]


def gather_pieces(solves, rows, ready):
    block, panel = solves.shape
    if rows != 4:
        return [lax.all_gather(solves.T, "row", axis=1, tiled=True)]
    half = pltpu.VMEM((panel // 2, block), BF16)
    upper, lower = call(
        turn_kernel, (half, half), solves, remain=1,
        scratch=[pltpu.VMEM((2, block, panel // 2), BF16), pltpu.SemaphoreType.DMA((2,))],
    )
    lower_x, upper_y = swap(lower, "row", 1), swap(upper, "row", 2)
    upper_x, lower_y = swap(upper, "row", 1), swap(lower, "row", 2)
    upper_far, lower_far = swap(after(upper_y, *ready), "row", 1), swap(after(lower_x, *ready), "row", 2)
    return [upper, lower, upper_x, lower_x, upper_y, lower_y, upper_far, lower_far]


def shards(coupling, solves, border_diagonal, panel_rows):
    half = HALF
    coupling, solves = coupling[0], solves[0]
    local, row_count = coupling.shape
    panel = solves.shape[1]
    scen, rows = lax.axis_size("scen"), lax.axis_size("row")
    layers = scen // 2
    row, place = lax.axis_index("row"), lax.axis_index("scen")
    share = row_count // scen
    size = panel // (2 * rows)
    shape = pltpu.VMEM
    panel_row, diagonal_row = panel_rows[None, :], border_diagonal.T
    first_row = row * row_count + place * share
    picked = shape((local, panel), BF16)
    chunk_room = [
        pltpu.VMEM((CHUNKS // 2, local // CHUNKS, row_count), BF16), pltpu.SemaphoreType.DMA((CHUNKS // 2,))
    ]
    chosen, entry, one, panel_row, diagonal_row = call(
        pick_kernel,
        (
            picked, shape((8, panel), F32), shape((row_count, panel), BF16),
            shape((1, panel), jnp.int32), shape((1, share), F32),
        ),
        panel_row, diagonal_row, coupling, remain=3,
        scratch=[chunk_room[0], pltpu.SemaphoreType.DMA((2,)), chunk_room[1]],
    )
    pieces = gather_pieces(solves, rows, (entry,))
    near, far = pieces[:6], pieces[6:]
    chosen = call(rest_kernel, picked, chosen, one, coupling, remain=1, scratch=chunk_room, aliases={0: 0})
    room = [pltpu.VMEM((panel // 2, panel), F32)]
    turned, terms = call(
        early_kernel, (shape((panel, local), BF16), shape((panel, panel), F32)), chosen, *near
    )
    send = call(
        functools.partial(send_kernel, rows), shape((panel // 2 + 8, panel), F32),
        chosen, entry, terms, *far, scratch=room,
    )
    turned, keep = call(
        functools.partial(keep_kernel, rows), (shape((panel, local), BF16), shape((panel // 2, panel), F32)),
        turned, chosen, terms, *far, scratch=room, aliases={0: 0},
    )
    coded = shape((size + SHORT, panel), I16)
    codes = call(
        functools.partial(pair_kernel, rows), (coded,) * rows, keep, swap(send, "scen", 1), entry
    )
    arrived = [swap(codes[k], "row", k) for k in range(rows - 1, 0, -1)]
    part = codes[0]
    steps = bits_of(layers)
    split = share % 128 == 0
    if split:
        count = layers // 2
        bulk = shape((layers * panel, share), F32)
        halved = lambda count: (shape((count * panel, share), F32), shape((count * (panel + TAIL), share), I16))
        own, send_rows = call(
            schur_kernel, (bulk, bulk), panel_row, diagonal_row, coupling, after(turned, part), micros=2.0
        )
        part = call(sum_kernel, coded, after(part, own), *arrived, micros=10.0)
        got = swap(send_rows, "scen", 1)
    else:
        own, got = lax.psum_scatter(dot(turned, coupling), "scen", scatter_dimension=1, tiled=True), []
        mine = first_row + jnp.arange(share, dtype=jnp.int32)
        own = own + jnp.where(panel_rows[:, None] == mine[None, :], border_diagonal[:, 0][None, :], F32(0.0))
        part = call(sum_kernel, coded, part, *arrived)
    if split:
        others = [swap(part, "scen", 2 * k) for k in range(1, layers)]
        own, bulk_codes = call(functools.partial(bulk_pair_kernel, panel), halved(count), after(own, part), got)
        part = call(sum_kernel, coded, after(part, bulk_codes), *others, micros=5.0)
    else:
        for bit in steps:
            part = call(sum_kernel, coded, part, swap(part, "scen", 2 * bit))
    shared = [swap(part, "row", k) for k in range(1, rows)]
    if split:
        for bit in steps[:-1]:
            count //= 2
            got = swap(bulk_codes, "scen", 2 * bit)
            own, bulk_codes = call(functools.partial(bulk_sum_kernel, panel), halved(count), own, got)
        got = [swap(bulk_codes, "scen", layers)]
    if split:
        part = after(part, bulk_codes)
    joined = call(join_kernel, shape((rows * (size + TAIL), panel), I16), part, *shared)
    other = swap(joined, "scen", 1)
    own_half = call(
        functools.partial(own_kernel, rows), shape((panel // 2, panel), F32), joined
    )
    inverse_first, inverse_second = call(
        functools.partial(newton_kernel, rows), (shape((half, half), F32), shape((half, panel), F32)),
        own_half, other, scratch=[pltpu.VMEM((panel, panel), F32)],
    )
    out = jax.ShapeDtypeStruct((share, 1, half), F32)
    room = [pltpu.VMEM(out.shape, F32)] * 2 + [pltpu.SemaphoreType.DMA((2,))]
    return call(
        factor_kernel, (out, out), inverse_first, inverse_second, own, *got, scratch=room, out_space=pltpu.HBM
    )


def solution(mesh):
    placed = (P("scen", None, "row"), P("scen", "row", None), P("scen", "row"), P())
    return jax.shard_map(
        shards,
        mesh=mesh,
        in_specs=placed,
        out_specs=(P("scen", "row", None), P("scen", "row", None)),
        check_vma=False,
    )
```

```python
import functools

import jax
import jax.numpy as jnp
from jax import lax
from jax.experimental import pallas as pl
from jax.experimental.pallas import tpu as pltpu
from jax.sharding import PartitionSpec as P

HALF = 256
NEWTON = 8
TAIL = 16
SHORT = 8
CHUNKS = 4
LEVELS = 32000.0
F32 = jnp.float32
BF16 = jnp.bfloat16
I16 = jnp.int16


def halves(a):
    high = a.astype(BF16)
    low = (a - high.astype(F32)).astype(BF16)
    return high, low


def left_of(a):
    high, low = halves(a)
    return jnp.concatenate([high, high, low], axis=1)


def right_of(b):
    high, low = halves(b)
    return jnp.concatenate([high, low, high], axis=0)


def dot(a, b):
    return jnp.dot(a, b, preferred_element_type=F32)


def product(a, b):
    return dot(left_of(a), right_of(b))


def nearly(pivot):
    size = jnp.abs(pivot)
    turned = pivot.T
    square = product(turned, pivot)
    norm_one = jnp.max(jnp.sum(size, axis=0, keepdims=True))
    norm_inf = jnp.max(jnp.sum(size, axis=1, keepdims=True))
    scale = F32(1.0) / (norm_one * norm_inf)
    count = pivot.shape[0]
    one = lax.broadcasted_iota(jnp.int32, pivot.shape, 0) == lax.broadcasted_iota(jnp.int32, pivot.shape, 1)
    rest = jnp.where(one, F32(1.0), F32(0.0)) - square * scale
    approx = turned * scale
    for step in range(NEWTON - 2):
        both = product(rest, jnp.concatenate([rest, approx], axis=1))
        rest, approx = both[:, :count], approx + both[:, count:]
    return approx + product(rest, approx)


def newton_beside(pivot, beside):
    approx = nearly(pivot)
    count = pivot.shape[0]
    both = product(approx, jnp.concatenate([pivot, beside], axis=1))
    stacked = jnp.concatenate([approx, both[:, count:]], axis=1)
    return 2.0 * stacked - product(both[:, :count], stacked)


def whereabouts():
    place = lax.axis_index("scen")
    return lax.axis_index("row"), lax.rem(place, 2), lax.div(place, 2)


def aligned(index, size):
    return pl.multiple_of(index * size, size)


def encode(values, out_ref, base, tail_rows, diagonal=None):
    rows, lanes = values.shape
    top = jnp.maximum(jnp.max(jnp.abs(values), axis=0, keepdims=True), F32(1e-30))
    power = jnp.ceil(jnp.log2(top))
    unit = jnp.exp2(power)
    mantissa = jnp.ceil(top / unit * F32(16384.0))
    scale = mantissa * unit * F32(1.0 / (16384.0 * LEVELS))
    codes = jnp.round(values * (F32(1.0) / scale)).astype(jnp.int32)
    out_ref[base:base + rows, :] = codes.astype(I16)
    row = lax.broadcasted_iota(jnp.int32, (tail_rows, lanes), 0)
    tail = jnp.where(row == 0, power, jnp.where(row == 1, mantissa, F32(0.0)))
    if diagonal is not None:
        coarse = jnp.floor(diagonal * F32(64.0))
        fine = (diagonal * F32(64.0) - coarse) * F32(4096.0)
        tail = jnp.where(row == 2, coarse, jnp.where(row == 3, fine, tail))
    out_ref[base + rows:base + rows + tail_rows, :] = tail.astype(jnp.int32).astype(I16)


def decode(ref, base, rows, tail_rows):
    tail = ref[base + rows:base + rows + tail_rows, :].astype(jnp.int32).astype(F32)
    scale = tail[1:2] * jnp.exp2(tail[0:1]) * F32(1.0 / (16384.0 * LEVELS))
    diagonal = tail[2:3] * F32(1.0 / 64.0) + tail[3:4] * F32(1.0 / (64.0 * 4096.0))
    return ref[base:base + rows, :].astype(jnp.int32).astype(F32) * scale, diagonal


def turn_kernel(solves_ref, upper_ref, lower_ref, solves_copy, done):
    half = upper_ref.shape[0]
    copies = [
        pltpu.make_async_copy(solves_ref.at[:, pl.ds(i * half, half)], solves_copy.at[i], done.at[i]) for i in (0, 1)
    ]
    for copy in copies:
        copy.start()
    for i, out_ref in enumerate((upper_ref, lower_ref)):
        copies[i].wait()
        out_ref[...] = solves_copy[i].T


def order_of(rows):
    row = lax.axis_index("row")
    return [row ^ 3, row, row ^ 1, row ^ 2] if rows == 4 else list(range(CHUNKS))


def fetch(source_ref, target_ref, done, blocks):
    size = target_ref.shape[1]
    copies = [
        pltpu.make_async_copy(source_ref.at[pl.ds(aligned(block, size), size), :], target_ref.at[i], done.at[i])
        for i, block in enumerate(blocks)
    ]
    for copy in copies:
        copy.start()
    return copies


def pick_kernel(
    rows, panel_ref, own_diagonal_ref, coupling_ref,
    chosen_ref, far_ref, entry_ref, one_ref, panel_out, diagonal_out, coupling_copy, small_done, done,
):
    small = [
        pltpu.make_async_copy(panel_ref, panel_out, small_done.at[0]),
        pltpu.make_async_copy(own_diagonal_ref, diagonal_out, small_done.at[1]),
    ]
    for copy in small:
        copy.start()
    block = order_of(rows)[0]
    copies = fetch(coupling_ref, coupling_copy, done, [block])
    for copy in small:
        copy.wait()
    columns, panel = one_ref.shape
    share = diagonal_out.shape[1]
    first_column = lax.axis_index("row") * columns
    first_row = first_column + lax.axis_index("scen") * share
    here = panel_out[...] - first_column == lax.broadcasted_iota(jnp.int32, (columns, panel), 0)
    one_ref[...] = jnp.where(here, F32(1.0), F32(0.0)).astype(BF16)
    owned = panel_out[...] - first_row == lax.broadcasted_iota(jnp.int32, (share, panel), 0)
    own = jnp.broadcast_to(diagonal_out[...], (8, share)).T[:, :1]
    entry = jnp.sum(jnp.where(owned, own, F32(0.0)), axis=0, keepdims=True)
    entry_ref[...] = jnp.broadcast_to(entry, entry_ref.shape)
    copies[0].wait()
    size = far_ref.shape[0]
    far_ref[...] = dot(coupling_copy[0], one_ref[...]).astype(BF16)
    chosen_ref[pl.ds(aligned(block, size), size), :] = far_ref[...]


def rest_kernel(rows, chosen_in, one_ref, coupling_ref, chosen_ref, coupling_copy, done):
    blocks = order_of(rows)[1:]
    size = coupling_copy.shape[1]
    for i, copy in enumerate(fetch(coupling_ref, coupling_copy, done, blocks)):
        copy.wait()
        chosen_ref[pl.ds(aligned(blocks[i], size), size), :] = dot(coupling_copy[i], one_ref[...]).astype(BF16)


def early_kernel(rows, chosen_ref, entry_ref, *refs):
    *pieces, turned_ref, own_ref, send_ref, terms_ref = refs
    row, core, _ = whereabouts()
    if len(pieces) == 1:
        turned_ref[...] = pieces[0][...]
    else:
        half, width = pieces[0].shape
        for i, piece in enumerate(pieces):
            start = aligned(row ^ (i // 2), width)
            turned_ref[i % 2 * half:(i % 2 + 1) * half, pl.ds(start, width)] = piece[...]
        start = aligned(row ^ (len(pieces) // 2), width)
        turned_ref[:, pl.ds(start, width)] = jnp.zeros((2 * half, width), BF16)
    terms_ref[...] = dot(turned_ref[...], chosen_ref[...])
    size = own_ref.shape[0] // rows
    for out_ref, whose in ((own_ref, core), (send_ref, 1 - core)):
        for k in range(rows):
            out_ref[k * size:(k + 1) * size, :] = terms_ref[pl.ds(aligned(whose * rows + (row ^ k), size), size), :]
    send_ref[rows * size:, :] = entry_ref[...]


def select_kernel(upper_ref, lower_ref, out_ref):
    out_ref[...] = jnp.where(whereabouts()[1] == 0, lower_ref[...], upper_ref[...])


def add_far(rows, block, chosen, far_ref):
    row = lax.axis_index("row")
    size = far_ref.shape[0] // rows
    far_ref[...] = dot(block, chosen)
    return [far_ref[pl.ds(aligned(row ^ k, size), size), :] for k in range(rows)]


def keep_kernel(rows, turned_in, own_ref, got_ref, entry_ref, *refs):
    *far, turned_ref, keep_ref, both_ref, far_ref = refs
    row, core, _ = whereabouts()
    half = keep_ref.shape[0]
    size = half // rows
    both_ref[...] = jnp.broadcast_to(entry_ref[:1, :] + got_ref[half:half + 1, :], both_ref.shape)
    keep_ref[...] = own_ref[...] + got_ref[:half, :]
    if far:
        upper_ref, lower_ref, chosen_ref = far
        width = upper_ref.shape[1]
        start = aligned(row ^ (rows - 1), width)
        turned_ref[:half, pl.ds(start, width)] = upper_ref[...]
        turned_ref[half:, pl.ds(start, width)] = lower_ref[...]
        block = jnp.where(core == 0, upper_ref[...], lower_ref[...])
        for k, piece in enumerate(add_far(rows, block, chosen_ref[...], far_ref)):
            keep_ref[k * size:(k + 1) * size, :] += piece


def pair_kernel(rows, keep_ref, entry_ref, *refs):
    *far, far_ref = refs
    far, out_refs = far[:-rows], far[-rows:]
    size = keep_ref.shape[0] // rows
    pieces = add_far(rows, far[0][...], far[1][...], far_ref) if far else None
    for k, out_ref in enumerate(out_refs):
        value = keep_ref[k * size:(k + 1) * size, :]
        encode(value + pieces[k] if far else value, out_ref, 0, SHORT, entry_ref[:1, :])


def sum_kernel(*refs):
    *in_refs, out_ref = refs
    size = out_ref.shape[0] - SHORT
    parts = [decode(ref, 0, size, SHORT) for ref in in_refs]
    encode(sum(p[0] for p in parts), out_ref, 0, SHORT, sum(p[1] for p in parts))


def join_kernel(*refs):
    *in_refs, out_ref = refs
    size = in_refs[0].shape[0] - SHORT
    for k, ref in enumerate(in_refs[:1] + in_refs[:0:-1]):
        start = k * (size + TAIL)
        out_ref[start:start + size, :] = ref[:size, :]
        tail = ref[size:, :].astype(jnp.int32)
        out_ref[start + size:start + size + TAIL, :] = jnp.concatenate([tail, jnp.zeros_like(tail)], axis=0).astype(I16)


def place_pieces(row, whose, ref, pivots_ref, rows, base):
    panel = pivots_ref.shape[1]
    size = panel // (2 * rows)
    index = lax.broadcasted_iota(jnp.int32, (size, panel), 1)
    for k in range(rows):
        start = aligned(whose * rows + (row ^ k), size)
        values, diagonal = decode(ref, k * (size + TAIL), size, TAIL)
        at = lax.broadcasted_iota(jnp.int32, (size, panel), 0) + start == index
        pivots_ref[pl.ds(start - base, size), :] = values + jnp.where(at, diagonal, F32(0.0))


def own_kernel(rows, own_ref, half_ref):
    row, core, _ = whereabouts()
    place_pieces(row, core, own_ref, half_ref, rows, core * half_ref.shape[0])


def newton_kernel(rows, half_ref, other_ref, inverse_ref, second_ref, pivots_ref):
    row, core, _ = whereabouts()
    half = half_ref.shape[0]
    pivots_ref[pl.ds(aligned(core, half), half), :] = half_ref[...]
    place_pieces(row, 1 - core, other_ref, pivots_ref, rows, 0)
    both = newton_beside(pivots_ref[:half, :half], pivots_ref[:half, half:])
    inverse_first = both[:, :half]
    inverse_ref[...] = inverse_first
    corner = pivots_ref[half:, :half]
    pivot = pivots_ref[half:, half:] - product(corner, both[:, half:])
    second_ref[...] = newton_beside(pivot, -product(corner, inverse_first))


def schur_kernel(panel_ref, own_diagonal_ref, coupling_ref, turned_ref, keep_ref, send_ref):
    row, core, layer = whereabouts()
    panel, share = turned_ref.shape[0], keep_ref.shape[1]
    first_row = row * coupling_ref.shape[1] + (2 * layer + core) * share
    layers = keep_ref.shape[0] // panel
    for position, k in enumerate(reversed_order(layers)):
        start = aligned(layer ^ k, 2 * share)
        both = dot(turned_ref[...], coupling_ref[:, pl.ds(start, 2 * share)])
        rows = slice(position * panel, (position + 1) * panel)
        one, two = both[:, :share], both[:, share:]
        kept = jnp.where(core == 0, one, two)
        if position == 0:
            wanted = jnp.broadcast_to(panel_ref[...].astype(F32), (share, panel)).T.astype(jnp.int32)
            here = wanted - first_row == lax.broadcasted_iota(jnp.int32, (panel, share), 1)
            kept = kept + jnp.where(here, own_diagonal_ref[...], F32(0.0))
        keep_ref[rows, :] = kept
        send_ref[rows, :] = jnp.where(core == 0, two, one)


def bulk_pair_kernel(panel, keep_ref, got_ref, own_ref, coded_ref):
    half = own_ref.shape[0]
    own_ref[...] = keep_ref[:half, :] + got_ref[:half, :]
    for i in range(half // panel):
        part = slice(half + i * panel, half + (i + 1) * panel)
        encode(keep_ref[part, :] + got_ref[part, :], coded_ref, i * (panel + TAIL), TAIL)


def bulk_sum_kernel(panel, keep_ref, got_ref, own_ref, coded_ref):
    half = own_ref.shape[0]
    for i in range(keep_ref.shape[0] // panel):
        value = keep_ref[i * panel:(i + 1) * panel, :] + decode(got_ref, i * (panel + TAIL), panel, TAIL)[0]
        if i * panel < half:
            own_ref[i * panel:(i + 1) * panel, :] = value
        else:
            encode(value, coded_ref, (i - half // panel) * (panel + TAIL), TAIL)


def factor_kernel(inverse_first_ref, inverse_second_ref, rows_ref, *refs):
    *got, first_out, second_out = refs
    panel = rows_ref.shape[0]
    half = panel // 2
    rows = rows_ref[...]
    for ref in got:
        rows = rows + decode(ref, 0, panel, TAIL)[0]
    first, second = rows[:half], rows[half:]
    first_out[...] = product(inverse_first_ref[...], first).T[:, None, :]
    second_out[...] = product(inverse_second_ref[...], jnp.concatenate([second, first], axis=0)).T[:, None, :]


def call(kernel, out_shape, *args, scratch=(), remain=0, micros=0.0, aliases=None):
    hbm = pl.BlockSpec(memory_space=pltpu.HBM)
    vmem = pl.BlockSpec(memory_space=pltpu.VMEM)
    stay = len(args) - remain
    args = args[:stay] + tuple(pltpu.with_memory_space_constraint(x, pltpu.HBM) for x in args[stay:])
    return pl.pallas_call(
        kernel,
        name=getattr(kernel, "func", kernel).__name__,
        out_shape=out_shape,
        in_specs=[vmem] * (len(args) - remain) + [hbm] * remain,
        out_specs=jax.tree.map(lambda _: vmem, out_shape),
        scratch_shapes=scratch,
        input_output_aliases=aliases or {},
        compiler_params=pltpu.CompilerParams(vmem_limit_bytes=12 << 20),
        cost_estimate=pl.CostEstimate(flops=int(micros * 1.15e9), bytes_accessed=1024, transcendentals=0),
    )(*args)


def swap(x, axis, bit):
    count = lax.axis_size(axis)
    return lax.ppermute(x, axis, [(i, i ^ bit) for i in range(count)])


def after(x, *others):
    return lax.optimization_barrier((x,) + others)[0]


def bits_of(count):
    return [1 << i for i in range(count.bit_length() - 1)]


def reversed_order(count):
    width = count.bit_length() - 1
    return [int(f"{p:0{width}b}"[::-1], 2) for p in range(count)]


def turn(solves, rows):
    block, panel = solves.shape
    if rows != 4:
        return None, None
    half = pltpu.VMEM((panel // 2, block), BF16)
    return call(
        turn_kernel, (half, half), solves, remain=1,
        scratch=[pltpu.VMEM((2, block, panel // 2), BF16), pltpu.SemaphoreType.DMA((2,))],
    )


def gather_pieces(solves, upper, lower, ready):
    if upper is None:
        return [lax.all_gather(solves.T, "row", axis=1, tiled=True)]
    lower_x, upper_y = swap(lower, "row", 1), swap(upper, "row", 2)
    upper_x, lower_y = swap(upper, "row", 1), swap(lower, "row", 2)
    upper_far, lower_far = swap(after(upper_y, *ready), "row", 1), swap(after(lower_x, *ready), "row", 2)
    return [upper, lower, upper_x, lower_x, upper_y, lower_y, upper_far, lower_far]


def shards(coupling, solves, border_diagonal, panel_rows):
    half = HALF
    coupling, solves = coupling[0], solves[0]
    local, row_count = coupling.shape
    panel = solves.shape[1]
    scen, rows = lax.axis_size("scen"), lax.axis_size("row")
    layers = scen // 2
    row, place = lax.axis_index("row"), lax.axis_index("scen")
    share = row_count // scen
    size = panel // (2 * rows)
    shape = pltpu.VMEM
    panel_row, diagonal_row = panel_rows[None, :], border_diagonal.T
    first_row = row * row_count + place * share
    picked, part_picked = shape((local, panel), BF16), shape((local // CHUNKS, panel), BF16)
    chunk_room = lambda count: [
        pltpu.VMEM((count, local // CHUNKS, row_count), BF16), pltpu.SemaphoreType.DMA((count,))
    ]
    room, done = chunk_room(1)
    upper, lower = turn(solves, rows)
    chosen, far_chosen, entry, one, panel_row, diagonal_row = call(
        functools.partial(pick_kernel, rows),
        (
            picked, part_picked, shape((8, panel), F32), shape((row_count, panel), BF16),
            shape((1, panel), jnp.int32), shape((1, share), F32),
        ),
        panel_row, diagonal_row, coupling, remain=3, scratch=[room, pltpu.SemaphoreType.DMA((2,)), done],
    )
    pieces = gather_pieces(solves, upper, lower, (entry,))
    near, far = pieces[:6], pieces[6:]
    split = rows == 4 and share % 128 == 0
    chosen = call(
        functools.partial(rest_kernel, rows), picked, chosen, one, coupling, remain=1,
        scratch=chunk_room(CHUNKS - 1), aliases={0: 0},
    )
    other_chosen = swap(after(far_chosen, near[2], near[5]), "scen", 1) if split else None
    half_shape, room = shape((panel // 2, panel), F32), [pltpu.VMEM((panel // 2, panel), F32)]
    turned, own_near, send_near = call(
        functools.partial(early_kernel, rows),
        (shape((panel, local), BF16), half_shape, shape((panel // 2 + 8, panel), F32)),
        chosen, entry, *near, scratch=[pltpu.VMEM((panel, panel), F32)],
    )
    got_near = swap(send_near, "scen", 1)
    if split:
        far_send = call(select_kernel, shape(far[0].shape, BF16), far[0], far[1], micros=3.0)
        other_far = [swap(far_send, "scen", 1), other_chosen]
        own_far = [*far, far_chosen]
    else:
        other_far = own_far = []
    turned, keep, entry = call(
        functools.partial(keep_kernel, rows), (shape((panel, local), BF16), half_shape, shape((8, panel), F32)),
        turned, own_near, got_near, entry, *own_far, scratch=room, aliases={0: 0},
    )
    coded = shape((size + SHORT, panel), I16)
    codes = call(functools.partial(pair_kernel, rows), (coded,) * rows, keep, entry, *other_far, scratch=room)
    arrived = [swap(codes[k], "row", k) for k in [1, *range(rows - 1, 1, -1)]]
    part = codes[0]
    steps = bits_of(layers)
    if split:
        count = layers // 2
        bulk = shape((layers * panel, share), F32)
        halved = lambda count: (shape((count * panel, share), F32), shape((count * (panel + TAIL), share), I16))
        own, send_rows = call(
            schur_kernel, (bulk, bulk), panel_row, diagonal_row, coupling, after(turned, part), micros=2.0
        )
        part = call(sum_kernel, coded, after(part, own), *arrived, micros=10.0)
        got = swap(send_rows, "scen", 1)
    else:
        own, got = lax.psum_scatter(dot(turned, coupling), "scen", scatter_dimension=1, tiled=True), []
        mine = first_row + jnp.arange(share, dtype=jnp.int32)
        own = own + jnp.where(panel_rows[:, None] == mine[None, :], border_diagonal[:, 0][None, :], F32(0.0))
        part = call(sum_kernel, coded, part, *arrived)
    if split:
        others = [swap(part, "scen", 2 * k) for k in range(layers - 1, 0, -1)]
        own, bulk_codes = call(functools.partial(bulk_pair_kernel, panel), halved(count), after(own, part), got)
        part = call(sum_kernel, coded, after(part, bulk_codes), *others, micros=5.0)
    else:
        for bit in steps:
            part = call(sum_kernel, coded, part, swap(part, "scen", 2 * bit))
    shared = [swap(part, "row", k) for k in range(1, rows)]
    if split:
        for bit in steps[:-1]:
            count //= 2
            got = swap(bulk_codes, "scen", 2 * bit)
            own, bulk_codes = call(functools.partial(bulk_sum_kernel, panel), halved(count), own, got)
        got = [swap(bulk_codes, "scen", layers)]
    if split:
        part = after(part, bulk_codes)
    joined = call(join_kernel, shape((rows * (size + TAIL), panel), I16), part, *shared[::-1])
    other = swap(joined, "scen", 1)
    own_half = call(
        functools.partial(own_kernel, rows), shape((panel // 2, panel), F32), joined
    )
    inverse_first, inverse_second = call(
        functools.partial(newton_kernel, rows), (shape((half, half), F32), shape((half, panel), F32)),
        own_half, other, scratch=[pltpu.VMEM((panel, panel), F32)],
    )
    out = jax.ShapeDtypeStruct((share, 1, half), F32)
    return call(
        factor_kernel, (out, out),
        inverse_first, inverse_second, own, *got,
    )


def solution(mesh):
    placed = (P("scen", None, "row"), P("scen", "row", None), P("scen", "row"), P())
    return jax.shard_map(
        shards,
        mesh=mesh,
        in_specs=placed,
        out_specs=(P("scen", "row", None), P("scen", "row", None)),
        check_vma=False,
    )
```

```python
import functools

import jax
import jax.numpy as jnp
from jax import lax
from jax.experimental import pallas as pl
from jax.experimental.pallas import tpu as pltpu
from jax.sharding import PartitionSpec as P

HALF = 256
NEWTON = 8
TAIL = 16
SHORT = 8
CHUNKS = 4
FIRST = 2
LEVELS = 32000.0
F32 = jnp.float32
BF16 = jnp.bfloat16
I16 = jnp.int16


def halves(a):
    high = a.astype(BF16)
    low = (a - high.astype(F32)).astype(BF16)
    return high, low


def left_of(a):
    high, low = halves(a)
    return jnp.concatenate([high, high, low], axis=1)


def right_of(b):
    high, low = halves(b)
    return jnp.concatenate([high, low, high], axis=0)


def dot(a, b):
    return jnp.dot(a, b, preferred_element_type=F32)


def product(a, b):
    return dot(left_of(a), right_of(b))


def nearly(pivot):
    size = jnp.abs(pivot)
    turned = pivot.T
    square = product(turned, pivot)
    norm_one = jnp.max(jnp.sum(size, axis=0, keepdims=True))
    norm_inf = jnp.max(jnp.sum(size, axis=1, keepdims=True))
    scale = F32(1.0) / (norm_one * norm_inf)
    count = pivot.shape[0]
    one = lax.broadcasted_iota(jnp.int32, pivot.shape, 0) == lax.broadcasted_iota(jnp.int32, pivot.shape, 1)
    rest = jnp.where(one, F32(1.0), F32(0.0)) - square * scale
    approx = turned * scale
    for step in range(NEWTON - 2):
        both = product(rest, jnp.concatenate([rest, approx], axis=1))
        rest, approx = both[:, :count], approx + both[:, count:]
    return approx + product(rest, approx)


def newton_beside(pivot, beside):
    approx = nearly(pivot)
    count = pivot.shape[0]
    both = product(approx, jnp.concatenate([pivot, beside], axis=1))
    stacked = jnp.concatenate([approx, both[:, count:]], axis=1)
    return 2.0 * stacked - product(both[:, :count], stacked)


def whereabouts():
    place = lax.axis_index("scen")
    return lax.axis_index("row"), lax.rem(place, 2), lax.div(place, 2)


def aligned(index, size):
    return pl.multiple_of(index * size, size)


def encode(values, out_ref, base, tail_rows, diagonal=None):
    rows, lanes = values.shape
    top = jnp.maximum(jnp.max(jnp.abs(values), axis=0, keepdims=True), F32(1e-30))
    power = jnp.ceil(jnp.log2(top))
    unit = jnp.exp2(power)
    mantissa = jnp.ceil(top / unit * F32(16384.0))
    scale = mantissa * unit * F32(1.0 / (16384.0 * LEVELS))
    codes = jnp.round(values * (F32(1.0) / scale)).astype(jnp.int32)
    out_ref[base:base + rows, :] = codes.astype(I16)
    row = lax.broadcasted_iota(jnp.int32, (tail_rows, lanes), 0)
    tail = jnp.where(row == 0, power, jnp.where(row == 1, mantissa, F32(0.0)))
    if diagonal is not None:
        coarse = jnp.floor(diagonal * F32(64.0))
        fine = (diagonal * F32(64.0) - coarse) * F32(4096.0)
        tail = jnp.where(row == 2, coarse, jnp.where(row == 3, fine, tail))
    out_ref[base + rows:base + rows + tail_rows, :] = tail.astype(jnp.int32).astype(I16)


def decode(ref, base, rows, tail_rows):
    tail = ref[base + rows:base + rows + tail_rows, :].astype(jnp.int32).astype(F32)
    scale = tail[1:2] * jnp.exp2(tail[0:1]) * F32(1.0 / (16384.0 * LEVELS))
    diagonal = tail[2:3] * F32(1.0 / 64.0) + tail[3:4] * F32(1.0 / (64.0 * 4096.0))
    return ref[base:base + rows, :].astype(jnp.int32).astype(F32) * scale, diagonal


def turn_kernel(solves_ref, upper_ref, lower_ref, solves_copy, done):
    half = upper_ref.shape[0]
    copies = [
        pltpu.make_async_copy(solves_ref.at[:, pl.ds(i * half, half)], solves_copy.at[i], done.at[i]) for i in (0, 1)
    ]
    for copy in copies:
        copy.start()
    for i, out_ref in enumerate((upper_ref, lower_ref)):
        copies[i].wait()
        out_ref[...] = solves_copy[i].T


def order_of(rows):
    row = lax.axis_index("row")
    return [row ^ 3, row, row ^ 1, row ^ 2] if rows == 4 else list(range(CHUNKS))


def fetch(source_ref, target_ref, done, blocks):
    size = target_ref.shape[1]
    copies = [
        pltpu.make_async_copy(source_ref.at[pl.ds(aligned(block, size), size), :], target_ref.at[i], done.at[i])
        for i, block in enumerate(blocks)
    ]
    for copy in copies:
        copy.start()
    return copies


def pick_kernel(
    rows, panel_ref, own_diagonal_ref, coupling_ref,
    chosen_ref, far_ref, entry_ref, one_ref, panel_out, diagonal_out, coupling_copy, small_done, done,
):
    small = [
        pltpu.make_async_copy(panel_ref, panel_out, small_done.at[0]),
        pltpu.make_async_copy(own_diagonal_ref, diagonal_out, small_done.at[1]),
    ]
    for copy in small:
        copy.start()
    blocks = order_of(rows)[:FIRST]
    copies = fetch(coupling_ref, coupling_copy, done, blocks)
    for copy in small:
        copy.wait()
    columns, panel = one_ref.shape
    share = diagonal_out.shape[1]
    first_column = lax.axis_index("row") * columns
    first_row = first_column + lax.axis_index("scen") * share
    here = panel_out[...] - first_column == lax.broadcasted_iota(jnp.int32, (columns, panel), 0)
    one_ref[...] = jnp.where(here, F32(1.0), F32(0.0)).astype(BF16)
    owned = panel_out[...] - first_row == lax.broadcasted_iota(jnp.int32, (share, panel), 0)
    own = jnp.broadcast_to(diagonal_out[...], (8, share)).T[:, :1]
    entry = jnp.sum(jnp.where(owned, own, F32(0.0)), axis=0, keepdims=True)
    entry_ref[...] = jnp.broadcast_to(entry, entry_ref.shape)
    copies[0].wait()
    size = far_ref.shape[0]
    far_ref[...] = dot(coupling_copy[0], one_ref[...]).astype(BF16)
    chosen_ref[pl.ds(aligned(blocks[0], size), size), :] = far_ref[...]
    for i in range(1, FIRST):
        copies[i].wait()
        chosen_ref[pl.ds(aligned(blocks[i], size), size), :] = dot(coupling_copy[i], one_ref[...]).astype(BF16)


def rest_kernel(rows, chosen_in, one_ref, coupling_ref, chosen_ref, coupling_copy, done):
    blocks = order_of(rows)[FIRST:]
    size = coupling_copy.shape[1]
    for i, copy in enumerate(fetch(coupling_ref, coupling_copy, done, blocks)):
        copy.wait()
        chosen_ref[pl.ds(aligned(blocks[i], size), size), :] = dot(coupling_copy[i], one_ref[...]).astype(BF16)


def early_kernel(rows, chosen_ref, entry_ref, *refs):
    *pieces, turned_ref, own_ref, send_ref, terms_ref = refs
    row, core, _ = whereabouts()
    if len(pieces) == 1:
        turned_ref[...] = pieces[0][...]
    else:
        half, width = pieces[0].shape
        for i, piece in enumerate(pieces):
            start = aligned(row ^ (i // 2), width)
            turned_ref[i % 2 * half:(i % 2 + 1) * half, pl.ds(start, width)] = piece[...]
        start = aligned(row ^ (len(pieces) // 2), width)
        turned_ref[:, pl.ds(start, width)] = jnp.zeros((2 * half, width), BF16)
    terms_ref[...] = dot(turned_ref[...], chosen_ref[...])
    size = own_ref.shape[0] // rows
    for out_ref, whose in ((own_ref, core), (send_ref, 1 - core)):
        for k in range(rows):
            out_ref[k * size:(k + 1) * size, :] = terms_ref[pl.ds(aligned(whose * rows + (row ^ k), size), size), :]
    send_ref[rows * size:, :] = entry_ref[...]


def select_kernel(upper_ref, lower_ref, out_ref):
    out_ref[...] = jnp.where(whereabouts()[1] == 0, lower_ref[...], upper_ref[...])


def add_far(rows, block, chosen, far_ref):
    row = lax.axis_index("row")
    size = far_ref.shape[0] // rows
    far_ref[...] = dot(block, chosen)
    return [far_ref[pl.ds(aligned(row ^ k, size), size), :] for k in range(rows)]


def keep_kernel(rows, turned_in, own_ref, got_ref, entry_ref, *refs):
    *far, turned_ref, keep_ref, both_ref, far_ref = refs
    row, core, _ = whereabouts()
    half = keep_ref.shape[0]
    size = half // rows
    both_ref[...] = jnp.broadcast_to(entry_ref[:1, :] + got_ref[half:half + 1, :], both_ref.shape)
    keep_ref[...] = own_ref[...] + got_ref[:half, :]
    if far:
        upper_ref, lower_ref, chosen_ref = far
        width = upper_ref.shape[1]
        start = aligned(row ^ (rows - 1), width)
        turned_ref[:half, pl.ds(start, width)] = upper_ref[...]
        turned_ref[half:, pl.ds(start, width)] = lower_ref[...]
        block = jnp.where(core == 0, upper_ref[...], lower_ref[...])
        for k, piece in enumerate(add_far(rows, block, chosen_ref[...], far_ref)):
            keep_ref[k * size:(k + 1) * size, :] += piece


def pair_kernel(rows, keep_ref, entry_ref, *refs):
    *far, far_ref = refs
    far, out_refs = far[:-rows], far[-rows:]
    size = keep_ref.shape[0] // rows
    pieces = add_far(rows, far[0][...], far[1][...], far_ref) if far else None
    for k, out_ref in enumerate(out_refs):
        value = keep_ref[k * size:(k + 1) * size, :]
        encode(value + pieces[k] if far else value, out_ref, 0, SHORT, entry_ref[:1, :])


def sum_kernel(*refs):
    *in_refs, out_ref = refs
    size = out_ref.shape[0] - SHORT
    parts = [decode(ref, 0, size, SHORT) for ref in in_refs]
    encode(sum(p[0] for p in parts), out_ref, 0, SHORT, sum(p[1] for p in parts))


def join_kernel(*refs):
    *in_refs, out_ref = refs
    size = in_refs[0].shape[0] - SHORT
    for k, ref in enumerate(in_refs[:1] + in_refs[:0:-1]):
        start = k * (size + TAIL)
        out_ref[start:start + size, :] = ref[:size, :]
        tail = ref[size:, :].astype(jnp.int32)
        out_ref[start + size:start + size + TAIL, :] = jnp.concatenate([tail, jnp.zeros_like(tail)], axis=0).astype(I16)


def place_pieces(row, whose, ref, pivots_ref, rows, base):
    panel = pivots_ref.shape[1]
    size = panel // (2 * rows)
    index = lax.broadcasted_iota(jnp.int32, (size, panel), 1)
    for k in range(rows):
        start = aligned(whose * rows + (row ^ k), size)
        values, diagonal = decode(ref, k * (size + TAIL), size, TAIL)
        at = lax.broadcasted_iota(jnp.int32, (size, panel), 0) + start == index
        pivots_ref[pl.ds(start - base, size), :] = values + jnp.where(at, diagonal, F32(0.0))


def own_kernel(rows, own_ref, half_ref):
    row, core, _ = whereabouts()
    place_pieces(row, core, own_ref, half_ref, rows, core * half_ref.shape[0])


def newton_kernel(rows, half_ref, other_ref, inverse_ref, second_ref, pivots_ref):
    row, core, _ = whereabouts()
    half = half_ref.shape[0]
    pivots_ref[pl.ds(aligned(core, half), half), :] = half_ref[...]
    place_pieces(row, 1 - core, other_ref, pivots_ref, rows, 0)
    both = newton_beside(pivots_ref[:half, :half], pivots_ref[:half, half:])
    inverse_first = both[:, :half]
    inverse_ref[...] = inverse_first
    corner = pivots_ref[half:, :half]
    pivot = pivots_ref[half:, half:] - product(corner, both[:, half:])
    second_ref[...] = newton_beside(pivot, -product(corner, inverse_first))


def schur_kernel(panel_ref, own_diagonal_ref, coupling_ref, turned_ref, keep_ref, send_ref):
    row, core, layer = whereabouts()
    panel, share = turned_ref.shape[0], keep_ref.shape[1]
    first_row = row * coupling_ref.shape[1] + (2 * layer + core) * share
    layers = keep_ref.shape[0] // panel
    for position, k in enumerate(reversed_order(layers)):
        start = aligned(layer ^ k, 2 * share)
        both = dot(turned_ref[...], coupling_ref[:, pl.ds(start, 2 * share)])
        rows = slice(position * panel, (position + 1) * panel)
        one, two = both[:, :share], both[:, share:]
        kept = jnp.where(core == 0, one, two)
        if position == 0:
            wanted = jnp.broadcast_to(panel_ref[...].astype(F32), (share, panel)).T.astype(jnp.int32)
            here = wanted - first_row == lax.broadcasted_iota(jnp.int32, (panel, share), 1)
            kept = kept + jnp.where(here, own_diagonal_ref[...], F32(0.0))
        keep_ref[rows, :] = kept
        send_ref[rows, :] = jnp.where(core == 0, two, one)


def bulk_pair_kernel(panel, keep_ref, got_ref, own_ref, coded_ref):
    half = own_ref.shape[0]
    own_ref[...] = keep_ref[:half, :] + got_ref[:half, :]
    for i in range(half // panel):
        part = slice(half + i * panel, half + (i + 1) * panel)
        encode(keep_ref[part, :] + got_ref[part, :], coded_ref, i * (panel + TAIL), TAIL)


def bulk_sum_kernel(panel, keep_ref, got_ref, own_ref, coded_ref):
    half = own_ref.shape[0]
    for i in range(keep_ref.shape[0] // panel):
        value = keep_ref[i * panel:(i + 1) * panel, :] + decode(got_ref, i * (panel + TAIL), panel, TAIL)[0]
        if i * panel < half:
            own_ref[i * panel:(i + 1) * panel, :] = value
        else:
            encode(value, coded_ref, (i - half // panel) * (panel + TAIL), TAIL)


def factor_kernel(inverse_first_ref, inverse_second_ref, rows_ref, *refs):
    *got, first_out, second_out = refs
    panel = rows_ref.shape[0]
    half = panel // 2
    rows = rows_ref[...]
    for ref in got:
        rows = rows + decode(ref, 0, panel, TAIL)[0]
    first, second = rows[:half], rows[half:]
    first_out[...] = product(inverse_first_ref[...], first).T[:, None, :]
    second_out[...] = product(inverse_second_ref[...], jnp.concatenate([second, first], axis=0)).T[:, None, :]


def call(kernel, out_shape, *args, scratch=(), remain=0, micros=0.0, aliases=None):
    hbm = pl.BlockSpec(memory_space=pltpu.HBM)
    vmem = pl.BlockSpec(memory_space=pltpu.VMEM)
    stay = len(args) - remain
    args = args[:stay] + tuple(pltpu.with_memory_space_constraint(x, pltpu.HBM) for x in args[stay:])
    return pl.pallas_call(
        kernel,
        name=getattr(kernel, "func", kernel).__name__,
        out_shape=out_shape,
        in_specs=[vmem] * (len(args) - remain) + [hbm] * remain,
        out_specs=jax.tree.map(lambda _: vmem, out_shape),
        scratch_shapes=scratch,
        input_output_aliases=aliases or {},
        compiler_params=pltpu.CompilerParams(vmem_limit_bytes=12 << 20),
        cost_estimate=pl.CostEstimate(flops=int(micros * 1.15e9), bytes_accessed=1024, transcendentals=0),
    )(*args)


def swap(x, axis, bit):
    count = lax.axis_size(axis)
    return lax.ppermute(x, axis, [(i, i ^ bit) for i in range(count)])


def after(x, *others):
    return lax.optimization_barrier((x,) + others)[0]


def bits_of(count):
    return [1 << i for i in range(count.bit_length() - 1)]


def reversed_order(count):
    width = count.bit_length() - 1
    return [int(f"{p:0{width}b}"[::-1], 2) for p in range(count)]


def turn(solves, rows):
    block, panel = solves.shape
    if rows != 4:
        return None, None
    half = pltpu.VMEM((panel // 2, block), BF16)
    return call(
        turn_kernel, (half, half), solves, remain=1,
        scratch=[pltpu.VMEM((2, block, panel // 2), BF16), pltpu.SemaphoreType.DMA((2,))],
    )


def gather_pieces(solves, upper, lower, ready):
    if upper is None:
        return [lax.all_gather(solves.T, "row", axis=1, tiled=True)]
    lower_x, upper_y = swap(lower, "row", 1), swap(upper, "row", 2)
    upper_x, lower_y = swap(upper, "row", 1), swap(lower, "row", 2)
    upper_far, lower_far = swap(after(upper_y, *ready), "row", 1), swap(after(lower_x, *ready), "row", 2)
    return [upper, lower, upper_x, lower_x, upper_y, lower_y, upper_far, lower_far]


def shards(coupling, solves, border_diagonal, panel_rows):
    half = HALF
    coupling, solves = coupling[0], solves[0]
    local, row_count = coupling.shape
    panel = solves.shape[1]
    scen, rows = lax.axis_size("scen"), lax.axis_size("row")
    layers = scen // 2
    row, place = lax.axis_index("row"), lax.axis_index("scen")
    share = row_count // scen
    size = panel // (2 * rows)
    shape = pltpu.VMEM
    panel_row, diagonal_row = panel_rows[None, :], border_diagonal.T
    first_row = row * row_count + place * share
    picked, part_picked = shape((local, panel), BF16), shape((local // CHUNKS, panel), BF16)
    chunk_room = lambda count: [
        pltpu.VMEM((count, local // CHUNKS, row_count), BF16), pltpu.SemaphoreType.DMA((count,))
    ]
    room, done = chunk_room(FIRST)
    upper, lower = turn(solves, rows)
    chosen, far_chosen, entry, one, panel_row, diagonal_row = call(
        functools.partial(pick_kernel, rows),
        (
            picked, part_picked, shape((8, panel), F32), shape((row_count, panel), BF16),
            shape((1, panel), jnp.int32), shape((1, share), F32),
        ),
        panel_row, diagonal_row, coupling, remain=3, scratch=[room, pltpu.SemaphoreType.DMA((2,)), done],
    )
    pieces = gather_pieces(solves, upper, lower, (entry,))
    near, far = pieces[:6], pieces[6:]
    split = rows == 4 and share % 128 == 0
    chosen = call(
        functools.partial(rest_kernel, rows), picked, chosen, one, coupling, remain=1,
        scratch=chunk_room(CHUNKS - FIRST), aliases={0: 0},
    )
    other_chosen = swap(after(far_chosen, near[2], near[5]), "scen", 1) if split else None
    half_shape, room = shape((panel // 2, panel), F32), [pltpu.VMEM((panel // 2, panel), F32)]
    turned, own_near, send_near = call(
        functools.partial(early_kernel, rows),
        (shape((panel, local), BF16), half_shape, shape((panel // 2 + 8, panel), F32)),
        chosen, entry, *near, scratch=[pltpu.VMEM((panel, panel), F32)],
    )
    got_near = swap(send_near, "scen", 1)
    if split:
        far_send = call(select_kernel, shape(far[0].shape, BF16), far[0], far[1], micros=3.0)
        other_far = [swap(far_send, "scen", 1), other_chosen]
        own_far = [*far, far_chosen]
    else:
        other_far = own_far = []
    turned, keep, entry = call(
        functools.partial(keep_kernel, rows), (shape((panel, local), BF16), half_shape, shape((8, panel), F32)),
        turned, own_near, got_near, entry, *own_far, scratch=room, aliases={0: 0},
    )
    coded = shape((size + SHORT, panel), I16)
    codes = call(functools.partial(pair_kernel, rows), (coded,) * rows, keep, entry, *other_far, scratch=room)
    arrived = [swap(codes[k], "row", k) for k in [1, *range(rows - 1, 1, -1)]]
    part = codes[0]
    steps = bits_of(layers)
    if split:
        count = layers // 2
        bulk = shape((layers * panel, share), F32)
        halved = lambda count: (shape((count * panel, share), F32), shape((count * (panel + TAIL), share), I16))
        own, send_rows = call(
            schur_kernel, (bulk, bulk), panel_row, diagonal_row, coupling, after(turned, part), micros=2.0
        )
        part = call(sum_kernel, coded, after(part, own), *arrived, micros=10.0)
        got = swap(send_rows, "scen", 1)
    else:
        own, got = lax.psum_scatter(dot(turned, coupling), "scen", scatter_dimension=1, tiled=True), []
        mine = first_row + jnp.arange(share, dtype=jnp.int32)
        own = own + jnp.where(panel_rows[:, None] == mine[None, :], border_diagonal[:, 0][None, :], F32(0.0))
        part = call(sum_kernel, coded, part, *arrived)
    if split:
        others = [swap(part, "scen", 2 * k) for k in range(layers - 1, 0, -1)]
        own, bulk_codes = call(functools.partial(bulk_pair_kernel, panel), halved(count), after(own, part), got)
        part = call(sum_kernel, coded, after(part, bulk_codes), *others, micros=5.0)
    else:
        for bit in steps:
            part = call(sum_kernel, coded, part, swap(part, "scen", 2 * bit))
    shared = [swap(part, "row", k) for k in range(1, rows)]
    if split:
        for bit in steps[:-1]:
            count //= 2
            got = swap(bulk_codes, "scen", 2 * bit)
            own, bulk_codes = call(functools.partial(bulk_sum_kernel, panel), halved(count), own, got)
        got = [swap(bulk_codes, "scen", layers)]
    if split:
        part = after(part, bulk_codes)
    joined = call(join_kernel, shape((rows * (size + TAIL), panel), I16), part, *shared[::-1])
    other = swap(joined, "scen", 1)
    own_half = call(
        functools.partial(own_kernel, rows), shape((panel // 2, panel), F32), joined
    )
    inverse_first, inverse_second = call(
        functools.partial(newton_kernel, rows), (shape((half, half), F32), shape((half, panel), F32)),
        own_half, other, scratch=[pltpu.VMEM((panel, panel), F32)],
    )
    out = jax.ShapeDtypeStruct((share, 1, half), F32)
    return call(
        factor_kernel, (out, out),
        inverse_first, inverse_second, own, *got,
    )


def solution(mesh):
    placed = (P("scen", None, "row"), P("scen", "row", None), P("scen", "row"), P())
    return jax.shard_map(
        shards,
        mesh=mesh,
        in_specs=placed,
        out_specs=(P("scen", "row", None), P("scen", "row", None)),
        check_vma=False,
    )
```

```python
import functools

import jax
import jax.numpy as jnp
from jax import lax
from jax.experimental import pallas as pl
from jax.experimental.pallas import tpu as pltpu
from jax.sharding import PartitionSpec as P

HALF = 256
NEWTON = 8
TAIL = 16
SHORT = 8
CHUNKS = 4
LEVELS = 32000.0
F32 = jnp.float32
BF16 = jnp.bfloat16
I16 = jnp.int16


def halves(a):
    high = a.astype(BF16)
    low = (a - high.astype(F32)).astype(BF16)
    return high, low


def left_of(a):
    high, low = halves(a)
    return jnp.concatenate([high, high, low], axis=1)


def right_of(b):
    high, low = halves(b)
    return jnp.concatenate([high, low, high], axis=0)


def dot(a, b):
    return jnp.dot(a, b, preferred_element_type=F32)


def contract(a, b, dims):
    return lax.dot_general(a, b, (dims, ((), ())), preferred_element_type=F32)


def product(a, b):
    return dot(left_of(a), right_of(b))


def nearly(pivot):
    size = jnp.abs(pivot)
    turned = pivot.T
    square = product(turned, pivot)
    norm_one = jnp.max(jnp.sum(size, axis=0, keepdims=True))
    norm_inf = jnp.max(jnp.sum(size, axis=1, keepdims=True))
    scale = F32(1.0) / (norm_one * norm_inf)
    count = pivot.shape[0]
    one = lax.broadcasted_iota(jnp.int32, pivot.shape, 0) == lax.broadcasted_iota(jnp.int32, pivot.shape, 1)
    rest = jnp.where(one, F32(1.0), F32(0.0)) - square * scale
    approx = turned * scale
    for step in range(NEWTON - 2):
        both = product(rest, jnp.concatenate([rest, approx], axis=1))
        rest, approx = both[:, :count], approx + both[:, count:]
    return approx + product(rest, approx)


def newton_beside(pivot, beside):
    approx = nearly(pivot)
    count = pivot.shape[0]
    both = product(approx, jnp.concatenate([pivot, beside], axis=1))
    stacked = jnp.concatenate([approx, both[:, count:]], axis=1)
    return 2.0 * stacked - product(both[:, :count], stacked)


def whereabouts():
    place = lax.axis_index("scen")
    return lax.axis_index("row"), lax.rem(place, 2), lax.div(place, 2)


def aligned(index, size):
    return pl.multiple_of(index * size, size)


def encode(values, out_ref, base, tail_rows, diagonal=None):
    rows, lanes = values.shape
    top = jnp.maximum(jnp.max(jnp.abs(values), axis=0, keepdims=True), F32(1e-30))
    power = jnp.ceil(jnp.log2(top))
    unit = jnp.exp2(power)
    mantissa = jnp.ceil(top / unit * F32(16384.0))
    scale = mantissa * unit * F32(1.0 / (16384.0 * LEVELS))
    codes = jnp.round(values * (F32(1.0) / scale)).astype(jnp.int32)
    out_ref[base:base + rows, :] = codes.astype(I16)
    row = lax.broadcasted_iota(jnp.int32, (tail_rows, lanes), 0)
    tail = jnp.where(row == 0, power, jnp.where(row == 1, mantissa, F32(0.0)))
    if diagonal is not None:
        coarse = jnp.floor(diagonal * F32(64.0))
        fine = (diagonal * F32(64.0) - coarse) * F32(4096.0)
        tail = jnp.where(row == 2, coarse, jnp.where(row == 3, fine, tail))
    out_ref[base + rows:base + rows + tail_rows, :] = tail.astype(jnp.int32).astype(I16)


def decode(ref, base, rows, tail_rows):
    tail = ref[base + rows:base + rows + tail_rows, :].astype(jnp.int32).astype(F32)
    scale = tail[1:2] * jnp.exp2(tail[0:1]) * F32(1.0 / (16384.0 * LEVELS))
    diagonal = tail[2:3] * F32(1.0 / 64.0) + tail[3:4] * F32(1.0 / (64.0 * 4096.0))
    return ref[base:base + rows, :].astype(jnp.int32).astype(F32) * scale, diagonal


def turn_kernel(solves_ref, upper_ref, lower_ref, solves_copy, done):
    half = upper_ref.shape[0]
    copies = [
        pltpu.make_async_copy(solves_ref.at[:, pl.ds(i * half, half)], solves_copy.at[i], done.at[i]) for i in (0, 1)
    ]
    for copy in copies:
        copy.start()
    same = lax.broadcasted_iota(jnp.int32, (half, half), 0) == lax.broadcasted_iota(jnp.int32, (half, half), 1)
    one = jnp.where(same, F32(1.0), F32(0.0)).astype(BF16)
    for i, out_ref in enumerate((upper_ref, lower_ref)):
        copies[i].wait()
        out_ref[...] = contract(one, solves_copy[i], ((1,), (1,))).astype(BF16)


def order_of(rows):
    row = lax.axis_index("row")
    return [row ^ 3, row, row ^ 1, row ^ 2] if rows == 4 else list(range(CHUNKS))


def fetch(source_ref, target_ref, done, blocks):
    size = target_ref.shape[1]
    copies = [
        pltpu.make_async_copy(source_ref.at[pl.ds(aligned(block, size), size), :], target_ref.at[i], done.at[i])
        for i, block in enumerate(blocks)
    ]
    for copy in copies:
        copy.start()
    return copies


def pick_kernel(
    rows, panel_ref, own_diagonal_ref, coupling_ref,
    chosen_ref, far_ref, entry_ref, one_ref, panel_out, diagonal_out, coupling_copy, small_done, done,
):
    small = [
        pltpu.make_async_copy(panel_ref, panel_out, small_done.at[0]),
        pltpu.make_async_copy(own_diagonal_ref, diagonal_out, small_done.at[1]),
    ]
    for copy in small:
        copy.start()
    block = order_of(rows)[0]
    copies = fetch(coupling_ref, coupling_copy, done, [block])
    for copy in small:
        copy.wait()
    columns, panel = one_ref.shape
    share = diagonal_out.shape[1]
    first_column = lax.axis_index("row") * columns
    first_row = first_column + lax.axis_index("scen") * share
    here = panel_out[...] - first_column == lax.broadcasted_iota(jnp.int32, (columns, panel), 0)
    one_ref[...] = jnp.where(here, F32(1.0), F32(0.0)).astype(BF16)
    owned = panel_out[...] - first_row == lax.broadcasted_iota(jnp.int32, (share, panel), 0)
    own = jnp.broadcast_to(diagonal_out[...], (8, share)).T[:, :1]
    entry = jnp.sum(jnp.where(owned, own, F32(0.0)), axis=0, keepdims=True)
    entry_ref[...] = jnp.broadcast_to(entry, entry_ref.shape)
    copies[0].wait()
    size = far_ref.shape[0]
    far_ref[...] = dot(coupling_copy[0], one_ref[...]).astype(BF16)
    chosen_ref[pl.ds(aligned(block, size), size), :] = far_ref[...]


def rest_kernel(rows, chosen_in, one_ref, coupling_ref, chosen_ref, coupling_copy, done):
    blocks = order_of(rows)[1:]
    size = coupling_copy.shape[1]
    for i, copy in enumerate(fetch(coupling_ref, coupling_copy, done, blocks)):
        copy.wait()
        chosen_ref[pl.ds(aligned(blocks[i], size), size), :] = dot(coupling_copy[i], one_ref[...]).astype(BF16)


def early_kernel(rows, chosen_ref, entry_ref, *refs):
    *pieces, turned_ref, own_ref, send_ref, terms_ref = refs
    row, core, _ = whereabouts()
    if len(pieces) == 1:
        turned_ref[...] = pieces[0][...]
    else:
        half, width = pieces[0].shape
        for i, piece in enumerate(pieces):
            start = aligned(row ^ (i // 2), width)
            turned_ref[i % 2 * half:(i % 2 + 1) * half, pl.ds(start, width)] = piece[...]
        start = aligned(row ^ (len(pieces) // 2), width)
        turned_ref[:, pl.ds(start, width)] = jnp.zeros((2 * half, width), BF16)
    terms_ref[...] = dot(turned_ref[...], chosen_ref[...])
    size = own_ref.shape[0] // rows
    for out_ref, whose in ((own_ref, core), (send_ref, 1 - core)):
        for k in range(rows):
            out_ref[k * size:(k + 1) * size, :] = terms_ref[pl.ds(aligned(whose * rows + (row ^ k), size), size), :]
    send_ref[rows * size:, :] = entry_ref[...]


def select_kernel(upper_ref, lower_ref, out_ref):
    out_ref[...] = jnp.where(whereabouts()[1] == 0, lower_ref[...], upper_ref[...])


def add_far(rows, block, chosen, far_ref):
    row = lax.axis_index("row")
    size = far_ref.shape[0] // rows
    far_ref[...] = dot(block, chosen)
    return [far_ref[pl.ds(aligned(row ^ k, size), size), :] for k in range(rows)]


def keep_kernel(rows, turned_in, own_ref, got_ref, entry_ref, *refs):
    *far, turned_ref, keep_ref, both_ref, far_ref = refs
    row, core, _ = whereabouts()
    half = keep_ref.shape[0]
    size = half // rows
    both_ref[...] = jnp.broadcast_to(entry_ref[:1, :] + got_ref[half:half + 1, :], both_ref.shape)
    keep_ref[...] = own_ref[...] + got_ref[:half, :]
    if far:
        upper_ref, lower_ref, chosen_ref = far
        width = upper_ref.shape[1]
        start = aligned(row ^ (rows - 1), width)
        turned_ref[:half, pl.ds(start, width)] = upper_ref[...]
        turned_ref[half:, pl.ds(start, width)] = lower_ref[...]
        block = jnp.where(core == 0, upper_ref[...], lower_ref[...])
        for k, piece in enumerate(add_far(rows, block, chosen_ref[...], far_ref)):
            keep_ref[k * size:(k + 1) * size, :] += piece


def pair_kernel(rows, keep_ref, entry_ref, *refs):
    *far, far_ref = refs
    far, out_refs = far[:-rows], far[-rows:]
    size = keep_ref.shape[0] // rows
    pieces = add_far(rows, far[0][...], far[1][...], far_ref) if far else None
    for k, out_ref in enumerate(out_refs):
        value = keep_ref[k * size:(k + 1) * size, :]
        encode(value + pieces[k] if far else value, out_ref, 0, SHORT, entry_ref[:1, :])


def sum_kernel(*refs):
    *in_refs, out_ref = refs
    size = out_ref.shape[0] - SHORT
    parts = [decode(ref, 0, size, SHORT) for ref in in_refs]
    encode(sum(p[0] for p in parts), out_ref, 0, SHORT, sum(p[1] for p in parts))


def join_kernel(*refs):
    *in_refs, out_ref = refs
    size = in_refs[0].shape[0] - SHORT
    for k, ref in enumerate(in_refs[:1] + in_refs[:0:-1]):
        start = k * (size + TAIL)
        out_ref[start:start + size, :] = ref[:size, :]
        tail = ref[size:, :].astype(jnp.int32)
        out_ref[start + size:start + size + TAIL, :] = jnp.concatenate([tail, jnp.zeros_like(tail)], axis=0).astype(I16)


def place_pieces(row, whose, ref, pivots_ref, rows, base):
    panel = pivots_ref.shape[1]
    size = panel // (2 * rows)
    index = lax.broadcasted_iota(jnp.int32, (size, panel), 1)
    for k in range(rows):
        start = aligned(whose * rows + (row ^ k), size)
        values, diagonal = decode(ref, k * (size + TAIL), size, TAIL)
        at = lax.broadcasted_iota(jnp.int32, (size, panel), 0) + start == index
        pivots_ref[pl.ds(start - base, size), :] = values + jnp.where(at, diagonal, F32(0.0))


def own_kernel(rows, own_ref, half_ref):
    row, core, _ = whereabouts()
    place_pieces(row, core, own_ref, half_ref, rows, core * half_ref.shape[0])


def newton_kernel(rows, half_ref, other_ref, inverse_ref, second_ref, pivots_ref):
    row, core, _ = whereabouts()
    half = half_ref.shape[0]
    pivots_ref[pl.ds(aligned(core, half), half), :] = half_ref[...]
    place_pieces(row, 1 - core, other_ref, pivots_ref, rows, 0)
    both = newton_beside(pivots_ref[:half, :half], pivots_ref[:half, half:])
    inverse_first = both[:, :half]
    inverse_ref[...] = inverse_first
    corner = pivots_ref[half:, :half]
    pivot = pivots_ref[half:, half:] - product(corner, both[:, half:])
    second_ref[...] = newton_beside(pivot, -product(corner, inverse_first))


def schur_kernel(panel_ref, own_diagonal_ref, coupling_ref, turned_ref, keep_ref, send_ref):
    row, core, layer = whereabouts()
    panel, share = turned_ref.shape[0], keep_ref.shape[1]
    first_row = row * coupling_ref.shape[1] + (2 * layer + core) * share
    layers = keep_ref.shape[0] // panel
    for position, k in enumerate(reversed_order(layers)):
        start = aligned(layer ^ k, 2 * share)
        both = dot(turned_ref[...], coupling_ref[:, pl.ds(start, 2 * share)])
        rows = slice(position * panel, (position + 1) * panel)
        one, two = both[:, :share], both[:, share:]
        kept = jnp.where(core == 0, one, two)
        if position == 0:
            wanted = jnp.broadcast_to(panel_ref[...].astype(F32), (share, panel)).T.astype(jnp.int32)
            here = wanted - first_row == lax.broadcasted_iota(jnp.int32, (panel, share), 1)
            kept = kept + jnp.where(here, own_diagonal_ref[...], F32(0.0))
        keep_ref[rows, :] = kept
        send_ref[rows, :] = jnp.where(core == 0, two, one)


def bulk_pair_kernel(panel, keep_ref, got_ref, own_ref, coded_ref):
    half = own_ref.shape[0]
    own_ref[...] = keep_ref[:half, :] + got_ref[:half, :]
    for i in range(half // panel):
        part = slice(half + i * panel, half + (i + 1) * panel)
        encode(keep_ref[part, :] + got_ref[part, :], coded_ref, i * (panel + TAIL), TAIL)


def bulk_sum_kernel(panel, keep_ref, got_ref, own_ref, coded_ref):
    half = own_ref.shape[0]
    for i in range(keep_ref.shape[0] // panel):
        value = keep_ref[i * panel:(i + 1) * panel, :] + decode(got_ref, i * (panel + TAIL), panel, TAIL)[0]
        if i * panel < half:
            own_ref[i * panel:(i + 1) * panel, :] = value
        else:
            encode(value, coded_ref, (i - half // panel) * (panel + TAIL), TAIL)


def factor_kernel(inverse_first_ref, inverse_second_ref, rows_ref, *refs):
    *got, first_out, second_out = refs
    panel = rows_ref.shape[0]
    half = panel // 2
    rows = rows_ref[...]
    for ref in got:
        rows = rows + decode(ref, 0, panel, TAIL)[0]
    first, second = rows[:half], rows[half:]
    first_out[...] = product(inverse_first_ref[...], first).T[:, None, :]
    second_out[...] = product(inverse_second_ref[...], jnp.concatenate([second, first], axis=0)).T[:, None, :]


def call(kernel, out_shape, *args, scratch=(), remain=0, micros=0.0, aliases=None):
    hbm = pl.BlockSpec(memory_space=pltpu.HBM)
    vmem = pl.BlockSpec(memory_space=pltpu.VMEM)
    stay = len(args) - remain
    args = args[:stay] + tuple(pltpu.with_memory_space_constraint(x, pltpu.HBM) for x in args[stay:])
    return pl.pallas_call(
        kernel,
        name=getattr(kernel, "func", kernel).__name__,
        out_shape=out_shape,
        in_specs=[vmem] * (len(args) - remain) + [hbm] * remain,
        out_specs=jax.tree.map(lambda _: vmem, out_shape),
        scratch_shapes=scratch,
        input_output_aliases=aliases or {},
        compiler_params=pltpu.CompilerParams(vmem_limit_bytes=12 << 20),
        cost_estimate=pl.CostEstimate(flops=int(micros * 1.15e9), bytes_accessed=1024, transcendentals=0),
    )(*args)


def swap(x, axis, bit):
    count = lax.axis_size(axis)
    return lax.ppermute(x, axis, [(i, i ^ bit) for i in range(count)])


def after(x, *others):
    return lax.optimization_barrier((x,) + others)[0]


def bits_of(count):
    return [1 << i for i in range(count.bit_length() - 1)]


def reversed_order(count):
    width = count.bit_length() - 1
    return [int(f"{p:0{width}b}"[::-1], 2) for p in range(count)]


def turn(solves, rows):
    block, panel = solves.shape
    if rows != 4:
        return None, None
    half = pltpu.VMEM((panel // 2, block), BF16)
    return call(
        turn_kernel, (half, half), solves, remain=1,
        scratch=[pltpu.VMEM((2, block, panel // 2), BF16), pltpu.SemaphoreType.DMA((2,))],
    )


def gather_pieces(solves, upper, lower, ready):
    if upper is None:
        return [lax.all_gather(solves.T, "row", axis=1, tiled=True)]
    lower_x, upper_y = swap(lower, "row", 1), swap(upper, "row", 2)
    upper_x, lower_y = swap(upper, "row", 1), swap(lower, "row", 2)
    upper_far, lower_far = swap(after(upper_y, *ready), "row", 1), swap(after(lower_x, *ready), "row", 2)
    return [upper, lower, upper_x, lower_x, upper_y, lower_y, upper_far, lower_far]


def shards(coupling, solves, border_diagonal, panel_rows):
    half = HALF
    coupling, solves = coupling[0], solves[0]
    local, row_count = coupling.shape
    panel = solves.shape[1]
    scen, rows = lax.axis_size("scen"), lax.axis_size("row")
    layers = scen // 2
    row, place = lax.axis_index("row"), lax.axis_index("scen")
    share = row_count // scen
    size = panel // (2 * rows)
    shape = pltpu.VMEM
    panel_row, diagonal_row = panel_rows[None, :], border_diagonal.T
    first_row = row * row_count + place * share
    picked, part_picked = shape((local, panel), BF16), shape((local // CHUNKS, panel), BF16)
    chunk_room = lambda count: [
        pltpu.VMEM((count, local // CHUNKS, row_count), BF16), pltpu.SemaphoreType.DMA((count,))
    ]
    room, done = chunk_room(1)
    upper, lower = turn(solves, rows)
    chosen, far_chosen, entry, one, panel_row, diagonal_row = call(
        functools.partial(pick_kernel, rows),
        (
            picked, part_picked, shape((8, panel), F32), shape((row_count, panel), BF16),
            shape((1, panel), jnp.int32), shape((1, share), F32),
        ),
        panel_row, diagonal_row, coupling, remain=3, scratch=[room, pltpu.SemaphoreType.DMA((2,)), done],
    )
    pieces = gather_pieces(solves, upper, lower, (entry,))
    near, far = pieces[:6], pieces[6:]
    split = rows == 4 and share % 128 == 0
    chosen = call(
        functools.partial(rest_kernel, rows), picked, chosen, one, coupling, remain=1,
        scratch=chunk_room(CHUNKS - 1), aliases={0: 0},
    )
    other_chosen = swap(after(far_chosen, near[2], near[5]), "scen", 1) if split else None
    half_shape, room = shape((panel // 2, panel), F32), [pltpu.VMEM((panel // 2, panel), F32)]
    turned, own_near, send_near = call(
        functools.partial(early_kernel, rows),
        (shape((panel, local), BF16), half_shape, shape((panel // 2 + 8, panel), F32)),
        chosen, entry, *near, scratch=[pltpu.VMEM((panel, panel), F32)],
    )
    got_near = swap(send_near, "scen", 1)
    if split:
        far_send = call(select_kernel, shape(far[0].shape, BF16), far[0], far[1], micros=3.0)
        other_far = [swap(far_send, "scen", 1), other_chosen]
        own_far = [*far, far_chosen]
    else:
        other_far = own_far = []
    turned, keep, entry = call(
        functools.partial(keep_kernel, rows), (shape((panel, local), BF16), half_shape, shape((8, panel), F32)),
        turned, own_near, got_near, entry, *own_far, scratch=room, aliases={0: 0},
    )
    coded = shape((size + SHORT, panel), I16)
    codes = call(functools.partial(pair_kernel, rows), (coded,) * rows, keep, entry, *other_far, scratch=room)
    arrived = [swap(codes[k], "row", k) for k in [1, *range(rows - 1, 1, -1)]]
    part = codes[0]
    steps = bits_of(layers)
    if split:
        count = layers // 2
        bulk = shape((layers * panel, share), F32)
        halved = lambda count: (shape((count * panel, share), F32), shape((count * (panel + TAIL), share), I16))
        own, send_rows = call(
            schur_kernel, (bulk, bulk), panel_row, diagonal_row, coupling, after(turned, part), micros=2.0
        )
        part = call(sum_kernel, coded, after(part, own), *arrived, micros=10.0)
        got = swap(send_rows, "scen", 1)
    else:
        own, got = lax.psum_scatter(dot(turned, coupling), "scen", scatter_dimension=1, tiled=True), []
        mine = first_row + jnp.arange(share, dtype=jnp.int32)
        own = own + jnp.where(panel_rows[:, None] == mine[None, :], border_diagonal[:, 0][None, :], F32(0.0))
        part = call(sum_kernel, coded, part, *arrived)
    if split:
        others = [swap(part, "scen", 2 * k) for k in range(layers - 1, 0, -1)]
        own, bulk_codes = call(functools.partial(bulk_pair_kernel, panel), halved(count), after(own, part), got)
        part = call(sum_kernel, coded, after(part, bulk_codes), *others, micros=5.0)
    else:
        for bit in steps:
            part = call(sum_kernel, coded, part, swap(part, "scen", 2 * bit))
    shared = [swap(part, "row", k) for k in range(1, rows)]
    if split:
        for bit in steps[:-1]:
            count //= 2
            got = swap(bulk_codes, "scen", 2 * bit)
            own, bulk_codes = call(functools.partial(bulk_sum_kernel, panel), halved(count), own, got)
        got = [swap(bulk_codes, "scen", layers)]
    if split:
        part = after(part, bulk_codes)
    joined = call(join_kernel, shape((rows * (size + TAIL), panel), I16), part, *shared[::-1])
    other = swap(joined, "scen", 1)
    own_half = call(
        functools.partial(own_kernel, rows), shape((panel // 2, panel), F32), joined
    )
    inverse_first, inverse_second = call(
        functools.partial(newton_kernel, rows), (shape((half, half), F32), shape((half, panel), F32)),
        own_half, other, scratch=[pltpu.VMEM((panel, panel), F32)],
    )
    out = jax.ShapeDtypeStruct((share, 1, half), F32)
    return call(
        factor_kernel, (out, out),
        inverse_first, inverse_second, own, *got,
    )


def solution(mesh):
    placed = (P("scen", None, "row"), P("scen", "row", None), P("scen", "row"), P())
    return jax.shard_map(
        shards,
        mesh=mesh,
        in_specs=placed,
        out_specs=(P("scen", "row", None), P("scen", "row", None)),
        check_vma=False,
    )
```

```python
import functools

import jax
import jax.numpy as jnp
from jax import lax
from jax.experimental import pallas as pl
from jax.experimental.pallas import tpu as pltpu
from jax.sharding import PartitionSpec as P

HALF = 256
NEWTON = 8
TAIL = 16
SHORT = 8
CHUNKS = 4
LEVELS = 32000.0
F32 = jnp.float32
BF16 = jnp.bfloat16
I16 = jnp.int16


def halves(a):
    high = a.astype(BF16)
    low = (a - high.astype(F32)).astype(BF16)
    return high, low


def left_of(a):
    high, low = halves(a)
    return jnp.concatenate([high, high, low], axis=1)


def right_of(b):
    high, low = halves(b)
    return jnp.concatenate([high, low, high], axis=0)


def dot(a, b):
    return jnp.dot(a, b, preferred_element_type=F32)


def product(a, b):
    return dot(left_of(a), right_of(b))


def nearly(pivot):
    size = jnp.abs(pivot)
    turned = pivot.T
    square = product(turned, pivot)
    norm_one = jnp.max(jnp.sum(size, axis=0, keepdims=True))
    norm_inf = jnp.max(jnp.sum(size, axis=1, keepdims=True))
    scale = F32(1.0) / (norm_one * norm_inf)
    count = pivot.shape[0]
    one = lax.broadcasted_iota(jnp.int32, pivot.shape, 0) == lax.broadcasted_iota(jnp.int32, pivot.shape, 1)
    rest = jnp.where(one, F32(1.0), F32(0.0)) - square * scale
    approx = turned * scale
    for step in range(NEWTON - 2):
        both = product(rest, jnp.concatenate([rest, approx], axis=1))
        rest, approx = both[:, :count], approx + both[:, count:]
    return approx + product(rest, approx)


def newton_beside(pivot, beside):
    approx = nearly(pivot)
    count = pivot.shape[0]
    both = product(approx, jnp.concatenate([pivot, beside], axis=1))
    stacked = jnp.concatenate([approx, both[:, count:]], axis=1)
    return 2.0 * stacked - product(both[:, :count], stacked)


def whereabouts():
    place = lax.axis_index("scen")
    return lax.axis_index("row"), lax.rem(place, 2), lax.div(place, 2)


def aligned(index, size):
    return pl.multiple_of(index * size, size)


def encode(values, out_ref, base, tail_rows, diagonal=None):
    rows, lanes = values.shape
    top = jnp.maximum(jnp.max(jnp.abs(values), axis=0, keepdims=True), F32(1e-30))
    power = jnp.ceil(jnp.log2(top))
    unit = jnp.exp2(power)
    mantissa = jnp.ceil(top / unit * F32(16384.0))
    scale = mantissa * unit * F32(1.0 / (16384.0 * LEVELS))
    codes = jnp.round(values * (F32(1.0) / scale)).astype(jnp.int32)
    out_ref[base:base + rows, :] = codes.astype(I16)
    row = lax.broadcasted_iota(jnp.int32, (tail_rows, lanes), 0)
    tail = jnp.where(row == 0, power, jnp.where(row == 1, mantissa, F32(0.0)))
    if diagonal is not None:
        coarse = jnp.floor(diagonal * F32(64.0))
        fine = (diagonal * F32(64.0) - coarse) * F32(4096.0)
        tail = jnp.where(row == 2, coarse, jnp.where(row == 3, fine, tail))
    out_ref[base + rows:base + rows + tail_rows, :] = tail.astype(jnp.int32).astype(I16)


def decode(ref, base, rows, tail_rows):
    tail = ref[base + rows:base + rows + tail_rows, :].astype(jnp.int32).astype(F32)
    scale = tail[1:2] * jnp.exp2(tail[0:1]) * F32(1.0 / (16384.0 * LEVELS))
    diagonal = tail[2:3] * F32(1.0 / 64.0) + tail[3:4] * F32(1.0 / (64.0 * 4096.0))
    return ref[base:base + rows, :].astype(jnp.int32).astype(F32) * scale, diagonal


def turn_kernel(solves_ref, upper_ref, lower_ref, solves_copy, done):
    half = upper_ref.shape[0]
    copies = [
        pltpu.make_async_copy(solves_ref.at[:, pl.ds(i * half, half)], solves_copy.at[i], done.at[i]) for i in (0, 1)
    ]
    for copy in copies:
        copy.start()
    for i, out_ref in enumerate((upper_ref, lower_ref)):
        copies[i].wait()
        out_ref[...] = solves_copy[i].T


def order_of(rows):
    row = lax.axis_index("row")
    return [row ^ 3, row, row ^ 1, row ^ 2] if rows == 4 else list(range(CHUNKS))


def fetch(source_ref, target_ref, done, blocks):
    size = target_ref.shape[1]
    copies = [
        pltpu.make_async_copy(source_ref.at[pl.ds(aligned(block, size), size), :], target_ref.at[i], done.at[i])
        for i, block in enumerate(blocks)
    ]
    for copy in copies:
        copy.start()
    return copies


def pick_kernel(
    rows, panel_ref, own_diagonal_ref, coupling_ref,
    chosen_ref, far_ref, entry_ref, one_ref, panel_out, diagonal_out, coupling_copy, small_done, done,
):
    small = [
        pltpu.make_async_copy(panel_ref, panel_out, small_done.at[0]),
        pltpu.make_async_copy(own_diagonal_ref, diagonal_out, small_done.at[1]),
    ]
    for copy in small:
        copy.start()
    block = order_of(rows)[0]
    copies = fetch(coupling_ref, coupling_copy, done, [block])
    for copy in small:
        copy.wait()
    columns, panel = one_ref.shape
    share = diagonal_out.shape[1]
    first_column = lax.axis_index("row") * columns
    first_row = first_column + lax.axis_index("scen") * share
    here = panel_out[...] - first_column == lax.broadcasted_iota(jnp.int32, (columns, panel), 0)
    one_ref[...] = jnp.where(here, F32(1.0), F32(0.0)).astype(BF16)
    owned = panel_out[...] - first_row == lax.broadcasted_iota(jnp.int32, (share, panel), 0)
    own = jnp.broadcast_to(diagonal_out[...], (8, share)).T[:, :1]
    entry = jnp.sum(jnp.where(owned, own, F32(0.0)), axis=0, keepdims=True)
    entry_ref[...] = jnp.broadcast_to(entry, entry_ref.shape)
    copies[0].wait()
    size = far_ref.shape[0]
    far_ref[...] = dot(coupling_copy[0], one_ref[...]).astype(BF16)
    chosen_ref[pl.ds(aligned(block, size), size), :] = far_ref[...]


def rest_kernel(rows, chosen_in, one_ref, coupling_ref, chosen_ref, coupling_copy, done):
    blocks = order_of(rows)[1:]
    size = coupling_copy.shape[1]
    for i, copy in enumerate(fetch(coupling_ref, coupling_copy, done, blocks)):
        copy.wait()
        chosen_ref[pl.ds(aligned(blocks[i], size), size), :] = dot(coupling_copy[i], one_ref[...]).astype(BF16)


def early_kernel(rows, chosen_ref, entry_ref, *refs):
    *pieces, turned_ref, own_ref, send_ref, terms_ref = refs
    row, core, _ = whereabouts()
    if len(pieces) == 1:
        turned_ref[...] = pieces[0][...]
    else:
        half, width = pieces[0].shape
        for i, piece in enumerate(pieces):
            start = aligned(row ^ (i // 2), width)
            turned_ref[i % 2 * half:(i % 2 + 1) * half, pl.ds(start, width)] = piece[...]
        start = aligned(row ^ (len(pieces) // 2), width)
        turned_ref[:, pl.ds(start, width)] = jnp.zeros((2 * half, width), BF16)
    terms_ref[...] = dot(turned_ref[...], chosen_ref[...])
    size = own_ref.shape[0] // rows
    for out_ref, whose in ((own_ref, core), (send_ref, 1 - core)):
        for k in range(rows):
            out_ref[k * size:(k + 1) * size, :] = terms_ref[pl.ds(aligned(whose * rows + (row ^ k), size), size), :]
    send_ref[rows * size:, :] = entry_ref[...]


def select_kernel(upper_ref, lower_ref, out_ref):
    out_ref[...] = jnp.where(whereabouts()[1] == 0, lower_ref[...], upper_ref[...])


def add_far(rows, block, chosen, far_ref):
    row = lax.axis_index("row")
    size = far_ref.shape[0] // rows
    far_ref[...] = dot(block, chosen)
    return [far_ref[pl.ds(aligned(row ^ k, size), size), :] for k in range(rows)]


def keep_kernel(rows, turned_in, own_ref, got_ref, entry_ref, *refs):
    *far, turned_ref, keep_ref, both_ref, far_ref = refs
    row, core, _ = whereabouts()
    half = keep_ref.shape[0]
    size = half // rows
    both_ref[...] = jnp.broadcast_to(entry_ref[:1, :] + got_ref[half:half + 1, :], both_ref.shape)
    keep_ref[...] = own_ref[...] + got_ref[:half, :]
    if far:
        upper_ref, lower_ref, chosen_ref = far
        width = upper_ref.shape[1]
        start = aligned(row ^ (rows - 1), width)
        turned_ref[:half, pl.ds(start, width)] = upper_ref[...]
        turned_ref[half:, pl.ds(start, width)] = lower_ref[...]
        block = jnp.where(core == 0, upper_ref[...], lower_ref[...])
        for k, piece in enumerate(add_far(rows, block, chosen_ref[...], far_ref)):
            keep_ref[k * size:(k + 1) * size, :] += piece


def pair_kernel(rows, keep_ref, entry_ref, *refs):
    *far, far_ref = refs
    far, out_refs = far[:-rows], far[-rows:]
    size = keep_ref.shape[0] // rows
    pieces = add_far(rows, far[0][...], far[1][...], far_ref) if far else None
    for k, out_ref in enumerate(out_refs):
        value = keep_ref[k * size:(k + 1) * size, :]
        encode(value + pieces[k] if far else value, out_ref, 0, SHORT, entry_ref[:1, :])


def sum_kernel(*refs):
    *in_refs, out_ref = refs
    size = out_ref.shape[0] - SHORT
    parts = [decode(ref, 0, size, SHORT) for ref in in_refs]
    encode(sum(p[0] for p in parts), out_ref, 0, SHORT, sum(p[1] for p in parts))


def join_kernel(*refs):
    *in_refs, out_ref = refs
    size = in_refs[0].shape[0] - SHORT
    for k, ref in enumerate(in_refs[:1] + in_refs[:0:-1]):
        start = k * (size + TAIL)
        out_ref[start:start + size, :] = ref[:size, :]
        tail = ref[size:, :].astype(jnp.int32)
        out_ref[start + size:start + size + TAIL, :] = jnp.concatenate([tail, jnp.zeros_like(tail)], axis=0).astype(I16)


def place_pieces(row, whose, ref, pivots_ref, rows, base):
    panel = pivots_ref.shape[1]
    size = panel // (2 * rows)
    index = lax.broadcasted_iota(jnp.int32, (size, panel), 1)
    for k in range(rows):
        start = aligned(whose * rows + (row ^ k), size)
        values, diagonal = decode(ref, k * (size + TAIL), size, TAIL)
        at = lax.broadcasted_iota(jnp.int32, (size, panel), 0) + start == index
        pivots_ref[pl.ds(start - base, size), :] = values + jnp.where(at, diagonal, F32(0.0))


def own_kernel(rows, own_ref, half_ref):
    row, core, _ = whereabouts()
    place_pieces(row, core, own_ref, half_ref, rows, core * half_ref.shape[0])


def newton_kernel(rows, half_ref, other_ref, inverse_ref, second_ref, pivots_ref):
    row, core, _ = whereabouts()
    half = half_ref.shape[0]
    pivots_ref[pl.ds(aligned(core, half), half), :] = half_ref[...]
    place_pieces(row, 1 - core, other_ref, pivots_ref, rows, 0)
    both = newton_beside(pivots_ref[:half, :half], pivots_ref[:half, half:])
    inverse_first = both[:, :half]
    inverse_ref[...] = left_of(inverse_first)
    corner = pivots_ref[half:, :half]
    pivot = pivots_ref[half:, half:] - product(corner, both[:, half:])
    second_ref[...] = left_of(newton_beside(pivot, -product(corner, inverse_first)))


def schur_kernel(panel_ref, own_diagonal_ref, coupling_ref, turned_ref, keep_ref, send_ref):
    row, core, layer = whereabouts()
    panel, share = turned_ref.shape[0], keep_ref.shape[1]
    first_row = row * coupling_ref.shape[1] + (2 * layer + core) * share
    layers = keep_ref.shape[0] // panel
    for position, k in enumerate(reversed_order(layers)):
        start = aligned(layer ^ k, 2 * share)
        both = dot(turned_ref[...], coupling_ref[:, pl.ds(start, 2 * share)])
        rows = slice(position * panel, (position + 1) * panel)
        one, two = both[:, :share], both[:, share:]
        kept = jnp.where(core == 0, one, two)
        if position == 0:
            wanted = jnp.broadcast_to(panel_ref[...].astype(F32), (share, panel)).T.astype(jnp.int32)
            here = wanted - first_row == lax.broadcasted_iota(jnp.int32, (panel, share), 1)
            kept = kept + jnp.where(here, own_diagonal_ref[...], F32(0.0))
        keep_ref[rows, :] = kept
        send_ref[rows, :] = jnp.where(core == 0, two, one)


def bulk_pair_kernel(panel, keep_ref, got_ref, own_ref, coded_ref):
    half = own_ref.shape[0]
    own_ref[...] = keep_ref[:half, :] + got_ref[:half, :]
    for i in range(half // panel):
        part = slice(half + i * panel, half + (i + 1) * panel)
        encode(keep_ref[part, :] + got_ref[part, :], coded_ref, i * (panel + TAIL), TAIL)


def bulk_sum_kernel(panel, keep_ref, got_ref, own_ref, coded_ref):
    half = own_ref.shape[0]
    for i in range(keep_ref.shape[0] // panel):
        value = keep_ref[i * panel:(i + 1) * panel, :] + decode(got_ref, i * (panel + TAIL), panel, TAIL)[0]
        if i * panel < half:
            own_ref[i * panel:(i + 1) * panel, :] = value
        else:
            encode(value, coded_ref, (i - half // panel) * (panel + TAIL), TAIL)


def factor_kernel(inverse_first_ref, inverse_second_ref, rows_ref, *refs):
    *got, first_out, second_out = refs
    panel = rows_ref.shape[0]
    half = panel // 2
    rows = rows_ref[...]
    for ref in got:
        rows = rows + decode(ref, 0, panel, TAIL)[0]
    first, second = rows[:half], rows[half:]
    first_out[...] = dot(inverse_first_ref[...], right_of(first)).T[:, None, :]
    second_out[...] = dot(inverse_second_ref[...], right_of(jnp.concatenate([second, first], axis=0))).T[:, None, :]


def call(kernel, out_shape, *args, scratch=(), remain=0, micros=0.0, aliases=None):
    hbm = pl.BlockSpec(memory_space=pltpu.HBM)
    vmem = pl.BlockSpec(memory_space=pltpu.VMEM)
    stay = len(args) - remain
    args = args[:stay] + tuple(pltpu.with_memory_space_constraint(x, pltpu.HBM) for x in args[stay:])
    return pl.pallas_call(
        kernel,
        name=getattr(kernel, "func", kernel).__name__,
        out_shape=out_shape,
        in_specs=[vmem] * (len(args) - remain) + [hbm] * remain,
        out_specs=jax.tree.map(lambda _: vmem, out_shape),
        scratch_shapes=scratch,
        input_output_aliases=aliases or {},
        compiler_params=pltpu.CompilerParams(vmem_limit_bytes=12 << 20),
        cost_estimate=pl.CostEstimate(flops=int(micros * 1.15e9), bytes_accessed=1024, transcendentals=0),
    )(*args)


def swap(x, axis, bit):
    count = lax.axis_size(axis)
    return lax.ppermute(x, axis, [(i, i ^ bit) for i in range(count)])


def after(x, *others):
    return lax.optimization_barrier((x,) + others)[0]


def bits_of(count):
    return [1 << i for i in range(count.bit_length() - 1)]


def reversed_order(count):
    width = count.bit_length() - 1
    return [int(f"{p:0{width}b}"[::-1], 2) for p in range(count)]


def turn(solves, rows):
    block, panel = solves.shape
    if rows != 4:
        return None, None
    half = pltpu.VMEM((panel // 2, block), BF16)
    return call(
        turn_kernel, (half, half), solves, remain=1,
        scratch=[pltpu.VMEM((2, block, panel // 2), BF16), pltpu.SemaphoreType.DMA((2,))],
    )


def gather_pieces(solves, upper, lower, ready):
    if upper is None:
        return [lax.all_gather(solves.T, "row", axis=1, tiled=True)]
    lower_x, upper_y = swap(lower, "row", 1), swap(upper, "row", 2)
    upper_x, lower_y = swap(upper, "row", 1), swap(lower, "row", 2)
    upper_far, lower_far = swap(after(upper_y, *ready), "row", 1), swap(after(lower_x, *ready), "row", 2)
    return [upper, lower, upper_x, lower_x, upper_y, lower_y, upper_far, lower_far]


def shards(coupling, solves, border_diagonal, panel_rows):
    half = HALF
    coupling, solves = coupling[0], solves[0]
    local, row_count = coupling.shape
    panel = solves.shape[1]
    scen, rows = lax.axis_size("scen"), lax.axis_size("row")
    layers = scen // 2
    row, place = lax.axis_index("row"), lax.axis_index("scen")
    share = row_count // scen
    size = panel // (2 * rows)
    shape = pltpu.VMEM
    panel_row, diagonal_row = panel_rows[None, :], border_diagonal.T
    first_row = row * row_count + place * share
    picked, part_picked = shape((local, panel), BF16), shape((local // CHUNKS, panel), BF16)
    chunk_room = lambda count: [
        pltpu.VMEM((count, local // CHUNKS, row_count), BF16), pltpu.SemaphoreType.DMA((count,))
    ]
    room, done = chunk_room(1)
    upper, lower = turn(solves, rows)
    chosen, far_chosen, entry, one, panel_row, diagonal_row = call(
        functools.partial(pick_kernel, rows),
        (
            picked, part_picked, shape((8, panel), F32), shape((row_count, panel), BF16),
            shape((1, panel), jnp.int32), shape((1, share), F32),
        ),
        panel_row, diagonal_row, coupling, remain=3, scratch=[room, pltpu.SemaphoreType.DMA((2,)), done],
    )
    pieces = gather_pieces(solves, upper, lower, (entry,))
    near, far = pieces[:6], pieces[6:]
    split = rows == 4 and share % 128 == 0
    chosen = call(
        functools.partial(rest_kernel, rows), picked, chosen, one, coupling, remain=1,
        scratch=chunk_room(CHUNKS - 1), aliases={0: 0},
    )
    other_chosen = swap(after(far_chosen, near[2], near[5]), "scen", 1) if split else None
    half_shape, room = shape((panel // 2, panel), F32), [pltpu.VMEM((panel // 2, panel), F32)]
    turned, own_near, send_near = call(
        functools.partial(early_kernel, rows),
        (shape((panel, local), BF16), half_shape, shape((panel // 2 + 8, panel), F32)),
        chosen, entry, *near, scratch=[pltpu.VMEM((panel, panel), F32)],
    )
    got_near = swap(send_near, "scen", 1)
    if split:
        far_send = call(select_kernel, shape(far[0].shape, BF16), far[0], far[1], micros=3.0)
        other_far = [swap(far_send, "scen", 1), other_chosen]
        own_far = [*far, far_chosen]
    else:
        other_far = own_far = []
    turned, keep, entry = call(
        functools.partial(keep_kernel, rows), (shape((panel, local), BF16), half_shape, shape((8, panel), F32)),
        turned, own_near, got_near, entry, *own_far, scratch=room, aliases={0: 0},
    )
    coded = shape((size + SHORT, panel), I16)
    codes = call(functools.partial(pair_kernel, rows), (coded,) * rows, keep, entry, *other_far, scratch=room)
    arrived = [swap(codes[k], "row", k) for k in [1, *range(rows - 1, 1, -1)]]
    part = codes[0]
    steps = bits_of(layers)
    if split:
        count = layers // 2
        bulk = shape((layers * panel, share), F32)
        halved = lambda count: (shape((count * panel, share), F32), shape((count * (panel + TAIL), share), I16))
        own, send_rows = call(
            schur_kernel, (bulk, bulk), panel_row, diagonal_row, coupling, after(turned, part), micros=2.0
        )
        part = call(sum_kernel, coded, after(part, own), *arrived, micros=10.0)
        got = swap(send_rows, "scen", 1)
    else:
        own, got = lax.psum_scatter(dot(turned, coupling), "scen", scatter_dimension=1, tiled=True), []
        mine = first_row + jnp.arange(share, dtype=jnp.int32)
        own = own + jnp.where(panel_rows[:, None] == mine[None, :], border_diagonal[:, 0][None, :], F32(0.0))
        part = call(sum_kernel, coded, part, *arrived)
    if split:
        others = [swap(part, "scen", 2 * k) for k in range(layers - 1, 0, -1)]
        own, bulk_codes = call(functools.partial(bulk_pair_kernel, panel), halved(count), after(own, part), got)
        part = call(sum_kernel, coded, after(part, bulk_codes), *others, micros=5.0)
    else:
        for bit in steps:
            part = call(sum_kernel, coded, part, swap(part, "scen", 2 * bit))
    shared = [swap(part, "row", k) for k in range(1, rows)]
    if split:
        for bit in steps[:-1]:
            count //= 2
            got = swap(bulk_codes, "scen", 2 * bit)
            own, bulk_codes = call(functools.partial(bulk_sum_kernel, panel), halved(count), own, got)
        got = [swap(bulk_codes, "scen", layers)]
    if split:
        part = after(part, bulk_codes)
    joined = call(join_kernel, shape((rows * (size + TAIL), panel), I16), part, *shared[::-1])
    other = swap(joined, "scen", 1)
    own_half = call(
        functools.partial(own_kernel, rows), shape((panel // 2, panel), F32), joined
    )
    inverse_first, inverse_second = call(
        functools.partial(newton_kernel, rows), (shape((half, 3 * half), BF16), shape((half, 3 * panel), BF16)),
        own_half, other, scratch=[pltpu.VMEM((panel, panel), F32)],
    )
    out = jax.ShapeDtypeStruct((share, 1, half), F32)
    return call(
        factor_kernel, (out, out),
        inverse_first, inverse_second, own, *got,
    )


def solution(mesh):
    placed = (P("scen", None, "row"), P("scen", "row", None), P("scen", "row"), P())
    return jax.shard_map(
        shards,
        mesh=mesh,
        in_specs=placed,
        out_specs=(P("scen", "row", None), P("scen", "row", None)),
        check_vma=False,
    )
```

```python
import functools

import jax
import jax.numpy as jnp
from jax import lax
from jax.experimental import pallas as pl
from jax.experimental.pallas import tpu as pltpu
from jax.sharding import PartitionSpec as P

HALF = 256
NEWTON = 8
TAIL = 16
SHORT = 8
CHUNKS = 4
LEVELS = 32000.0
F32 = jnp.float32
BF16 = jnp.bfloat16
I16 = jnp.int16


def halves(a):
    high = a.astype(BF16)
    low = (a - high.astype(F32)).astype(BF16)
    return high, low


def left_of(a):
    high, low = halves(a)
    return jnp.concatenate([high, high, low], axis=1)


def right_of(b):
    high, low = halves(b)
    return jnp.concatenate([high, low, high], axis=0)


def dot(a, b):
    return jnp.dot(a, b, preferred_element_type=F32)


def product(a, b):
    return dot(left_of(a), right_of(b))


def nearly(pivot):
    size = jnp.abs(pivot)
    turned = pivot.T
    square = product(turned, pivot)
    norm_one = jnp.max(jnp.sum(size, axis=0, keepdims=True))
    norm_inf = jnp.max(jnp.sum(size, axis=1, keepdims=True))
    scale = F32(1.0) / (norm_one * norm_inf)
    count = pivot.shape[0]
    one = lax.broadcasted_iota(jnp.int32, pivot.shape, 0) == lax.broadcasted_iota(jnp.int32, pivot.shape, 1)
    rest = jnp.where(one, F32(1.0), F32(0.0)) - square * scale
    approx = turned * scale
    for step in range(NEWTON - 2):
        both = product(rest, jnp.concatenate([rest, approx], axis=1))
        rest, approx = both[:, :count], approx + both[:, count:]
    return approx + product(rest, approx)


def newton_beside(pivot, beside):
    approx = nearly(pivot)
    count = pivot.shape[0]
    both = product(approx, jnp.concatenate([pivot, beside], axis=1))
    stacked = jnp.concatenate([approx, both[:, count:]], axis=1)
    return 2.0 * stacked - product(both[:, :count], stacked)


def whereabouts():
    place = lax.axis_index("scen")
    return lax.axis_index("row"), lax.rem(place, 2), lax.div(place, 2)


def aligned(index, size):
    return pl.multiple_of(index * size, size)


def encode(values, out_ref, base, tail_rows, diagonal=None):
    rows, lanes = values.shape
    top = jnp.maximum(jnp.max(jnp.abs(values), axis=0, keepdims=True), F32(1e-30))
    power = jnp.ceil(jnp.log2(top))
    unit = jnp.exp2(power)
    mantissa = jnp.ceil(top / unit * F32(16384.0))
    scale = mantissa * unit * F32(1.0 / (16384.0 * LEVELS))
    codes = jnp.round(values * (F32(1.0) / scale)).astype(jnp.int32)
    out_ref[base:base + rows, :] = codes.astype(I16)
    row = lax.broadcasted_iota(jnp.int32, (tail_rows, lanes), 0)
    tail = jnp.where(row == 0, power, jnp.where(row == 1, mantissa, F32(0.0)))
    if diagonal is not None:
        coarse = jnp.floor(diagonal * F32(64.0))
        fine = (diagonal * F32(64.0) - coarse) * F32(4096.0)
        tail = jnp.where(row == 2, coarse, jnp.where(row == 3, fine, tail))
    out_ref[base + rows:base + rows + tail_rows, :] = tail.astype(jnp.int32).astype(I16)


def decode(ref, base, rows, tail_rows):
    tail = ref[base + rows:base + rows + tail_rows, :].astype(jnp.int32).astype(F32)
    scale = tail[1:2] * jnp.exp2(tail[0:1]) * F32(1.0 / (16384.0 * LEVELS))
    diagonal = tail[2:3] * F32(1.0 / 64.0) + tail[3:4] * F32(1.0 / (64.0 * 4096.0))
    return ref[base:base + rows, :].astype(jnp.int32).astype(F32) * scale, diagonal


def turn_kernel(solves_ref, upper_ref, lower_ref, solves_copy, done):
    half = upper_ref.shape[0]
    copies = [
        pltpu.make_async_copy(solves_ref.at[:, pl.ds(i * half, half)], solves_copy.at[i], done.at[i]) for i in (0, 1)
    ]
    for copy in copies:
        copy.start()
    for i, out_ref in enumerate((upper_ref, lower_ref)):
        copies[i].wait()
        out_ref[...] = solves_copy[i].T


def order_of(rows):
    row = lax.axis_index("row")
    return [row ^ 3, row, row ^ 1, row ^ 2] if rows == 4 else list(range(CHUNKS))


def fetch(source_ref, target_ref, done, blocks):
    size = target_ref.shape[1]
    copies = [
        pltpu.make_async_copy(source_ref.at[pl.ds(aligned(block, size), size), :], target_ref.at[i], done.at[i])
        for i, block in enumerate(blocks)
    ]
    for copy in copies:
        copy.start()
    return copies


def pick_kernel(
    rows, panel_ref, own_diagonal_ref, coupling_ref,
    chosen_ref, far_ref, entry_ref, one_ref, panel_out, diagonal_out, coupling_copy, small_done, done,
):
    small = [
        pltpu.make_async_copy(panel_ref, panel_out, small_done.at[0]),
        pltpu.make_async_copy(own_diagonal_ref, diagonal_out, small_done.at[1]),
    ]
    for copy in small:
        copy.start()
    block = order_of(rows)[0]
    copies = fetch(coupling_ref, coupling_copy, done, [block])
    for copy in small:
        copy.wait()
    columns, panel = one_ref.shape
    share = diagonal_out.shape[1]
    first_column = lax.axis_index("row") * columns
    first_row = first_column + lax.axis_index("scen") * share
    here = panel_out[...] - first_column == lax.broadcasted_iota(jnp.int32, (columns, panel), 0)
    one_ref[...] = jnp.where(here, F32(1.0), F32(0.0)).astype(BF16)
    owned = panel_out[...] - first_row == lax.broadcasted_iota(jnp.int32, (share, panel), 0)
    own = jnp.broadcast_to(diagonal_out[...], (8, share)).T[:, :1]
    entry = jnp.sum(jnp.where(owned, own, F32(0.0)), axis=0, keepdims=True)
    entry_ref[...] = jnp.broadcast_to(entry, entry_ref.shape)
    copies[0].wait()
    size = far_ref.shape[0]
    far_ref[...] = dot(coupling_copy[0], one_ref[...]).astype(BF16)
    chosen_ref[pl.ds(aligned(block, size), size), :] = far_ref[...]


def rest_kernel(rows, chosen_in, one_ref, coupling_ref, chosen_ref, coupling_copy, done):
    blocks = order_of(rows)[1:]
    size = coupling_copy.shape[1]
    for i, copy in enumerate(fetch(coupling_ref, coupling_copy, done, blocks)):
        copy.wait()
        chosen_ref[pl.ds(aligned(blocks[i], size), size), :] = dot(coupling_copy[i], one_ref[...]).astype(BF16)


def early_kernel(rows, chosen_ref, entry_ref, *refs):
    *pieces, turned_ref, own_ref, send_ref, terms_ref = refs
    row, core, _ = whereabouts()
    if len(pieces) == 1:
        turned_ref[...] = pieces[0][...]
    else:
        half, width = pieces[0].shape
        for i, piece in enumerate(pieces):
            start = aligned(row ^ (i // 2), width)
            turned_ref[i % 2 * half:(i % 2 + 1) * half, pl.ds(start, width)] = piece[...]
        start = aligned(row ^ (len(pieces) // 2), width)
        turned_ref[:, pl.ds(start, width)] = jnp.zeros((2 * half, width), BF16)
    terms_ref[...] = dot(turned_ref[...], chosen_ref[...])
    size = own_ref.shape[0] // rows
    for out_ref, whose in ((own_ref, core), (send_ref, 1 - core)):
        for k in range(rows):
            out_ref[k * size:(k + 1) * size, :] = terms_ref[pl.ds(aligned(whose * rows + (row ^ k), size), size), :]
    send_ref[rows * size:, :] = entry_ref[...]


def select_kernel(upper_ref, lower_ref, out_ref):
    out_ref[...] = jnp.where(whereabouts()[1] == 0, lower_ref[...], upper_ref[...])


def add_far(rows, block, chosen, far_ref):
    row = lax.axis_index("row")
    size = far_ref.shape[0] // rows
    far_ref[...] = dot(block, chosen)
    return [far_ref[pl.ds(aligned(row ^ k, size), size), :] for k in range(rows)]


def keep_kernel(rows, turned_in, own_ref, got_ref, entry_ref, *refs):
    *far, turned_ref, keep_ref, both_ref, far_ref = refs
    row, core, _ = whereabouts()
    half = keep_ref.shape[0]
    size = half // rows
    both_ref[...] = jnp.broadcast_to(entry_ref[:1, :] + got_ref[half:half + 1, :], both_ref.shape)
    keep_ref[...] = own_ref[...] + got_ref[:half, :]
    if far:
        upper_ref, lower_ref, chosen_ref = far
        width = upper_ref.shape[1]
        start = aligned(row ^ (rows - 1), width)
        turned_ref[:half, pl.ds(start, width)] = upper_ref[...]
        turned_ref[half:, pl.ds(start, width)] = lower_ref[...]
        block = jnp.where(core == 0, upper_ref[...], lower_ref[...])
        for k, piece in enumerate(add_far(rows, block, chosen_ref[...], far_ref)):
            keep_ref[k * size:(k + 1) * size, :] += piece


def pair_kernel(rows, keep_ref, entry_ref, *refs):
    *far, far_ref = refs
    far, out_refs = far[:-rows], far[-rows:]
    size = keep_ref.shape[0] // rows
    pieces = add_far(rows, far[0][...], far[1][...], far_ref) if far else None
    for k, out_ref in enumerate(out_refs):
        value = keep_ref[k * size:(k + 1) * size, :]
        encode(value + pieces[k] if far else value, out_ref, 0, SHORT, entry_ref[:1, :])


def sum_kernel(*refs):
    *in_refs, out_ref = refs
    size = out_ref.shape[0] - SHORT
    parts = [decode(ref, 0, size, SHORT) for ref in in_refs]
    encode(sum(p[0] for p in parts), out_ref, 0, SHORT, sum(p[1] for p in parts))


def join_kernel(*refs):
    *in_refs, out_ref = refs
    size = in_refs[0].shape[0] - SHORT
    for k, ref in enumerate(in_refs[:1] + in_refs[:0:-1]):
        start = k * (size + TAIL)
        out_ref[start:start + size, :] = ref[:size, :]
        tail = ref[size:, :].astype(jnp.int32)
        out_ref[start + size:start + size + TAIL, :] = jnp.concatenate([tail, jnp.zeros_like(tail)], axis=0).astype(I16)


def place_pieces(row, whose, ref, pivots_ref, rows, base):
    panel = pivots_ref.shape[1]
    size = panel // (2 * rows)
    index = lax.broadcasted_iota(jnp.int32, (size, panel), 1)
    for k in range(rows):
        start = aligned(whose * rows + (row ^ k), size)
        values, diagonal = decode(ref, k * (size + TAIL), size, TAIL)
        at = lax.broadcasted_iota(jnp.int32, (size, panel), 0) + start == index
        pivots_ref[pl.ds(start - base, size), :] = values + jnp.where(at, diagonal, F32(0.0))


def own_kernel(rows, own_ref, half_ref):
    row, core, _ = whereabouts()
    place_pieces(row, core, own_ref, half_ref, rows, core * half_ref.shape[0])


def newton_kernel(rows, half_ref, other_ref, inverse_ref, second_ref, pivots_ref):
    row, core, _ = whereabouts()
    half = half_ref.shape[0]
    pivots_ref[pl.ds(aligned(core, half), half), :] = half_ref[...]
    place_pieces(row, 1 - core, other_ref, pivots_ref, rows, 0)
    both = newton_beside(pivots_ref[:half, :half], pivots_ref[:half, half:])
    inverse_first = both[:, :half]
    inverse_ref[...] = inverse_first
    corner = pivots_ref[half:, :half]
    pivot = pivots_ref[half:, half:] - product(corner, both[:, half:])
    second_ref[...] = newton_beside(pivot, -product(corner, inverse_first))


def schur_kernel(panel_ref, own_diagonal_ref, coupling_ref, turned_ref, keep_ref, send_ref):
    row, core, layer = whereabouts()
    panel, share = turned_ref.shape[0], keep_ref.shape[1]
    first_row = row * coupling_ref.shape[1] + (2 * layer + core) * share
    layers = keep_ref.shape[0] // panel
    for position, k in enumerate(reversed_order(layers)):
        start = aligned(layer ^ k, 2 * share)
        both = dot(turned_ref[...], coupling_ref[:, pl.ds(start, 2 * share)])
        rows = slice(position * panel, (position + 1) * panel)
        one, two = both[:, :share], both[:, share:]
        kept = jnp.where(core == 0, one, two)
        if position == 0:
            wanted = jnp.broadcast_to(panel_ref[...].astype(F32), (share, panel)).T.astype(jnp.int32)
            here = wanted - first_row == lax.broadcasted_iota(jnp.int32, (panel, share), 1)
            kept = kept + jnp.where(here, own_diagonal_ref[...], F32(0.0))
        keep_ref[rows, :] = kept
        send_ref[rows, :] = jnp.where(core == 0, two, one)


def bulk_pair_kernel(panel, keep_ref, got_ref, own_ref, coded_ref):
    half = own_ref.shape[0]
    own_ref[...] = keep_ref[:half, :] + got_ref[:half, :]
    for i in range(half // panel):
        part = slice(half + i * panel, half + (i + 1) * panel)
        encode(keep_ref[part, :] + got_ref[part, :], coded_ref, i * (panel + TAIL), TAIL)


def bulk_sum_kernel(panel, keep_ref, got_ref, own_ref, coded_ref):
    half = own_ref.shape[0]
    for i in range(keep_ref.shape[0] // panel):
        value = keep_ref[i * panel:(i + 1) * panel, :] + decode(got_ref, i * (panel + TAIL), panel, TAIL)[0]
        if i * panel < half:
            own_ref[i * panel:(i + 1) * panel, :] = value
        else:
            encode(value, coded_ref, (i - half // panel) * (panel + TAIL), TAIL)


def product_turned(a, b):
    high, low = halves(b)
    right = jnp.concatenate([high, low, high], axis=1)
    return lax.dot_general(left_of(a), right, (((1,), (1,)), ((), ())), preferred_element_type=F32)


def factor_kernel(inverse_first_ref, inverse_second_ref, rows_ref, *refs):
    *got, first_out, second_out = refs
    panel = rows_ref.shape[0]
    half = panel // 2
    rows = rows_ref[...]
    for ref in got:
        rows = rows + decode(ref, 0, panel, TAIL)[0]
    first, second = rows[:half], rows[half:]
    first_out[...] = product_turned(first.T, inverse_first_ref[...])[:, None, :]
    second_out[...] = product_turned(jnp.concatenate([second.T, first.T], axis=1), inverse_second_ref[...])[:, None, :]


def call(kernel, out_shape, *args, scratch=(), remain=0, micros=0.0, aliases=None):
    hbm = pl.BlockSpec(memory_space=pltpu.HBM)
    vmem = pl.BlockSpec(memory_space=pltpu.VMEM)
    stay = len(args) - remain
    args = args[:stay] + tuple(pltpu.with_memory_space_constraint(x, pltpu.HBM) for x in args[stay:])
    return pl.pallas_call(
        kernel,
        name=getattr(kernel, "func", kernel).__name__,
        out_shape=out_shape,
        in_specs=[vmem] * (len(args) - remain) + [hbm] * remain,
        out_specs=jax.tree.map(lambda _: vmem, out_shape),
        scratch_shapes=scratch,
        input_output_aliases=aliases or {},
        compiler_params=pltpu.CompilerParams(vmem_limit_bytes=12 << 20),
        cost_estimate=pl.CostEstimate(flops=int(micros * 1.15e9), bytes_accessed=1024, transcendentals=0),
    )(*args)


def swap(x, axis, bit):
    count = lax.axis_size(axis)
    return lax.ppermute(x, axis, [(i, i ^ bit) for i in range(count)])


def after(x, *others):
    return lax.optimization_barrier((x,) + others)[0]


def bits_of(count):
    return [1 << i for i in range(count.bit_length() - 1)]


def reversed_order(count):
    width = count.bit_length() - 1
    return [int(f"{p:0{width}b}"[::-1], 2) for p in range(count)]


def turn(solves, rows):
    block, panel = solves.shape
    if rows != 4:
        return None, None
    half = pltpu.VMEM((panel // 2, block), BF16)
    return call(
        turn_kernel, (half, half), solves, remain=1,
        scratch=[pltpu.VMEM((2, block, panel // 2), BF16), pltpu.SemaphoreType.DMA((2,))],
    )


def gather_pieces(solves, upper, lower, ready):
    if upper is None:
        return [lax.all_gather(solves.T, "row", axis=1, tiled=True)]
    lower_x, upper_y = swap(lower, "row", 1), swap(upper, "row", 2)
    upper_x, lower_y = swap(upper, "row", 1), swap(lower, "row", 2)
    upper_far, lower_far = swap(after(upper_y, *ready), "row", 1), swap(after(lower_x, *ready), "row", 2)
    return [upper, lower, upper_x, lower_x, upper_y, lower_y, upper_far, lower_far]


def shards(coupling, solves, border_diagonal, panel_rows):
    half = HALF
    coupling, solves = coupling[0], solves[0]
    local, row_count = coupling.shape
    panel = solves.shape[1]
    scen, rows = lax.axis_size("scen"), lax.axis_size("row")
    layers = scen // 2
    row, place = lax.axis_index("row"), lax.axis_index("scen")
    share = row_count // scen
    size = panel // (2 * rows)
    shape = pltpu.VMEM
    panel_row, diagonal_row = panel_rows[None, :], border_diagonal.T
    first_row = row * row_count + place * share
    picked, part_picked = shape((local, panel), BF16), shape((local // CHUNKS, panel), BF16)
    chunk_room = lambda count: [
        pltpu.VMEM((count, local // CHUNKS, row_count), BF16), pltpu.SemaphoreType.DMA((count,))
    ]
    room, done = chunk_room(1)
    upper, lower = turn(solves, rows)
    chosen, far_chosen, entry, one, panel_row, diagonal_row = call(
        functools.partial(pick_kernel, rows),
        (
            picked, part_picked, shape((8, panel), F32), shape((row_count, panel), BF16),
            shape((1, panel), jnp.int32), shape((1, share), F32),
        ),
        panel_row, diagonal_row, coupling, remain=3, scratch=[room, pltpu.SemaphoreType.DMA((2,)), done],
    )
    pieces = gather_pieces(solves, upper, lower, (entry,))
    near, far = pieces[:6], pieces[6:]
    split = rows == 4 and share % 128 == 0
    chosen = call(
        functools.partial(rest_kernel, rows), picked, chosen, one, coupling, remain=1,
        scratch=chunk_room(CHUNKS - 1), aliases={0: 0},
    )
    other_chosen = swap(after(far_chosen, near[2], near[5]), "scen", 1) if split else None
    half_shape, room = shape((panel // 2, panel), F32), [pltpu.VMEM((panel // 2, panel), F32)]
    turned, own_near, send_near = call(
        functools.partial(early_kernel, rows),
        (shape((panel, local), BF16), half_shape, shape((panel // 2 + 8, panel), F32)),
        chosen, entry, *near, scratch=[pltpu.VMEM((panel, panel), F32)],
    )
    got_near = swap(send_near, "scen", 1)
    if split:
        far_send = call(select_kernel, shape(far[0].shape, BF16), far[0], far[1], micros=3.0)
        other_far = [swap(far_send, "scen", 1), other_chosen]
        own_far = [*far, far_chosen]
    else:
        other_far = own_far = []
    turned, keep, entry = call(
        functools.partial(keep_kernel, rows), (shape((panel, local), BF16), half_shape, shape((8, panel), F32)),
        turned, own_near, got_near, entry, *own_far, scratch=room, aliases={0: 0},
    )
    coded = shape((size + SHORT, panel), I16)
    codes = call(functools.partial(pair_kernel, rows), (coded,) * rows, keep, entry, *other_far, scratch=room)
    arrived = [swap(codes[k], "row", k) for k in [1, *range(rows - 1, 1, -1)]]
    part = codes[0]
    steps = bits_of(layers)
    if split:
        count = layers // 2
        bulk = shape((layers * panel, share), F32)
        halved = lambda count: (shape((count * panel, share), F32), shape((count * (panel + TAIL), share), I16))
        own, send_rows = call(
            schur_kernel, (bulk, bulk), panel_row, diagonal_row, coupling, after(turned, part), micros=2.0
        )
        part = call(sum_kernel, coded, after(part, own), *arrived, micros=10.0)
        got = swap(send_rows, "scen", 1)
    else:
        own, got = lax.psum_scatter(dot(turned, coupling), "scen", scatter_dimension=1, tiled=True), []
        mine = first_row + jnp.arange(share, dtype=jnp.int32)
        own = own + jnp.where(panel_rows[:, None] == mine[None, :], border_diagonal[:, 0][None, :], F32(0.0))
        part = call(sum_kernel, coded, part, *arrived)
    if split:
        others = [swap(part, "scen", 2 * k) for k in range(layers - 1, 0, -1)]
        own, bulk_codes = call(functools.partial(bulk_pair_kernel, panel), halved(count), after(own, part), got)
        part = call(sum_kernel, coded, after(part, bulk_codes), *others, micros=5.0)
    else:
        for bit in steps:
            part = call(sum_kernel, coded, part, swap(part, "scen", 2 * bit))
    shared = [swap(part, "row", k) for k in range(1, rows)]
    if split:
        for bit in steps[:-1]:
            count //= 2
            got = swap(bulk_codes, "scen", 2 * bit)
            own, bulk_codes = call(functools.partial(bulk_sum_kernel, panel), halved(count), own, got)
        got = [swap(bulk_codes, "scen", layers)]
    if split:
        part = after(part, bulk_codes)
    joined = call(join_kernel, shape((rows * (size + TAIL), panel), I16), part, *shared[::-1])
    other = swap(joined, "scen", 1)
    own_half = call(
        functools.partial(own_kernel, rows), shape((panel // 2, panel), F32), joined
    )
    inverse_first, inverse_second = call(
        functools.partial(newton_kernel, rows), (shape((half, half), F32), shape((half, panel), F32)),
        own_half, other, scratch=[pltpu.VMEM((panel, panel), F32)],
    )
    out = jax.ShapeDtypeStruct((share, 1, half), F32)
    return call(
        factor_kernel, (out, out),
        inverse_first, inverse_second, own, *got,
    )


def solution(mesh):
    placed = (P("scen", None, "row"), P("scen", "row", None), P("scen", "row"), P())
    return jax.shard_map(
        shards,
        mesh=mesh,
        in_specs=placed,
        out_specs=(P("scen", "row", None), P("scen", "row", None)),
        check_vma=False,
    )
```
